512 devices in a mesh: inp: 64 (over z, y_hi, core), tm: 8 (over x, y_lo).
Axes of the slice: x: 4, y: 4 (y_hi: 2, y_lo: 2; y = y_hi * 2 + y_lo), z: 16, core: 2. Of those that a mesh axis runs over, the one named last changes fastest.
Arguments:
- samples: bfloat16 [512, 262144], P('inp', 'tm'), may hold values from -6 to 6
- gains: float32 [2, 256, 512], P(None, None, 'inp'), may hold values from -4 to 4
Outputs:
- spectra: bfloat16 [2, 256, 512, 128], P(None, None, 'inp', 'tm')
- visibilities: float32 [512, 256, 512], P('tm', 'inp')
The draws below stay inside these ranges and needn't reach their ends.
All inputs are finite; a program needn't handle non-finite values.
Results may differ from the reference program's by a relative error of at most 0.0057.
Values may be sent and summed in bfloat16 or wider, within the bound.
No kernel may reach another device: no remote copies, remote signals or barrier semaphores. Data moves between devices by JAX's collectives and lax.ppermute only.
A program may use at most 64 MiB of HBM per device.

```python
import math
import jax
import jax.numpy as jnp
from jax import lax

INPUTS = 512
NFFT = 2048
CH = 256
FIRST = 384
TAPS = 4
FRAMES = 128
SAMPLES = 262144


def level_of(key, dims, cuts, least, top_value):
    factor_of = 1.0
    for dim, shards_of in cuts:
        steps = jax.random.uniform(jax.random.fold_in(jax.random.fold_in(key, 6), dim), (shards_of,), jnp.float32, least / len(cuts), top_value / len(cuts))
        factor_of = factor_of * jnp.repeat(jnp.exp(steps), dims[dim] // shards_of).reshape((-1,) + (1,) * (len(dims) - 1 - dim))
    return factor_of


def bell_draw(key, dims, width, limit, cuts=(), held_as=jnp.bfloat16):
    factor_of = level_of(key, dims, cuts, -0.22, 0.18) if cuts else 1.0
    values = jax.random.normal(key, dims, jnp.float32) * width * factor_of
    return jnp.minimum(jnp.maximum(values, -limit), limit).astype(held_as)


def setup_inputs(seed: int = 0) -> dict:
    arg_keys = jax.random.split(jax.random.key(seed), 3)
    samples = bell_draw(arg_keys[0], (INPUTS, SAMPLES), 1.0, 6.0, ((0, 64), (1, 8)))
    gains = bell_draw(arg_keys[1], (2, CH, INPUTS), 1.0, 4.0, ((2, 64),), jnp.float32)
    return dict(samples=samples, gains=gains)


def filter_window():
    length = TAPS * NFFT
    position = jnp.arange(length, dtype=jnp.float32)
    centred = (position - 0.5 * length + 0.5) / NFFT
    hann_taper = 0.5 - 0.5 * jnp.cos(2.0 * math.pi * (position + 0.5) / length)
    return jnp.sinc(centred) * hann_taper

def build_table(window):
    norm_scale = 1.0 / jnp.sqrt(jnp.sum(window * window))
    sample = jnp.arange(NFFT, dtype=jnp.int32)[:, None]
    channel = FIRST + jnp.arange(CH, dtype=jnp.int32)[None, :]
    phase_index = sample * channel % NFFT
    phase_angle = 2.0 * math.pi / NFFT * phase_index.astype(jnp.float32)
    cosine = jnp.cos(phase_angle) * norm_scale
    sine = -jnp.sin(phase_angle) * norm_scale
    return jnp.concatenate([cosine, sine], axis=1).astype(jnp.bfloat16)

def reference(samples, gains):
    window = filter_window()
    twiddle = build_table(window)
    window_taps = window.reshape(TAPS, NFFT)
    groups = 8
    per_group = INPUTS // groups

    def channelize(operands):
        row_block, gain_block = operands
        padding = jnp.zeros((per_group, (TAPS - 1) * NFFT), jnp.bfloat16)
        extended = jnp.concatenate([padding, row_block], axis=1).reshape(per_group, FRAMES + TAPS - 1, NFFT)
        summed = jnp.zeros((per_group, FRAMES, NFFT), jnp.float32)
        for tap_index in range(TAPS):
            summed = summed + window_taps[tap_index] * extended[:, tap_index:tap_index + FRAMES, :].astype(jnp.float32)
        tapped = summed.astype(jnp.bfloat16)
        direct = jnp.dot(tapped.reshape(per_group * FRAMES, NFFT), twiddle, preferred_element_type=jnp.float32)
        direct = direct.reshape(per_group, FRAMES, 2, CH).transpose(2, 3, 0, 1)
        real_part = gain_block[0][:, :, None] * direct[0] - gain_block[1][:, :, None] * direct[1]
        imag_part = gain_block[0][:, :, None] * direct[1] + gain_block[1][:, :, None] * direct[0]
        return jnp.stack([real_part, imag_part]).astype(jnp.bfloat16)
    row_blocks = samples.reshape(groups, per_group, SAMPLES)
    gain_blocks = gains.reshape(2, CH, groups, per_group).transpose(2, 0, 1, 3)
    pieces = lax.map(channelize, (row_blocks, gain_blocks))
    spectra = pieces.transpose(1, 2, 0, 3, 4).reshape(2, CH, INPUTS, FRAMES)
    row_index = jnp.arange(INPUTS, dtype=jnp.int32)
    upper_mask = row_index[:, None] <= row_index[None, :]

    def correlate(channel_pair):
        real_part = channel_pair[0]
        imag_part = channel_pair[1]
        stacked = jnp.concatenate([real_part, imag_part], axis=1)
        twisted = jnp.concatenate([imag_part, -real_part], axis=1)
        re_part = jnp.dot(stacked, stacked.T, preferred_element_type=jnp.float32)
        im_part = jnp.dot(twisted, stacked.T, preferred_element_type=jnp.float32)
        return jnp.where(upper_mask, re_part, im_part) / FRAMES
    packed = lax.map(correlate, spectra.transpose(1, 0, 2, 3))
    return (spectra, packed.transpose(1, 0, 2))
```

```python
import math

import jax
import jax.numpy as jnp
import numpy as np
from jax import lax
from jax.sharding import PartitionSpec as P

NFFT = 2048
CH = 256
FIRST = 384
TAPS = 4


def filter_window():
    length = TAPS * NFFT
    position = np.arange(length, dtype=np.float64)
    centred = (position - 0.5 * length + 0.5) / NFFT
    hann_taper = 0.5 - 0.5 * np.cos(2.0 * math.pi * (position + 0.5) / length)
    return np.sinc(centred) * hann_taper


def build_table(window):
    norm_scale = 1.0 / np.sqrt(np.sum(window * window))
    sample = np.arange(NFFT)[:, None]
    channel = FIRST + np.arange(CH)[None, :]
    phase_angle = 2.0 * math.pi / NFFT * (sample * channel % NFFT)
    cosine = np.cos(phase_angle) * norm_scale
    sine = -np.sin(phase_angle) * norm_scale
    return np.concatenate([cosine, sine], axis=1).astype(jnp.bfloat16)


def body(samples, gains):
    inputs_here = samples.shape[0]
    frames_here = samples.shape[1] // NFFT
    times = lax.axis_size("tm")
    groups = lax.axis_size("inp")
    near = 8
    far = groups // near
    per_group = CH // groups
    inputs_all = inputs_here * groups
    frames_all = frames_here * times

    window = filter_window()
    twiddle = jnp.asarray(build_table(window))
    window_taps = jnp.asarray(window.astype(np.float32).reshape(TAPS, NFFT))

    history = lax.ppermute(
        samples[:, (frames_here - TAPS + 1) * NFFT :],
        "tm",
        [(source, source + 1) for source in range(times - 1)],
    )
    extended = jnp.concatenate([history, samples], axis=1).reshape(
        inputs_here, frames_here + TAPS - 1, NFFT
    )
    summed = jnp.zeros((inputs_here, frames_here, NFFT), jnp.float32)
    for tap_index in range(TAPS):
        summed = summed + window_taps[tap_index] * extended[
            :, tap_index : tap_index + frames_here, :
        ].astype(jnp.float32)
    tapped = summed.astype(jnp.bfloat16)
    direct = jnp.einsum("ifn,nk->kif", tapped, twiddle, preferred_element_type=jnp.float32)
    direct = direct.reshape(2, CH, inputs_here, frames_here)
    real_part = gains[0][:, :, None] * direct[0] - gains[1][:, :, None] * direct[1]
    imag_part = gains[0][:, :, None] * direct[1] + gains[1][:, :, None] * direct[0]
    spectra = jnp.stack([real_part, imag_part]).astype(jnp.bfloat16)

    near_groups = [[a * near + b for b in range(near)] for a in range(far)]
    far_groups = [[a * near + b for a in range(far)] for b in range(near)]
    block = inputs_here * frames_here
    arranged = spectra.reshape(2, far, near, per_group, block).transpose(2, 1, 0, 3, 4)
    arranged = arranged.reshape(near, far * 2 * per_group, block)
    first = lax.all_to_all(arranged, "inp", 0, 0, axis_index_groups=near_groups)
    first = first.reshape(near, far, 2 * per_group, block).transpose(1, 0, 2, 3)
    first = first.reshape(far, near * 2 * per_group, block)
    second = lax.all_to_all(first, "inp", 0, 0, axis_index_groups=far_groups)
    mine = second.reshape(groups, 2, per_group, inputs_here, frames_here)
    mine = mine.transpose(2, 1, 4, 0, 3).reshape(per_group * 2 * frames_here, inputs_all)

    every = lax.all_gather(mine, "tm", axis=0, tiled=False)
    every = every.reshape(times, per_group, 2, frames_here, inputs_all)
    right = every.transpose(1, 2, 0, 3, 4).reshape(per_group, 2, frames_all, inputs_all)
    rows = inputs_all // times
    start = lax.axis_index("tm") * rows
    left = lax.dynamic_slice_in_dim(right, start, rows, axis=3)
    twisted = jnp.stack([left[:, 1], -left[:, 0]], axis=1)
    re_part = jnp.einsum("kpfi,kpfj->ikj", left, right, preferred_element_type=jnp.float32)
    im_part = jnp.einsum("kpfi,kpfj->ikj", twisted, right, preferred_element_type=jnp.float32)
    row_index = start + jnp.arange(rows, dtype=jnp.int32)
    col_index = jnp.arange(inputs_all, dtype=jnp.int32)
    upper_mask = row_index[:, None, None] <= col_index[None, None, :]
    visibilities = jnp.where(upper_mask, re_part, im_part) / frames_all
    return (spectra, visibilities)


def solution(mesh):
    return jax.shard_map(
        body,
        mesh=mesh,
        in_specs=(P("inp", "tm"), P(None, None, "inp")),
        out_specs=(P(None, None, "inp", "tm"), P("tm", "inp", None)),
        check_vma=False,
    )
```

```python
import math

import jax
import jax.numpy as jnp
import numpy as np
from jax import lax
from jax.experimental import pallas as pl
from jax.experimental.pallas import tpu as pltpu
from jax.sharding import PartitionSpec as P

NFFT = 2048
CH = 256
FIRST = 384
TAPS = 4
EARLY = 4
STEP = 512
LANES = 128
VMEM = pl.BlockSpec(memory_space=pltpu.VMEM)
SMEM = pl.BlockSpec(memory_space=pltpu.SMEM)
PARAMS = pltpu.CompilerParams(vmem_limit_bytes=32 * 1024 * 1024)


def filter_window():
    length = TAPS * NFFT
    position = np.arange(length, dtype=np.float64)
    centred = (position - 0.5 * length + 0.5) / NFFT
    hann_taper = 0.5 - 0.5 * np.cos(2.0 * math.pi * (position + 0.5) / length)
    return np.sinc(centred) * hann_taper


def build_table(window):
    norm_scale = 1.0 / np.sqrt(np.sum(window * window))
    sample = np.arange(NFFT)[:, None]
    channel = FIRST + np.arange(CH)[None, :]
    phase_angle = 2.0 * math.pi / NFFT * (sample * channel % NFFT)
    cosine = np.cos(phase_angle) * norm_scale
    sine = -np.sin(phase_angle) * norm_scale
    return np.concatenate([cosine, sine], axis=1).astype(jnp.bfloat16)


def tap_frames(frame_at, window_ref, tapped_ref, first, count):
    for pair in range(0, count, 2):
        for low in range(0, NFFT, STEP):
            sums = []
            for frame in (first + pair, first + pair + 1):
                total = None
                for tap in range(TAPS):
                    values = frame_at(frame - TAPS + 1 + tap, low).astype(jnp.float32)
                    term = window_ref[tap : tap + 1, low : low + STEP] * values
                    total = term if total is None else total + term
                sums.append(total)
            inputs_here = sums[0].shape[0]
            tapped_ref[pair * inputs_here : (pair + 2) * inputs_here, low : low + STEP] = (
                jnp.concatenate(sums, axis=0).astype(jnp.bfloat16)
            )


def late_frames_kernel(samples_ref, window_ref, twiddle_ref, direct_ref, tapped_ref):
    frames_here = samples_ref.shape[1] // NFFT

    def frame_at(frame, low):
        start = frame * NFFT + low
        return samples_ref[:, start : start + STEP]

    tap_frames(frame_at, window_ref, tapped_ref, EARLY, frames_here - EARLY)
    direct_ref[...] = jnp.dot(
        tapped_ref[...], twiddle_ref[...], preferred_element_type=jnp.float32
    )


def channels_kernel(
    groups,
    history_ref,
    samples_ref,
    window_ref,
    twiddle_ref,
    late_ref,
    gains_ref,
    spectra_ref,
    parcels_ref,
    tapped_ref,
    early_ref,
    rows_ref,
    columns_ref,
    turned_ref,
):
    inputs_here = samples_ref.shape[0]
    frames_here = EARLY + late_ref.shape[0] // inputs_here
    per_group = CH // groups
    parts = 2 * per_group
    slabs = CH // LANES

    def frame_at(frame, low):
        if frame < 0:
            start = (frame + TAPS - 1) * NFFT + low
            return history_ref[:, start : start + STEP]
        start = frame * NFFT + low
        return samples_ref[:, start : start + STEP]

    tap_frames(frame_at, window_ref, tapped_ref, 0, EARLY)
    early_ref[...] = jnp.dot(
        tapped_ref[...], twiddle_ref[...], preferred_element_type=jnp.float32
    )
    gain_re = gains_ref[0]
    gain_im = gains_ref[1]
    for frame in range(frames_here):
        if frame < EARLY:
            direct = early_ref[frame * inputs_here : (frame + 1) * inputs_here, :]
        else:
            start = (frame - EARLY) * inputs_here
            direct = late_ref[start : start + inputs_here, :]
        direct_re = direct[:, :CH]
        direct_im = direct[:, CH:]
        rows = pl.ds(frame, inputs_here, stride=frames_here)
        real_part = gain_re * direct_re - gain_im * direct_im
        imag_part = gain_re * direct_im + gain_im * direct_re
        for slab in range(slabs):
            columns = slice(slab * LANES, (slab + 1) * LANES)
            rows_ref[slab, rows, :] = real_part[:, columns]
            rows_ref[slabs + slab, rows, :] = imag_part[:, columns]
    for part in range(2):
        for slab in range(slabs):
            values = rows_ref[part * slabs + slab]
            start = slab * LANES
            spectra_ref[part, :, start : start + LANES] = values.astype(jnp.bfloat16)
            start += part * CH
            columns_ref[start : start + LANES, :] = values.T
    blocks = []
    for channel in range(per_group):
        for part in range(2):
            blocks.append(columns_ref[pl.ds(part * CH + channel, groups, stride=per_group), :])
    lanes = inputs_here * frames_here
    granule = lax.broadcasted_iota(jnp.int32, (groups, lanes), 1) // frames_here
    distance = parts // 2
    while distance:
        upper = (granule & distance) != 0
        shift = distance * frames_here
        for index in range(parts):
            if index & distance:
                continue
            low, high = blocks[index], blocks[index + distance]
            blocks[index] = jnp.where(upper, pltpu.roll(high, shift, 1), low)
            blocks[index + distance] = jnp.where(upper, high, pltpu.roll(low, lanes - shift, 1))
        distance //= 2
    for index in range(inputs_here):
        turned_ref[pl.ds(index, groups, stride=inputs_here), :] = blocks[index]
    parcels_ref[...] = turned_ref[...].astype(jnp.bfloat16)


def spread_kernel(mine_ref, copies_ref):
    turned = mine_ref[...].T
    for index in range(copies_ref.shape[0]):
        copies_ref[index] = turned


def correlate_kernel(frames_all, place_ref, every_ref, packed_ref):
    times, lines, inputs_all = every_ref.shape
    rows, per_group, _ = packed_ref.shape
    frames_here = lines // (2 * per_group)
    place = place_ref[0]
    wide = 2 * rows
    base = pl.multiple_of((place // 2) * wide, wide)
    odd = place % 2 == 1
    row_index = place * rows + lax.broadcasted_iota(jnp.int32, (rows, inputs_all), 0)
    col_index = lax.broadcasted_iota(jnp.int32, (rows, inputs_all), 1)
    upper = row_index <= col_index
    for channel in range(per_group):
        start = channel * 2 * frames_here
        right, left = [], []
        for time in range(times):
            right.append(every_ref[time, start : start + 2 * frames_here, :])
            real_part = every_ref[time, start : start + frames_here, pl.ds(base, wide)]
            imag_part = every_ref[
                time, start + frames_here : start + 2 * frames_here, pl.ds(base, wide)
            ]
            plain = jnp.concatenate([real_part, imag_part], axis=0)
            twisted = jnp.concatenate([imag_part, -real_part], axis=0)
            left.append(jnp.concatenate([plain, twisted], axis=1))
        both = lax.dot_general(
            jnp.concatenate(left, axis=0),
            jnp.concatenate(right, axis=0),
            (((0,), (0,)), ((), ())),
            preferred_element_type=jnp.float32,
        )
        re_part = jnp.where(odd, both[rows:wide], both[:rows])
        im_part = jnp.where(odd, both[wide + rows :], both[wide : wide + rows])
        packed_ref[:, channel, :] = jnp.where(upper, re_part, im_part) * (1.0 / frames_all)


def body(samples, gains):
    inputs_here = samples.shape[0]
    frames_here = samples.shape[1] // NFFT
    times = lax.axis_size("tm")
    groups = lax.axis_size("inp")
    per_group = CH // groups
    inputs_all = inputs_here * groups
    frames_all = frames_here * times
    block = inputs_here * frames_here

    window = filter_window()
    twiddle = jnp.asarray(build_table(window))
    window_taps = jnp.asarray(window.astype(np.float32).reshape(TAPS, NFFT))

    history = lax.ppermute(
        samples[:, (frames_here - TAPS + 1) * NFFT :],
        "tm",
        [(source, source + 1) for source in range(times - 1)],
    )
    late_rows = (frames_here - EARLY) * inputs_here
    late = pl.pallas_call(
        late_frames_kernel,
        out_shape=jax.ShapeDtypeStruct((late_rows, 2 * CH), jnp.float32),
        in_specs=[VMEM] * 3,
        out_specs=VMEM,
        scratch_shapes=[pltpu.VMEM((late_rows, NFFT), jnp.bfloat16)],
        compiler_params=PARAMS,
        cost_estimate=pl.CostEstimate(
            flops=2 * late_rows * NFFT * 2 * CH,
            bytes_accessed=3 * 1024 * 1024,
            transcendentals=0,
        ),
        name="late_frames",
    )(samples, window_taps, twiddle)

    def channels(*refs):
        channels_kernel(groups, *refs)

    early_rows = EARLY * inputs_here
    spectra, parcels = pl.pallas_call(
        channels,
        grid=(1,),
        out_shape=(
            jax.ShapeDtypeStruct((2, block, CH), jnp.bfloat16),
            jax.ShapeDtypeStruct((inputs_all, 2 * per_group * frames_here), jnp.bfloat16),
        ),
        in_specs=[
            VMEM,
            pl.BlockSpec((inputs_here, EARLY * NFFT), lambda step: (0, 0)),
            VMEM,
            VMEM,
            VMEM,
            VMEM,
        ],
        out_specs=(VMEM, VMEM),
        scratch_shapes=[
            pltpu.VMEM((early_rows, NFFT), jnp.bfloat16),
            pltpu.VMEM((early_rows, 2 * CH), jnp.float32),
            pltpu.VMEM((2 * CH // LANES, block, LANES), jnp.float32),
            pltpu.VMEM((2 * CH, block), jnp.float32),
            pltpu.VMEM((inputs_all, 2 * per_group * frames_here), jnp.float32),
        ],
        compiler_params=PARAMS,
        cost_estimate=pl.CostEstimate(
            flops=2 * early_rows * NFFT * 2 * CH,
            bytes_accessed=3 * 1024 * 1024,
            transcendentals=0,
        ),
        name="channels",
    )(history, samples, window_taps, twiddle, late, gains.transpose(0, 2, 1))
    spectra = spectra.reshape(2, inputs_here, frames_here, CH).transpose(0, 3, 1, 2)

    parcels = parcels.reshape(groups, inputs_here, 2 * per_group * frames_here)
    mine = lax.all_to_all(parcels, "inp", 0, 0)
    mine = mine.reshape(inputs_all, 2 * per_group * frames_here)
    copies = pl.pallas_call(
        spread_kernel,
        out_shape=jax.ShapeDtypeStruct(
            (times, 2 * per_group * frames_here, inputs_all), jnp.bfloat16
        ),
        in_specs=[VMEM],
        out_specs=VMEM,
        compiler_params=PARAMS,
        name="spread",
    )(mine)
    every = lax.all_to_all(copies, "tm", 0, 0)

    def correlate(*refs):
        correlate_kernel(frames_all, *refs)

    rows = inputs_all // times
    visibilities = pl.pallas_call(
        correlate,
        out_shape=jax.ShapeDtypeStruct((rows, per_group, inputs_all), jnp.float32),
        in_specs=[SMEM, VMEM],
        out_specs=VMEM,
        compiler_params=PARAMS,
        name="correlate",
    )(lax.axis_index("tm").astype(jnp.int32)[None], every)
    return (spectra, visibilities)


def solution(mesh):
    return jax.shard_map(
        body,
        mesh=mesh,
        in_specs=(P("inp", "tm"), P(None, None, "inp")),
        out_specs=(P(None, None, "inp", "tm"), P("tm", "inp", None)),
        check_vma=False,
    )
```

```python
import math

import jax
import jax.numpy as jnp
import numpy as np
from jax import lax
from jax.experimental import pallas as pl
from jax.experimental.pallas import tpu as pltpu
from jax.sharding import PartitionSpec as P

NFFT = 2048
CH = 256
FIRST = 384
TAPS = 4
EARLY = 4
STEP = 512
LANES = 128
VMEM = pl.BlockSpec(memory_space=pltpu.VMEM)
SMEM = pl.BlockSpec(memory_space=pltpu.SMEM)
PARAMS = pltpu.CompilerParams(vmem_limit_bytes=32 * 1024 * 1024)


def filter_window():
    length = TAPS * NFFT
    position = np.arange(length, dtype=np.float64)
    centred = (position - 0.5 * length + 0.5) / NFFT
    hann_taper = 0.5 - 0.5 * np.cos(2.0 * math.pi * (position + 0.5) / length)
    return np.sinc(centred) * hann_taper


def build_table(window):
    norm_scale = 1.0 / np.sqrt(np.sum(window * window))
    sample = np.arange(NFFT)[:, None]
    channel = FIRST + np.arange(CH)[None, :]
    phase_angle = 2.0 * math.pi / NFFT * (sample * channel % NFFT)
    cosine = np.cos(phase_angle) * norm_scale
    sine = -np.sin(phase_angle) * norm_scale
    return np.concatenate([cosine, sine], axis=1).astype(jnp.bfloat16)


def tap_frames(frame_at, window_ref, tapped_ref, first, count):
    for pair in range(0, count, 2):
        for low in range(0, NFFT, STEP):
            sums = []
            for frame in (first + pair, first + pair + 1):
                total = None
                for tap in range(TAPS):
                    values = frame_at(frame - TAPS + 1 + tap, low).astype(jnp.float32)
                    term = window_ref[tap : tap + 1, low : low + STEP] * values
                    total = term if total is None else total + term
                sums.append(total)
            inputs_here = sums[0].shape[0]
            tapped_ref[pair * inputs_here : (pair + 2) * inputs_here, low : low + STEP] = (
                jnp.concatenate(sums, axis=0).astype(jnp.bfloat16)
            )


def late_frames_kernel(samples_ref, window_ref, twiddle_ref, direct_ref, tapped_ref):
    frames_here = samples_ref.shape[1] // NFFT

    def frame_at(frame, low):
        start = frame * NFFT + low
        return samples_ref[:, start : start + STEP]

    tap_frames(frame_at, window_ref, tapped_ref, EARLY, frames_here - EARLY)
    direct_ref[...] = jnp.dot(
        tapped_ref[...], twiddle_ref[...], preferred_element_type=jnp.float32
    )


def channels_kernel(
    groups,
    history_ref,
    samples_ref,
    window_ref,
    twiddle_ref,
    late_ref,
    gains_ref,
    spectra_ref,
    parcels_ref,
    tapped_ref,
    early_ref,
    rows_ref,
    columns_ref,
    turned_ref,
):
    inputs_here = samples_ref.shape[0]
    frames_here = EARLY + late_ref.shape[0] // inputs_here
    per_group = CH // groups
    parts = 2 * per_group
    slabs = CH // LANES

    def frame_at(frame, low):
        if frame < 0:
            start = (frame + TAPS - 1) * NFFT + low
            return history_ref[:, start : start + STEP]
        start = frame * NFFT + low
        return samples_ref[:, start : start + STEP]

    tap_frames(frame_at, window_ref, tapped_ref, 0, EARLY)
    early_ref[...] = jnp.dot(
        tapped_ref[...], twiddle_ref[...], preferred_element_type=jnp.float32
    )
    gain_re = gains_ref[0]
    gain_im = gains_ref[1]
    for frame in range(frames_here):
        if frame < EARLY:
            direct = early_ref[frame * inputs_here : (frame + 1) * inputs_here, :]
        else:
            start = (frame - EARLY) * inputs_here
            direct = late_ref[start : start + inputs_here, :]
        direct_re = direct[:, :CH]
        direct_im = direct[:, CH:]
        rows = pl.ds(frame, inputs_here, stride=frames_here)
        real_part = gain_re * direct_re - gain_im * direct_im
        imag_part = gain_re * direct_im + gain_im * direct_re
        for slab in range(slabs):
            columns = slice(slab * LANES, (slab + 1) * LANES)
            rows_ref[slab, rows, :] = real_part[:, columns]
            rows_ref[slabs + slab, rows, :] = imag_part[:, columns]
    for part in range(2):
        for slab in range(slabs):
            values = rows_ref[part * slabs + slab]
            start = slab * LANES
            spectra_ref[part, :, start : start + LANES] = values.astype(jnp.bfloat16)
            start += part * CH
            columns_ref[start : start + LANES, :] = values.T
    blocks = []
    for channel in range(per_group):
        for part in range(2):
            blocks.append(columns_ref[pl.ds(part * CH + channel, groups, stride=per_group), :])
    lanes = inputs_here * frames_here
    granule = lax.broadcasted_iota(jnp.int32, (groups, lanes), 1) // frames_here
    distance = parts // 2
    while distance:
        upper = (granule & distance) != 0
        shift = distance * frames_here
        for index in range(parts):
            if index & distance:
                continue
            low, high = blocks[index], blocks[index + distance]
            blocks[index] = jnp.where(upper, pltpu.roll(high, shift, 1), low)
            blocks[index + distance] = jnp.where(upper, high, pltpu.roll(low, lanes - shift, 1))
        distance //= 2
    for index in range(inputs_here):
        turned_ref[pl.ds(index, groups, stride=inputs_here), :] = blocks[index]
    parcels_ref[...] = turned_ref[...].astype(jnp.bfloat16)


def spread_kernel(mine_ref, parcels_ref):
    turned = mine_ref[...].T
    count, rows, _ = parcels_ref.shape
    for index in range(count):
        start = index // 2 * rows
        parcels_ref[index] = turned[start : start + rows]


def correlate_kernel(frames_all, place_ref, every_ref, packed_ref):
    times, lines, inputs_all = every_ref.shape
    blocks, rows, _ = packed_ref.shape
    frames_here = lines // 2
    parity = place_ref[0]
    odd = parity == 1
    right, twisted = [], []
    for time in range(times):
        right.append(every_ref[time])
        twisted.append(every_ref[time, frames_here:, :])
        twisted.append(-every_ref[time, :frames_here, :])
    right = jnp.concatenate(right, axis=0)
    twisted = jnp.concatenate(twisted, axis=0)
    col_index = lax.broadcasted_iota(jnp.int32, (rows, inputs_all), 1)
    row_index = lax.broadcasted_iota(jnp.int32, (rows, inputs_all), 0) + parity * rows
    for block in range(blocks):
        start = block * 2 * rows
        both = []
        for left in (right, twisted):
            product = lax.dot_general(
                left[:, start : start + 2 * rows],
                right,
                (((0,), (0,)), ((), ())),
                preferred_element_type=jnp.float32,
            )
            both.append(jnp.where(odd, product[rows:], product[:rows]))
        upper = row_index + start <= col_index
        values = jnp.where(upper, both[0], both[1]) * (1.0 / frames_all)
        packed_ref[block] = values.astype(jnp.bfloat16)


def unpack_kernel(packed_ref, visibilities_ref):
    for channel in range(packed_ref.shape[0]):
        visibilities_ref[:, channel, :] = packed_ref[channel].astype(jnp.float32)


def body(samples, gains):
    inputs_here = samples.shape[0]
    frames_here = samples.shape[1] // NFFT
    times = lax.axis_size("tm")
    groups = lax.axis_size("inp")
    per_group = CH // groups
    inputs_all = inputs_here * groups
    frames_all = frames_here * times
    block = inputs_here * frames_here

    window = filter_window()
    twiddle = jnp.asarray(build_table(window))
    window_taps = jnp.asarray(window.astype(np.float32).reshape(TAPS, NFFT))

    history = lax.ppermute(
        samples[:, (frames_here - TAPS + 1) * NFFT :],
        "tm",
        [(source, source + 1) for source in range(times - 1)],
    )
    late_rows = (frames_here - EARLY) * inputs_here
    late = pl.pallas_call(
        late_frames_kernel,
        out_shape=jax.ShapeDtypeStruct((late_rows, 2 * CH), jnp.float32),
        in_specs=[VMEM] * 3,
        out_specs=VMEM,
        scratch_shapes=[pltpu.VMEM((late_rows, NFFT), jnp.bfloat16)],
        compiler_params=PARAMS,
        cost_estimate=pl.CostEstimate(
            flops=2 * late_rows * NFFT * 2 * CH,
            bytes_accessed=3 * 1024 * 1024,
            transcendentals=0,
        ),
        name="late_frames",
    )(samples, window_taps, twiddle)

    def channels(*refs):
        channels_kernel(groups, *refs)

    early_rows = EARLY * inputs_here
    spectra, parcels = pl.pallas_call(
        channels,
        grid=(1,),
        out_shape=(
            jax.ShapeDtypeStruct((2, block, CH), jnp.bfloat16),
            jax.ShapeDtypeStruct((inputs_all, 2 * per_group * frames_here), jnp.bfloat16),
        ),
        in_specs=[
            VMEM,
            pl.BlockSpec((inputs_here, EARLY * NFFT), lambda step: (0, 0)),
            VMEM,
            VMEM,
            VMEM,
            VMEM,
        ],
        out_specs=(VMEM, VMEM),
        scratch_shapes=[
            pltpu.VMEM((early_rows, NFFT), jnp.bfloat16),
            pltpu.VMEM((early_rows, 2 * CH), jnp.float32),
            pltpu.VMEM((2 * CH // LANES, block, LANES), jnp.float32),
            pltpu.VMEM((2 * CH, block), jnp.float32),
            pltpu.VMEM((inputs_all, 2 * per_group * frames_here), jnp.float32),
        ],
        compiler_params=PARAMS,
        cost_estimate=pl.CostEstimate(
            flops=2 * early_rows * NFFT * 2 * CH,
            bytes_accessed=3 * 1024 * 1024,
            transcendentals=0,
        ),
        name="channels",
    )(history, samples, window_taps, twiddle, late, gains.transpose(0, 2, 1))
    spectra = spectra.reshape(2, inputs_here, frames_here, CH).transpose(0, 3, 1, 2)

    parcels = parcels.reshape(groups, inputs_here, 2 * per_group * frames_here)
    mine = lax.all_to_all(parcels, "inp", 0, 0)
    mine = mine.reshape(inputs_all, 2 * per_group * frames_here)
    spread = pl.pallas_call(
        spread_kernel,
        out_shape=jax.ShapeDtypeStruct((times, 2 * frames_here, inputs_all), jnp.bfloat16),
        in_specs=[VMEM],
        out_specs=VMEM,
        compiler_params=PARAMS,
        name="spread",
    )(mine)
    every = lax.all_to_all(spread, "tm", 0, 0)

    def correlate(*refs):
        correlate_kernel(frames_all, *refs)

    rows = inputs_all // times
    parity = lax.rem(lax.axis_index("tm").astype(jnp.int32), 2)
    packed = pl.pallas_call(
        correlate,
        out_shape=jax.ShapeDtypeStruct((times // 2, rows, inputs_all), jnp.bfloat16),
        in_specs=[SMEM, VMEM],
        out_specs=VMEM,
        compiler_params=PARAMS,
        name="correlate",
    )(parity[None], every)
    same_parity = [[2 * place + side for place in range(times // 2)] for side in range(2)]
    packed = lax.all_to_all(packed, "tm", 0, 0, axis_index_groups=same_parity)
    visibilities = pl.pallas_call(
        unpack_kernel,
        out_shape=jax.ShapeDtypeStruct((rows, per_group, inputs_all), jnp.float32),
        in_specs=[VMEM],
        out_specs=VMEM,
        compiler_params=PARAMS,
        name="unpack",
    )(packed)
    return (spectra, visibilities)


def solution(mesh):
    return jax.shard_map(
        body,
        mesh=mesh,
        in_specs=(P("inp", "tm"), P(None, None, "inp")),
        out_specs=(P(None, None, "inp", "tm"), P("tm", "inp", None)),
        check_vma=False,
    )
```

```python
import math

import jax
import jax.numpy as jnp
import numpy as np
from jax import lax
from jax.experimental import pallas as pl
from jax.experimental.pallas import tpu as pltpu
from jax.sharding import Mesh, PartitionSpec as P

NFFT = 2048
CH = 256
FIRST = 384
TAPS = 4
NEAR = 4
EARLY = 4
STEP = 512
LANES = 128
VMEM = pl.BlockSpec(memory_space=pltpu.VMEM)
SMEM = pl.BlockSpec(memory_space=pltpu.SMEM)
PARAMS = pltpu.CompilerParams(vmem_limit_bytes=32 * 1024 * 1024)


def filter_window():
    length = TAPS * NFFT
    position = np.arange(length, dtype=np.float64)
    centred = (position - 0.5 * length + 0.5) / NFFT
    hann_taper = 0.5 - 0.5 * np.cos(2.0 * math.pi * (position + 0.5) / length)
    return np.sinc(centred) * hann_taper


def build_table(window):
    norm_scale = 1.0 / np.sqrt(np.sum(window * window))
    sample = np.arange(NFFT)[:, None]
    channel = FIRST + np.arange(CH)[None, :]
    phase_angle = 2.0 * math.pi / NFFT * (sample * channel % NFFT)
    cosine = np.cos(phase_angle) * norm_scale
    sine = -np.sin(phase_angle) * norm_scale
    return np.concatenate([cosine, sine], axis=1).astype(jnp.bfloat16)


def tap_frames(frame_at, window_ref, tapped_ref, first, count):
    for pair in range(0, count, 2):
        for low in range(0, NFFT, STEP):
            sums = []
            for frame in (first + pair, first + pair + 1):
                total = None
                for tap in range(TAPS):
                    values = frame_at(frame - TAPS + 1 + tap, low).astype(jnp.float32)
                    term = window_ref[tap : tap + 1, low : low + STEP] * values
                    total = term if total is None else total + term
                sums.append(total)
            inputs_here = sums[0].shape[0]
            tapped_ref[pair * inputs_here : (pair + 2) * inputs_here, low : low + STEP] = (
                jnp.concatenate(sums, axis=0).astype(jnp.bfloat16)
            )


def late_frames_kernel(samples_ref, window_ref, twiddle_ref, direct_ref, tapped_ref):
    frames_here = samples_ref.shape[1] // NFFT

    def frame_at(frame, low):
        start = frame * NFFT + low
        return samples_ref[:, start : start + STEP]

    tap_frames(frame_at, window_ref, tapped_ref, EARLY, frames_here - EARLY)
    direct_ref[...] = jnp.dot(
        tapped_ref[...], twiddle_ref[...], preferred_element_type=jnp.float32
    )


def channels_kernel(
    far,
    history_ref,
    samples_ref,
    window_ref,
    twiddle_ref,
    late_ref,
    gains_ref,
    spectra_ref,
    parcels_ref,
    tapped_ref,
    early_ref,
    rows_ref,
    columns_ref,
    turned_ref,
):
    inputs_here = samples_ref.shape[0]
    frames_here = EARLY + late_ref.shape[0] // inputs_here
    per_far = CH // far
    per_group = per_far // NEAR
    parts = 2 * per_group
    slabs = CH // LANES

    def frame_at(frame, low):
        if frame < 0:
            start = (frame + TAPS - 1) * NFFT + low
            return history_ref[:, start : start + STEP]
        start = frame * NFFT + low
        return samples_ref[:, start : start + STEP]

    tap_frames(frame_at, window_ref, tapped_ref, 0, EARLY)
    early_ref[...] = jnp.dot(
        tapped_ref[...], twiddle_ref[...], preferred_element_type=jnp.float32
    )
    gain_re = gains_ref[0]
    gain_im = gains_ref[1]
    for frame in range(frames_here):
        if frame < EARLY:
            direct = early_ref[frame * inputs_here : (frame + 1) * inputs_here, :]
        else:
            start = (frame - EARLY) * inputs_here
            direct = late_ref[start : start + inputs_here, :]
        direct_re = direct[:, :CH]
        direct_im = direct[:, CH:]
        rows = pl.ds(frame, inputs_here, stride=frames_here)
        real_part = gain_re * direct_re - gain_im * direct_im
        imag_part = gain_re * direct_im + gain_im * direct_re
        for slab in range(slabs):
            columns = slice(slab * LANES, (slab + 1) * LANES)
            rows_ref[slab, rows, :] = real_part[:, columns]
            rows_ref[slabs + slab, rows, :] = imag_part[:, columns]
    for part in range(2):
        for slab in range(slabs):
            values = rows_ref[part * slabs + slab]
            start = slab * LANES
            spectra_ref[part, :, start : start + LANES] = values.astype(jnp.bfloat16)
            start += part * CH
            columns_ref[start : start + LANES, :] = values.T
    lanes = inputs_here * frames_here
    granule = lax.broadcasted_iota(jnp.int32, (far, lanes), 1) // frames_here
    for near in range(NEAR):
        blocks = []
        for channel in range(per_group):
            for part in range(2):
                first = part * CH + near * per_group + channel
                blocks.append(columns_ref[pl.ds(first, far, stride=per_far), :])
        distance = parts // 2
        while distance:
            upper = (granule & distance) != 0
            shift = distance * frames_here
            for index in range(parts):
                if index & distance:
                    continue
                low, high = blocks[index], blocks[index + distance]
                blocks[index] = jnp.where(upper, pltpu.roll(high, shift, 1), low)
                blocks[index + distance] = jnp.where(
                    upper, high, pltpu.roll(low, lanes - shift, 1)
                )
            distance //= 2
        for index in range(inputs_here):
            turned_ref[near, pl.ds(index, far, stride=inputs_here), :] = blocks[index]
        parcels_ref[:, near * lanes : (near + 1) * lanes] = turned_ref[near].astype(jnp.bfloat16)


def spread_kernel(mine_ref, parcels_ref):
    count, rows, width = parcels_ref.shape
    times = count // NEAR
    for near in range(NEAR):
        turned = mine_ref[:, near * width : (near + 1) * width].T
        for time in range(times):
            start = time // 2 * rows
            parcels_ref[near * times + time] = turned[start : start + rows]


def correlate_kernel(frames_all, inputs_here, place_ref, every_ref, packed_ref):
    count, lines, width = every_ref.shape
    blocks, rows, inputs_all = packed_ref.shape
    times = count // NEAR
    frames_here = lines // 2
    parity = place_ref[0]
    odd = parity == 1
    lined = []
    for time in range(times):
        lined.append(
            jnp.concatenate([every_ref[near * times + time] for near in range(NEAR)], axis=1)
        )
    source = lax.broadcasted_iota(jnp.int32, (inputs_all, inputs_all), 0)
    target = lax.broadcasted_iota(jnp.int32, (inputs_all, inputs_all), 1)
    near, rest = source // width, source % width
    placed = (rest // inputs_here) * (NEAR * inputs_here) + near * inputs_here + rest % inputs_here
    right = jnp.dot(
        jnp.concatenate(lined, axis=0),
        (placed == target).astype(jnp.bfloat16),
        preferred_element_type=jnp.float32,
    ).astype(jnp.bfloat16)
    twisted = []
    for time in range(times):
        start = time * lines
        twisted.append(right[start + frames_here : start + lines])
        twisted.append(-right[start : start + frames_here])
    twisted = jnp.concatenate(twisted, axis=0)
    col_index = lax.broadcasted_iota(jnp.int32, (rows, inputs_all), 1)
    row_index = lax.broadcasted_iota(jnp.int32, (rows, inputs_all), 0) + parity * rows
    for block in range(blocks):
        start = block * 2 * rows
        both = []
        for left in (right, twisted):
            product = lax.dot_general(
                left[:, start : start + 2 * rows],
                right,
                (((0,), (0,)), ((), ())),
                preferred_element_type=jnp.float32,
            )
            both.append(jnp.where(odd, product[rows:], product[:rows]))
        upper = row_index + start <= col_index
        values = jnp.where(upper, both[0], both[1]) * (1.0 / frames_all)
        packed_ref[block] = values.astype(jnp.bfloat16)


def unpack_kernel(packed_ref, visibilities_ref):
    for channel in range(packed_ref.shape[0]):
        visibilities_ref[:, channel, :] = packed_ref[channel].astype(jnp.float32)


def body(samples, gains):
    inputs_here = samples.shape[0]
    frames_here = samples.shape[1] // NFFT
    times = lax.axis_size("tm")
    far = lax.axis_size("far")
    groups = far * NEAR
    per_group = CH // groups
    inputs_all = inputs_here * groups
    frames_all = frames_here * times
    block = inputs_here * frames_here

    window = filter_window()
    twiddle = jnp.asarray(build_table(window))
    window_taps = jnp.asarray(window.astype(np.float32).reshape(TAPS, NFFT))

    history = lax.ppermute(
        samples[:, (frames_here - TAPS + 1) * NFFT :],
        "tm",
        [(source, source + 1) for source in range(times - 1)],
    )
    late_rows = (frames_here - EARLY) * inputs_here
    late = pl.pallas_call(
        late_frames_kernel,
        out_shape=jax.ShapeDtypeStruct((late_rows, 2 * CH), jnp.float32),
        in_specs=[VMEM] * 3,
        out_specs=VMEM,
        scratch_shapes=[pltpu.VMEM((late_rows, NFFT), jnp.bfloat16)],
        compiler_params=PARAMS,
        cost_estimate=pl.CostEstimate(
            flops=2 * late_rows * NFFT * 2 * CH,
            bytes_accessed=3 * 1024 * 1024,
            transcendentals=0,
        ),
        name="late_frames",
    )(samples, window_taps, twiddle)

    def channels(*refs):
        channels_kernel(far, *refs)

    early_rows = EARLY * inputs_here
    spectra, parcels = pl.pallas_call(
        channels,
        grid=(1,),
        out_shape=(
            jax.ShapeDtypeStruct((2, block, CH), jnp.bfloat16),
            jax.ShapeDtypeStruct((far * inputs_here, NEAR * block), jnp.bfloat16),
        ),
        in_specs=[
            VMEM,
            pl.BlockSpec((inputs_here, EARLY * NFFT), lambda step: (0, 0)),
            VMEM,
            VMEM,
            VMEM,
            VMEM,
        ],
        out_specs=(VMEM, VMEM),
        scratch_shapes=[
            pltpu.VMEM((early_rows, NFFT), jnp.bfloat16),
            pltpu.VMEM((early_rows, 2 * CH), jnp.float32),
            pltpu.VMEM((2 * CH // LANES, block, LANES), jnp.float32),
            pltpu.VMEM((2 * CH, block), jnp.float32),
            pltpu.VMEM((NEAR, far * inputs_here, block), jnp.float32),
        ],
        compiler_params=PARAMS,
        cost_estimate=pl.CostEstimate(
            flops=2 * early_rows * NFFT * 2 * CH,
            bytes_accessed=3 * 1024 * 1024,
            transcendentals=0,
        ),
        name="channels",
    )(history, samples, window_taps, twiddle, late, gains.transpose(0, 2, 1))
    spectra = spectra.reshape(2, inputs_here, frames_here, CH).transpose(0, 3, 1, 2)

    parcels = parcels.reshape(far, inputs_here, NEAR * block)
    mine = lax.all_to_all(parcels, "far", 0, 0).reshape(far * inputs_here, NEAR * block)
    spread = pl.pallas_call(
        spread_kernel,
        out_shape=jax.ShapeDtypeStruct(
            (NEAR * times, 2 * frames_here, far * inputs_here), jnp.bfloat16
        ),
        in_specs=[VMEM],
        out_specs=VMEM,
        compiler_params=PARAMS,
        name="spread",
    )(mine)
    every = lax.all_to_all(spread, ("near", "tm"), 0, 0)

    def correlate(*refs):
        correlate_kernel(frames_all, inputs_here, *refs)

    rows = inputs_all // times
    parity = lax.rem(lax.axis_index("tm").astype(jnp.int32), 2)
    packed = pl.pallas_call(
        correlate,
        out_shape=jax.ShapeDtypeStruct((times // 2, rows, inputs_all), jnp.bfloat16),
        in_specs=[SMEM, VMEM],
        out_specs=VMEM,
        compiler_params=PARAMS,
        name="correlate",
    )(parity[None], every)
    same_parity = [[2 * place + side for place in range(times // 2)] for side in range(2)]
    packed = lax.all_to_all(packed, "tm", 0, 0, axis_index_groups=same_parity)
    visibilities = pl.pallas_call(
        unpack_kernel,
        out_shape=jax.ShapeDtypeStruct((rows, per_group, inputs_all), jnp.float32),
        in_specs=[VMEM],
        out_specs=VMEM,
        compiler_params=PARAMS,
        name="unpack",
    )(packed)
    return (spectra, visibilities)


def solution(mesh):
    groups, times = mesh.devices.shape
    split = Mesh(mesh.devices.reshape(groups // NEAR, NEAR, times), ("far", "near", "tm"))
    inputs = ("far", "near")
    return jax.shard_map(
        body,
        mesh=split,
        in_specs=(P(inputs, "tm"), P(None, None, inputs)),
        out_specs=(P(None, None, inputs, "tm"), P("tm", inputs, None)),
        check_vma=False,
    )
```

```python
import math

import jax
import jax.numpy as jnp
import numpy as np
from jax import lax
from jax.experimental import pallas as pl
from jax.experimental.pallas import tpu as pltpu
from jax.sharding import Mesh, PartitionSpec as P

NFFT = 2048
CH = 256
FIRST = 384
TAPS = 4
NEAR = 4
EARLY = 4
STEP = 512
LANES = 128
VMEM = pl.BlockSpec(memory_space=pltpu.VMEM)
ANY = pl.BlockSpec(memory_space=pl.ANY)
SMEM = pl.BlockSpec(memory_space=pltpu.SMEM)
OWN_PART_VMEM = 59 * 1024 * 1024 + 768 * 1024
PARAMS = pltpu.CompilerParams(vmem_limit_bytes=32 * 1024 * 1024)


def filter_window():
    length = TAPS * NFFT
    position = np.arange(length, dtype=np.float64)
    centred = (position - 0.5 * length + 0.5) / NFFT
    hann_taper = 0.5 - 0.5 * np.cos(2.0 * math.pi * (position + 0.5) / length)
    return np.sinc(centred) * hann_taper


def build_table(window):
    norm_scale = 1.0 / np.sqrt(np.sum(window * window))
    sample = np.arange(NFFT)[:, None]
    channel = FIRST + np.arange(CH)[None, :]
    phase_angle = 2.0 * math.pi / NFFT * (sample * channel % NFFT)
    cosine = np.cos(phase_angle) * norm_scale
    sine = -np.sin(phase_angle) * norm_scale
    return np.concatenate([cosine, sine], axis=1).astype(jnp.bfloat16)


def tap_frames(frame_at, window_ref, tapped_ref, first, count):
    inputs_here = tapped_ref.shape[0] // count
    for pair in range(0, count, 2):
        for low in range(0, NFFT, STEP):
            sums = []
            for frame in (first + pair, first + pair + 1):
                total = jnp.zeros((inputs_here, STEP), jnp.float32)
                for tap in range(TAPS):
                    values = frame_at(frame - TAPS + 1 + tap, low)
                    if values is not None:
                        weights = window_ref[tap : tap + 1, low : low + STEP]
                        total = total + weights * values.astype(jnp.float32)
                sums.append(total)
            tapped_ref[pair * inputs_here : (pair + 2) * inputs_here, low : low + STEP] = (
                jnp.concatenate(sums, axis=0).astype(jnp.bfloat16)
            )


def turn_granules(blocks, size):
    count = len(blocks)
    lanes = count * size
    granule = lax.broadcasted_iota(jnp.int32, blocks[0].shape, 1) // size
    blocks = list(blocks)
    distance = count // 2
    while distance:
        upper = (granule & distance) != 0
        shift = distance * size
        for index in range(count):
            if index & distance:
                continue
            low, high = blocks[index], blocks[index + distance]
            blocks[index] = jnp.where(upper, pltpu.roll(high, shift, 1), low)
            blocks[index + distance] = jnp.where(upper, high, pltpu.roll(low, lanes - shift, 1))
        distance //= 2
    return blocks


def own_part_kernel(
    far,
    samples_hbm,
    window_hbm,
    twiddle_hbm,
    gains_hbm,
    own_ref,
    passed_ref,
    parcels_ref,
    samples_ref,
    window_ref,
    twiddle_ref,
    gains_ref,
    tapped_ref,
    direct_ref,
    arrived,
):
    fetches = []
    for index, (source, target) in enumerate(
        (
            (samples_hbm, samples_ref),
            (window_hbm, window_ref),
            (twiddle_hbm, twiddle_ref),
            (gains_hbm, gains_ref),
        )
    ):
        fetches.append(pltpu.make_async_copy(source, target, arrived.at[index]))
        fetches[-1].start()
    inputs_here = samples_ref.shape[0]
    frames_here = samples_ref.shape[1] // NFFT

    def frame_at(frame, low):
        if not 0 <= frame < frames_here:
            return None
        start = frame * NFFT + low
        return samples_ref[:, start : start + STEP]

    fetches[0].wait()
    fetches[1].wait()
    tap_frames(frame_at, window_ref, tapped_ref, 0, frames_here + EARLY)
    fetches[2].wait()
    direct_ref[...] = jnp.dot(
        tapped_ref[...], twiddle_ref[...], preferred_element_type=jnp.float32
    )
    fetches[3].wait()
    own_rows = own_ref.shape[0]
    own_ref[...] = direct_ref[:own_rows, :]
    passed_ref[...] = direct_ref[own_rows : own_rows + passed_ref.shape[0], :]
    gain_re = gains_ref[0]
    gain_im = gains_ref[1]
    parts = []
    for frame in range(frames_here + EARLY):
        direct = direct_ref[frame * inputs_here : (frame + 1) * inputs_here, :]
        direct_re = direct[:, :CH]
        direct_im = direct[:, CH:]
        parts.append(
            (
                gain_re * direct_re - gain_im * direct_im,
                gain_re * direct_im + gain_im * direct_re,
            )
        )
    slots = [
        [(part, frame) for frame in range(first, first + 8)]
        for first in range(0, frames_here, 8)
        for part in range(2)
    ]
    slots.append([(part, frames_here + frame) for part in range(2) for frame in range(EARLY)])
    per_far = CH // far
    for place, slot in enumerate(slots):
        columns = slice(place * LANES, (place + 1) * LANES)
        for half in range(CH // LANES):
            lanes = slice(half * LANES, (half + 1) * LANES)
            blocks = turn_granules([parts[frame][part][:, lanes] for part, frame in slot], per_far)
            for index in range(0, len(blocks), 2):
                row = (half * len(blocks) + index) * inputs_here
                parcels_ref[row : row + 2 * inputs_here, columns] = jnp.concatenate(
                    blocks[index : index + 2], axis=0
                ).astype(jnp.bfloat16)


def spectra_kernel(passed_ref, own_ref, gains_ref, spectra_ref, rows_ref):
    inputs_here = gains_ref.shape[1]
    frames_here = own_ref.shape[0] // inputs_here
    slabs = CH // LANES
    gain_re = gains_ref[0]
    gain_im = gains_ref[1]
    for frame in range(frames_here):
        block = slice(frame * inputs_here, (frame + 1) * inputs_here)
        direct = own_ref[block, :]
        if frame < TAPS - 1:
            direct = direct + passed_ref[block, :]
        direct_re = direct[:, :CH]
        direct_im = direct[:, CH:]
        rows = pl.ds(frame, inputs_here, stride=frames_here)
        real_part = gain_re * direct_re - gain_im * direct_im
        imag_part = gain_re * direct_im + gain_im * direct_re
        for slab in range(slabs):
            columns = slice(slab * LANES, (slab + 1) * LANES)
            rows_ref[slab, rows, :] = real_part[:, columns]
            rows_ref[slabs + slab, rows, :] = imag_part[:, columns]
    for part in range(2):
        for slab in range(slabs):
            columns = slice(slab * LANES, (slab + 1) * LANES)
            spectra_ref[part, :, columns] = rows_ref[part * slabs + slab].astype(jnp.bfloat16)


def channel_of(time):
    return time // 4 * 2 + time % 2


def spread_kernel(mine_ref, parcels_ref, turned_ref):
    count, rows, width = parcels_ref.shape
    times = count // NEAR
    stride = mine_ref.shape[1] // rows
    for place in range(0, mine_ref.shape[1], LANES):
        values = mine_ref[:, place : place + LANES].astype(jnp.float32)
        turned_ref[place : place + LANES, :] = values.T
    for near in range(NEAR):
        for channel in range(stride // NEAR):
            start = near * (stride // NEAR) + channel
            values = turned_ref[pl.ds(start, rows, stride=stride), :].astype(jnp.bfloat16)
            for time in range(times):
                if channel_of(time) == channel:
                    parcels_ref[near * times + time] = values


def correlate_kernel(frames_all, inputs_here, place_ref, every_ref, packed_ref):
    count, lines, width = every_ref.shape
    blocks, rows, inputs_all = packed_ref.shape
    times = count // NEAR
    main = lines - 2 * EARLY
    carry = None
    lined = []
    for time in range(times):
        wide = jnp.concatenate(
            [every_ref[near * times + time].astype(jnp.float32) for near in range(NEAR)], axis=1
        )
        tiles = [wide[start : start + 8] for start in range(0, lines, 8)]
        if carry is not None:
            early = lax.broadcasted_iota(jnp.int32, carry.shape, 0) < EARLY
            tiles[0] = tiles[0] + jnp.where(early, carry, 0.0)
            tiles[1] = tiles[1] + jnp.where(early, pltpu.roll(carry, 8 - EARLY, 0), 0.0)
        carry = tiles[-1]
        lined += tiles[:-1]
    source = lax.broadcasted_iota(jnp.int32, (inputs_all, inputs_all), 0)
    target = lax.broadcasted_iota(jnp.int32, (inputs_all, inputs_all), 1)
    near, rest = source // width, source % width
    placed = (rest // inputs_here) * (NEAR * inputs_here) + near * inputs_here + rest % inputs_here
    ordered = jnp.dot(
        jnp.concatenate(lined, axis=0).astype(jnp.bfloat16),
        (placed == target).astype(jnp.bfloat16),
        preferred_element_type=jnp.float32,
    )
    right = ordered.astype(jnp.bfloat16)
    twisted = []
    for start in range(0, times * main, 16):
        twisted.append(ordered[start + 8 : start + 16])
        twisted.append(-ordered[start : start + 8])
    twisted = jnp.concatenate(twisted, axis=0).astype(jnp.bfloat16)
    inner = place_ref[0] == 1
    wide = 2 * rows
    col_index = lax.broadcasted_iota(jnp.int32, (wide, inputs_all), 1)
    row_index = lax.broadcasted_iota(jnp.int32, (wide, inputs_all), 0)
    for side in range(2):
        outer_start = side * (inputs_all - wide)
        inner_start = (1 + side) * wide
        both = []
        for left in (right, twisted):
            chosen = jnp.where(
                inner,
                left[:, inner_start : inner_start + wide],
                left[:, outer_start : outer_start + wide],
            )
            both.append(
                lax.dot_general(
                    chosen,
                    right,
                    (((0,), (0,)), ((), ())),
                    preferred_element_type=jnp.float32,
                )
            )
        upper = row_index + jnp.where(inner, inner_start, outer_start) <= col_index
        values = (jnp.where(upper, both[0], both[1]) * (1.0 / frames_all)).astype(jnp.bfloat16)
        packed_ref[2 * side] = values[:rows]
        packed_ref[2 * side + 1] = values[rows:]


def unpack_kernel(packed_ref, visibilities_ref):
    for channel in range(packed_ref.shape[0]):
        visibilities_ref[:, channel, :] = packed_ref[channel].astype(jnp.float32)


def body(samples, gains):
    inputs_here = samples.shape[0]
    frames_here = samples.shape[1] // NFFT
    times = lax.axis_size("tm")
    far = lax.axis_size("far")
    groups = far * NEAR
    per_group = CH // groups
    inputs_all = inputs_here * groups
    frames_all = frames_here * times
    block = inputs_here * frames_here

    window = filter_window()
    twiddle = jnp.asarray(build_table(window))
    window_taps = jnp.asarray(window.astype(np.float32).reshape(TAPS, NFFT))

    sent = frames_here + EARLY
    gains = gains.transpose(0, 2, 1)

    def own_part(*refs):
        own_part_kernel(far, *refs)

    own, passed, parcels = pl.pallas_call(
        own_part,
        out_shape=(
            jax.ShapeDtypeStruct((block, 2 * CH), jnp.float32),
            jax.ShapeDtypeStruct(((TAPS - 1) * inputs_here, 2 * CH), jnp.float32),
            jax.ShapeDtypeStruct((far * inputs_here, sent * 2 * CH // far), jnp.bfloat16),
        ),
        in_specs=[ANY] * 4,
        out_specs=(VMEM, VMEM, VMEM),
        scratch_shapes=[
            pltpu.VMEM(samples.shape, jnp.bfloat16),
            pltpu.VMEM(window_taps.shape, jnp.float32),
            pltpu.VMEM(twiddle.shape, jnp.bfloat16),
            pltpu.VMEM(gains.shape, jnp.float32),
            pltpu.VMEM((sent * inputs_here, NFFT), jnp.bfloat16),
            pltpu.VMEM((sent * inputs_here, 2 * CH), jnp.float32),
            pltpu.SemaphoreType.DMA((4,)),
        ],
        compiler_params=pltpu.CompilerParams(vmem_limit_bytes=OWN_PART_VMEM),
        cost_estimate=pl.CostEstimate(
            flops=2 * sent * inputs_here * NFFT * 2 * CH,
            bytes_accessed=3 * 1024 * 1024,
            transcendentals=0,
        ),
        name="own_part",
    )(samples, window_taps, twiddle, gains)

    parcels = parcels.reshape(far, inputs_here, sent * 2 * CH // far)
    mine = lax.all_to_all(parcels, "far", 0, 0).reshape(far * inputs_here, sent * 2 * CH // far)

    passed = lax.ppermute(passed, "tm", [(source, source + 1) for source in range(times - 1)])
    spectra = pl.pallas_call(
        spectra_kernel,
        out_shape=jax.ShapeDtypeStruct((2, block, CH), jnp.bfloat16),
        in_specs=[VMEM] * 3,
        out_specs=VMEM,
        scratch_shapes=[pltpu.VMEM((2 * CH // LANES, block, LANES), jnp.float32)],
        compiler_params=PARAMS,
        cost_estimate=pl.CostEstimate(
            flops=8 * block * 2 * CH, bytes_accessed=1024 * 1024, transcendentals=0
        ),
        name="spectra",
    )(passed, own, gains)
    mine, spectra = lax.optimization_barrier((mine, spectra))
    spectra = spectra.reshape(2, inputs_here, frames_here, CH).transpose(0, 3, 1, 2)

    lines = 2 * sent
    spread = pl.pallas_call(
        spread_kernel,
        out_shape=jax.ShapeDtypeStruct((NEAR * times, lines, far * inputs_here), jnp.bfloat16),
        in_specs=[VMEM],
        out_specs=VMEM,
        scratch_shapes=[pltpu.VMEM((sent * 2 * CH // far, far * inputs_here), jnp.float32)],
        compiler_params=PARAMS,
        name="spread",
    )(mine)
    every = lax.all_to_all(spread, ("near", "tm"), 0, 0)

    def correlate(*refs):
        correlate_kernel(frames_all, inputs_here, *refs)

    rows = inputs_all // times
    place = lax.axis_index("tm").astype(jnp.int32)
    inner = (place >= times // 4) & (place < times - times // 4)
    packed = pl.pallas_call(
        correlate,
        out_shape=jax.ShapeDtypeStruct((times // 2, rows, inputs_all), jnp.bfloat16),
        in_specs=[SMEM, VMEM],
        out_specs=VMEM,
        compiler_params=PARAMS,
        name="correlate",
    )(inner.astype(jnp.int32)[None], every)
    squares = [[0, 1, 6, 7], [2, 3, 4, 5]]
    packed = lax.all_to_all(packed, "tm", 0, 0, axis_index_groups=squares)
    visibilities = pl.pallas_call(
        unpack_kernel,
        out_shape=jax.ShapeDtypeStruct((rows, per_group, inputs_all), jnp.float32),
        in_specs=[VMEM],
        out_specs=VMEM,
        compiler_params=PARAMS,
        name="unpack",
    )(packed)
    return (spectra, visibilities)


def solution(mesh):
    groups, times = mesh.devices.shape
    split = Mesh(mesh.devices.reshape(groups // NEAR, NEAR, times), ("far", "near", "tm"))
    inputs = ("far", "near")
    return jax.shard_map(
        body,
        mesh=split,
        in_specs=(P(inputs, "tm"), P(None, None, inputs)),
        out_specs=(P(None, None, inputs, "tm"), P("tm", inputs, None)),
        check_vma=False,
    )
```

```python
import math

import jax
import jax.numpy as jnp
import numpy as np
from jax import lax
from jax.experimental import pallas as pl
from jax.experimental.pallas import tpu as pltpu
from jax.sharding import Mesh, PartitionSpec as P

NFFT = 2048
CH = 256
FIRST = 384
TAPS = 4
NEAR = 4
EARLY = 4
STEP = 256
LANES = 128
VMEM = pl.BlockSpec(memory_space=pltpu.VMEM)
ANY = pl.BlockSpec(memory_space=pl.ANY)
SMEM = pl.BlockSpec(memory_space=pltpu.SMEM)
OWN_PART_VMEM = 59 * 1024 * 1024 + 768 * 1024
PARAMS = pltpu.CompilerParams(vmem_limit_bytes=32 * 1024 * 1024)


def filter_window():
    length = TAPS * NFFT
    position = np.arange(length, dtype=np.float64)
    centred = (position - 0.5 * length + 0.5) / NFFT
    hann_taper = 0.5 - 0.5 * np.cos(2.0 * math.pi * (position + 0.5) / length)
    return np.sinc(centred) * hann_taper


def build_table(window):
    norm_scale = 1.0 / np.sqrt(np.sum(window * window))
    sample = np.arange(NFFT)[:, None]
    channel = FIRST + np.arange(CH)[None, :]
    phase_angle = 2.0 * math.pi / NFFT * (sample * channel % NFFT)
    cosine = np.cos(phase_angle) * norm_scale
    sine = -np.sin(phase_angle) * norm_scale
    return np.concatenate([cosine, sine], axis=1).astype(jnp.bfloat16)


def tap_frames(samples_ref, window_ref, tapped_ref):
    inputs_here = samples_ref.shape[0]
    frames_here = samples_ref.shape[1] // NFFT
    frames_sent = tapped_ref.shape[0] // inputs_here
    for low in range(0, NFFT, STEP):
        values = [
            samples_ref[:, start : start + STEP].astype(jnp.float32)
            for start in range(low, frames_here * NFFT, NFFT)
        ]
        weights = [window_ref[tap : tap + 1, low : low + STEP] for tap in range(TAPS)]
        sums = []
        for frame in range(frames_sent):
            total = jnp.zeros((inputs_here, STEP), jnp.float32)
            for tap in range(TAPS):
                source = frame - TAPS + 1 + tap
                if 0 <= source < frames_here:
                    total = total + weights[tap] * values[source]
            sums.append(total)
            if frame % 2:
                rows = slice((frame - 1) * inputs_here, (frame + 1) * inputs_here)
                tapped_ref[rows, low : low + STEP] = jnp.concatenate(
                    sums[-2:], axis=0
                ).astype(jnp.bfloat16)


def turn_granules(blocks, size):
    count = len(blocks)
    lanes = count * size
    granule = lax.broadcasted_iota(jnp.int32, blocks[0].shape, 1) // size
    blocks = list(blocks)
    distance = count // 2
    while distance:
        upper = (granule & distance) != 0
        shift = distance * size
        for index in range(count):
            if index & distance:
                continue
            low, high = blocks[index], blocks[index + distance]
            blocks[index] = jnp.where(upper, pltpu.roll(high, shift, 1), low)
            blocks[index + distance] = jnp.where(upper, high, pltpu.roll(low, lanes - shift, 1))
        distance //= 2
    return blocks


def own_part_kernel(
    far,
    samples_hbm,
    window_hbm,
    twiddle_hbm,
    gains_hbm,
    own_hbm,
    passed_hbm,
    parcels_ref,
    samples_ref,
    window_ref,
    twiddle_ref,
    gains_ref,
    tapped_ref,
    direct_ref,
    arrived,
    left,
):
    fetches = []
    for index, (source, target) in enumerate(
        (
            (samples_hbm, samples_ref),
            (window_hbm, window_ref),
            (twiddle_hbm, twiddle_ref),
            (gains_hbm, gains_ref),
        )
    ):
        fetches.append(pltpu.make_async_copy(source, target, arrived.at[index]))
        fetches[-1].start()
    inputs_here = samples_ref.shape[0]
    frames_here = samples_ref.shape[1] // NFFT
    fetches[0].wait()
    fetches[1].wait()
    tap_frames(samples_ref, window_ref, tapped_ref)
    fetches[2].wait()
    direct_ref[...] = jnp.dot(
        tapped_ref[...], twiddle_ref[...], preferred_element_type=jnp.float32
    )
    own_rows = own_hbm.shape[0]
    passed_rows = passed_hbm.shape[0]
    stores = [
        pltpu.make_async_copy(direct_ref.at[pl.ds(own_rows, passed_rows), :], passed_hbm, left.at[0]),
        pltpu.make_async_copy(direct_ref.at[pl.ds(0, own_rows), :], own_hbm, left.at[1]),
    ]
    for store in stores:
        store.start()
    fetches[3].wait()
    gain_re = gains_ref[0]
    gain_im = gains_ref[1]
    parts = []
    for frame in range(frames_here + EARLY):
        direct = direct_ref[frame * inputs_here : (frame + 1) * inputs_here, :]
        direct_re = direct[:, :CH]
        direct_im = direct[:, CH:]
        parts.append(
            (
                gain_re * direct_re - gain_im * direct_im,
                gain_re * direct_im + gain_im * direct_re,
            )
        )
    slots = [
        [(part, frame) for frame in range(first, first + 8)]
        for first in range(0, frames_here, 8)
        for part in range(2)
    ]
    slots.append([(part, frames_here + frame) for part in range(2) for frame in range(EARLY)])
    per_far = CH // far
    for place, slot in enumerate(slots):
        columns = slice(place * LANES, (place + 1) * LANES)
        for half in range(CH // LANES):
            lanes = slice(half * LANES, (half + 1) * LANES)
            blocks = turn_granules([parts[frame][part][:, lanes] for part, frame in slot], per_far)
            for index in range(0, len(blocks), 2):
                row = (half * len(blocks) + index) * inputs_here
                parcels_ref[row : row + 2 * inputs_here, columns] = jnp.concatenate(
                    blocks[index : index + 2], axis=0
                ).astype(jnp.bfloat16)
    for store in stores:
        store.wait()


def spectra_kernel(passed_ref, own_ref, gains_ref, spectra_ref, rows_ref):
    inputs_here = gains_ref.shape[1]
    frames_here = own_ref.shape[0] // inputs_here
    slabs = CH // LANES
    gain_re = gains_ref[0]
    gain_im = gains_ref[1]
    for frame in range(frames_here):
        block = slice(frame * inputs_here, (frame + 1) * inputs_here)
        direct = own_ref[block, :]
        if frame < TAPS - 1:
            direct = direct + passed_ref[block, :]
        direct_re = direct[:, :CH]
        direct_im = direct[:, CH:]
        rows = pl.ds(frame, inputs_here, stride=frames_here)
        real_part = gain_re * direct_re - gain_im * direct_im
        imag_part = gain_re * direct_im + gain_im * direct_re
        for slab in range(slabs):
            columns = slice(slab * LANES, (slab + 1) * LANES)
            rows_ref[slab, rows, :] = real_part[:, columns]
            rows_ref[slabs + slab, rows, :] = imag_part[:, columns]
    for part in range(2):
        for slab in range(slabs):
            columns = slice(slab * LANES, (slab + 1) * LANES)
            spectra_ref[part, :, columns] = rows_ref[part * slabs + slab].astype(jnp.bfloat16)


def channel_of(time):
    return time // 4 * 2 + time % 2


def spread_kernel(mine_ref, parcels_ref, turned_ref):
    count, rows, width = parcels_ref.shape
    times = count // NEAR
    stride = mine_ref.shape[1] // rows
    for place in range(0, mine_ref.shape[1], LANES):
        values = mine_ref[:, place : place + LANES].astype(jnp.float32)
        turned_ref[place : place + LANES, :] = values.T
    for near in range(NEAR):
        for channel in range(stride // NEAR):
            start = near * (stride // NEAR) + channel
            values = turned_ref[pl.ds(start, rows, stride=stride), :].astype(jnp.bfloat16)
            for time in range(times):
                if channel_of(time) == channel:
                    parcels_ref[near * times + time] = values


def correlate_kernel(frames_all, inputs_here, place_ref, every_ref, packed_ref):
    count, lines, width = every_ref.shape
    blocks, rows, inputs_all = packed_ref.shape
    times = count // NEAR
    main = lines - 2 * EARLY
    carry = None
    lined = []
    for time in range(times):
        wide = jnp.concatenate(
            [every_ref[near * times + time].astype(jnp.float32) for near in range(NEAR)], axis=1
        )
        tiles = [wide[start : start + 8] for start in range(0, lines, 8)]
        if carry is not None:
            early = lax.broadcasted_iota(jnp.int32, carry.shape, 0) < EARLY
            tiles[0] = tiles[0] + jnp.where(early, carry, 0.0)
            tiles[1] = tiles[1] + jnp.where(early, pltpu.roll(carry, 8 - EARLY, 0), 0.0)
        carry = tiles[-1]
        lined += tiles[:-1]
    source = lax.broadcasted_iota(jnp.int32, (inputs_all, inputs_all), 0)
    target = lax.broadcasted_iota(jnp.int32, (inputs_all, inputs_all), 1)
    near, rest = source // width, source % width
    placed = (rest // inputs_here) * (NEAR * inputs_here) + near * inputs_here + rest % inputs_here
    ordered = jnp.dot(
        jnp.concatenate(lined, axis=0).astype(jnp.bfloat16),
        (placed == target).astype(jnp.bfloat16),
        preferred_element_type=jnp.float32,
    )
    right = ordered.astype(jnp.bfloat16)
    twisted = []
    for start in range(0, times * main, 16):
        twisted.append(ordered[start + 8 : start + 16])
        twisted.append(-ordered[start : start + 8])
    twisted = jnp.concatenate(twisted, axis=0).astype(jnp.bfloat16)
    inner = place_ref[0] == 1
    wide = 2 * rows
    col_index = lax.broadcasted_iota(jnp.int32, (wide, inputs_all), 1)
    row_index = lax.broadcasted_iota(jnp.int32, (wide, inputs_all), 0)
    for side in range(2):
        outer_start = side * (inputs_all - wide)
        inner_start = (1 + side) * wide
        both = []
        for left in (right, twisted):
            chosen = jnp.where(
                inner,
                left[:, inner_start : inner_start + wide],
                left[:, outer_start : outer_start + wide],
            )
            both.append(
                lax.dot_general(
                    chosen,
                    right,
                    (((0,), (0,)), ((), ())),
                    preferred_element_type=jnp.float32,
                )
            )
        upper = row_index + jnp.where(inner, inner_start, outer_start) <= col_index
        values = (jnp.where(upper, both[0], both[1]) * (1.0 / frames_all)).astype(jnp.bfloat16)
        packed_ref[2 * side] = values[:rows]
        packed_ref[2 * side + 1] = values[rows:]


def unpack_kernel(packed_ref, visibilities_ref):
    for channel in range(packed_ref.shape[0]):
        visibilities_ref[:, channel, :] = packed_ref[channel].astype(jnp.float32)


def body(samples, gains):
    inputs_here = samples.shape[0]
    frames_here = samples.shape[1] // NFFT
    times = lax.axis_size("tm")
    far = lax.axis_size("far")
    groups = far * NEAR
    per_group = CH // groups
    inputs_all = inputs_here * groups
    frames_all = frames_here * times
    block = inputs_here * frames_here

    window = filter_window()
    twiddle = jnp.asarray(build_table(window))
    window_taps = jnp.asarray(window.astype(np.float32).reshape(TAPS, NFFT))

    sent = frames_here + EARLY
    gains = gains.transpose(0, 2, 1)

    def own_part(*refs):
        own_part_kernel(far, *refs)

    own, passed, parcels = pl.pallas_call(
        own_part,
        out_shape=(
            jax.ShapeDtypeStruct((block, 2 * CH), jnp.float32),
            jax.ShapeDtypeStruct(((TAPS - 1) * inputs_here, 2 * CH), jnp.float32),
            jax.ShapeDtypeStruct((far * inputs_here, sent * 2 * CH // far), jnp.bfloat16),
        ),
        in_specs=[ANY] * 4,
        out_specs=(ANY, ANY, VMEM),
        scratch_shapes=[
            pltpu.VMEM(samples.shape, jnp.bfloat16),
            pltpu.VMEM(window_taps.shape, jnp.float32),
            pltpu.VMEM(twiddle.shape, jnp.bfloat16),
            pltpu.VMEM(gains.shape, jnp.float32),
            pltpu.VMEM((sent * inputs_here, NFFT), jnp.bfloat16),
            pltpu.VMEM((sent * inputs_here, 2 * CH), jnp.float32),
            pltpu.SemaphoreType.DMA((4,)),
            pltpu.SemaphoreType.DMA((2,)),
        ],
        compiler_params=pltpu.CompilerParams(vmem_limit_bytes=OWN_PART_VMEM),
        cost_estimate=pl.CostEstimate(
            flops=2 * sent * inputs_here * NFFT * 2 * CH,
            bytes_accessed=3 * 1024 * 1024,
            transcendentals=0,
        ),
        name="own_part",
    )(samples, window_taps, twiddle, gains)

    parcels = parcels.reshape(far, inputs_here, sent * 2 * CH // far)
    mine = lax.all_to_all(parcels, "far", 0, 0).reshape(far * inputs_here, sent * 2 * CH // far)

    passed = lax.ppermute(passed, "tm", [(source, source + 1) for source in range(times - 1)])
    spectra = pl.pallas_call(
        spectra_kernel,
        out_shape=jax.ShapeDtypeStruct((2, block, CH), jnp.bfloat16),
        in_specs=[VMEM] * 3,
        out_specs=VMEM,
        scratch_shapes=[pltpu.VMEM((2 * CH // LANES, block, LANES), jnp.float32)],
        compiler_params=PARAMS,
        cost_estimate=pl.CostEstimate(
            flops=8 * block * 2 * CH, bytes_accessed=1024 * 1024, transcendentals=0
        ),
        name="spectra",
    )(passed, own, gains)
    spectra = spectra.reshape(2, inputs_here, frames_here, CH).transpose(0, 3, 1, 2)

    lines = 2 * sent
    spread = pl.pallas_call(
        spread_kernel,
        out_shape=jax.ShapeDtypeStruct((NEAR * times, lines, far * inputs_here), jnp.bfloat16),
        in_specs=[VMEM],
        out_specs=VMEM,
        scratch_shapes=[pltpu.VMEM((sent * 2 * CH // far, far * inputs_here), jnp.float32)],
        compiler_params=PARAMS,
        name="spread",
    )(mine)
    every = lax.all_to_all(spread, ("near", "tm"), 0, 0)
    every, spectra = lax.optimization_barrier((every, spectra))

    def correlate(*refs):
        correlate_kernel(frames_all, inputs_here, *refs)

    rows = inputs_all // times
    place = lax.axis_index("tm").astype(jnp.int32)
    inner = (place >= times // 4) & (place < times - times // 4)
    packed = pl.pallas_call(
        correlate,
        out_shape=jax.ShapeDtypeStruct((times // 2, rows, inputs_all), jnp.bfloat16),
        in_specs=[SMEM, VMEM],
        out_specs=VMEM,
        compiler_params=PARAMS,
        name="correlate",
    )(inner.astype(jnp.int32)[None], every)
    squares = [[0, 1, 6, 7], [2, 3, 4, 5]]
    packed = lax.all_to_all(packed, "tm", 0, 0, axis_index_groups=squares)
    visibilities = pl.pallas_call(
        unpack_kernel,
        out_shape=jax.ShapeDtypeStruct((rows, per_group, inputs_all), jnp.float32),
        in_specs=[VMEM],
        out_specs=VMEM,
        compiler_params=PARAMS,
        name="unpack",
    )(packed)
    return (spectra, visibilities)


def solution(mesh):
    groups, times = mesh.devices.shape
    split = Mesh(mesh.devices.reshape(groups // NEAR, NEAR, times), ("far", "near", "tm"))
    inputs = ("far", "near")
    return jax.shard_map(
        body,
        mesh=split,
        in_specs=(P(inputs, "tm"), P(None, None, inputs)),
        out_specs=(P(None, None, inputs, "tm"), P("tm", inputs, None)),
        check_vma=False,
    )
```

```python
import math

import jax
import jax.numpy as jnp
import numpy as np
from jax import lax
from jax.experimental import pallas as pl
from jax.experimental.pallas import tpu as pltpu
from jax.sharding import Mesh, PartitionSpec as P

NFFT = 2048
CH = 256
FIRST = 384
TAPS = 4
NEAR = 4
EARLY = 4
STEP = 512
LANES = 128
VMEM = pl.BlockSpec(memory_space=pltpu.VMEM)
ANY = pl.BlockSpec(memory_space=pl.ANY)
SMEM = pl.BlockSpec(memory_space=pltpu.SMEM)
OWN_PART_VMEM = 59 * 1024 * 1024 + 768 * 1024
PARAMS = pltpu.CompilerParams(vmem_limit_bytes=32 * 1024 * 1024)


def filter_window():
    length = TAPS * NFFT
    position = np.arange(length, dtype=np.float64)
    centred = (position - 0.5 * length + 0.5) / NFFT
    hann_taper = 0.5 - 0.5 * np.cos(2.0 * math.pi * (position + 0.5) / length)
    return np.sinc(centred) * hann_taper


def build_table(window):
    norm_scale = 1.0 / np.sqrt(np.sum(window * window))
    sample = np.arange(NFFT)[:, None]
    channel = FIRST + np.arange(CH)[None, :]
    phase_angle = 2.0 * math.pi / NFFT * (sample * channel % NFFT)
    cosine = np.cos(phase_angle) * norm_scale
    sine = -np.sin(phase_angle) * norm_scale
    return np.concatenate([cosine, sine], axis=1).astype(jnp.bfloat16)


def tap_frames(frame_at, window_ref, tapped_ref, first, count):
    inputs_here = tapped_ref.shape[0] // count
    for pair in range(0, count, 2):
        for low in range(0, NFFT, STEP):
            sums = []
            for frame in (first + pair, first + pair + 1):
                total = jnp.zeros((inputs_here, STEP), jnp.float32)
                for tap in range(TAPS):
                    values = frame_at(frame - TAPS + 1 + tap, low)
                    if values is not None:
                        weights = window_ref[tap : tap + 1, low : low + STEP]
                        total = total + weights * values.astype(jnp.float32)
                sums.append(total)
            tapped_ref[pair * inputs_here : (pair + 2) * inputs_here, low : low + STEP] = (
                jnp.concatenate(sums, axis=0).astype(jnp.bfloat16)
            )


def turn_granules(blocks, size):
    count = len(blocks)
    lanes = count * size
    granule = lax.broadcasted_iota(jnp.int32, blocks[0].shape, 1) // size
    blocks = list(blocks)
    distance = count // 2
    while distance:
        upper = (granule & distance) != 0
        shift = distance * size
        for index in range(count):
            if index & distance:
                continue
            low, high = blocks[index], blocks[index + distance]
            blocks[index] = jnp.where(upper, pltpu.roll(high, shift, 1), low)
            blocks[index + distance] = jnp.where(upper, high, pltpu.roll(low, lanes - shift, 1))
        distance //= 2
    return blocks


def own_part_kernel(
    far,
    samples_hbm,
    window_hbm,
    twiddle_hbm,
    gains_hbm,
    own_ref,
    passed_ref,
    parcels_ref,
    samples_ref,
    window_ref,
    twiddle_ref,
    gains_ref,
    tapped_ref,
    direct_ref,
    arrived,
):
    fetches = []
    for index, (source, target) in enumerate(
        (
            (samples_hbm, samples_ref),
            (window_hbm, window_ref),
            (twiddle_hbm, twiddle_ref),
            (gains_hbm, gains_ref),
        )
    ):
        fetches.append(pltpu.make_async_copy(source, target, arrived.at[index]))
        fetches[-1].start()
    inputs_here = samples_ref.shape[0]
    frames_here = samples_ref.shape[1] // NFFT

    def frame_at(frame, low):
        if not 0 <= frame < frames_here:
            return None
        start = frame * NFFT + low
        return samples_ref[:, start : start + STEP]

    fetches[0].wait()
    fetches[1].wait()
    tap_frames(frame_at, window_ref, tapped_ref, 0, frames_here + EARLY)
    fetches[2].wait()
    direct_ref[...] = jnp.dot(
        tapped_ref[...], twiddle_ref[...], preferred_element_type=jnp.float32
    )
    fetches[3].wait()
    own_rows = own_ref.shape[0]
    own_ref[...] = direct_ref[:own_rows, :]
    passed_ref[...] = direct_ref[own_rows : own_rows + passed_ref.shape[0], :]
    gain_re = gains_ref[0]
    gain_im = gains_ref[1]
    parts = []
    for frame in range(frames_here + EARLY):
        direct = direct_ref[frame * inputs_here : (frame + 1) * inputs_here, :]
        direct_re = direct[:, :CH]
        direct_im = direct[:, CH:]
        parts.append(
            (
                gain_re * direct_re - gain_im * direct_im,
                gain_re * direct_im + gain_im * direct_re,
            )
        )
    slots = [
        [(part, frame) for frame in range(first, first + 8)]
        for first in range(0, frames_here, 8)
        for part in range(2)
    ]
    slots.append([(part, frames_here + frame) for part in range(2) for frame in range(EARLY)])
    per_far = CH // far
    for place, slot in enumerate(slots):
        columns = slice(place * LANES, (place + 1) * LANES)
        for half in range(CH // LANES):
            lanes = slice(half * LANES, (half + 1) * LANES)
            blocks = turn_granules([parts[frame][part][:, lanes] for part, frame in slot], per_far)
            for index in range(0, len(blocks), 2):
                row = (half * len(blocks) + index + far // 2) % far * inputs_here
                parcels_ref[row : row + 2 * inputs_here, columns] = jnp.concatenate(
                    blocks[index : index + 2], axis=0
                ).astype(jnp.bfloat16)


def spectra_kernel(passed_ref, own_ref, gains_ref, spectra_ref, rows_ref):
    inputs_here = gains_ref.shape[1]
    frames_here = own_ref.shape[0] // inputs_here
    slabs = CH // LANES
    gain_re = gains_ref[0]
    gain_im = gains_ref[1]
    for frame in range(frames_here):
        block = slice(frame * inputs_here, (frame + 1) * inputs_here)
        direct = own_ref[block, :]
        if frame < TAPS - 1:
            direct = direct + passed_ref[block, :]
        direct_re = direct[:, :CH]
        direct_im = direct[:, CH:]
        rows = pl.ds(frame, inputs_here, stride=frames_here)
        real_part = gain_re * direct_re - gain_im * direct_im
        imag_part = gain_re * direct_im + gain_im * direct_re
        for slab in range(slabs):
            columns = slice(slab * LANES, (slab + 1) * LANES)
            rows_ref[slab, rows, :] = real_part[:, columns]
            rows_ref[slabs + slab, rows, :] = imag_part[:, columns]
    for part in range(2):
        for slab in range(slabs):
            columns = slice(slab * LANES, (slab + 1) * LANES)
            spectra_ref[part, :, columns] = rows_ref[part * slabs + slab].astype(jnp.bfloat16)


def channel_of(time):
    return time // 4 * 2 + time % 2


def spread_kernel(mine_ref, parcels_ref, turned_ref):
    count, rows, width = parcels_ref.shape
    times = count // NEAR
    stride = mine_ref.shape[1] // rows
    for place in range(0, mine_ref.shape[1], LANES):
        values = mine_ref[:, place : place + LANES].astype(jnp.float32)
        turned_ref[place : place + LANES, :] = values.T
    for near in range(NEAR):
        for channel in range(stride // NEAR):
            start = near * (stride // NEAR) + channel
            values = turned_ref[pl.ds(start, rows, stride=stride), :].astype(jnp.bfloat16)
            for time in range(times):
                if channel_of(time) == channel:
                    parcels_ref[near * times + time] = values


def correlate_kernel(frames_all, inputs_here, place_ref, every_ref, packed_ref):
    count, lines, width = every_ref.shape
    blocks, rows, inputs_all = packed_ref.shape
    times = count // NEAR
    main = lines - 2 * EARLY
    carry = None
    lined = []
    for time in range(times):
        wide = jnp.concatenate(
            [every_ref[near * times + time].astype(jnp.float32) for near in range(NEAR)], axis=1
        )
        tiles = [wide[start : start + 8] for start in range(0, lines, 8)]
        if carry is not None:
            early = lax.broadcasted_iota(jnp.int32, carry.shape, 0) < EARLY
            tiles[0] = tiles[0] + jnp.where(early, carry, 0.0)
            tiles[1] = tiles[1] + jnp.where(early, pltpu.roll(carry, 8 - EARLY, 0), 0.0)
        carry = tiles[-1]
        lined += tiles[:-1]
    source = lax.broadcasted_iota(jnp.int32, (inputs_all, inputs_all), 0)
    target = lax.broadcasted_iota(jnp.int32, (inputs_all, inputs_all), 1)
    near, rest = source // width, source % width
    far = width // inputs_here
    place = (rest // inputs_here + far // 2) % far
    placed = place * (NEAR * inputs_here) + near * inputs_here + rest % inputs_here
    ordered = jnp.dot(
        jnp.concatenate(lined, axis=0).astype(jnp.bfloat16),
        (placed == target).astype(jnp.bfloat16),
        preferred_element_type=jnp.float32,
    )
    right = ordered.astype(jnp.bfloat16)
    twisted = []
    for start in range(0, times * main, 16):
        twisted.append(ordered[start + 8 : start + 16])
        twisted.append(-ordered[start : start + 8])
    twisted = jnp.concatenate(twisted, axis=0).astype(jnp.bfloat16)
    inner = place_ref[0] == 1
    wide = 2 * rows
    col_index = lax.broadcasted_iota(jnp.int32, (wide, inputs_all), 1)
    row_index = lax.broadcasted_iota(jnp.int32, (wide, inputs_all), 0)
    for side in range(2):
        outer_start = side * (inputs_all - wide)
        inner_start = (1 + side) * wide
        both = []
        for left in (right, twisted):
            chosen = jnp.where(
                inner,
                left[:, inner_start : inner_start + wide],
                left[:, outer_start : outer_start + wide],
            )
            both.append(
                lax.dot_general(
                    chosen,
                    right,
                    (((0,), (0,)), ((), ())),
                    preferred_element_type=jnp.float32,
                )
            )
        upper = row_index + jnp.where(inner, inner_start, outer_start) <= col_index
        values = (jnp.where(upper, both[0], both[1]) * (1.0 / frames_all)).astype(jnp.bfloat16)
        packed_ref[2 * side] = values[:rows]
        packed_ref[2 * side + 1] = values[rows:]


def unpack_kernel(packed_ref, visibilities_ref):
    for channel in range(packed_ref.shape[0]):
        visibilities_ref[:, channel, :] = packed_ref[channel].astype(jnp.float32)


def body(samples, gains):
    inputs_here = samples.shape[0]
    frames_here = samples.shape[1] // NFFT
    times = lax.axis_size("tm")
    far = lax.axis_size("far")
    groups = far * NEAR
    per_group = CH // groups
    inputs_all = inputs_here * groups
    frames_all = frames_here * times
    block = inputs_here * frames_here

    window = filter_window()
    twiddle = jnp.asarray(build_table(window))
    window_taps = jnp.asarray(window.astype(np.float32).reshape(TAPS, NFFT))

    sent = frames_here + EARLY
    gains = gains.transpose(0, 2, 1)

    def own_part(*refs):
        own_part_kernel(far, *refs)

    own, passed, parcels = pl.pallas_call(
        own_part,
        out_shape=(
            jax.ShapeDtypeStruct((block, 2 * CH), jnp.float32),
            jax.ShapeDtypeStruct(((TAPS - 1) * inputs_here, 2 * CH), jnp.float32),
            jax.ShapeDtypeStruct((far * inputs_here, sent * 2 * CH // far), jnp.bfloat16),
        ),
        in_specs=[ANY] * 4,
        out_specs=(VMEM, VMEM, VMEM),
        scratch_shapes=[
            pltpu.VMEM(samples.shape, jnp.bfloat16),
            pltpu.VMEM(window_taps.shape, jnp.float32),
            pltpu.VMEM(twiddle.shape, jnp.bfloat16),
            pltpu.VMEM(gains.shape, jnp.float32),
            pltpu.VMEM((sent * inputs_here, NFFT), jnp.bfloat16),
            pltpu.VMEM((sent * inputs_here, 2 * CH), jnp.float32),
            pltpu.SemaphoreType.DMA((4,)),
        ],
        compiler_params=pltpu.CompilerParams(vmem_limit_bytes=OWN_PART_VMEM),
        cost_estimate=pl.CostEstimate(
            flops=2 * sent * inputs_here * NFFT * 2 * CH,
            bytes_accessed=3 * 1024 * 1024,
            transcendentals=0,
        ),
        name="own_part",
    )(samples, window_taps, twiddle, gains)

    parcels = parcels.reshape(far, inputs_here, sent * 2 * CH // far)
    middle_first = [[(place + far // 2) % far for place in range(far)]]
    mine = lax.all_to_all(parcels, "far", 0, 0, axis_index_groups=middle_first)
    mine = mine.reshape(far * inputs_here, sent * 2 * CH // far)

    passed = lax.ppermute(passed, "tm", [(source, source + 1) for source in range(times - 1)])
    spectra = pl.pallas_call(
        spectra_kernel,
        out_shape=jax.ShapeDtypeStruct((2, block, CH), jnp.bfloat16),
        in_specs=[VMEM] * 3,
        out_specs=VMEM,
        scratch_shapes=[pltpu.VMEM((2 * CH // LANES, block, LANES), jnp.float32)],
        compiler_params=PARAMS,
        cost_estimate=pl.CostEstimate(
            flops=8 * block * 2 * CH, bytes_accessed=1024 * 1024, transcendentals=0
        ),
        name="spectra",
    )(passed, own, gains)
    mine, spectra = lax.optimization_barrier((mine, spectra))
    spectra = spectra.reshape(2, inputs_here, frames_here, CH).transpose(0, 3, 1, 2)

    lines = 2 * sent
    spread = pl.pallas_call(
        spread_kernel,
        out_shape=jax.ShapeDtypeStruct((NEAR * times, lines, far * inputs_here), jnp.bfloat16),
        in_specs=[VMEM],
        out_specs=VMEM,
        scratch_shapes=[pltpu.VMEM((sent * 2 * CH // far, far * inputs_here), jnp.float32)],
        compiler_params=PARAMS,
        name="spread",
    )(mine)
    every = lax.all_to_all(spread, ("near", "tm"), 0, 0)

    def correlate(*refs):
        correlate_kernel(frames_all, inputs_here, *refs)

    rows = inputs_all // times
    place = lax.axis_index("tm").astype(jnp.int32)
    inner = (place >= times // 4) & (place < times - times // 4)
    packed = pl.pallas_call(
        correlate,
        out_shape=jax.ShapeDtypeStruct((times // 2, rows, inputs_all), jnp.bfloat16),
        in_specs=[SMEM, VMEM],
        out_specs=VMEM,
        compiler_params=PARAMS,
        name="correlate",
    )(inner.astype(jnp.int32)[None], every)
    squares = [[0, 1, 6, 7], [2, 3, 4, 5]]
    packed = lax.all_to_all(packed, "tm", 0, 0, axis_index_groups=squares)
    visibilities = pl.pallas_call(
        unpack_kernel,
        out_shape=jax.ShapeDtypeStruct((rows, per_group, inputs_all), jnp.float32),
        in_specs=[VMEM],
        out_specs=VMEM,
        compiler_params=PARAMS,
        name="unpack",
    )(packed)
    return (spectra, visibilities)


def solution(mesh):
    groups, times = mesh.devices.shape
    split = Mesh(mesh.devices.reshape(groups // NEAR, NEAR, times), ("far", "near", "tm"))
    inputs = ("far", "near")
    return jax.shard_map(
        body,
        mesh=split,
        in_specs=(P(inputs, "tm"), P(None, None, inputs)),
        out_specs=(P(None, None, inputs, "tm"), P("tm", inputs, None)),
        check_vma=False,
    )
```

```python
import math

import jax
import jax.numpy as jnp
import numpy as np
from jax import lax
from jax.experimental import pallas as pl
from jax.experimental.pallas import tpu as pltpu
from jax.sharding import Mesh, PartitionSpec as P

NFFT = 2048
CH = 256
FIRST = 384
TAPS = 4
NEAR = 4
EARLY = 4
STEP = 512
LANES = 128
VMEM = pl.BlockSpec(memory_space=pltpu.VMEM)
ANY = pl.BlockSpec(memory_space=pl.ANY)
SMEM = pl.BlockSpec(memory_space=pltpu.SMEM)
OWN_PART_VMEM = 59 * 1024 * 1024 + 768 * 1024
PARAMS = pltpu.CompilerParams(vmem_limit_bytes=32 * 1024 * 1024)


def filter_window():
    length = TAPS * NFFT
    position = np.arange(length, dtype=np.float64)
    centred = (position - 0.5 * length + 0.5) / NFFT
    hann_taper = 0.5 - 0.5 * np.cos(2.0 * math.pi * (position + 0.5) / length)
    return np.sinc(centred) * hann_taper


def build_table(window):
    norm_scale = 1.0 / np.sqrt(np.sum(window * window))
    sample = np.arange(NFFT)[:, None]
    channel = FIRST + np.arange(CH)[None, :]
    phase_angle = 2.0 * math.pi / NFFT * (sample * channel % NFFT)
    cosine = np.cos(phase_angle) * norm_scale
    sine = -np.sin(phase_angle) * norm_scale
    return np.concatenate([cosine, sine], axis=1).astype(jnp.bfloat16)


def tap_frames(frame_at, window_ref, tapped_ref, first, count):
    inputs_here = tapped_ref.shape[0] // count
    for pair in range(0, count, 2):
        for low in range(0, NFFT, STEP):
            sums = []
            for frame in (first + pair, first + pair + 1):
                total = jnp.zeros((inputs_here, STEP), jnp.float32)
                for tap in range(TAPS):
                    values = frame_at(frame - TAPS + 1 + tap, low)
                    if values is not None:
                        weights = window_ref[tap : tap + 1, low : low + STEP]
                        total = total + weights * values.astype(jnp.float32)
                sums.append(total)
            tapped_ref[pair * inputs_here : (pair + 2) * inputs_here, low : low + STEP] = (
                jnp.concatenate(sums, axis=0).astype(jnp.bfloat16)
            )


def turn_granules(blocks, size):
    count = len(blocks)
    lanes = count * size
    granule = lax.broadcasted_iota(jnp.int32, blocks[0].shape, 1) // size
    blocks = list(blocks)
    distance = count // 2
    while distance:
        upper = (granule & distance) != 0
        shift = distance * size
        for index in range(count):
            if index & distance:
                continue
            low, high = blocks[index], blocks[index + distance]
            blocks[index] = jnp.where(upper, pltpu.roll(high, shift, 1), low)
            blocks[index + distance] = jnp.where(upper, high, pltpu.roll(low, lanes - shift, 1))
        distance //= 2
    return blocks


def own_part_kernel(
    far,
    samples_hbm,
    window_hbm,
    twiddle_hbm,
    gains_hbm,
    own_ref,
    passed_ref,
    parcels_ref,
    samples_ref,
    window_ref,
    twiddle_ref,
    gains_ref,
    tapped_ref,
    direct_ref,
    arrived,
):
    fetches = []
    for index, (source, target) in enumerate(
        (
            (samples_hbm, samples_ref),
            (window_hbm, window_ref),
            (twiddle_hbm, twiddle_ref),
            (gains_hbm, gains_ref),
        )
    ):
        fetches.append(pltpu.make_async_copy(source, target, arrived.at[index]))
        fetches[-1].start()
    inputs_here = samples_ref.shape[0]
    frames_here = samples_ref.shape[1] // NFFT

    def frame_at(frame, low):
        if not 0 <= frame < frames_here:
            return None
        start = frame * NFFT + low
        return samples_ref[:, start : start + STEP]

    fetches[0].wait()
    fetches[1].wait()
    tap_frames(frame_at, window_ref, tapped_ref, 0, frames_here + EARLY)
    fetches[2].wait()
    direct_ref[...] = jnp.dot(
        tapped_ref[...], twiddle_ref[...], preferred_element_type=jnp.float32
    )
    fetches[3].wait()
    own_rows = own_ref.shape[0]
    own_ref[...] = direct_ref[:own_rows, :]
    passed_ref[...] = direct_ref[own_rows : own_rows + passed_ref.shape[0], :]
    gain_re = gains_ref[0]
    gain_im = gains_ref[1]
    parts = []
    for frame in range(frames_here + EARLY):
        direct = direct_ref[frame * inputs_here : (frame + 1) * inputs_here, :]
        direct_re = direct[:, :CH]
        direct_im = direct[:, CH:]
        parts.append(
            (
                gain_re * direct_re - gain_im * direct_im,
                gain_re * direct_im + gain_im * direct_re,
            )
        )
    slots = [
        [(part, frame) for frame in range(first, first + 8)]
        for first in range(0, frames_here, 8)
        for part in range(2)
    ]
    slots.append([(part, frames_here + frame) for part in range(2) for frame in range(EARLY)])
    per_far = CH // far
    for place, slot in enumerate(slots):
        columns = slice(place * LANES, (place + 1) * LANES)
        for half in range(CH // LANES):
            lanes = slice(half * LANES, (half + 1) * LANES)
            blocks = turn_granules([parts[frame][part][:, lanes] for part, frame in slot], per_far)
            for index in range(0, len(blocks), 2):
                row = (half * len(blocks) + index + far // 2) % far * inputs_here
                parcels_ref[row : row + 2 * inputs_here, columns] = jnp.concatenate(
                    blocks[index : index + 2], axis=0
                ).astype(jnp.bfloat16)


def spectra_kernel(passed_ref, own_ref, gains_ref, spectra_ref, rows_ref):
    inputs_here = gains_ref.shape[1]
    frames_here = own_ref.shape[0] // inputs_here
    slabs = CH // LANES
    gain_re = gains_ref[0]
    gain_im = gains_ref[1]
    for frame in range(frames_here):
        block = slice(frame * inputs_here, (frame + 1) * inputs_here)
        direct = own_ref[block, :]
        if frame < TAPS - 1:
            direct = direct + passed_ref[block, :]
        direct_re = direct[:, :CH]
        direct_im = direct[:, CH:]
        rows = pl.ds(frame, inputs_here, stride=frames_here)
        real_part = gain_re * direct_re - gain_im * direct_im
        imag_part = gain_re * direct_im + gain_im * direct_re
        for slab in range(slabs):
            columns = slice(slab * LANES, (slab + 1) * LANES)
            rows_ref[slab, rows, :] = real_part[:, columns]
            rows_ref[slabs + slab, rows, :] = imag_part[:, columns]
    for part in range(2):
        for slab in range(slabs):
            columns = slice(slab * LANES, (slab + 1) * LANES)
            spectra_ref[part, :, columns] = rows_ref[part * slabs + slab].astype(jnp.bfloat16)


def channel_of(time):
    return time // 4 * 2 + time % 2


def place_in_plane(near, time, times):
    return (near + NEAR // 2) % NEAR * times + (time + times // 2) % times


def spread_kernel(mine_ref, parcels_ref, turned_ref):
    count, rows, width = parcels_ref.shape
    times = count // NEAR
    stride = mine_ref.shape[1] // rows
    for place in range(0, mine_ref.shape[1], LANES):
        values = mine_ref[:, place : place + LANES].astype(jnp.float32)
        turned_ref[place : place + LANES, :] = values.T
    for near in range(NEAR):
        for channel in range(stride // NEAR):
            start = near * (stride // NEAR) + channel
            values = turned_ref[pl.ds(start, rows, stride=stride), :].astype(jnp.bfloat16)
            for time in range(times):
                if channel_of(time) == channel:
                    parcels_ref[place_in_plane(near, time, times)] = values


def correlate_kernel(frames_all, inputs_here, place_ref, every_ref, packed_ref):
    count, lines, width = every_ref.shape
    blocks, rows, inputs_all = packed_ref.shape
    times = count // NEAR
    main = lines - 2 * EARLY
    carry = None
    lined = []
    for time in range(times):
        pieces = [every_ref[place_in_plane(near, time, times)] for near in range(NEAR)]
        wide = jnp.concatenate([piece.astype(jnp.float32) for piece in pieces], axis=1)
        tiles = [wide[start : start + 8] for start in range(0, lines, 8)]
        if carry is not None:
            early = lax.broadcasted_iota(jnp.int32, carry.shape, 0) < EARLY
            tiles[0] = tiles[0] + jnp.where(early, carry, 0.0)
            tiles[1] = tiles[1] + jnp.where(early, pltpu.roll(carry, 8 - EARLY, 0), 0.0)
        carry = tiles[-1]
        lined += tiles[:-1]
    source = lax.broadcasted_iota(jnp.int32, (inputs_all, inputs_all), 0)
    target = lax.broadcasted_iota(jnp.int32, (inputs_all, inputs_all), 1)
    near, rest = source // width, source % width
    far = width // inputs_here
    place = (rest // inputs_here + far // 2) % far
    placed = place * (NEAR * inputs_here) + near * inputs_here + rest % inputs_here
    ordered = jnp.dot(
        jnp.concatenate(lined, axis=0).astype(jnp.bfloat16),
        (placed == target).astype(jnp.bfloat16),
        preferred_element_type=jnp.float32,
    )
    right = ordered.astype(jnp.bfloat16)
    twisted = []
    for start in range(0, times * main, 16):
        twisted.append(ordered[start + 8 : start + 16])
        twisted.append(-ordered[start : start + 8])
    twisted = jnp.concatenate(twisted, axis=0).astype(jnp.bfloat16)
    inner = place_ref[0] == 1
    wide = 2 * rows
    col_index = lax.broadcasted_iota(jnp.int32, (wide, inputs_all), 1)
    row_index = lax.broadcasted_iota(jnp.int32, (wide, inputs_all), 0)
    for side in range(2):
        outer_start = side * (inputs_all - wide)
        inner_start = (1 + side) * wide
        both = []
        for left in (right, twisted):
            chosen = jnp.where(
                inner,
                left[:, inner_start : inner_start + wide],
                left[:, outer_start : outer_start + wide],
            )
            both.append(
                lax.dot_general(
                    chosen,
                    right,
                    (((0,), (0,)), ((), ())),
                    preferred_element_type=jnp.float32,
                )
            )
        upper = row_index + jnp.where(inner, inner_start, outer_start) <= col_index
        values = (jnp.where(upper, both[0], both[1]) * (1.0 / frames_all)).astype(jnp.bfloat16)
        packed_ref[blocks - 1 - 2 * side] = values[:rows]
        packed_ref[blocks - 2 - 2 * side] = values[rows:]


def unpack_kernel(packed_ref, visibilities_ref):
    channels = packed_ref.shape[0]
    for channel in range(channels):
        values = packed_ref[channels - 1 - channel]
        visibilities_ref[:, channel, :] = values.astype(jnp.float32)


def body(samples, gains):
    inputs_here = samples.shape[0]
    frames_here = samples.shape[1] // NFFT
    times = lax.axis_size("tm")
    far = lax.axis_size("far")
    groups = far * NEAR
    per_group = CH // groups
    inputs_all = inputs_here * groups
    frames_all = frames_here * times
    block = inputs_here * frames_here

    window = filter_window()
    twiddle = jnp.asarray(build_table(window))
    window_taps = jnp.asarray(window.astype(np.float32).reshape(TAPS, NFFT))

    sent = frames_here + EARLY
    gains = gains.transpose(0, 2, 1)

    def own_part(*refs):
        own_part_kernel(far, *refs)

    own, passed, parcels = pl.pallas_call(
        own_part,
        out_shape=(
            jax.ShapeDtypeStruct((block, 2 * CH), jnp.float32),
            jax.ShapeDtypeStruct(((TAPS - 1) * inputs_here, 2 * CH), jnp.float32),
            jax.ShapeDtypeStruct((far * inputs_here, sent * 2 * CH // far), jnp.bfloat16),
        ),
        in_specs=[ANY] * 4,
        out_specs=(VMEM, VMEM, VMEM),
        scratch_shapes=[
            pltpu.VMEM(samples.shape, jnp.bfloat16),
            pltpu.VMEM(window_taps.shape, jnp.float32),
            pltpu.VMEM(twiddle.shape, jnp.bfloat16),
            pltpu.VMEM(gains.shape, jnp.float32),
            pltpu.VMEM((sent * inputs_here, NFFT), jnp.bfloat16),
            pltpu.VMEM((sent * inputs_here, 2 * CH), jnp.float32),
            pltpu.SemaphoreType.DMA((4,)),
        ],
        compiler_params=pltpu.CompilerParams(vmem_limit_bytes=OWN_PART_VMEM),
        cost_estimate=pl.CostEstimate(
            flops=2 * sent * inputs_here * NFFT * 2 * CH,
            bytes_accessed=3 * 1024 * 1024,
            transcendentals=0,
        ),
        name="own_part",
    )(samples, window_taps, twiddle, gains)

    parcels = parcels.reshape(far, inputs_here, sent * 2 * CH // far)
    middle_first = [[(place + far // 2) % far for place in range(far)]]
    mine = lax.all_to_all(parcels, "far", 0, 0, axis_index_groups=middle_first)
    mine = mine.reshape(far * inputs_here, sent * 2 * CH // far)

    passed = lax.ppermute(passed, "tm", [(source, source + 1) for source in range(times - 1)])
    spectra = pl.pallas_call(
        spectra_kernel,
        out_shape=jax.ShapeDtypeStruct((2, block, CH), jnp.bfloat16),
        in_specs=[VMEM] * 3,
        out_specs=VMEM,
        scratch_shapes=[pltpu.VMEM((2 * CH // LANES, block, LANES), jnp.float32)],
        compiler_params=PARAMS,
        cost_estimate=pl.CostEstimate(
            flops=8 * block * 2 * CH, bytes_accessed=1024 * 1024, transcendentals=0
        ),
        name="spectra",
    )(passed, own, gains)
    mine, spectra = lax.optimization_barrier((mine, spectra))
    spectra = spectra.reshape(2, inputs_here, frames_here, CH).transpose(0, 3, 1, 2)

    lines = 2 * sent
    spread = pl.pallas_call(
        spread_kernel,
        out_shape=jax.ShapeDtypeStruct((NEAR * times, lines, far * inputs_here), jnp.bfloat16),
        in_specs=[VMEM],
        out_specs=VMEM,
        scratch_shapes=[pltpu.VMEM((sent * 2 * CH // far, far * inputs_here), jnp.float32)],
        compiler_params=PARAMS,
        name="spread",
    )(mine)
    members = [(near, time) for near in range(NEAR) for time in range(times)]
    members.sort(key=lambda member: place_in_plane(*member, times))
    plane = [[near * times + time for near, time in members]]
    every = lax.all_to_all(spread, ("near", "tm"), 0, 0, axis_index_groups=plane)

    def correlate(*refs):
        correlate_kernel(frames_all, inputs_here, *refs)

    rows = inputs_all // times
    place = lax.axis_index("tm").astype(jnp.int32)
    inner = (place >= times // 4) & (place < times - times // 4)
    packed = pl.pallas_call(
        correlate,
        out_shape=jax.ShapeDtypeStruct((times // 2, rows, inputs_all), jnp.bfloat16),
        in_specs=[SMEM, VMEM],
        out_specs=VMEM,
        compiler_params=PARAMS,
        name="correlate",
    )(inner.astype(jnp.int32)[None], every)
    squares = [[7, 6, 1, 0], [5, 4, 3, 2]]
    packed = lax.all_to_all(packed, "tm", 0, 0, axis_index_groups=squares)
    visibilities = pl.pallas_call(
        unpack_kernel,
        out_shape=jax.ShapeDtypeStruct((rows, per_group, inputs_all), jnp.float32),
        in_specs=[VMEM],
        out_specs=VMEM,
        compiler_params=PARAMS,
        name="unpack",
    )(packed)
    return (spectra, visibilities)


def solution(mesh):
    groups, times = mesh.devices.shape
    split = Mesh(mesh.devices.reshape(groups // NEAR, NEAR, times), ("far", "near", "tm"))
    inputs = ("far", "near")
    return jax.shard_map(
        body,
        mesh=split,
        in_specs=(P(inputs, "tm"), P(None, None, inputs)),
        out_specs=(P(None, None, inputs, "tm"), P("tm", inputs, None)),
        check_vma=False,
    )
```

```python
import math

import jax
import jax.numpy as jnp
import numpy as np
from jax import lax
from jax.experimental import pallas as pl
from jax.experimental.pallas import tpu as pltpu
from jax.sharding import Mesh, PartitionSpec as P

NFFT = 2048
CH = 256
FIRST = 384
TAPS = 4
NEAR = 4
EARLY = 4
STEP = 512
LANES = 128
VMEM = pl.BlockSpec(memory_space=pltpu.VMEM)
ANY = pl.BlockSpec(memory_space=pl.ANY)
SMEM = pl.BlockSpec(memory_space=pltpu.SMEM)
OWN_PART_VMEM = 59 * 1024 * 1024 + 768 * 1024
PARAMS = pltpu.CompilerParams(vmem_limit_bytes=32 * 1024 * 1024)


def filter_window():
    length = TAPS * NFFT
    position = np.arange(length, dtype=np.float64)
    centred = (position - 0.5 * length + 0.5) / NFFT
    hann_taper = 0.5 - 0.5 * np.cos(2.0 * math.pi * (position + 0.5) / length)
    return np.sinc(centred) * hann_taper


def build_table(window):
    norm_scale = 1.0 / np.sqrt(np.sum(window * window))
    sample = np.arange(NFFT)[:, None]
    channel = FIRST + np.arange(CH)[None, :]
    phase_angle = 2.0 * math.pi / NFFT * (sample * channel % NFFT)
    cosine = np.cos(phase_angle) * norm_scale
    sine = -np.sin(phase_angle) * norm_scale
    return np.concatenate([cosine, sine], axis=1).astype(jnp.bfloat16)


def tapped_block(samples_ref, window_ref, frames_sent, low):
    inputs_here = samples_ref.shape[0]
    frames_here = samples_ref.shape[1] // NFFT
    sums = []
    for frame in range(frames_sent):
        total = jnp.zeros((inputs_here, STEP), jnp.float32)
        for tap in range(TAPS):
            source = frame - TAPS + 1 + tap
            if 0 <= source < frames_here:
                start = source * NFFT + low
                values = samples_ref[:, start : start + STEP].astype(jnp.float32)
                total = total + window_ref[tap : tap + 1, low : low + STEP] * values
        sums.append(total)
    pairs = [
        jnp.concatenate(sums[frame : frame + 2], axis=0).astype(jnp.bfloat16)
        for frame in range(0, frames_sent, 2)
    ]
    return jnp.concatenate(pairs, axis=0)


def turn_granules(blocks, size):
    count = len(blocks)
    lanes = count * size
    granule = lax.broadcasted_iota(jnp.int32, blocks[0].shape, 1) // size
    blocks = list(blocks)
    distance = count // 2
    while distance:
        upper = (granule & distance) != 0
        shift = distance * size
        for index in range(count):
            if index & distance:
                continue
            low, high = blocks[index], blocks[index + distance]
            blocks[index] = jnp.where(upper, pltpu.roll(high, shift, 1), low)
            blocks[index + distance] = jnp.where(upper, high, pltpu.roll(low, lanes - shift, 1))
        distance //= 2
    return blocks


def place_in_column(place, far):
    return (place + far // 4) % far


def own_part_kernel(
    far,
    samples_hbm,
    window_hbm,
    twiddle_hbm,
    gains_hbm,
    own_ref,
    passed_ref,
    parcels_ref,
    samples_ref,
    window_ref,
    twiddle_ref,
    gains_ref,
    direct_ref,
    arrived,
):
    blocks = range(0, NFFT, STEP)
    moves = [(samples_hbm, samples_ref), (window_hbm, window_ref)]
    for low in blocks:
        moves.append((twiddle_hbm.at[pl.ds(low, STEP), :], twiddle_ref.at[pl.ds(low, STEP), :]))
    moves.append((gains_hbm, gains_ref))
    fetches = []
    for index, (source, target) in enumerate(moves):
        fetches.append(pltpu.make_async_copy(source, target, arrived.at[index]))
        fetches[-1].start()
    inputs_here = samples_ref.shape[0]
    frames_here = samples_ref.shape[1] // NFFT
    fetches[0].wait()
    fetches[1].wait()
    direct = None
    for index, low in enumerate(blocks):
        tapped = tapped_block(samples_ref, window_ref, frames_here + EARLY, low)
        fetches[2 + index].wait()
        product = jnp.dot(
            tapped, twiddle_ref[low : low + STEP, :], preferred_element_type=jnp.float32
        )
        direct = product if direct is None else direct + product
    direct_ref[...] = direct
    fetches[-1].wait()
    own_rows = own_ref.shape[0]
    own_ref[...] = direct_ref[:own_rows, :]
    passed_ref[...] = direct_ref[own_rows : own_rows + passed_ref.shape[0], :]
    gain_re = gains_ref[0]
    gain_im = gains_ref[1]
    parts = []
    for frame in range(frames_here + EARLY):
        direct = direct_ref[frame * inputs_here : (frame + 1) * inputs_here, :]
        direct_re = direct[:, :CH]
        direct_im = direct[:, CH:]
        parts.append(
            (
                gain_re * direct_re - gain_im * direct_im,
                gain_re * direct_im + gain_im * direct_re,
            )
        )
    slots = [
        [(part, frame) for frame in range(first, first + 8)]
        for first in range(0, frames_here, 8)
        for part in range(2)
    ]
    slots.append([(part, frames_here + frame) for part in range(2) for frame in range(EARLY)])
    per_far = CH // far
    for place, slot in enumerate(slots):
        columns = slice(place * LANES, (place + 1) * LANES)
        for half in range(CH // LANES):
            lanes = slice(half * LANES, (half + 1) * LANES)
            blocks = turn_granules([parts[frame][part][:, lanes] for part, frame in slot], per_far)
            for index in range(0, len(blocks), 2):
                row = place_in_column(half * len(blocks) + index, far) * inputs_here
                parcels_ref[row : row + 2 * inputs_here, columns] = jnp.concatenate(
                    blocks[index : index + 2], axis=0
                ).astype(jnp.bfloat16)


def spectra_kernel(passed_ref, own_ref, gains_ref, spectra_ref, rows_ref):
    inputs_here = gains_ref.shape[1]
    frames_here = own_ref.shape[0] // inputs_here
    slabs = CH // LANES
    gain_re = gains_ref[0]
    gain_im = gains_ref[1]
    for frame in range(frames_here):
        block = slice(frame * inputs_here, (frame + 1) * inputs_here)
        direct = own_ref[block, :]
        if frame < TAPS - 1:
            direct = direct + passed_ref[block, :]
        direct_re = direct[:, :CH]
        direct_im = direct[:, CH:]
        rows = pl.ds(frame, inputs_here, stride=frames_here)
        real_part = gain_re * direct_re - gain_im * direct_im
        imag_part = gain_re * direct_im + gain_im * direct_re
        for slab in range(slabs):
            columns = slice(slab * LANES, (slab + 1) * LANES)
            rows_ref[slab, rows, :] = real_part[:, columns]
            rows_ref[slabs + slab, rows, :] = imag_part[:, columns]
    for part in range(2):
        for slab in range(slabs):
            columns = slice(slab * LANES, (slab + 1) * LANES)
            spectra_ref[part, :, columns] = rows_ref[part * slabs + slab].astype(jnp.bfloat16)


def channel_of(time):
    return time // 4 * 2 + time % 2


def place_in_plane(near, time, times):
    return (near + NEAR // 2) % NEAR * times + (time + times // 2) % times


def spread_kernel(mine_ref, parcels_ref, turned_ref):
    count, rows, width = parcels_ref.shape
    times = count // NEAR
    stride = mine_ref.shape[1] // rows
    for place in range(0, mine_ref.shape[1], LANES):
        values = mine_ref[:, place : place + LANES].astype(jnp.float32)
        turned_ref[place : place + LANES, :] = values.T
    for near in range(NEAR):
        for channel in range(stride // NEAR):
            start = near * (stride // NEAR) + channel
            values = turned_ref[pl.ds(start, rows, stride=stride), :].astype(jnp.bfloat16)
            for time in range(times):
                if channel_of(time) == channel:
                    parcels_ref[place_in_plane(near, time, times)] = values


def correlate_kernel(frames_all, inputs_here, place_ref, every_ref, packed_ref):
    count, lines, width = every_ref.shape
    blocks, rows, inputs_all = packed_ref.shape
    times = count // NEAR
    main = lines - 2 * EARLY
    carry = None
    lined = []
    for time in range(times):
        pieces = [every_ref[place_in_plane(near, time, times)] for near in range(NEAR)]
        wide = jnp.concatenate([piece.astype(jnp.float32) for piece in pieces], axis=1)
        tiles = [wide[start : start + 8] for start in range(0, lines, 8)]
        if carry is not None:
            early = lax.broadcasted_iota(jnp.int32, carry.shape, 0) < EARLY
            tiles[0] = tiles[0] + jnp.where(early, carry, 0.0)
            tiles[1] = tiles[1] + jnp.where(early, pltpu.roll(carry, 8 - EARLY, 0), 0.0)
        carry = tiles[-1]
        lined += tiles[:-1]
    source = lax.broadcasted_iota(jnp.int32, (inputs_all, inputs_all), 0)
    target = lax.broadcasted_iota(jnp.int32, (inputs_all, inputs_all), 1)
    near, rest = source // width, source % width
    far = width // inputs_here
    place = (rest // inputs_here + far - far // 4) % far
    placed = place * (NEAR * inputs_here) + near * inputs_here + rest % inputs_here
    ordered = jnp.dot(
        jnp.concatenate(lined, axis=0).astype(jnp.bfloat16),
        (placed == target).astype(jnp.bfloat16),
        preferred_element_type=jnp.float32,
    )
    right = ordered.astype(jnp.bfloat16)
    twisted = []
    for start in range(0, times * main, 16):
        twisted.append(ordered[start + 8 : start + 16])
        twisted.append(-ordered[start : start + 8])
    twisted = jnp.concatenate(twisted, axis=0).astype(jnp.bfloat16)
    inner = place_ref[0] == 1
    wide = 2 * rows
    col_index = lax.broadcasted_iota(jnp.int32, (wide, inputs_all), 1)
    row_index = lax.broadcasted_iota(jnp.int32, (wide, inputs_all), 0)
    for side in range(2):
        outer_start = side * (inputs_all - wide)
        inner_start = (1 + side) * wide
        both = []
        for left in (right, twisted):
            chosen = jnp.where(
                inner,
                left[:, inner_start : inner_start + wide],
                left[:, outer_start : outer_start + wide],
            )
            both.append(
                lax.dot_general(
                    chosen,
                    right,
                    (((0,), (0,)), ((), ())),
                    preferred_element_type=jnp.float32,
                )
            )
        upper = row_index + jnp.where(inner, inner_start, outer_start) <= col_index
        values = (jnp.where(upper, both[0], both[1]) * (1.0 / frames_all)).astype(jnp.bfloat16)
        packed_ref[blocks - 1 - 2 * side] = values[:rows]
        packed_ref[blocks - 2 - 2 * side] = values[rows:]


def unpack_kernel(packed_ref, visibilities_ref):
    channels = packed_ref.shape[0]
    for channel in range(channels):
        values = packed_ref[channels - 1 - channel]
        visibilities_ref[:, channel, :] = values.astype(jnp.float32)


def body(samples, gains):
    inputs_here = samples.shape[0]
    frames_here = samples.shape[1] // NFFT
    times = lax.axis_size("tm")
    far = lax.axis_size("far")
    groups = far * NEAR
    per_group = CH // groups
    inputs_all = inputs_here * groups
    frames_all = frames_here * times
    block = inputs_here * frames_here

    window = filter_window()
    twiddle = jnp.asarray(build_table(window))
    window_taps = jnp.asarray(window.astype(np.float32).reshape(TAPS, NFFT))

    sent = frames_here + EARLY
    gains = gains.transpose(0, 2, 1)

    def own_part(*refs):
        own_part_kernel(far, *refs)

    own, passed, parcels = pl.pallas_call(
        own_part,
        out_shape=(
            jax.ShapeDtypeStruct((block, 2 * CH), jnp.float32),
            jax.ShapeDtypeStruct(((TAPS - 1) * inputs_here, 2 * CH), jnp.float32),
            jax.ShapeDtypeStruct((far * inputs_here, sent * 2 * CH // far), jnp.bfloat16),
        ),
        in_specs=[ANY] * 4,
        out_specs=(VMEM, VMEM, VMEM),
        scratch_shapes=[
            pltpu.VMEM(samples.shape, jnp.bfloat16),
            pltpu.VMEM(window_taps.shape, jnp.float32),
            pltpu.VMEM(twiddle.shape, jnp.bfloat16),
            pltpu.VMEM(gains.shape, jnp.float32),
            pltpu.VMEM((sent * inputs_here, 2 * CH), jnp.float32),
            pltpu.SemaphoreType.DMA((3 + NFFT // STEP,)),
        ],
        compiler_params=pltpu.CompilerParams(vmem_limit_bytes=OWN_PART_VMEM),
        cost_estimate=pl.CostEstimate(
            flops=2 * sent * inputs_here * NFFT * 2 * CH,
            bytes_accessed=3 * 1024 * 1024,
            transcendentals=0,
        ),
        name="own_part",
    )(samples, window_taps, twiddle, gains)

    parcels = parcels.reshape(far, inputs_here, sent * 2 * CH // far)
    column = [sorted(range(far), key=lambda place: place_in_column(place, far))]
    mine = lax.all_to_all(parcels, "far", 0, 0, axis_index_groups=column)
    mine = mine.reshape(far * inputs_here, sent * 2 * CH // far)

    passed = lax.ppermute(passed, "tm", [(source, source + 1) for source in range(times - 1)])
    spectra = pl.pallas_call(
        spectra_kernel,
        out_shape=jax.ShapeDtypeStruct((2, block, CH), jnp.bfloat16),
        in_specs=[VMEM] * 3,
        out_specs=VMEM,
        scratch_shapes=[pltpu.VMEM((2 * CH // LANES, block, LANES), jnp.float32)],
        compiler_params=PARAMS,
        cost_estimate=pl.CostEstimate(
            flops=8 * block * 2 * CH, bytes_accessed=1024 * 1024, transcendentals=0
        ),
        name="spectra",
    )(passed, own, gains)
    mine, spectra = lax.optimization_barrier((mine, spectra))
    spectra = spectra.reshape(2, inputs_here, frames_here, CH).transpose(0, 3, 1, 2)

    lines = 2 * sent
    spread = pl.pallas_call(
        spread_kernel,
        out_shape=jax.ShapeDtypeStruct((NEAR * times, lines, far * inputs_here), jnp.bfloat16),
        in_specs=[VMEM],
        out_specs=VMEM,
        scratch_shapes=[pltpu.VMEM((sent * 2 * CH // far, far * inputs_here), jnp.float32)],
        compiler_params=PARAMS,
        name="spread",
    )(mine)
    members = [(near, time) for near in range(NEAR) for time in range(times)]
    members.sort(key=lambda member: place_in_plane(*member, times))
    plane = [[near * times + time for near, time in members]]
    every = lax.all_to_all(spread, ("near", "tm"), 0, 0, axis_index_groups=plane)

    def correlate(*refs):
        correlate_kernel(frames_all, inputs_here, *refs)

    rows = inputs_all // times
    place = lax.axis_index("tm").astype(jnp.int32)
    inner = (place >= times // 4) & (place < times - times // 4)
    packed = pl.pallas_call(
        correlate,
        out_shape=jax.ShapeDtypeStruct((times // 2, rows, inputs_all), jnp.bfloat16),
        in_specs=[SMEM, VMEM],
        out_specs=VMEM,
        compiler_params=PARAMS,
        name="correlate",
    )(inner.astype(jnp.int32)[None], every)
    squares = [[7, 6, 1, 0], [5, 4, 3, 2]]
    packed = lax.all_to_all(packed, "tm", 0, 0, axis_index_groups=squares)
    visibilities = pl.pallas_call(
        unpack_kernel,
        out_shape=jax.ShapeDtypeStruct((rows, per_group, inputs_all), jnp.float32),
        in_specs=[VMEM],
        out_specs=VMEM,
        compiler_params=PARAMS,
        name="unpack",
    )(packed)
    return (spectra, visibilities)


def solution(mesh):
    groups, times = mesh.devices.shape
    split = Mesh(mesh.devices.reshape(groups // NEAR, NEAR, times), ("far", "near", "tm"))
    inputs = ("far", "near")
    return jax.shard_map(
        body,
        mesh=split,
        in_specs=(P(inputs, "tm"), P(None, None, inputs)),
        out_specs=(P(None, None, inputs, "tm"), P("tm", inputs, None)),
        check_vma=False,
    )
```

```python
import math

import jax
import jax.numpy as jnp
import numpy as np
from jax import lax
from jax.experimental import pallas as pl
from jax.experimental.pallas import tpu as pltpu
from jax.sharding import Mesh, PartitionSpec as P

NFFT = 2048
CH = 256
FIRST = 384
TAPS = 4
NEAR = 4
EARLY = 4
STEP = 512
LANES = 128
VMEM = pl.BlockSpec(memory_space=pltpu.VMEM)
ANY = pl.BlockSpec(memory_space=pl.ANY)
SMEM = pl.BlockSpec(memory_space=pltpu.SMEM)
OWN_PART_VMEM = 59 * 1024 * 1024 + 768 * 1024
PARAMS = pltpu.CompilerParams(vmem_limit_bytes=32 * 1024 * 1024)


def filter_window():
    length = TAPS * NFFT
    position = np.arange(length, dtype=np.float64)
    centred = (position - 0.5 * length + 0.5) / NFFT
    hann_taper = 0.5 - 0.5 * np.cos(2.0 * math.pi * (position + 0.5) / length)
    return np.sinc(centred) * hann_taper


def build_table(window):
    norm_scale = 1.0 / np.sqrt(np.sum(window * window))
    sample = np.arange(NFFT)[:, None]
    channel = FIRST + np.arange(CH)[None, :]
    phase_angle = 2.0 * math.pi / NFFT * (sample * channel % NFFT)
    cosine = np.cos(phase_angle) * norm_scale
    sine = -np.sin(phase_angle) * norm_scale
    return np.concatenate([cosine, sine], axis=1).astype(jnp.bfloat16)


def tapped_block(samples_ref, window_ref, frames_sent, block):
    inputs_here, count = samples_ref.shape
    frames_here = count // NFFT
    low = block * STEP
    sums = []
    for frame in range(frames_sent):
        total = jnp.zeros((inputs_here, STEP), jnp.float32)
        for tap in range(TAPS):
            source = frame - TAPS + 1 + tap
            if 0 <= source < frames_here:
                start = source * NFFT + low
                values = samples_ref[:, start : start + STEP]
                weights = window_ref[tap : tap + 1, low : low + STEP]
                total = total + weights * values.astype(jnp.float32)
        sums.append(total)
    pairs = [
        jnp.concatenate(sums[frame : frame + 2], axis=0).astype(jnp.bfloat16)
        for frame in range(0, frames_sent, 2)
    ]
    return jnp.concatenate(pairs, axis=0)


def turn_granules(blocks, size):
    count = len(blocks)
    lanes = count * size
    granule = lax.broadcasted_iota(jnp.int32, blocks[0].shape, 1) // size
    blocks = list(blocks)
    distance = count // 2
    while distance:
        upper = (granule & distance) != 0
        shift = distance * size
        for index in range(count):
            if index & distance:
                continue
            low, high = blocks[index], blocks[index + distance]
            blocks[index] = jnp.where(upper, pltpu.roll(high, shift, 1), low)
            blocks[index + distance] = jnp.where(upper, high, pltpu.roll(low, lanes - shift, 1))
        distance //= 2
    return blocks


def place_in_column(place, far):
    return (place + far * 3 // 8) % far


def own_part_kernel(
    far,
    samples_hbm,
    window_hbm,
    twiddle_hbm,
    gains_hbm,
    own_hbm,
    passed_hbm,
    parcels_hbm,
    samples_ref,
    window_ref,
    twiddle_ref,
    gains_ref,
    direct_ref,
    parcels_ref,
    arrived,
    left,
):
    inputs_here = gains_ref.shape[1]
    frames_here = samples_hbm.shape[1] // NFFT
    blocks = range(NFFT // STEP)
    fetches = []

    def fetch(source, target):
        fetches.append(pltpu.make_async_copy(source, target, arrived.at[len(fetches)]))
        fetches[-1].start()
        return fetches[-1]

    samples_in = fetch(samples_hbm, samples_ref)
    window_in = fetch(window_hbm, window_ref)
    table_in = []
    for block in blocks:
        rows = pl.ds(block * STEP, STEP)
        table_in.append(fetch(twiddle_hbm.at[rows, :], twiddle_ref.at[rows, :]))
    gains_in = fetch(gains_hbm, gains_ref)
    samples_in.wait()
    window_in.wait()
    direct = None
    for block in blocks:
        tapped = tapped_block(samples_ref, window_ref, frames_here + EARLY, block)
        table_in[block].wait()
        product = jnp.dot(
            tapped,
            twiddle_ref[block * STEP : (block + 1) * STEP, :],
            preferred_element_type=jnp.float32,
        )
        direct = product if direct is None else direct + product
    direct_ref[...] = direct
    own_rows = own_hbm.shape[0]
    passed_rows = passed_hbm.shape[0]
    stores = [
        pltpu.make_async_copy(direct_ref.at[pl.ds(0, own_rows), :], own_hbm, left.at[0]),
        pltpu.make_async_copy(
            direct_ref.at[pl.ds(own_rows, passed_rows), :], passed_hbm, left.at[1]
        ),
    ]
    for store in stores:
        store.start()
    gains_in.wait()
    gain_re = gains_ref[0]
    gain_im = gains_ref[1]
    parts = []
    for frame in range(frames_here + EARLY):
        direct = direct_ref[frame * inputs_here : (frame + 1) * inputs_here, :]
        direct_re = direct[:, :CH]
        direct_im = direct[:, CH:]
        parts.append(
            (
                gain_re * direct_re - gain_im * direct_im,
                gain_re * direct_im + gain_im * direct_re,
            )
        )
    slots = [
        [(part, frame) for frame in range(first, first + 8)]
        for first in range(0, frames_here, 8)
        for part in range(2)
    ]
    slots.append([(part, frames_here + frame) for part in range(2) for frame in range(EARLY)])
    per_far = CH // far
    for place, slot in enumerate(slots):
        columns = slice(place * LANES, (place + 1) * LANES)
        for half in range(CH // LANES):
            lanes = slice(half * LANES, (half + 1) * LANES)
            blocks = turn_granules([parts[frame][part][:, lanes] for part, frame in slot], per_far)
            for index in range(0, len(blocks), 2):
                row = place_in_column(half * len(blocks) + index, far) * inputs_here
                parcels_ref[row : row + 2 * inputs_here, columns] = jnp.concatenate(
                    blocks[index : index + 2], axis=0
                ).astype(jnp.bfloat16)
        lanes = pl.ds(place * LANES, LANES)
        stores.append(
            pltpu.make_async_copy(
                parcels_ref.at[:, lanes], parcels_hbm.at[:, lanes], left.at[len(stores)]
            )
        )
        stores[-1].start()
    for store in stores:
        store.wait()


def spectra_kernel(passed_ref, own_ref, gains_ref, spectra_ref, rows_ref):
    inputs_here = gains_ref.shape[1]
    frames_here = own_ref.shape[0] // inputs_here
    slabs = CH // LANES
    gain_re = gains_ref[0]
    gain_im = gains_ref[1]
    for frame in range(frames_here):
        block = slice(frame * inputs_here, (frame + 1) * inputs_here)
        direct = own_ref[block, :]
        if frame < TAPS - 1:
            direct = direct + passed_ref[block, :]
        direct_re = direct[:, :CH]
        direct_im = direct[:, CH:]
        rows = pl.ds(frame, inputs_here, stride=frames_here)
        real_part = gain_re * direct_re - gain_im * direct_im
        imag_part = gain_re * direct_im + gain_im * direct_re
        for slab in range(slabs):
            columns = slice(slab * LANES, (slab + 1) * LANES)
            rows_ref[slab, rows, :] = real_part[:, columns]
            rows_ref[slabs + slab, rows, :] = imag_part[:, columns]
    for part in range(2):
        for slab in range(slabs):
            columns = slice(slab * LANES, (slab + 1) * LANES)
            spectra_ref[part, :, columns] = rows_ref[part * slabs + slab].astype(jnp.bfloat16)


def channel_of(time):
    return time // 4 * 2 + time % 2


def place_in_plane(near, time, times):
    return (near + NEAR // 2) % NEAR * times + (time + times // 2) % times


def spread_kernel(mine_ref, parcels_ref, turned_ref):
    count, rows, width = parcels_ref.shape
    times = count // NEAR
    stride = mine_ref.shape[1] // rows
    for place in range(0, mine_ref.shape[1], LANES):
        values = mine_ref[:, place : place + LANES].astype(jnp.float32)
        turned_ref[place : place + LANES, :] = values.T
    for near in range(NEAR):
        for channel in range(stride // NEAR):
            start = near * (stride // NEAR) + channel
            values = turned_ref[pl.ds(start, rows, stride=stride), :].astype(jnp.bfloat16)
            for time in range(times):
                if channel_of(time) == channel:
                    parcels_ref[place_in_plane(near, time, times)] = values


def correlate_kernel(frames_all, inputs_here, place_ref, every_ref, packed_ref):
    count, lines, width = every_ref.shape
    blocks, rows, inputs_all = packed_ref.shape
    times = count // NEAR
    main = lines - 2 * EARLY
    carry = None
    lined = []
    for time in range(times):
        pieces = [every_ref[place_in_plane(near, time, times)] for near in range(NEAR)]
        wide = jnp.concatenate([piece.astype(jnp.float32) for piece in pieces], axis=1)
        tiles = [wide[start : start + 8] for start in range(0, lines, 8)]
        if carry is not None:
            early = lax.broadcasted_iota(jnp.int32, carry.shape, 0) < EARLY
            tiles[0] = tiles[0] + jnp.where(early, carry, 0.0)
            tiles[1] = tiles[1] + jnp.where(early, pltpu.roll(carry, 8 - EARLY, 0), 0.0)
        carry = tiles[-1]
        lined += tiles[:-1]
    source = lax.broadcasted_iota(jnp.int32, (inputs_all, inputs_all), 0)
    target = lax.broadcasted_iota(jnp.int32, (inputs_all, inputs_all), 1)
    near, rest = source // width, source % width
    far = width // inputs_here
    place = (rest // inputs_here + far - far * 3 // 8) % far
    placed = place * (NEAR * inputs_here) + near * inputs_here + rest % inputs_here
    ordered = jnp.dot(
        jnp.concatenate(lined, axis=0).astype(jnp.bfloat16),
        (placed == target).astype(jnp.bfloat16),
        preferred_element_type=jnp.float32,
    )
    right = ordered.astype(jnp.bfloat16)
    twisted = []
    for start in range(0, times * main, 16):
        twisted.append(ordered[start + 8 : start + 16])
        twisted.append(-ordered[start : start + 8])
    twisted = jnp.concatenate(twisted, axis=0).astype(jnp.bfloat16)
    inner = place_ref[0] == 1
    wide = 2 * rows
    col_index = lax.broadcasted_iota(jnp.int32, (wide, inputs_all), 1)
    row_index = lax.broadcasted_iota(jnp.int32, (wide, inputs_all), 0)
    for side in range(2):
        outer_start = side * (inputs_all - wide)
        inner_start = (1 + side) * wide
        both = []
        for left in (right, twisted):
            chosen = jnp.where(
                inner,
                left[:, inner_start : inner_start + wide],
                left[:, outer_start : outer_start + wide],
            )
            both.append(
                lax.dot_general(
                    chosen,
                    right,
                    (((0,), (0,)), ((), ())),
                    preferred_element_type=jnp.float32,
                )
            )
        upper = row_index + jnp.where(inner, inner_start, outer_start) <= col_index
        values = (jnp.where(upper, both[0], both[1]) * (1.0 / frames_all)).astype(jnp.bfloat16)
        packed_ref[blocks - 1 - 2 * side] = values[:rows]
        packed_ref[blocks - 2 - 2 * side] = values[rows:]


def unpack_kernel(packed_ref, visibilities_ref):
    channels = packed_ref.shape[0]
    for channel in range(channels):
        values = packed_ref[channels - 1 - channel]
        visibilities_ref[:, channel, :] = values.astype(jnp.float32)


def body(samples, gains):
    inputs_here = samples.shape[0]
    frames_here = samples.shape[1] // NFFT
    times = lax.axis_size("tm")
    far = lax.axis_size("far")
    groups = far * NEAR
    per_group = CH // groups
    inputs_all = inputs_here * groups
    frames_all = frames_here * times
    block = inputs_here * frames_here

    window = filter_window()
    twiddle = jnp.asarray(build_table(window))
    window_taps = jnp.asarray(window.astype(np.float32).reshape(TAPS, NFFT))

    sent = frames_here + EARLY
    gains = gains.transpose(0, 2, 1)

    def own_part(*refs):
        own_part_kernel(far, *refs)

    own, passed, parcels = pl.pallas_call(
        own_part,
        out_shape=(
            jax.ShapeDtypeStruct((block, 2 * CH), jnp.float32),
            jax.ShapeDtypeStruct(((TAPS - 1) * inputs_here, 2 * CH), jnp.float32),
            jax.ShapeDtypeStruct((far * inputs_here, sent * 2 * CH // far), jnp.bfloat16),
        ),
        in_specs=[ANY] * 4,
        out_specs=(ANY, ANY, ANY),
        scratch_shapes=[
            pltpu.VMEM(samples.shape, jnp.bfloat16),
            pltpu.VMEM(window_taps.shape, jnp.float32),
            pltpu.VMEM(twiddle.shape, jnp.bfloat16),
            pltpu.VMEM(gains.shape, jnp.float32),
            pltpu.VMEM((sent * inputs_here, 2 * CH), jnp.float32),
            pltpu.VMEM((far * inputs_here, sent * 2 * CH // far), jnp.bfloat16),
            pltpu.SemaphoreType.DMA((3 + NFFT // STEP,)),
            pltpu.SemaphoreType.DMA((2 + sent // 4,)),
        ],
        compiler_params=pltpu.CompilerParams(vmem_limit_bytes=OWN_PART_VMEM),
        cost_estimate=pl.CostEstimate(
            flops=2 * sent * inputs_here * NFFT * 2 * CH,
            bytes_accessed=3 * 1024 * 1024,
            transcendentals=0,
        ),
        name="own_part",
    )(samples, window_taps, twiddle, gains)

    parcels = parcels.reshape(far, inputs_here, sent * 2 * CH // far)
    column = [sorted(range(far), key=lambda place: place_in_column(place, far))]
    mine = lax.all_to_all(parcels, "far", 0, 0, axis_index_groups=column)
    mine = mine.reshape(far * inputs_here, sent * 2 * CH // far)

    passed = lax.ppermute(passed, "tm", [(source, source + 1) for source in range(times - 1)])
    spectra = pl.pallas_call(
        spectra_kernel,
        out_shape=jax.ShapeDtypeStruct((2, block, CH), jnp.bfloat16),
        in_specs=[VMEM] * 3,
        out_specs=VMEM,
        scratch_shapes=[pltpu.VMEM((2 * CH // LANES, block, LANES), jnp.float32)],
        compiler_params=PARAMS,
        cost_estimate=pl.CostEstimate(
            flops=8 * block * 2 * CH, bytes_accessed=1024 * 1024, transcendentals=0
        ),
        name="spectra",
    )(passed, own, gains)
    mine, spectra = lax.optimization_barrier((mine, spectra))
    spectra = spectra.reshape(2, inputs_here, frames_here, CH).transpose(0, 3, 1, 2)

    lines = 2 * sent
    spread = pl.pallas_call(
        spread_kernel,
        out_shape=jax.ShapeDtypeStruct((NEAR * times, lines, far * inputs_here), jnp.bfloat16),
        in_specs=[VMEM],
        out_specs=VMEM,
        scratch_shapes=[pltpu.VMEM((sent * 2 * CH // far, far * inputs_here), jnp.float32)],
        compiler_params=PARAMS,
        name="spread",
    )(mine)
    members = [(near, time) for near in range(NEAR) for time in range(times)]
    members.sort(key=lambda member: place_in_plane(*member, times))
    plane = [[near * times + time for near, time in members]]
    every = lax.all_to_all(spread, ("near", "tm"), 0, 0, axis_index_groups=plane)

    def correlate(*refs):
        correlate_kernel(frames_all, inputs_here, *refs)

    rows = inputs_all // times
    place = lax.axis_index("tm").astype(jnp.int32)
    inner = (place >= times // 4) & (place < times - times // 4)
    packed = pl.pallas_call(
        correlate,
        out_shape=jax.ShapeDtypeStruct((times // 2, rows, inputs_all), jnp.bfloat16),
        in_specs=[SMEM, VMEM],
        out_specs=VMEM,
        compiler_params=PARAMS,
        name="correlate",
    )(inner.astype(jnp.int32)[None], every)
    squares = [[7, 6, 1, 0], [5, 4, 3, 2]]
    packed = lax.all_to_all(packed, "tm", 0, 0, axis_index_groups=squares)
    visibilities = pl.pallas_call(
        unpack_kernel,
        out_shape=jax.ShapeDtypeStruct((rows, per_group, inputs_all), jnp.float32),
        in_specs=[VMEM],
        out_specs=VMEM,
        compiler_params=PARAMS,
        name="unpack",
    )(packed)
    return (spectra, visibilities)


def solution(mesh):
    groups, times = mesh.devices.shape
    split = Mesh(mesh.devices.reshape(groups // NEAR, NEAR, times), ("far", "near", "tm"))
    inputs = ("far", "near")
    return jax.shard_map(
        body,
        mesh=split,
        in_specs=(P(inputs, "tm"), P(None, None, inputs)),
        out_specs=(P(None, None, inputs, "tm"), P("tm", inputs, None)),
        check_vma=False,
    )
```

```python
import math

import jax
import jax.numpy as jnp
import numpy as np
from jax import lax
from jax.experimental import pallas as pl
from jax.experimental.pallas import tpu as pltpu
from jax.sharding import Mesh, PartitionSpec as P

NFFT = 2048
CH = 256
FIRST = 384
TAPS = 4
NEAR = 4
EARLY = 4
STEP = 512
LANES = 128
VMEM = pl.BlockSpec(memory_space=pltpu.VMEM)
ANY = pl.BlockSpec(memory_space=pl.ANY)
SMEM = pl.BlockSpec(memory_space=pltpu.SMEM)
OWN_PART_VMEM = 59 * 1024 * 1024 + 768 * 1024
PARAMS = pltpu.CompilerParams(vmem_limit_bytes=32 * 1024 * 1024)


def filter_window():
    length = TAPS * NFFT
    position = np.arange(length, dtype=np.float64)
    centred = (position - 0.5 * length + 0.5) / NFFT
    hann_taper = 0.5 - 0.5 * np.cos(2.0 * math.pi * (position + 0.5) / length)
    return np.sinc(centred) * hann_taper


def build_table(window):
    norm_scale = 1.0 / np.sqrt(np.sum(window * window))
    sample = np.arange(NFFT)[:, None]
    channel = FIRST + np.arange(CH)[None, :]
    phase_angle = 2.0 * math.pi / NFFT * (sample * channel % NFFT)
    cosine = np.cos(phase_angle) * norm_scale
    sine = -np.sin(phase_angle) * norm_scale
    return np.concatenate([cosine, sine], axis=1).astype(jnp.bfloat16)


def tapped_block(samples_ref, window_ref, frames_sent, block):
    inputs_here, count = samples_ref.shape
    frames_here = count // NFFT
    low = block * STEP
    sums = []
    for frame in range(frames_sent):
        total = jnp.zeros((inputs_here, STEP), jnp.float32)
        for tap in range(TAPS):
            source = frame - TAPS + 1 + tap
            if 0 <= source < frames_here:
                start = source * NFFT + low
                values = samples_ref[:, start : start + STEP]
                weights = window_ref[tap : tap + 1, low : low + STEP]
                total = total + weights * values.astype(jnp.float32)
        sums.append(total)
    pairs = [
        jnp.concatenate(sums[frame : frame + 2], axis=0).astype(jnp.bfloat16)
        for frame in range(0, frames_sent, 2)
    ]
    return jnp.concatenate(pairs, axis=0)


def turn_granules(blocks, size):
    count = len(blocks)
    lanes = count * size
    granule = lax.broadcasted_iota(jnp.int32, blocks[0].shape, 1) // size
    blocks = list(blocks)
    distance = count // 2
    while distance:
        upper = (granule & distance) != 0
        shift = distance * size
        for index in range(count):
            if index & distance:
                continue
            low, high = blocks[index], blocks[index + distance]
            blocks[index] = jnp.where(upper, pltpu.roll(high, shift, 1), low)
            blocks[index + distance] = jnp.where(upper, high, pltpu.roll(low, lanes - shift, 1))
        distance //= 2
    return blocks


def place_in_column(place, far):
    return (7 * (place + far * 3 // 8)) % far


def own_part_kernel(
    far,
    samples_hbm,
    window_hbm,
    twiddle_hbm,
    gains_hbm,
    own_hbm,
    passed_hbm,
    parcels_hbm,
    samples_ref,
    window_ref,
    twiddle_ref,
    gains_ref,
    direct_ref,
    parcels_ref,
    arrived,
    left,
):
    inputs_here = gains_ref.shape[1]
    frames_here = samples_hbm.shape[1] // NFFT
    blocks = range(NFFT // STEP)
    fetches = []

    def fetch(source, target):
        fetches.append(pltpu.make_async_copy(source, target, arrived.at[len(fetches)]))
        fetches[-1].start()
        return fetches[-1]

    samples_in = fetch(samples_hbm, samples_ref)
    window_in = fetch(window_hbm, window_ref)
    table_in = []
    for block in blocks:
        rows = pl.ds(block * STEP, STEP)
        table_in.append(fetch(twiddle_hbm.at[rows, :], twiddle_ref.at[rows, :]))
    gains_in = fetch(gains_hbm, gains_ref)
    samples_in.wait()
    window_in.wait()
    direct = None
    for block in blocks:
        tapped = tapped_block(samples_ref, window_ref, frames_here + EARLY, block)
        table_in[block].wait()
        product = jnp.dot(
            tapped,
            twiddle_ref[block * STEP : (block + 1) * STEP, :],
            preferred_element_type=jnp.float32,
        )
        direct = product if direct is None else direct + product
    direct_ref[...] = direct
    own_rows = own_hbm.shape[0]
    passed_rows = passed_hbm.shape[0]
    stores = [
        pltpu.make_async_copy(direct_ref.at[pl.ds(0, own_rows), :], own_hbm, left.at[0]),
        pltpu.make_async_copy(
            direct_ref.at[pl.ds(own_rows, passed_rows), :], passed_hbm, left.at[1]
        ),
    ]
    for store in stores:
        store.start()
    gains_in.wait()
    gain_re = gains_ref[0]
    gain_im = gains_ref[1]
    parts = []
    for frame in range(frames_here + EARLY):
        direct = direct_ref[frame * inputs_here : (frame + 1) * inputs_here, :]
        direct_re = direct[:, :CH]
        direct_im = direct[:, CH:]
        parts.append(
            (
                gain_re * direct_re - gain_im * direct_im,
                gain_re * direct_im + gain_im * direct_re,
            )
        )
    slots = [
        [(part, frame) for frame in range(first, first + 8)]
        for first in range(0, frames_here, 8)
        for part in range(2)
    ]
    slots.append([(part, frames_here + frame) for part in range(2) for frame in range(EARLY)])
    per_far = CH // far
    for place, slot in enumerate(slots):
        columns = slice(place * LANES, (place + 1) * LANES)
        blocks = []
        for half in range(CH // LANES):
            lanes = slice(half * LANES, (half + 1) * LANES)
            blocks += turn_granules([parts[frame][part][:, lanes] for part, frame in slot], per_far)
        listed = sorted(range(far), key=lambda target: place_in_column(target, far))
        for index in range(0, far, 2):
            rows = slice(index * inputs_here, (index + 2) * inputs_here)
            parcels_ref[rows, columns] = jnp.concatenate(
                [blocks[target] for target in listed[index : index + 2]], axis=0
            ).astype(jnp.bfloat16)
        lanes = pl.ds(place * LANES, LANES)
        stores.append(
            pltpu.make_async_copy(
                parcels_ref.at[:, lanes], parcels_hbm.at[:, lanes], left.at[len(stores)]
            )
        )
        stores[-1].start()
    for store in stores:
        store.wait()


def spectra_kernel(passed_ref, own_ref, gains_ref, spectra_ref, rows_ref):
    inputs_here = gains_ref.shape[1]
    frames_here = own_ref.shape[0] // inputs_here
    slabs = CH // LANES
    gain_re = gains_ref[0]
    gain_im = gains_ref[1]
    for frame in range(frames_here):
        block = slice(frame * inputs_here, (frame + 1) * inputs_here)
        direct = own_ref[block, :]
        if frame < TAPS - 1:
            direct = direct + passed_ref[block, :]
        direct_re = direct[:, :CH]
        direct_im = direct[:, CH:]
        rows = pl.ds(frame, inputs_here, stride=frames_here)
        real_part = gain_re * direct_re - gain_im * direct_im
        imag_part = gain_re * direct_im + gain_im * direct_re
        for slab in range(slabs):
            columns = slice(slab * LANES, (slab + 1) * LANES)
            rows_ref[slab, rows, :] = real_part[:, columns]
            rows_ref[slabs + slab, rows, :] = imag_part[:, columns]
    for part in range(2):
        for slab in range(slabs):
            columns = slice(slab * LANES, (slab + 1) * LANES)
            spectra_ref[part, :, columns] = rows_ref[part * slabs + slab].astype(jnp.bfloat16)


def channel_of(time):
    return time // 4 * 2 + time % 2


def place_in_plane(near, time, times):
    return (near + NEAR // 2) % NEAR * times + (time + times // 2) % times


def spread_kernel(mine_ref, parcels_hbm, turned_ref, staged_ref, left):
    count, rows, _ = parcels_hbm.shape
    times = count // NEAR
    stride = mine_ref.shape[1] // rows
    for place in range(0, mine_ref.shape[1], LANES):
        values = mine_ref[:, place : place + LANES].astype(jnp.float32)
        turned_ref[place : place + LANES, :] = values.T
    stores = []
    for start in range(stride):
        near, channel = divmod(start, stride // NEAR)
        staged_ref[start] = turned_ref[pl.ds(start, rows, stride=stride), :].astype(jnp.bfloat16)
        for time in range(times):
            if channel_of(time) == channel:
                place = place_in_plane(near, time, times)
                stores.append(
                    pltpu.make_async_copy(
                        staged_ref.at[start], parcels_hbm.at[place], left.at[len(stores)]
                    )
                )
                stores[-1].start()
    for store in stores:
        store.wait()


def correlate_kernel(frames_all, inputs_here, place_ref, every_ref, packed_ref):
    count, lines, width = every_ref.shape
    blocks, rows, inputs_all = packed_ref.shape
    times = count // NEAR
    main = lines - 2 * EARLY
    carry = None
    lined = []
    for time in range(times):
        pieces = [every_ref[place_in_plane(near, time, times)] for near in range(NEAR)]
        wide = jnp.concatenate([piece.astype(jnp.float32) for piece in pieces], axis=1)
        tiles = [wide[start : start + 8] for start in range(0, lines, 8)]
        if carry is not None:
            early = lax.broadcasted_iota(jnp.int32, carry.shape, 0) < EARLY
            tiles[0] = tiles[0] + jnp.where(early, carry, 0.0)
            tiles[1] = tiles[1] + jnp.where(early, pltpu.roll(carry, 8 - EARLY, 0), 0.0)
        carry = tiles[-1]
        lined += tiles[:-1]
    source = lax.broadcasted_iota(jnp.int32, (inputs_all, inputs_all), 0)
    target = lax.broadcasted_iota(jnp.int32, (inputs_all, inputs_all), 1)
    near, rest = source // width, source % width
    far = width // inputs_here
    place = (7 * (rest // inputs_here) + far - far * 3 // 8) % far
    placed = place * (NEAR * inputs_here) + near * inputs_here + rest % inputs_here
    ordered = jnp.dot(
        jnp.concatenate(lined, axis=0).astype(jnp.bfloat16),
        (placed == target).astype(jnp.bfloat16),
        preferred_element_type=jnp.float32,
    )
    right = ordered.astype(jnp.bfloat16)
    twisted = []
    for start in range(0, times * main, 16):
        twisted.append(ordered[start + 8 : start + 16])
        twisted.append(-ordered[start : start + 8])
    twisted = jnp.concatenate(twisted, axis=0).astype(jnp.bfloat16)
    inner = place_ref[0] == 1
    wide = 2 * rows
    col_index = lax.broadcasted_iota(jnp.int32, (wide, inputs_all), 1)
    row_index = lax.broadcasted_iota(jnp.int32, (wide, inputs_all), 0)
    for side in range(2):
        outer_start = side * (inputs_all - wide)
        inner_start = (1 + side) * wide
        both = []
        for left in (right, twisted):
            chosen = jnp.where(
                inner,
                left[:, inner_start : inner_start + wide],
                left[:, outer_start : outer_start + wide],
            )
            both.append(
                lax.dot_general(
                    chosen,
                    right,
                    (((0,), (0,)), ((), ())),
                    preferred_element_type=jnp.float32,
                )
            )
        upper = row_index + jnp.where(inner, inner_start, outer_start) <= col_index
        values = (jnp.where(upper, both[0], both[1]) * (1.0 / frames_all)).astype(jnp.bfloat16)
        packed_ref[blocks - 1 - 2 * side] = values[:rows]
        packed_ref[blocks - 2 - 2 * side] = values[rows:]


def unpack_kernel(packed_ref, visibilities_hbm, rows_ref, left):
    channels, count, _ = packed_ref.shape
    stores = []
    for start in range(0, count, 16):
        rows = slice(start, start + 16)
        for channel in range(channels):
            values = packed_ref[channels - 1 - channel, rows, :]
            rows_ref[rows, channel, :] = values.astype(jnp.float32)
        block = pl.ds(start, 16)
        stores.append(
            pltpu.make_async_copy(
                rows_ref.at[block], visibilities_hbm.at[block], left.at[len(stores)]
            )
        )
        stores[-1].start()
    for store in stores:
        store.wait()


def body(samples, gains):
    inputs_here = samples.shape[0]
    frames_here = samples.shape[1] // NFFT
    times = lax.axis_size("tm")
    far = lax.axis_size("far")
    groups = far * NEAR
    per_group = CH // groups
    inputs_all = inputs_here * groups
    frames_all = frames_here * times
    block = inputs_here * frames_here

    window = filter_window()
    twiddle = jnp.asarray(build_table(window))
    window_taps = jnp.asarray(window.astype(np.float32).reshape(TAPS, NFFT))

    sent = frames_here + EARLY
    gains = gains.transpose(0, 2, 1)

    def own_part(*refs):
        own_part_kernel(far, *refs)

    own, passed, parcels = pl.pallas_call(
        own_part,
        out_shape=(
            jax.ShapeDtypeStruct((block, 2 * CH), jnp.float32),
            jax.ShapeDtypeStruct(((TAPS - 1) * inputs_here, 2 * CH), jnp.float32),
            jax.ShapeDtypeStruct((far * inputs_here, sent * 2 * CH // far), jnp.bfloat16),
        ),
        in_specs=[ANY] * 4,
        out_specs=(ANY, ANY, ANY),
        scratch_shapes=[
            pltpu.VMEM(samples.shape, jnp.bfloat16),
            pltpu.VMEM(window_taps.shape, jnp.float32),
            pltpu.VMEM(twiddle.shape, jnp.bfloat16),
            pltpu.VMEM(gains.shape, jnp.float32),
            pltpu.VMEM((sent * inputs_here, 2 * CH), jnp.float32),
            pltpu.VMEM((far * inputs_here, sent * 2 * CH // far), jnp.bfloat16),
            pltpu.SemaphoreType.DMA((3 + NFFT // STEP,)),
            pltpu.SemaphoreType.DMA((2 + sent // 4,)),
        ],
        compiler_params=pltpu.CompilerParams(vmem_limit_bytes=OWN_PART_VMEM),
        cost_estimate=pl.CostEstimate(
            flops=2 * sent * inputs_here * NFFT * 2 * CH,
            bytes_accessed=3 * 1024 * 1024,
            transcendentals=0,
        ),
        name="own_part",
    )(samples, window_taps, twiddle, gains)

    parcels = parcels.reshape(far, inputs_here, sent * 2 * CH // far)
    column = [sorted(range(far), key=lambda place: place_in_column(place, far))]
    mine = lax.all_to_all(parcels, "far", 0, 0, axis_index_groups=column)
    mine = mine.reshape(far * inputs_here, sent * 2 * CH // far)

    passed = lax.ppermute(passed, "tm", [(source, source + 1) for source in range(times - 1)])
    spectra = pl.pallas_call(
        spectra_kernel,
        out_shape=jax.ShapeDtypeStruct((2, block, CH), jnp.bfloat16),
        in_specs=[VMEM] * 3,
        out_specs=VMEM,
        scratch_shapes=[pltpu.VMEM((2 * CH // LANES, block, LANES), jnp.float32)],
        compiler_params=PARAMS,
        cost_estimate=pl.CostEstimate(
            flops=8 * block * 2 * CH, bytes_accessed=1024 * 1024, transcendentals=0
        ),
        name="spectra",
    )(passed, own, gains)
    mine, spectra = lax.optimization_barrier((mine, spectra))
    spectra = spectra.reshape(2, inputs_here, frames_here, CH).transpose(0, 3, 1, 2)

    lines = 2 * sent
    spread = pl.pallas_call(
        spread_kernel,
        out_shape=jax.ShapeDtypeStruct((NEAR * times, lines, far * inputs_here), jnp.bfloat16),
        in_specs=[VMEM],
        out_specs=ANY,
        scratch_shapes=[
            pltpu.VMEM((sent * 2 * CH // far, far * inputs_here), jnp.float32),
            pltpu.VMEM((NEAR * per_group, lines, far * inputs_here), jnp.bfloat16),
            pltpu.SemaphoreType.DMA((NEAR * times,)),
        ],
        compiler_params=PARAMS,
        name="spread",
    )(mine)
    members = [(near, time) for near in range(NEAR) for time in range(times)]
    members.sort(key=lambda member: place_in_plane(*member, times))
    plane = [[near * times + time for near, time in members]]
    every = lax.all_to_all(spread, ("near", "tm"), 0, 0, axis_index_groups=plane)

    def correlate(*refs):
        correlate_kernel(frames_all, inputs_here, *refs)

    rows = inputs_all // times
    place = lax.axis_index("tm").astype(jnp.int32)
    inner = (place >= times // 4) & (place < times - times // 4)
    packed = pl.pallas_call(
        correlate,
        out_shape=jax.ShapeDtypeStruct((times // 2, rows, inputs_all), jnp.bfloat16),
        in_specs=[SMEM, VMEM],
        out_specs=VMEM,
        compiler_params=PARAMS,
        name="correlate",
    )(inner.astype(jnp.int32)[None], every)
    squares = [[7, 6, 1, 0], [5, 4, 3, 2]]
    packed = lax.all_to_all(packed, "tm", 0, 0, axis_index_groups=squares)
    visibilities = pl.pallas_call(
        unpack_kernel,
        out_shape=jax.ShapeDtypeStruct((rows, per_group, inputs_all), jnp.float32),
        in_specs=[VMEM],
        out_specs=ANY,
        scratch_shapes=[
            pltpu.VMEM((rows, per_group, inputs_all), jnp.float32),
            pltpu.SemaphoreType.DMA((rows // 16,)),
        ],
        compiler_params=PARAMS,
        name="unpack",
    )(packed)
    return (spectra, visibilities)


def solution(mesh):
    groups, times = mesh.devices.shape
    split = Mesh(mesh.devices.reshape(groups // NEAR, NEAR, times), ("far", "near", "tm"))
    inputs = ("far", "near")
    return jax.shard_map(
        body,
        mesh=split,
        in_specs=(P(inputs, "tm"), P(None, None, inputs)),
        out_specs=(P(None, None, inputs, "tm"), P("tm", inputs, None)),
        check_vma=False,
    )
```

```python
import math

import jax
import jax.numpy as jnp
import numpy as np
from jax import lax
from jax.experimental import pallas as pl
from jax.experimental.pallas import tpu as pltpu
from jax.sharding import Mesh, PartitionSpec as P

NFFT = 2048
CH = 256
FIRST = 384
TAPS = 4
NEAR = 4
EARLY = 4
STEP = 512
LANES = 128
VMEM = pl.BlockSpec(memory_space=pltpu.VMEM)
ANY = pl.BlockSpec(memory_space=pl.ANY)
SMEM = pl.BlockSpec(memory_space=pltpu.SMEM)
OWN_PART_VMEM = 59 * 1024 * 1024 + 768 * 1024
PARAMS = pltpu.CompilerParams(vmem_limit_bytes=32 * 1024 * 1024)


def filter_window():
    length = TAPS * NFFT
    position = np.arange(length, dtype=np.float64)
    centred = (position - 0.5 * length + 0.5) / NFFT
    hann_taper = 0.5 - 0.5 * np.cos(2.0 * math.pi * (position + 0.5) / length)
    return np.sinc(centred) * hann_taper


def build_table(window):
    norm_scale = 1.0 / np.sqrt(np.sum(window * window))
    sample = np.arange(NFFT)[:, None]
    channel = FIRST + np.arange(CH)[None, :]
    phase_angle = 2.0 * math.pi / NFFT * (sample * channel % NFFT)
    cosine = np.cos(phase_angle) * norm_scale
    sine = -np.sin(phase_angle) * norm_scale
    return np.concatenate([cosine, sine], axis=1).astype(jnp.bfloat16)


def tapped_block(samples_ref, window_ref, frames_sent, block):
    inputs_here, count = samples_ref.shape
    frames_here = count // NFFT
    low = block * STEP
    sums = []
    for frame in range(frames_sent):
        total = jnp.zeros((inputs_here, STEP), jnp.float32)
        for tap in range(TAPS):
            source = frame - TAPS + 1 + tap
            if 0 <= source < frames_here:
                start = source * NFFT + low
                values = samples_ref[:, start : start + STEP]
                weights = window_ref[tap : tap + 1, low : low + STEP]
                total = total + weights * values.astype(jnp.float32)
        sums.append(total)
    pairs = [
        jnp.concatenate(sums[frame : frame + 2], axis=0).astype(jnp.bfloat16)
        for frame in range(0, frames_sent, 2)
    ]
    return jnp.concatenate(pairs, axis=0)


def turn_granules(blocks, size):
    count = len(blocks)
    lanes = count * size
    granule = lax.broadcasted_iota(jnp.int32, blocks[0].shape, 1) // size
    blocks = list(blocks)
    distance = count // 2
    while distance:
        upper = (granule & distance) != 0
        shift = distance * size
        for index in range(count):
            if index & distance:
                continue
            low, high = blocks[index], blocks[index + distance]
            blocks[index] = jnp.where(upper, pltpu.roll(high, shift, 1), low)
            blocks[index + distance] = jnp.where(upper, high, pltpu.roll(low, lanes - shift, 1))
        distance //= 2
    return blocks


def place_in_column(place, far):
    return (place + far * 3 // 8) % far


def own_part_kernel(
    far,
    samples_hbm,
    window_hbm,
    twiddle_hbm,
    gains_hbm,
    own_hbm,
    passed_hbm,
    parcels_hbm,
    samples_ref,
    window_ref,
    twiddle_ref,
    gains_ref,
    direct_ref,
    parcels_ref,
    arrived,
    left,
):
    inputs_here = gains_ref.shape[1]
    frames_here = samples_hbm.shape[1] // NFFT
    blocks = range(NFFT // STEP)
    fetches = []

    def fetch(source, target):
        fetches.append(pltpu.make_async_copy(source, target, arrived.at[len(fetches)]))
        fetches[-1].start()
        return fetches[-1]

    samples_in = fetch(samples_hbm, samples_ref)
    window_in = fetch(window_hbm, window_ref)
    table_in = []
    for block in blocks[: len(blocks) // 2]:
        rows = pl.ds(block * STEP, STEP)
        table_in.append(fetch(twiddle_hbm.at[rows, :], twiddle_ref.at[rows, :]))
    gains_in = fetch(gains_hbm, gains_ref)
    samples_in.wait()
    window_in.wait()
    halves = []
    for first in (0, len(table_in)):
        total = None
        for block, table in enumerate(table_in):
            tapped = tapped_block(samples_ref, window_ref, frames_here + EARLY, first + block)
            if not first:
                table.wait()
            product = jnp.dot(
                tapped,
                twiddle_ref[block * STEP : (block + 1) * STEP, :],
                preferred_element_type=jnp.float32,
            )
            total = product if total is None else total + product
        halves.append(total)
    channel = FIRST + lax.broadcasted_iota(jnp.int32, (1, 2 * CH), 1)
    sign = (1 - 2 * (channel % 2)).astype(jnp.float32)
    direct_ref[...] = halves[0] + sign * halves[1]
    own_rows = own_hbm.shape[0]
    passed_rows = passed_hbm.shape[0]
    stores = [
        pltpu.make_async_copy(direct_ref.at[pl.ds(0, own_rows), :], own_hbm, left.at[0]),
        pltpu.make_async_copy(
            direct_ref.at[pl.ds(own_rows, passed_rows), :], passed_hbm, left.at[1]
        ),
    ]
    for store in stores:
        store.start()
    gains_in.wait()
    gain_re = gains_ref[0]
    gain_im = gains_ref[1]
    parts = []
    for frame in range(frames_here + EARLY):
        direct = direct_ref[frame * inputs_here : (frame + 1) * inputs_here, :]
        direct_re = direct[:, :CH]
        direct_im = direct[:, CH:]
        parts.append(
            (
                gain_re * direct_re - gain_im * direct_im,
                gain_re * direct_im + gain_im * direct_re,
            )
        )
    slots = [
        [(part, frame) for frame in range(first, first + 8)]
        for first in range(0, frames_here, 8)
        for part in range(2)
    ]
    slots.append([(part, frames_here + frame) for part in range(2) for frame in range(EARLY)])
    per_far = CH // far
    for place, slot in enumerate(slots):
        columns = slice(place * LANES, (place + 1) * LANES)
        for half in range(CH // LANES):
            lanes = slice(half * LANES, (half + 1) * LANES)
            blocks = turn_granules([parts[frame][part][:, lanes] for part, frame in slot], per_far)
            for index in range(0, len(blocks), 2):
                row = place_in_column(half * len(blocks) + index, far) * inputs_here
                parcels_ref[row : row + 2 * inputs_here, columns] = jnp.concatenate(
                    blocks[index : index + 2], axis=0
                ).astype(jnp.bfloat16)
        lanes = pl.ds(place * LANES, LANES)
        stores.append(
            pltpu.make_async_copy(
                parcels_ref.at[:, lanes], parcels_hbm.at[:, lanes], left.at[len(stores)]
            )
        )
        stores[-1].start()
    for store in stores:
        store.wait()


def spectra_kernel(passed_ref, own_ref, gains_ref, spectra_ref, rows_ref):
    inputs_here = gains_ref.shape[1]
    frames_here = own_ref.shape[0] // inputs_here
    slabs = CH // LANES
    gain_re = gains_ref[0]
    gain_im = gains_ref[1]
    for frame in range(frames_here):
        block = slice(frame * inputs_here, (frame + 1) * inputs_here)
        direct = own_ref[block, :]
        if frame < TAPS - 1:
            direct = direct + passed_ref[block, :]
        direct_re = direct[:, :CH]
        direct_im = direct[:, CH:]
        rows = pl.ds(frame, inputs_here, stride=frames_here)
        real_part = gain_re * direct_re - gain_im * direct_im
        imag_part = gain_re * direct_im + gain_im * direct_re
        for slab in range(slabs):
            columns = slice(slab * LANES, (slab + 1) * LANES)
            rows_ref[slab, rows, :] = real_part[:, columns]
            rows_ref[slabs + slab, rows, :] = imag_part[:, columns]
    for part in range(2):
        for slab in range(slabs):
            columns = slice(slab * LANES, (slab + 1) * LANES)
            spectra_ref[part, :, columns] = rows_ref[part * slabs + slab].astype(jnp.bfloat16)


def channel_of(time):
    return time // 4 * 2 + time % 2


def place_in_plane(near, time, times):
    return (near + NEAR // 2) % NEAR * times + (time + times // 2) % times


def spread_kernel(mine_ref, parcels_ref):
    count, rows, _ = parcels_ref.shape
    times = count // NEAR
    stride = mine_ref.shape[1] // rows
    slots = LANES // stride
    row = lax.broadcasted_iota(jnp.int32, (LANES, 1), 0)
    source = row % slots * stride + row // slots
    chosen = source == lax.broadcasted_iota(jnp.int32, (LANES, LANES), 1)
    chosen = chosen.astype(jnp.float32).astype(jnp.bfloat16)
    tiles = []
    for start in range(0, mine_ref.shape[1], LANES):
        tiles.append(
            lax.dot_general(
                chosen,
                mine_ref[:, start : start + LANES],
                (((1,), (1,)), ((), ())),
                preferred_element_type=jnp.float32,
            )
        )
    for start in range(stride):
        near, channel = divmod(start, stride // NEAR)
        lines = [tile[start * slots : (start + 1) * slots] for tile in tiles]
        values = jnp.concatenate(lines, axis=0).astype(jnp.bfloat16)
        for time in range(times):
            if channel_of(time) == channel:
                parcels_ref[place_in_plane(near, time, times)] = values


def correlate_kernel(frames_all, inputs_here, place_ref, every_ref, packed_ref):
    count, lines, width = every_ref.shape
    blocks, rows, inputs_all = packed_ref.shape
    times = count // NEAR
    main = lines - 2 * EARLY
    carry = None
    lined = []
    for time in range(times):
        pieces = [every_ref[place_in_plane(near, time, times)] for near in range(NEAR)]
        wide = jnp.concatenate([piece.astype(jnp.float32) for piece in pieces], axis=1)
        tiles = [wide[start : start + 8] for start in range(0, lines, 8)]
        if carry is not None:
            early = lax.broadcasted_iota(jnp.int32, carry.shape, 0) < EARLY
            tiles[0] = tiles[0] + jnp.where(early, carry, 0.0)
            tiles[1] = tiles[1] + jnp.where(early, pltpu.roll(carry, 8 - EARLY, 0), 0.0)
        carry = tiles[-1]
        lined += tiles[:-1]
    far = width // inputs_here
    target = lax.broadcasted_iota(jnp.int32, (1, inputs_all), 1)
    near = target // inputs_here % NEAR
    listed = place_in_column(target // (inputs_here * NEAR), far)
    source = near * width + listed * inputs_here + target % inputs_here
    chosen = lax.broadcasted_iota(jnp.int32, (inputs_all, inputs_all), 0) == source
    ordered = jnp.dot(
        jnp.concatenate(lined, axis=0).astype(jnp.bfloat16),
        chosen.astype(jnp.float32).astype(jnp.bfloat16),
        preferred_element_type=jnp.float32,
    )
    right = ordered.astype(jnp.bfloat16)
    twisted = []
    for start in range(0, times * main, 16):
        twisted.append(ordered[start + 8 : start + 16])
        twisted.append(-ordered[start : start + 8])
    twisted = jnp.concatenate(twisted, axis=0).astype(jnp.bfloat16)
    inner = place_ref[0] == 1
    wide = 2 * rows
    col_index = lax.broadcasted_iota(jnp.int32, (wide, inputs_all), 1)
    row_index = lax.broadcasted_iota(jnp.int32, (wide, inputs_all), 0)
    for side in range(2):
        outer_start = side * (inputs_all - wide)
        inner_start = (1 + side) * wide
        both = []
        for left in (right, twisted):
            chosen = jnp.where(
                inner,
                left[:, inner_start : inner_start + wide],
                left[:, outer_start : outer_start + wide],
            )
            both.append(
                lax.dot_general(
                    chosen,
                    right,
                    (((0,), (0,)), ((), ())),
                    preferred_element_type=jnp.float32,
                )
            )
        upper = row_index + jnp.where(inner, inner_start, outer_start) <= col_index
        values = (jnp.where(upper, both[0], both[1]) * (1.0 / frames_all)).astype(jnp.bfloat16)
        packed_ref[blocks - 1 - 2 * side] = values[:rows]
        packed_ref[blocks - 2 - 2 * side] = values[rows:]


def unpack_kernel(packed_ref, lines_ref):
    channels, count, width = packed_ref.shape
    tiles = width // LANES
    for channel in range(channels):
        values = packed_ref[channels - 1 - channel].astype(jnp.float32)
        for tile in range(tiles):
            lines = pl.ds(tile * channels + channel, count, stride=tiles * channels)
            lines_ref[lines, :] = values[:, tile * LANES : (tile + 1) * LANES]


def body(samples, gains):
    inputs_here = samples.shape[0]
    frames_here = samples.shape[1] // NFFT
    times = lax.axis_size("tm")
    far = lax.axis_size("far")
    groups = far * NEAR
    per_group = CH // groups
    inputs_all = inputs_here * groups
    frames_all = frames_here * times
    block = inputs_here * frames_here

    window = filter_window()
    twiddle = jnp.asarray(build_table(window)[: NFFT // 2])
    window_taps = jnp.asarray(window.astype(np.float32).reshape(TAPS, NFFT))

    sent = frames_here + EARLY
    gains = gains.transpose(0, 2, 1)

    def own_part(*refs):
        own_part_kernel(far, *refs)

    own, passed, parcels = pl.pallas_call(
        own_part,
        out_shape=(
            jax.ShapeDtypeStruct((block, 2 * CH), jnp.float32),
            jax.ShapeDtypeStruct(((TAPS - 1) * inputs_here, 2 * CH), jnp.float32),
            jax.ShapeDtypeStruct((far * inputs_here, sent * 2 * CH // far), jnp.bfloat16),
        ),
        in_specs=[ANY] * 4,
        out_specs=(ANY, ANY, ANY),
        scratch_shapes=[
            pltpu.VMEM(samples.shape, jnp.bfloat16),
            pltpu.VMEM(window_taps.shape, jnp.float32),
            pltpu.VMEM(twiddle.shape, jnp.bfloat16),
            pltpu.VMEM(gains.shape, jnp.float32),
            pltpu.VMEM((sent * inputs_here, 2 * CH), jnp.float32),
            pltpu.VMEM((far * inputs_here, sent * 2 * CH // far), jnp.bfloat16),
            pltpu.SemaphoreType.DMA((3 + NFFT // (2 * STEP),)),
            pltpu.SemaphoreType.DMA((2 + sent // 4,)),
        ],
        compiler_params=pltpu.CompilerParams(vmem_limit_bytes=OWN_PART_VMEM),
        cost_estimate=pl.CostEstimate(
            flops=2 * sent * inputs_here * NFFT * 2 * CH,
            bytes_accessed=3 * 1024 * 1024,
            transcendentals=0,
        ),
        name="own_part",
    )(samples, window_taps, twiddle, gains)

    parcels = parcels.reshape(far, inputs_here, sent * 2 * CH // far)
    column = [sorted(range(far), key=lambda place: place_in_column(place, far))]
    mine = lax.all_to_all(parcels, "far", 0, 0, axis_index_groups=column)
    mine = mine.reshape(far * inputs_here, sent * 2 * CH // far)

    passed = lax.ppermute(passed, "tm", [(source, source + 1) for source in range(times - 1)])
    spectra = pl.pallas_call(
        spectra_kernel,
        out_shape=jax.ShapeDtypeStruct((2, block, CH), jnp.bfloat16),
        in_specs=[VMEM] * 3,
        out_specs=VMEM,
        scratch_shapes=[pltpu.VMEM((2 * CH // LANES, block, LANES), jnp.float32)],
        compiler_params=PARAMS,
        cost_estimate=pl.CostEstimate(
            flops=8 * block * 2 * CH, bytes_accessed=1024 * 1024, transcendentals=0
        ),
        name="spectra",
    )(passed, own, gains)
    mine, spectra = lax.optimization_barrier((mine, spectra))
    spectra = spectra.reshape(2, inputs_here, frames_here, CH).transpose(0, 3, 1, 2)

    lines = 2 * sent
    spread = pl.pallas_call(
        spread_kernel,
        out_shape=jax.ShapeDtypeStruct((NEAR * times, lines, far * inputs_here), jnp.bfloat16),
        in_specs=[VMEM],
        out_specs=VMEM,
        compiler_params=PARAMS,
        name="spread",
    )(mine)
    members = [(near, time) for near in range(NEAR) for time in range(times)]
    members.sort(key=lambda member: place_in_plane(*member, times))
    plane = [[near * times + time for near, time in members]]
    every = lax.all_to_all(spread, ("near", "tm"), 0, 0, axis_index_groups=plane)

    def correlate(*refs):
        correlate_kernel(frames_all, inputs_here, *refs)

    rows = inputs_all // times
    place = lax.axis_index("tm").astype(jnp.int32)
    inner = (place >= times // 4) & (place < times - times // 4)
    packed = pl.pallas_call(
        correlate,
        out_shape=jax.ShapeDtypeStruct((times // 2, rows, inputs_all), jnp.bfloat16),
        in_specs=[SMEM, VMEM],
        out_specs=VMEM,
        compiler_params=PARAMS,
        name="correlate",
    )(inner.astype(jnp.int32)[None], every)
    squares = [[7, 6, 1, 0], [5, 4, 3, 2]]
    packed = lax.all_to_all(packed, "tm", 0, 0, axis_index_groups=squares)
    tiles = inputs_all // LANES
    visibilities = pl.pallas_call(
        unpack_kernel,
        out_shape=jax.ShapeDtypeStruct((rows * tiles * per_group, LANES), jnp.float32),
        in_specs=[VMEM],
        out_specs=VMEM,
        compiler_params=PARAMS,
        name="unpack",
    )(packed)
    visibilities = visibilities.reshape(rows, tiles, per_group, LANES).transpose(0, 2, 1, 3)
    visibilities = visibilities.reshape(rows, per_group, inputs_all)
    return (spectra, visibilities)


def solution(mesh):
    groups, times = mesh.devices.shape
    split = Mesh(mesh.devices.reshape(groups // NEAR, NEAR, times), ("far", "near", "tm"))
    inputs = ("far", "near")
    return jax.shard_map(
        body,
        mesh=split,
        in_specs=(P(inputs, "tm"), P(None, None, inputs)),
        out_specs=(P(None, None, inputs, "tm"), P("tm", inputs, None)),
        check_vma=False,
    )
```

```python
import math

import jax
import jax.numpy as jnp
import numpy as np
from jax import lax
from jax.experimental import pallas as pl
from jax.experimental.pallas import tpu as pltpu
from jax.sharding import Mesh, PartitionSpec as P

NFFT = 2048
CH = 256
FIRST = 384
TAPS = 4
NEAR = 4
EARLY = 4
STEP = 512
LANES = 128
VMEM = pl.BlockSpec(memory_space=pltpu.VMEM)
ANY = pl.BlockSpec(memory_space=pl.ANY)
SMEM = pl.BlockSpec(memory_space=pltpu.SMEM)
OWN_PART_VMEM = 59 * 1024 * 1024 + 768 * 1024
PARAMS = pltpu.CompilerParams(vmem_limit_bytes=32 * 1024 * 1024)


def filter_window():
    length = TAPS * NFFT
    position = np.arange(length, dtype=np.float64)
    centred = (position - 0.5 * length + 0.5) / NFFT
    hann_taper = 0.5 - 0.5 * np.cos(2.0 * math.pi * (position + 0.5) / length)
    return np.sinc(centred) * hann_taper


def build_table(window):
    norm_scale = 1.0 / np.sqrt(np.sum(window * window))
    sample = np.arange(NFFT)[:, None]
    channel = FIRST + np.arange(CH)[None, :]
    phase_angle = 2.0 * math.pi / NFFT * (sample * channel % NFFT)
    cosine = np.cos(phase_angle) * norm_scale
    sine = -np.sin(phase_angle) * norm_scale
    return np.concatenate([cosine, sine], axis=1).astype(jnp.bfloat16)


def tapped_block(samples_ref, window_ref, frames_sent, block):
    inputs_here, count = samples_ref.shape
    frames_here = count // NFFT
    low = block * STEP
    sums = []
    for frame in range(frames_sent):
        total = jnp.zeros((inputs_here, STEP), jnp.float32)
        for tap in range(TAPS):
            source = frame - TAPS + 1 + tap
            if 0 <= source < frames_here:
                start = source * NFFT + low
                values = samples_ref[:, start : start + STEP]
                weights = window_ref[tap : tap + 1, low : low + STEP]
                total = total + weights * values.astype(jnp.float32)
        sums.append(total)
    pairs = [
        jnp.concatenate(sums[frame : frame + 2], axis=0).astype(jnp.bfloat16)
        for frame in range(0, frames_sent, 2)
    ]
    return jnp.concatenate(pairs, axis=0)


def turn_granules(blocks, size):
    count = len(blocks)
    lanes = count * size
    granule = lax.broadcasted_iota(jnp.int32, blocks[0].shape, 1) // size
    blocks = list(blocks)
    distance = count // 2
    while distance:
        upper = (granule & distance) != 0
        shift = distance * size
        for index in range(count):
            if index & distance:
                continue
            low, high = blocks[index], blocks[index + distance]
            blocks[index] = jnp.where(upper, pltpu.roll(high, shift, 1), low)
            blocks[index + distance] = jnp.where(upper, high, pltpu.roll(low, lanes - shift, 1))
        distance //= 2
    return blocks


def place_in_column(place, far):
    return (place + far * 3 // 8) % far


def own_part_kernel(
    far,
    samples_hbm,
    window_hbm,
    twiddle_hbm,
    gains_hbm,
    own_hbm,
    passed_hbm,
    parcels_hbm,
    samples_ref,
    window_ref,
    twiddle_ref,
    gains_ref,
    direct_ref,
    parcels_ref,
    arrived,
    left,
):
    inputs_here = gains_ref.shape[1]
    frames_here = samples_hbm.shape[1] // NFFT
    blocks = range(NFFT // STEP)
    fetches = []

    def fetch(source, target):
        fetches.append(pltpu.make_async_copy(source, target, arrived.at[len(fetches)]))
        fetches[-1].start()
        return fetches[-1]

    samples_in = fetch(samples_hbm, samples_ref)
    window_in = fetch(window_hbm, window_ref)
    table_in = []
    for block in blocks[: len(blocks) // 2]:
        rows = pl.ds(block * STEP, STEP)
        table_in.append(fetch(twiddle_hbm.at[rows, :], twiddle_ref.at[rows, :]))
    gains_in = fetch(gains_hbm, gains_ref)
    samples_in.wait()
    window_in.wait()
    halves = []
    for first in (0, len(table_in)):
        total = None
        for block, table in enumerate(table_in):
            tapped = tapped_block(samples_ref, window_ref, frames_here + EARLY, first + block)
            if not first:
                table.wait()
            product = jnp.dot(
                tapped,
                twiddle_ref[block * STEP : (block + 1) * STEP, :],
                preferred_element_type=jnp.float32,
            )
            total = product if total is None else total + product
        halves.append(total)
    channel = FIRST + lax.broadcasted_iota(jnp.int32, (1, 2 * CH), 1)
    sign = (1 - 2 * (channel % 2)).astype(jnp.float32)
    direct_ref[...] = halves[0] + sign * halves[1]
    own_rows = own_hbm.shape[0]
    passed_rows = passed_hbm.shape[0]
    stores = [
        pltpu.make_async_copy(direct_ref.at[pl.ds(0, own_rows), :], own_hbm, left.at[0]),
        pltpu.make_async_copy(
            direct_ref.at[pl.ds(own_rows, passed_rows), :], passed_hbm, left.at[1]
        ),
    ]
    for store in stores:
        store.start()
    gains_in.wait()
    gain_re = gains_ref[0]
    gain_im = gains_ref[1]
    parts = []
    for frame in range(frames_here + EARLY):
        direct = direct_ref[frame * inputs_here : (frame + 1) * inputs_here, :]
        direct_re = direct[:, :CH]
        direct_im = direct[:, CH:]
        parts.append(
            (
                gain_re * direct_re - gain_im * direct_im,
                gain_re * direct_im + gain_im * direct_re,
            )
        )
    slots = [
        [(part, frame) for frame in range(first, first + 8)]
        for first in range(0, frames_here, 8)
        for part in range(2)
    ]
    slots.append([(part, frames_here + frame) for part in range(2) for frame in range(EARLY)])
    per_far = CH // far
    for place, slot in enumerate(slots):
        columns = slice(place * LANES, (place + 1) * LANES)
        for half in range(CH // LANES):
            lanes = slice(half * LANES, (half + 1) * LANES)
            blocks = turn_granules([parts[frame][part][:, lanes] for part, frame in slot], per_far)
            for index in range(0, len(blocks), 2):
                row = place_in_column(half * len(blocks) + index, far) * inputs_here
                parcels_ref[row : row + 2 * inputs_here, columns] = jnp.concatenate(
                    blocks[index : index + 2], axis=0
                ).astype(jnp.bfloat16)
        lanes = pl.ds(place * LANES, LANES)
        stores.append(
            pltpu.make_async_copy(
                parcels_ref.at[:, lanes], parcels_hbm.at[:, lanes], left.at[len(stores)]
            )
        )
        stores[-1].start()
    for store in stores:
        store.wait()


def spectra_kernel(passed_ref, own_ref, gains_ref, spectra_ref, rows_ref):
    inputs_here = gains_ref.shape[1]
    frames_here = own_ref.shape[0] // inputs_here
    slabs = CH // LANES
    gain_re = gains_ref[0]
    gain_im = gains_ref[1]
    for frame in range(frames_here):
        block = slice(frame * inputs_here, (frame + 1) * inputs_here)
        direct = own_ref[block, :]
        if frame < TAPS - 1:
            direct = direct + passed_ref[block, :]
        direct_re = direct[:, :CH]
        direct_im = direct[:, CH:]
        rows = pl.ds(frame, inputs_here, stride=frames_here)
        real_part = gain_re * direct_re - gain_im * direct_im
        imag_part = gain_re * direct_im + gain_im * direct_re
        for slab in range(slabs):
            columns = slice(slab * LANES, (slab + 1) * LANES)
            rows_ref[slab, rows, :] = real_part[:, columns]
            rows_ref[slabs + slab, rows, :] = imag_part[:, columns]
    for part in range(2):
        for slab in range(slabs):
            columns = slice(slab * LANES, (slab + 1) * LANES)
            spectra_ref[part, :, columns] = rows_ref[part * slabs + slab].astype(jnp.bfloat16)


def channel_of(time):
    return time // 4 * 2 + time % 2


def place_in_plane(near, time, times):
    return (near + NEAR // 2) % NEAR * times + (time + times // 2) % times


def spread_kernel(mine_ref, parcels_ref, turned_ref):
    count, rows, width = parcels_ref.shape
    times = count // NEAR
    stride = mine_ref.shape[1] // rows
    for place in range(0, mine_ref.shape[1], LANES):
        values = mine_ref[:, place : place + LANES].astype(jnp.float32)
        turned_ref[place : place + LANES, :] = values.T
    for near in range(NEAR):
        for channel in range(stride // NEAR):
            start = near * (stride // NEAR) + channel
            values = turned_ref[pl.ds(start, rows, stride=stride), :].astype(jnp.bfloat16)
            for time in range(times):
                if channel_of(time) == channel:
                    parcels_ref[place_in_plane(near, time, times)] = values


def correlate_kernel(frames_all, inputs_here, place_ref, every_ref, packed_ref):
    count, lines, width = every_ref.shape
    blocks, rows, inputs_all = packed_ref.shape
    times = count // NEAR
    main = lines - 2 * EARLY
    carry = None
    lined = []
    for time in range(times):
        pieces = [every_ref[place_in_plane(near, time, times)] for near in range(NEAR)]
        wide = jnp.concatenate([piece.astype(jnp.float32) for piece in pieces], axis=1)
        tiles = [wide[start : start + 8] for start in range(0, lines, 8)]
        if carry is not None:
            early = lax.broadcasted_iota(jnp.int32, carry.shape, 0) < EARLY
            tiles[0] = tiles[0] + jnp.where(early, carry, 0.0)
            tiles[1] = tiles[1] + jnp.where(early, pltpu.roll(carry, 8 - EARLY, 0), 0.0)
        carry = tiles[-1]
        lined += tiles[:-1]
    far = width // inputs_here
    target = lax.broadcasted_iota(jnp.int32, (1, inputs_all), 1)
    near = target // inputs_here % NEAR
    listed = place_in_column(target // (inputs_here * NEAR), far)
    source = near * width + listed * inputs_here + target % inputs_here
    chosen = lax.broadcasted_iota(jnp.int32, (inputs_all, inputs_all), 0) == source
    ordered = jnp.dot(
        jnp.concatenate(lined, axis=0).astype(jnp.bfloat16),
        chosen.astype(jnp.float32).astype(jnp.bfloat16),
        preferred_element_type=jnp.float32,
    )
    right = ordered.astype(jnp.bfloat16)
    twisted = []
    for start in range(0, times * main, 16):
        twisted.append(ordered[start + 8 : start + 16])
        twisted.append(-ordered[start : start + 8])
    twisted = jnp.concatenate(twisted, axis=0).astype(jnp.bfloat16)
    inner = place_ref[0] == 1
    wide = 2 * rows
    col_index = lax.broadcasted_iota(jnp.int32, (wide, inputs_all), 1)
    row_index = lax.broadcasted_iota(jnp.int32, (wide, inputs_all), 0)
    for side in range(2):
        outer_start = side * (inputs_all - wide)
        inner_start = (1 + side) * wide
        both = []
        for left in (right, twisted):
            chosen = jnp.where(
                inner,
                left[:, inner_start : inner_start + wide],
                left[:, outer_start : outer_start + wide],
            )
            both.append(
                lax.dot_general(
                    chosen,
                    right,
                    (((0,), (0,)), ((), ())),
                    preferred_element_type=jnp.float32,
                )
            )
        upper = row_index + jnp.where(inner, inner_start, outer_start) <= col_index
        values = (jnp.where(upper, both[0], both[1]) * (1.0 / frames_all)).astype(jnp.bfloat16)
        packed_ref[blocks - 1 - 2 * side] = values[:rows]
        packed_ref[blocks - 2 - 2 * side] = values[rows:]


def unpack_kernel(packed_ref, lines_hbm, lines_ref, left):
    channels, count, width = packed_ref.shape
    tiles = width // LANES
    stores = []
    for first in range(0, count, 16):
        start = first * tiles * channels
        for channel in range(channels):
            values = packed_ref[channels - 1 - channel, first : first + 16, :].astype(jnp.float32)
            for tile in range(tiles):
                lines = pl.ds(start + tile * channels + channel, 16, stride=tiles * channels)
                lines_ref[lines, :] = values[:, tile * LANES : (tile + 1) * LANES]
        block = pl.ds(start, 16 * tiles * channels)
        stores.append(
            pltpu.make_async_copy(lines_ref.at[block, :], lines_hbm.at[block, :], left.at[len(stores)])
        )
        stores[-1].start()
    for store in stores:
        store.wait()


def body(samples, gains):
    inputs_here = samples.shape[0]
    frames_here = samples.shape[1] // NFFT
    times = lax.axis_size("tm")
    far = lax.axis_size("far")
    groups = far * NEAR
    per_group = CH // groups
    inputs_all = inputs_here * groups
    frames_all = frames_here * times
    block = inputs_here * frames_here

    window = filter_window()
    twiddle = jnp.asarray(build_table(window)[: NFFT // 2])
    window_taps = jnp.asarray(window.astype(np.float32).reshape(TAPS, NFFT))

    sent = frames_here + EARLY
    gains = gains.transpose(0, 2, 1)

    def own_part(*refs):
        own_part_kernel(far, *refs)

    own, passed, parcels = pl.pallas_call(
        own_part,
        out_shape=(
            jax.ShapeDtypeStruct((block, 2 * CH), jnp.float32),
            jax.ShapeDtypeStruct(((TAPS - 1) * inputs_here, 2 * CH), jnp.float32),
            jax.ShapeDtypeStruct((far * inputs_here, sent * 2 * CH // far), jnp.bfloat16),
        ),
        in_specs=[ANY] * 4,
        out_specs=(ANY, ANY, ANY),
        scratch_shapes=[
            pltpu.VMEM(samples.shape, jnp.bfloat16),
            pltpu.VMEM(window_taps.shape, jnp.float32),
            pltpu.VMEM(twiddle.shape, jnp.bfloat16),
            pltpu.VMEM(gains.shape, jnp.float32),
            pltpu.VMEM((sent * inputs_here, 2 * CH), jnp.float32),
            pltpu.VMEM((far * inputs_here, sent * 2 * CH // far), jnp.bfloat16),
            pltpu.SemaphoreType.DMA((3 + NFFT // (2 * STEP),)),
            pltpu.SemaphoreType.DMA((2 + sent // 4,)),
        ],
        compiler_params=pltpu.CompilerParams(vmem_limit_bytes=OWN_PART_VMEM),
        cost_estimate=pl.CostEstimate(
            flops=2 * sent * inputs_here * NFFT * 2 * CH,
            bytes_accessed=3 * 1024 * 1024,
            transcendentals=0,
        ),
        name="own_part",
    )(samples, window_taps, twiddle, gains)

    parcels = parcels.reshape(far, inputs_here, sent * 2 * CH // far)
    column = [sorted(range(far), key=lambda place: place_in_column(place, far))]
    mine = lax.all_to_all(parcels, "far", 0, 0, axis_index_groups=column)
    mine = mine.reshape(far * inputs_here, sent * 2 * CH // far)

    passed = lax.ppermute(passed, "tm", [(source, source + 1) for source in range(times - 1)])
    mine, passed = lax.optimization_barrier((mine, passed))

    lines = 2 * sent
    spread = pl.pallas_call(
        spread_kernel,
        out_shape=jax.ShapeDtypeStruct((NEAR * times, lines, far * inputs_here), jnp.bfloat16),
        in_specs=[VMEM],
        out_specs=VMEM,
        scratch_shapes=[pltpu.VMEM((sent * 2 * CH // far, far * inputs_here), jnp.float32)],
        compiler_params=PARAMS,
        name="spread",
    )(mine)
    members = [(near, time) for near in range(NEAR) for time in range(times)]
    members.sort(key=lambda member: place_in_plane(*member, times))
    plane = [[near * times + time for near, time in members]]
    every = lax.all_to_all(spread, ("near", "tm"), 0, 0, axis_index_groups=plane)

    def correlate(*refs):
        correlate_kernel(frames_all, inputs_here, *refs)

    rows = inputs_all // times
    place = lax.axis_index("tm").astype(jnp.int32)
    inner = (place >= times // 4) & (place < times - times // 4)
    packed = pl.pallas_call(
        correlate,
        out_shape=jax.ShapeDtypeStruct((times // 2, rows, inputs_all), jnp.bfloat16),
        in_specs=[SMEM, VMEM],
        out_specs=VMEM,
        compiler_params=PARAMS,
        name="correlate",
    )(inner.astype(jnp.int32)[None], every)
    squares = [[7, 6, 1, 0], [5, 4, 3, 2]]
    own, packed = lax.optimization_barrier((own, packed))
    packed = lax.all_to_all(packed, "tm", 0, 0, axis_index_groups=squares)

    spectra = pl.pallas_call(
        spectra_kernel,
        out_shape=jax.ShapeDtypeStruct((2, block, CH), jnp.bfloat16),
        in_specs=[VMEM] * 3,
        out_specs=VMEM,
        scratch_shapes=[pltpu.VMEM((2 * CH // LANES, block, LANES), jnp.float32)],
        compiler_params=PARAMS,
        cost_estimate=pl.CostEstimate(
            flops=8 * block * 2 * CH, bytes_accessed=1024 * 1024, transcendentals=0
        ),
        name="spectra",
    )(passed, own, gains)
    spectra = spectra.reshape(2, inputs_here, frames_here, CH).transpose(0, 3, 1, 2)
    packed, spectra = lax.optimization_barrier((packed, spectra))

    tiles = inputs_all // LANES
    visibilities = pl.pallas_call(
        unpack_kernel,
        out_shape=jax.ShapeDtypeStruct((rows * tiles * per_group, LANES), jnp.float32),
        in_specs=[VMEM],
        out_specs=ANY,
        scratch_shapes=[
            pltpu.VMEM((rows * tiles * per_group, LANES), jnp.float32),
            pltpu.SemaphoreType.DMA((rows // 16,)),
        ],
        compiler_params=PARAMS,
        name="unpack",
    )(packed)
    visibilities = visibilities.reshape(rows, tiles, per_group, LANES).transpose(0, 2, 1, 3)
    visibilities = visibilities.reshape(rows, per_group, inputs_all)
    return (spectra, visibilities)


def solution(mesh):
    groups, times = mesh.devices.shape
    split = Mesh(mesh.devices.reshape(groups // NEAR, NEAR, times), ("far", "near", "tm"))
    inputs = ("far", "near")
    return jax.shard_map(
        body,
        mesh=split,
        in_specs=(P(inputs, "tm"), P(None, None, inputs)),
        out_specs=(P(None, None, inputs, "tm"), P("tm", inputs, None)),
        check_vma=False,
    )
```

```python
import math

import jax
import jax.numpy as jnp
import numpy as np
from jax import lax
from jax.experimental import pallas as pl
from jax.experimental.pallas import tpu as pltpu
from jax.sharding import Mesh, PartitionSpec as P

NFFT = 2048
CH = 256
FIRST = 384
TAPS = 4
NEAR = 4
EARLY = 4
STEP = 512
LANES = 128
VMEM = pl.BlockSpec(memory_space=pltpu.VMEM)
ANY = pl.BlockSpec(memory_space=pl.ANY)
SMEM = pl.BlockSpec(memory_space=pltpu.SMEM)
OWN_PART_VMEM = 59 * 1024 * 1024 + 768 * 1024
PARAMS = pltpu.CompilerParams(vmem_limit_bytes=32 * 1024 * 1024)


def filter_window():
    length = TAPS * NFFT
    position = np.arange(length, dtype=np.float64)
    centred = (position - 0.5 * length + 0.5) / NFFT
    hann_taper = 0.5 - 0.5 * np.cos(2.0 * math.pi * (position + 0.5) / length)
    return np.sinc(centred) * hann_taper


def build_table(window):
    norm_scale = 1.0 / np.sqrt(np.sum(window * window))
    sample = np.arange(NFFT)[:, None]
    channel = FIRST + np.arange(CH)[None, :]
    phase_angle = 2.0 * math.pi / NFFT * (sample * channel % NFFT)
    cosine = np.cos(phase_angle) * norm_scale
    sine = -np.sin(phase_angle) * norm_scale
    return np.concatenate([cosine, sine], axis=1).astype(jnp.bfloat16)


def tapped_block(samples_ref, window_ref, frames_sent, block):
    inputs_here, count = samples_ref.shape
    frames_here = count // NFFT
    low = block * STEP
    sums = []
    for frame in range(frames_sent):
        total = jnp.zeros((inputs_here, STEP), jnp.float32)
        for tap in range(TAPS):
            source = frame - TAPS + 1 + tap
            if 0 <= source < frames_here:
                start = source * NFFT + low
                values = samples_ref[:, start : start + STEP]
                weights = window_ref[tap : tap + 1, low : low + STEP]
                total = total + weights * values.astype(jnp.float32)
        sums.append(total)
    pairs = [
        jnp.concatenate(sums[frame : frame + 2], axis=0).astype(jnp.bfloat16)
        for frame in range(0, frames_sent, 2)
    ]
    return jnp.concatenate(pairs, axis=0)


def turn_granules(blocks, size):
    count = len(blocks)
    lanes = count * size
    granule = lax.broadcasted_iota(jnp.int32, blocks[0].shape, 1) // size
    blocks = list(blocks)
    distance = count // 2
    while distance:
        upper = (granule & distance) != 0
        shift = distance * size
        for index in range(count):
            if index & distance:
                continue
            low, high = blocks[index], blocks[index + distance]
            blocks[index] = jnp.where(upper, pltpu.roll(high, shift, 1), low)
            blocks[index + distance] = jnp.where(upper, high, pltpu.roll(low, lanes - shift, 1))
        distance //= 2
    return blocks


def place_in_column(place, far):
    return (place + far * 3 // 8) % far


def own_part_kernel(
    far,
    samples_hbm,
    window_hbm,
    twiddle_hbm,
    gains_hbm,
    own_hbm,
    passed_hbm,
    parcels_hbm,
    samples_ref,
    window_ref,
    twiddle_ref,
    gains_ref,
    direct_ref,
    parcels_ref,
    arrived,
    left,
):
    inputs_here = gains_ref.shape[1]
    frames_here = samples_hbm.shape[1] // NFFT
    blocks = range(NFFT // STEP)
    fetches = []

    def fetch(source, target):
        fetches.append(pltpu.make_async_copy(source, target, arrived.at[len(fetches)]))
        fetches[-1].start()
        return fetches[-1]

    samples_in = fetch(samples_hbm, samples_ref)
    window_in = fetch(window_hbm, window_ref)
    table_in = []
    for block in blocks[: len(blocks) // 2]:
        rows = pl.ds(block * STEP, STEP)
        table_in.append(fetch(twiddle_hbm.at[rows, :], twiddle_ref.at[rows, :]))
    gains_in = fetch(gains_hbm, gains_ref)
    samples_in.wait()
    window_in.wait()
    halves = []
    for first in (0, len(table_in)):
        total = None
        for block, table in enumerate(table_in):
            tapped = tapped_block(samples_ref, window_ref, frames_here + EARLY, first + block)
            if not first:
                table.wait()
            product = jnp.dot(
                tapped,
                twiddle_ref[block * STEP : (block + 1) * STEP, :],
                preferred_element_type=jnp.float32,
            )
            total = product if total is None else total + product
        halves.append(total)
    channel = FIRST + lax.broadcasted_iota(jnp.int32, (1, 2 * CH), 1)
    sign = (1 - 2 * (channel % 2)).astype(jnp.float32)
    direct_ref[...] = halves[0] + sign * halves[1]
    own_rows = own_hbm.shape[0]
    passed_rows = passed_hbm.shape[0]
    stores = [
        pltpu.make_async_copy(direct_ref.at[pl.ds(0, own_rows), :], own_hbm, left.at[0]),
        pltpu.make_async_copy(
            direct_ref.at[pl.ds(own_rows, passed_rows), :], passed_hbm, left.at[1]
        ),
    ]
    for store in stores:
        store.start()
    gains_in.wait()
    gain_re = gains_ref[0]
    gain_im = gains_ref[1]
    parts = []
    for frame in range(frames_here + EARLY):
        direct = direct_ref[frame * inputs_here : (frame + 1) * inputs_here, :]
        direct_re = direct[:, :CH]
        direct_im = direct[:, CH:]
        parts.append(
            (
                gain_re * direct_re - gain_im * direct_im,
                gain_re * direct_im + gain_im * direct_re,
            )
        )
    slots = [
        [(part, frame) for frame in range(first, first + 8)]
        for first in range(0, frames_here, 8)
        for part in range(2)
    ]
    slots.append([(part, frames_here + frame) for part in range(2) for frame in range(EARLY)])
    per_far = CH // far
    for place, slot in enumerate(slots):
        columns = slice(place * LANES, (place + 1) * LANES)
        for half in range(CH // LANES):
            lanes = slice(half * LANES, (half + 1) * LANES)
            blocks = turn_granules([parts[frame][part][:, lanes] for part, frame in slot], per_far)
            for index in range(0, len(blocks), 2):
                row = place_in_column(half * len(blocks) + index, far) * inputs_here
                parcels_ref[row : row + 2 * inputs_here, columns] = jnp.concatenate(
                    blocks[index : index + 2], axis=0
                ).astype(jnp.bfloat16)
        lanes = pl.ds(place * LANES, LANES)
        stores.append(
            pltpu.make_async_copy(
                parcels_ref.at[:, lanes], parcels_hbm.at[:, lanes], left.at[len(stores)]
            )
        )
        stores[-1].start()
    for store in stores:
        store.wait()


def spectra_kernel(passed_ref, own_ref, gains_ref, spectra_ref, rows_ref):
    inputs_here = gains_ref.shape[1]
    frames_here = own_ref.shape[0] // inputs_here
    slabs = CH // LANES
    gain_re = gains_ref[0]
    gain_im = gains_ref[1]
    for frame in range(frames_here):
        block = slice(frame * inputs_here, (frame + 1) * inputs_here)
        direct = own_ref[block, :]
        if frame < TAPS - 1:
            direct = direct + passed_ref[block, :]
        direct_re = direct[:, :CH]
        direct_im = direct[:, CH:]
        rows = pl.ds(frame, inputs_here, stride=frames_here)
        real_part = gain_re * direct_re - gain_im * direct_im
        imag_part = gain_re * direct_im + gain_im * direct_re
        for slab in range(slabs):
            columns = slice(slab * LANES, (slab + 1) * LANES)
            rows_ref[slab, rows, :] = real_part[:, columns]
            rows_ref[slabs + slab, rows, :] = imag_part[:, columns]
    for part in range(2):
        for slab in range(slabs):
            columns = slice(slab * LANES, (slab + 1) * LANES)
            spectra_ref[part, :, columns] = rows_ref[part * slabs + slab].astype(jnp.bfloat16)


def channel_of(time):
    return time // 4 * 2 + time % 2


def place_in_plane(near, time, times):
    return (near + NEAR // 2) % NEAR * times + (time + times // 2) % times


def spread_kernel(mine_ref, parcels_ref, turned_ref):
    count, rows, width = parcels_ref.shape
    times = count // NEAR
    stride = mine_ref.shape[1] // rows
    for place in range(0, mine_ref.shape[1], LANES):
        values = mine_ref[:, place : place + LANES].astype(jnp.float32)
        turned_ref[place : place + LANES, :] = values.T
    for near in range(NEAR):
        for channel in range(stride // NEAR):
            start = near * (stride // NEAR) + channel
            values = turned_ref[pl.ds(start, rows, stride=stride), :].astype(jnp.bfloat16)
            for time in range(times):
                if channel_of(time) == channel:
                    parcels_ref[place_in_plane(near, time, times)] = values


def correlate_kernel(frames_all, inputs_here, place_ref, every_ref, packed_ref):
    count, lines, width = every_ref.shape
    blocks, rows, inputs_all = packed_ref.shape
    times = count // NEAR
    main = lines - 2 * EARLY
    carry = None
    lined = []
    for time in range(times):
        pieces = [every_ref[place_in_plane(near, time, times)] for near in range(NEAR)]
        wide = jnp.concatenate([piece.astype(jnp.float32) for piece in pieces], axis=1)
        tiles = [wide[start : start + 8] for start in range(0, lines, 8)]
        if carry is not None:
            early = lax.broadcasted_iota(jnp.int32, carry.shape, 0) < EARLY
            tiles[0] = tiles[0] + jnp.where(early, carry, 0.0)
            tiles[1] = tiles[1] + jnp.where(early, pltpu.roll(carry, 8 - EARLY, 0), 0.0)
        carry = tiles[-1]
        lined += tiles[:-1]
    far = width // inputs_here
    target = lax.broadcasted_iota(jnp.int32, (1, inputs_all), 1)
    near = target // inputs_here % NEAR
    listed = place_in_column(target // (inputs_here * NEAR), far)
    source = near * width + listed * inputs_here + target % inputs_here
    chosen = lax.broadcasted_iota(jnp.int32, (inputs_all, inputs_all), 0) == source
    ordered = jnp.dot(
        jnp.concatenate(lined, axis=0).astype(jnp.bfloat16),
        chosen.astype(jnp.float32).astype(jnp.bfloat16),
        preferred_element_type=jnp.float32,
    )
    right = ordered.astype(jnp.bfloat16)
    twisted = []
    for start in range(0, times * main, 16):
        twisted.append(ordered[start + 8 : start + 16])
        twisted.append(-ordered[start : start + 8])
    twisted = jnp.concatenate(twisted, axis=0).astype(jnp.bfloat16)
    inner = place_ref[0] == 1
    wide = 2 * rows
    col_index = lax.broadcasted_iota(jnp.int32, (wide, inputs_all), 1)
    row_index = lax.broadcasted_iota(jnp.int32, (wide, inputs_all), 0)
    for side in range(2):
        outer_start = side * (inputs_all - wide)
        inner_start = (1 + side) * wide
        both = []
        for left in (right, twisted):
            chosen = jnp.where(
                inner,
                left[:, inner_start : inner_start + wide],
                left[:, outer_start : outer_start + wide],
            )
            both.append(
                lax.dot_general(
                    chosen,
                    right,
                    (((0,), (0,)), ((), ())),
                    preferred_element_type=jnp.float32,
                )
            )
        upper = row_index + jnp.where(inner, inner_start, outer_start) <= col_index
        values = (jnp.where(upper, both[0], both[1]) * (1.0 / frames_all)).astype(jnp.bfloat16)
        packed_ref[blocks - 1 - 2 * side] = values[:rows]
        packed_ref[blocks - 2 - 2 * side] = values[rows:]


def unpack_kernel(packed_ref, lines_hbm, lines_ref, left):
    channels, count, width = packed_ref.shape
    tiles = width // LANES
    stores = []
    for first in range(0, count, 16):
        start = first * tiles * channels
        for channel in range(channels):
            values = packed_ref[channels - 1 - channel, first : first + 16, :].astype(jnp.float32)
            for tile in range(tiles):
                lines = pl.ds(start + tile * channels + channel, 16, stride=tiles * channels)
                lines_ref[lines, :] = values[:, tile * LANES : (tile + 1) * LANES]
        block = pl.ds(start, 16 * tiles * channels)
        stores.append(
            pltpu.make_async_copy(lines_ref.at[block, :], lines_hbm.at[block, :], left.at[len(stores)])
        )
        stores[-1].start()
    for store in stores:
        store.wait()


def body(samples, gains):
    inputs_here = samples.shape[0]
    frames_here = samples.shape[1] // NFFT
    times = lax.axis_size("tm")
    far = lax.axis_size("far")
    groups = far * NEAR
    per_group = CH // groups
    inputs_all = inputs_here * groups
    frames_all = frames_here * times
    block = inputs_here * frames_here

    window = filter_window()
    twiddle = jnp.asarray(build_table(window)[: NFFT // 2])
    window_taps = jnp.asarray(window.astype(np.float32).reshape(TAPS, NFFT))

    sent = frames_here + EARLY
    gains = gains.transpose(0, 2, 1)

    def own_part(*refs):
        own_part_kernel(far, *refs)

    own, passed, parcels = pl.pallas_call(
        own_part,
        out_shape=(
            jax.ShapeDtypeStruct((block, 2 * CH), jnp.float32),
            jax.ShapeDtypeStruct(((TAPS - 1) * inputs_here, 2 * CH), jnp.float32),
            jax.ShapeDtypeStruct((far * inputs_here, sent * 2 * CH // far), jnp.bfloat16),
        ),
        in_specs=[ANY] * 4,
        out_specs=(ANY, ANY, ANY),
        scratch_shapes=[
            pltpu.VMEM(samples.shape, jnp.bfloat16),
            pltpu.VMEM(window_taps.shape, jnp.float32),
            pltpu.VMEM(twiddle.shape, jnp.bfloat16),
            pltpu.VMEM(gains.shape, jnp.float32),
            pltpu.VMEM((sent * inputs_here, 2 * CH), jnp.float32),
            pltpu.VMEM((far * inputs_here, sent * 2 * CH // far), jnp.bfloat16),
            pltpu.SemaphoreType.DMA((3 + NFFT // (2 * STEP),)),
            pltpu.SemaphoreType.DMA((2 + sent // 4,)),
        ],
        compiler_params=pltpu.CompilerParams(vmem_limit_bytes=OWN_PART_VMEM),
        cost_estimate=pl.CostEstimate(
            flops=2 * sent * inputs_here * NFFT * 2 * CH,
            bytes_accessed=3 * 1024 * 1024,
            transcendentals=0,
        ),
        name="own_part",
    )(samples, window_taps, twiddle, gains)

    parcels = parcels.reshape(far, inputs_here, sent * 2 * CH // far)
    column = [sorted(range(far), key=lambda place: place_in_column(place, far))]
    mine = lax.all_to_all(parcels, "far", 0, 0, axis_index_groups=column)
    mine = mine.reshape(far * inputs_here, sent * 2 * CH // far)

    passed = lax.ppermute(passed, "tm", [(source, source + 1) for source in range(times - 1)])
    spectra = pl.pallas_call(
        spectra_kernel,
        out_shape=jax.ShapeDtypeStruct((2, block, CH), jnp.bfloat16),
        in_specs=[VMEM] * 3,
        out_specs=VMEM,
        scratch_shapes=[pltpu.VMEM((2 * CH // LANES, block, LANES), jnp.float32)],
        compiler_params=PARAMS,
        cost_estimate=pl.CostEstimate(
            flops=8 * block * 2 * CH, bytes_accessed=1024 * 1024, transcendentals=0
        ),
        name="spectra",
    )(passed, own, gains)
    mine, spectra = lax.optimization_barrier((mine, spectra))
    spectra = spectra.reshape(2, inputs_here, frames_here, CH).transpose(0, 3, 1, 2)

    lines = 2 * sent
    spread = pl.pallas_call(
        spread_kernel,
        out_shape=jax.ShapeDtypeStruct((NEAR * times, lines, far * inputs_here), jnp.bfloat16),
        in_specs=[VMEM],
        out_specs=VMEM,
        scratch_shapes=[pltpu.VMEM((sent * 2 * CH // far, far * inputs_here), jnp.float32)],
        compiler_params=PARAMS,
        name="spread",
    )(mine)
    place = lax.axis_index("tm").astype(jnp.int32)
    inner = ((place >= times // 4) & (place < times - times // 4)).astype(jnp.int32)[None]
    spread, inner = lax.optimization_barrier((spread, inner))
    members = [(near, time) for near in range(NEAR) for time in range(times)]
    members.sort(key=lambda member: place_in_plane(*member, times))
    plane = [[near * times + time for near, time in members]]
    every = lax.all_to_all(spread, ("near", "tm"), 0, 0, axis_index_groups=plane)

    def correlate(*refs):
        correlate_kernel(frames_all, inputs_here, *refs)

    rows = inputs_all // times
    packed = pl.pallas_call(
        correlate,
        out_shape=jax.ShapeDtypeStruct((times // 2, rows, inputs_all), jnp.bfloat16),
        in_specs=[SMEM, VMEM],
        out_specs=VMEM,
        compiler_params=PARAMS,
        name="correlate",
    )(inner, every)
    squares = [[7, 6, 1, 0], [5, 4, 3, 2]]
    packed = lax.all_to_all(packed, "tm", 0, 0, axis_index_groups=squares)
    tiles = inputs_all // LANES
    visibilities = pl.pallas_call(
        unpack_kernel,
        out_shape=jax.ShapeDtypeStruct((rows * tiles * per_group, LANES), jnp.float32),
        in_specs=[VMEM],
        out_specs=ANY,
        scratch_shapes=[
            pltpu.VMEM((rows * tiles * per_group, LANES), jnp.float32),
            pltpu.SemaphoreType.DMA((rows // 16,)),
        ],
        compiler_params=PARAMS,
        name="unpack",
    )(packed)
    visibilities = visibilities.reshape(rows, tiles, per_group, LANES).transpose(0, 2, 1, 3)
    visibilities = visibilities.reshape(rows, per_group, inputs_all)
    return (spectra, visibilities)


def solution(mesh):
    groups, times = mesh.devices.shape
    split = Mesh(mesh.devices.reshape(groups // NEAR, NEAR, times), ("far", "near", "tm"))
    inputs = ("far", "near")
    return jax.shard_map(
        body,
        mesh=split,
        in_specs=(P(inputs, "tm"), P(None, None, inputs)),
        out_specs=(P(None, None, inputs, "tm"), P("tm", inputs, None)),
        check_vma=False,
    )
```

```python
import math

import jax
import jax.numpy as jnp
import numpy as np
from jax import lax
from jax.experimental import pallas as pl
from jax.experimental.pallas import tpu as pltpu
from jax.sharding import Mesh, PartitionSpec as P

NFFT = 2048
CH = 256
FIRST = 384
TAPS = 4
NEAR = 4
EARLY = 4
STEP = 512
LANES = 128
VMEM = pl.BlockSpec(memory_space=pltpu.VMEM)
ANY = pl.BlockSpec(memory_space=pl.ANY)
SMEM = pl.BlockSpec(memory_space=pltpu.SMEM)
OWN_PART_VMEM = 59 * 1024 * 1024 + 768 * 1024
PARAMS = pltpu.CompilerParams(vmem_limit_bytes=32 * 1024 * 1024)


def filter_window():
    length = TAPS * NFFT
    position = np.arange(length, dtype=np.float64)
    centred = (position - 0.5 * length + 0.5) / NFFT
    hann_taper = 0.5 - 0.5 * np.cos(2.0 * math.pi * (position + 0.5) / length)
    return np.sinc(centred) * hann_taper


def build_table(window):
    norm_scale = 1.0 / np.sqrt(np.sum(window * window))
    sample = np.arange(NFFT)[:, None]
    channel = FIRST + np.arange(CH)[None, :]
    phase_angle = 2.0 * math.pi / NFFT * (sample * channel % NFFT)
    cosine = np.cos(phase_angle) * norm_scale
    sine = -np.sin(phase_angle) * norm_scale
    return np.concatenate([cosine, sine], axis=1).astype(jnp.bfloat16)


def tapped_block(samples_ref, window_ref, frames_sent, block):
    inputs_here, count = samples_ref.shape
    frames_here = count // NFFT
    low = block * STEP
    sums = []
    for frame in range(frames_sent):
        total = jnp.zeros((inputs_here, STEP), jnp.float32)
        for tap in range(TAPS):
            source = frame - TAPS + 1 + tap
            if 0 <= source < frames_here:
                start = source * NFFT + low
                values = samples_ref[:, start : start + STEP]
                weights = window_ref[tap : tap + 1, low : low + STEP]
                total = total + weights * values.astype(jnp.float32)
        sums.append(total)
    pairs = [
        jnp.concatenate(sums[frame : frame + 2], axis=0).astype(jnp.bfloat16)
        for frame in range(0, frames_sent, 2)
    ]
    return jnp.concatenate(pairs, axis=0)


def turn_granules(blocks, size):
    count = len(blocks)
    lanes = count * size
    granule = lax.broadcasted_iota(jnp.int32, blocks[0].shape, 1) // size
    blocks = list(blocks)
    distance = count // 2
    while distance:
        upper = (granule & distance) != 0
        shift = distance * size
        for index in range(count):
            if index & distance:
                continue
            low, high = blocks[index], blocks[index + distance]
            blocks[index] = jnp.where(upper, pltpu.roll(high, shift, 1), low)
            blocks[index + distance] = jnp.where(upper, high, pltpu.roll(low, lanes - shift, 1))
        distance //= 2
    return blocks


def place_in_column(place, far):
    return (place + far * 3 // 8) % far


def own_part_kernel(
    far,
    samples_hbm,
    window_hbm,
    twiddle_hbm,
    gains_hbm,
    own_hbm,
    passed_hbm,
    parcels_hbm,
    samples_ref,
    window_ref,
    twiddle_ref,
    gains_ref,
    direct_ref,
    parcels_ref,
    arrived,
    left,
):
    inputs_here = gains_ref.shape[1]
    frames_here = samples_hbm.shape[1] // NFFT
    blocks = range(NFFT // STEP)
    fetches = []

    def fetch(source, target):
        fetches.append(pltpu.make_async_copy(source, target, arrived.at[len(fetches)]))
        fetches[-1].start()
        return fetches[-1]

    samples_in = fetch(samples_hbm, samples_ref)
    window_in = fetch(window_hbm, window_ref)
    table_in = []
    for block in blocks[: len(blocks) // 2]:
        rows = pl.ds(block * STEP, STEP)
        table_in.append(fetch(twiddle_hbm.at[rows, :], twiddle_ref.at[rows, :]))
    gains_in = fetch(gains_hbm, gains_ref)
    samples_in.wait()
    window_in.wait()
    halves = []
    for first in (0, len(table_in)):
        total = None
        for block, table in enumerate(table_in):
            tapped = tapped_block(samples_ref, window_ref, frames_here + EARLY, first + block)
            if not first:
                table.wait()
            product = jnp.dot(
                tapped,
                twiddle_ref[block * STEP : (block + 1) * STEP, :],
                preferred_element_type=jnp.float32,
            )
            total = product if total is None else total + product
        halves.append(total)
    channel = FIRST + lax.broadcasted_iota(jnp.int32, (1, 2 * CH), 1)
    sign = (1 - 2 * (channel % 2)).astype(jnp.float32)
    direct_ref[...] = halves[0] + sign * halves[1]
    own_rows = own_hbm.shape[0]
    passed_rows = passed_hbm.shape[0]
    stores = [
        pltpu.make_async_copy(direct_ref.at[pl.ds(0, own_rows), :], own_hbm, left.at[0]),
        pltpu.make_async_copy(
            direct_ref.at[pl.ds(own_rows, passed_rows), :], passed_hbm, left.at[1]
        ),
    ]
    for store in stores:
        store.start()
    gains_in.wait()
    gain_re = gains_ref[0]
    gain_im = gains_ref[1]
    parts = []
    for frame in range(frames_here + EARLY):
        direct = direct_ref[frame * inputs_here : (frame + 1) * inputs_here, :]
        direct_re = direct[:, :CH]
        direct_im = direct[:, CH:]
        parts.append(
            (
                gain_re * direct_re - gain_im * direct_im,
                gain_re * direct_im + gain_im * direct_re,
            )
        )
    slots = [
        [(part, frame) for frame in range(first, first + 8)]
        for first in range(0, frames_here, 8)
        for part in range(2)
    ]
    slots.append([(part, frames_here + frame) for part in range(2) for frame in range(EARLY)])
    per_far = CH // far
    for place, slot in enumerate(slots):
        columns = slice(place * LANES, (place + 1) * LANES)
        for half in range(CH // LANES):
            lanes = slice(half * LANES, (half + 1) * LANES)
            blocks = turn_granules([parts[frame][part][:, lanes] for part, frame in slot], per_far)
            for index in range(0, len(blocks), 2):
                row = place_in_column(half * len(blocks) + index, far) * inputs_here
                parcels_ref[row : row + 2 * inputs_here, columns] = jnp.concatenate(
                    blocks[index : index + 2], axis=0
                ).astype(jnp.bfloat16)
        lanes = pl.ds(place * LANES, LANES)
        stores.append(
            pltpu.make_async_copy(
                parcels_ref.at[:, lanes], parcels_hbm.at[:, lanes], left.at[len(stores)]
            )
        )
        stores[-1].start()
    for store in stores:
        store.wait()


def spectra_kernel(passed_ref, own_ref, gains_ref, spectra_ref, rows_ref):
    inputs_here = gains_ref.shape[1]
    frames_here = own_ref.shape[0] // inputs_here
    slabs = CH // LANES
    gain_re = gains_ref[0]
    gain_im = gains_ref[1]
    for frame in range(frames_here):
        block = slice(frame * inputs_here, (frame + 1) * inputs_here)
        direct = own_ref[block, :]
        if frame < TAPS - 1:
            direct = direct + passed_ref[block, :]
        direct_re = direct[:, :CH]
        direct_im = direct[:, CH:]
        rows = pl.ds(frame, inputs_here, stride=frames_here)
        real_part = gain_re * direct_re - gain_im * direct_im
        imag_part = gain_re * direct_im + gain_im * direct_re
        for slab in range(slabs):
            columns = slice(slab * LANES, (slab + 1) * LANES)
            rows_ref[slab, rows, :] = real_part[:, columns]
            rows_ref[slabs + slab, rows, :] = imag_part[:, columns]
    for part in range(2):
        for slab in range(slabs):
            columns = slice(slab * LANES, (slab + 1) * LANES)
            spectra_ref[part, :, columns] = rows_ref[part * slabs + slab].astype(jnp.bfloat16)


def channel_of(time):
    return time % 4


def place_in_plane(near, time, times):
    return (near + NEAR // 2) % NEAR * times + (time + times // 2) % times


def spread_kernel(mine_ref, parcels_ref, turned_ref):
    count, rows, width = parcels_ref.shape
    times = count // NEAR
    stride = mine_ref.shape[1] // rows
    for place in range(0, mine_ref.shape[1], LANES):
        values = mine_ref[:, place : place + LANES].astype(jnp.float32)
        turned_ref[place : place + LANES, :] = values.T
    for near in range(NEAR):
        for channel in range(stride // NEAR):
            start = near * (stride // NEAR) + channel
            values = turned_ref[pl.ds(start, rows, stride=stride), :].astype(jnp.bfloat16)
            for time in range(times):
                if channel_of(time) == channel:
                    parcels_ref[place_in_plane(near, time, times)] = values


def correlate_kernel(frames_all, inputs_here, place_ref, every_ref, packed_ref):
    count, lines, width = every_ref.shape
    blocks, rows, inputs_all = packed_ref.shape
    times = count // NEAR
    main = lines - 2 * EARLY
    carry = None
    lined = []
    for time in range(times):
        pieces = [every_ref[place_in_plane(near, time, times)] for near in range(NEAR)]
        wide = jnp.concatenate([piece.astype(jnp.float32) for piece in pieces], axis=1)
        tiles = [wide[start : start + 8] for start in range(0, lines, 8)]
        if carry is not None:
            early = lax.broadcasted_iota(jnp.int32, carry.shape, 0) < EARLY
            tiles[0] = tiles[0] + jnp.where(early, carry, 0.0)
            tiles[1] = tiles[1] + jnp.where(early, pltpu.roll(carry, 8 - EARLY, 0), 0.0)
        carry = tiles[-1]
        lined += tiles[:-1]
    far = width // inputs_here
    target = lax.broadcasted_iota(jnp.int32, (1, inputs_all), 1)
    near = target // inputs_here % NEAR
    listed = place_in_column(target // (inputs_here * NEAR), far)
    source = near * width + listed * inputs_here + target % inputs_here
    chosen = lax.broadcasted_iota(jnp.int32, (inputs_all, inputs_all), 0) == source
    ordered = jnp.dot(
        jnp.concatenate(lined, axis=0).astype(jnp.bfloat16),
        chosen.astype(jnp.float32).astype(jnp.bfloat16),
        preferred_element_type=jnp.float32,
    )
    right = ordered.astype(jnp.bfloat16)
    twisted = []
    for start in range(0, times * main, 16):
        twisted.append(ordered[start + 8 : start + 16])
        twisted.append(-ordered[start : start + 8])
    twisted = jnp.concatenate(twisted, axis=0).astype(jnp.bfloat16)
    held = blocks * rows
    first = place_ref[0] * held
    col_index = lax.broadcasted_iota(jnp.int32, (held, inputs_all), 1)
    row_index = lax.broadcasted_iota(jnp.int32, (held, inputs_all), 0) + first
    both = []
    for left in (right, twisted):
        both.append(
            lax.dot_general(
                jnp.where(first == 0, left[:, :held], left[:, held:]),
                right,
                (((0,), (0,)), ((), ())),
                preferred_element_type=jnp.float32,
            )
        )
    values = jnp.where(row_index <= col_index, both[0], both[1]) * (1.0 / frames_all)
    values = values.astype(jnp.bfloat16)
    for block in range(blocks):
        packed_ref[block] = values[block * rows : (block + 1) * rows]


def unpack_kernel(packed_ref, lines_hbm, lines_ref, left):
    channels, count, width = packed_ref.shape
    tiles = width // LANES
    stores = []
    for first in range(0, count, 16):
        start = first * tiles * channels
        for channel in range(channels):
            values = packed_ref[channel, first : first + 16, :].astype(jnp.float32)
            for tile in range(tiles):
                lines = pl.ds(start + tile * channels + channel, 16, stride=tiles * channels)
                lines_ref[lines, :] = values[:, tile * LANES : (tile + 1) * LANES]
        block = pl.ds(start, 16 * tiles * channels)
        stores.append(
            pltpu.make_async_copy(lines_ref.at[block, :], lines_hbm.at[block, :], left.at[len(stores)])
        )
        stores[-1].start()
    for store in stores:
        store.wait()


def body(samples, gains):
    inputs_here = samples.shape[0]
    frames_here = samples.shape[1] // NFFT
    times = lax.axis_size("tm")
    far = lax.axis_size("far")
    groups = far * NEAR
    per_group = CH // groups
    inputs_all = inputs_here * groups
    frames_all = frames_here * times
    block = inputs_here * frames_here

    window = filter_window()
    twiddle = jnp.asarray(build_table(window)[: NFFT // 2])
    window_taps = jnp.asarray(window.astype(np.float32).reshape(TAPS, NFFT))

    sent = frames_here + EARLY
    gains = gains.transpose(0, 2, 1)

    def own_part(*refs):
        own_part_kernel(far, *refs)

    own, passed, parcels = pl.pallas_call(
        own_part,
        out_shape=(
            jax.ShapeDtypeStruct((block, 2 * CH), jnp.float32),
            jax.ShapeDtypeStruct(((TAPS - 1) * inputs_here, 2 * CH), jnp.float32),
            jax.ShapeDtypeStruct((far * inputs_here, sent * 2 * CH // far), jnp.bfloat16),
        ),
        in_specs=[ANY] * 4,
        out_specs=(ANY, ANY, ANY),
        scratch_shapes=[
            pltpu.VMEM(samples.shape, jnp.bfloat16),
            pltpu.VMEM(window_taps.shape, jnp.float32),
            pltpu.VMEM(twiddle.shape, jnp.bfloat16),
            pltpu.VMEM(gains.shape, jnp.float32),
            pltpu.VMEM((sent * inputs_here, 2 * CH), jnp.float32),
            pltpu.VMEM((far * inputs_here, sent * 2 * CH // far), jnp.bfloat16),
            pltpu.SemaphoreType.DMA((3 + NFFT // (2 * STEP),)),
            pltpu.SemaphoreType.DMA((2 + sent // 4,)),
        ],
        compiler_params=pltpu.CompilerParams(vmem_limit_bytes=OWN_PART_VMEM),
        cost_estimate=pl.CostEstimate(
            flops=2 * sent * inputs_here * NFFT * 2 * CH,
            bytes_accessed=3 * 1024 * 1024,
            transcendentals=0,
        ),
        name="own_part",
    )(samples, window_taps, twiddle, gains)

    parcels = parcels.reshape(far, inputs_here, sent * 2 * CH // far)
    column = [sorted(range(far), key=lambda place: place_in_column(place, far))]
    mine = lax.all_to_all(parcels, "far", 0, 0, axis_index_groups=column)
    mine = mine.reshape(far * inputs_here, sent * 2 * CH // far)

    passed = lax.ppermute(passed, "tm", [(source, source + 1) for source in range(times - 1)])
    spectra = pl.pallas_call(
        spectra_kernel,
        out_shape=jax.ShapeDtypeStruct((2, block, CH), jnp.bfloat16),
        in_specs=[VMEM] * 3,
        out_specs=VMEM,
        scratch_shapes=[pltpu.VMEM((2 * CH // LANES, block, LANES), jnp.float32)],
        compiler_params=PARAMS,
        cost_estimate=pl.CostEstimate(
            flops=8 * block * 2 * CH, bytes_accessed=1024 * 1024, transcendentals=0
        ),
        name="spectra",
    )(passed, own, gains)
    mine, spectra = lax.optimization_barrier((mine, spectra))
    spectra = spectra.reshape(2, inputs_here, frames_here, CH).transpose(0, 3, 1, 2)

    lines = 2 * sent
    spread = pl.pallas_call(
        spread_kernel,
        out_shape=jax.ShapeDtypeStruct((NEAR * times, lines, far * inputs_here), jnp.bfloat16),
        in_specs=[VMEM],
        out_specs=VMEM,
        scratch_shapes=[pltpu.VMEM((sent * 2 * CH // far, far * inputs_here), jnp.float32)],
        compiler_params=PARAMS,
        name="spread",
    )(mine)
    place = lax.axis_index("tm").astype(jnp.int32)
    square = (place // 4)[None]
    spread, square = lax.optimization_barrier((spread, square))
    members = [(near, time) for near in range(NEAR) for time in range(times)]
    members.sort(key=lambda member: place_in_plane(*member, times))
    plane = [[near * times + time for near, time in members]]
    every = lax.all_to_all(spread, ("near", "tm"), 0, 0, axis_index_groups=plane)

    def correlate(*refs):
        correlate_kernel(frames_all, inputs_here, *refs)

    rows = inputs_all // times
    packed = pl.pallas_call(
        correlate,
        out_shape=jax.ShapeDtypeStruct((per_group, rows, inputs_all), jnp.bfloat16),
        in_specs=[SMEM, VMEM],
        out_specs=VMEM,
        compiler_params=PARAMS,
        name="correlate",
    )(square, every)
    squares = [[0, 1, 2, 3], [4, 5, 6, 7]]
    packed = lax.all_to_all(packed, "tm", 0, 0, axis_index_groups=squares)
    tiles = inputs_all // LANES
    visibilities = pl.pallas_call(
        unpack_kernel,
        out_shape=jax.ShapeDtypeStruct((rows * tiles * per_group, LANES), jnp.float32),
        in_specs=[VMEM],
        out_specs=ANY,
        scratch_shapes=[
            pltpu.VMEM((rows * tiles * per_group, LANES), jnp.float32),
            pltpu.SemaphoreType.DMA((rows // 16,)),
        ],
        compiler_params=PARAMS,
        name="unpack",
    )(packed)
    visibilities = visibilities.reshape(rows, tiles, per_group, LANES).transpose(0, 2, 1, 3)
    visibilities = visibilities.reshape(rows, per_group, inputs_all)
    return (spectra, visibilities)


def solution(mesh):
    groups, times = mesh.devices.shape
    split = Mesh(mesh.devices.reshape(groups // NEAR, NEAR, times), ("far", "near", "tm"))
    inputs = ("far", "near")
    return jax.shard_map(
        body,
        mesh=split,
        in_specs=(P(inputs, "tm"), P(None, None, inputs)),
        out_specs=(P(None, None, inputs, "tm"), P("tm", inputs, None)),
        check_vma=False,
    )
```

```python
import math

import jax
import jax.numpy as jnp
import numpy as np
from jax import lax
from jax.experimental import pallas as pl
from jax.experimental.pallas import tpu as pltpu
from jax.sharding import Mesh, PartitionSpec as P

NFFT = 2048
CH = 256
FIRST = 384
TAPS = 4
NEAR = 4
EARLY = 4
STEP = 256
LANES = 128
VMEM = pl.BlockSpec(memory_space=pltpu.VMEM)
ANY = pl.BlockSpec(memory_space=pl.ANY)
SMEM = pl.BlockSpec(memory_space=pltpu.SMEM)
OWN_PART_VMEM = 59 * 1024 * 1024 + 768 * 1024
PARAMS = pltpu.CompilerParams(vmem_limit_bytes=32 * 1024 * 1024)


def filter_window():
    length = TAPS * NFFT
    position = np.arange(length, dtype=np.float64)
    centred = (position - 0.5 * length + 0.5) / NFFT
    hann_taper = 0.5 - 0.5 * np.cos(2.0 * math.pi * (position + 0.5) / length)
    return np.sinc(centred) * hann_taper


def build_table(window):
    norm_scale = 1.0 / np.sqrt(np.sum(window * window))
    sample = np.arange(NFFT)[:, None]
    channel = FIRST + np.arange(CH)[None, :]
    phase_angle = 2.0 * math.pi / NFFT * (sample * channel % NFFT)
    cosine = np.cos(phase_angle) * norm_scale
    sine = -np.sin(phase_angle) * norm_scale
    return np.concatenate([cosine, sine], axis=1).astype(jnp.bfloat16)


def tapped_block(samples_ref, window_ref, frames_sent, block):
    inputs_here, count = samples_ref.shape
    frames_here = count // NFFT
    low = block * STEP
    sums = []
    for frame in range(frames_sent):
        total = jnp.zeros((inputs_here, STEP), jnp.float32)
        for tap in range(TAPS):
            source = frame - TAPS + 1 + tap
            if 0 <= source < frames_here:
                start = source * NFFT + low
                values = samples_ref[:, start : start + STEP]
                weights = window_ref[tap : tap + 1, low : low + STEP]
                total = total + weights * values.astype(jnp.float32)
        sums.append(total)
    pairs = [
        jnp.concatenate(sums[frame : frame + 2], axis=0).astype(jnp.bfloat16)
        for frame in range(0, frames_sent, 2)
    ]
    return jnp.concatenate(pairs, axis=0)


def turn_granules(blocks, size):
    count = len(blocks)
    lanes = count * size
    granule = lax.broadcasted_iota(jnp.int32, blocks[0].shape, 1) // size
    blocks = list(blocks)
    distance = count // 2
    while distance:
        upper = (granule & distance) != 0
        shift = distance * size
        for index in range(count):
            if index & distance:
                continue
            low, high = blocks[index], blocks[index + distance]
            blocks[index] = jnp.where(upper, pltpu.roll(high, shift, 1), low)
            blocks[index + distance] = jnp.where(upper, high, pltpu.roll(low, lanes - shift, 1))
        distance //= 2
    return blocks


def place_in_column(place, far):
    return (place + far * 3 // 8) % far


def own_part_kernel(
    far,
    samples_hbm,
    window_hbm,
    twiddle_hbm,
    gains_hbm,
    own_hbm,
    passed_hbm,
    parcels_hbm,
    samples_ref,
    window_ref,
    twiddle_ref,
    gains_ref,
    direct_ref,
    parcels_ref,
    arrived,
    left,
):
    inputs_here = gains_ref.shape[1]
    frames_here = samples_hbm.shape[1] // NFFT
    blocks = range(NFFT // STEP)
    fetches = []

    def fetch(source, target):
        fetches.append(pltpu.make_async_copy(source, target, arrived.at[len(fetches)]))
        fetches[-1].start()
        return fetches[-1]

    samples_in = fetch(samples_hbm, samples_ref)
    window_in = fetch(window_hbm, window_ref)
    table_in = []
    for block in blocks[: len(blocks) // 2]:
        rows = pl.ds(block * STEP, STEP)
        table_in.append(fetch(twiddle_hbm.at[rows, :], twiddle_ref.at[rows, :]))
    gains_in = fetch(gains_hbm, gains_ref)
    samples_in.wait()
    window_in.wait()
    total = None
    sent = frames_here + EARLY
    for block, table in enumerate(table_in):
        tapped = [
            tapped_block(samples_ref, window_ref, sent, half + block)
            for half in (0, len(table_in))
        ]
        table.wait()
        product = jnp.dot(
            jnp.concatenate(tapped, axis=0),
            twiddle_ref[block * STEP : (block + 1) * STEP, :],
            preferred_element_type=jnp.float32,
        )
        total = product if total is None else total + product
    channel = FIRST + lax.broadcasted_iota(jnp.int32, (1, 2 * CH), 1)
    sign = (1 - 2 * (channel % 2)).astype(jnp.float32)
    direct_ref[...] = total[: sent * inputs_here] + sign * total[sent * inputs_here :]
    own_rows = own_hbm.shape[0]
    passed_rows = passed_hbm.shape[0]
    stores = [
        pltpu.make_async_copy(direct_ref.at[pl.ds(0, own_rows), :], own_hbm, left.at[0]),
        pltpu.make_async_copy(
            direct_ref.at[pl.ds(own_rows, passed_rows), :], passed_hbm, left.at[1]
        ),
    ]
    for store in stores:
        store.start()
    gains_in.wait()
    gain_re = gains_ref[0]
    gain_im = gains_ref[1]
    parts = []
    for frame in range(frames_here + EARLY):
        direct = direct_ref[frame * inputs_here : (frame + 1) * inputs_here, :]
        direct_re = direct[:, :CH]
        direct_im = direct[:, CH:]
        parts.append(
            (
                gain_re * direct_re - gain_im * direct_im,
                gain_re * direct_im + gain_im * direct_re,
            )
        )
    slots = [
        [(part, frame) for frame in range(first, first + 8)]
        for first in range(0, frames_here, 8)
        for part in range(2)
    ]
    slots.append([(part, frames_here + frame) for part in range(2) for frame in range(EARLY)])
    per_far = CH // far
    for place, slot in enumerate(slots):
        columns = slice(place * LANES, (place + 1) * LANES)
        for half in range(CH // LANES):
            lanes = slice(half * LANES, (half + 1) * LANES)
            blocks = turn_granules([parts[frame][part][:, lanes] for part, frame in slot], per_far)
            for index in range(0, len(blocks), 2):
                row = place_in_column(half * len(blocks) + index, far) * inputs_here
                parcels_ref[row : row + 2 * inputs_here, columns] = jnp.concatenate(
                    blocks[index : index + 2], axis=0
                ).astype(jnp.bfloat16)
        lanes = pl.ds(place * LANES, LANES)
        stores.append(
            pltpu.make_async_copy(
                parcels_ref.at[:, lanes], parcels_hbm.at[:, lanes], left.at[len(stores)]
            )
        )
        stores[-1].start()
    for store in stores:
        store.wait()


def spectra_kernel(passed_ref, own_ref, gains_ref, spectra_ref, rows_ref):
    inputs_here = gains_ref.shape[1]
    frames_here = own_ref.shape[0] // inputs_here
    slabs = CH // LANES
    gain_re = gains_ref[0]
    gain_im = gains_ref[1]
    for frame in range(frames_here):
        block = slice(frame * inputs_here, (frame + 1) * inputs_here)
        direct = own_ref[block, :]
        if frame < TAPS - 1:
            direct = direct + passed_ref[block, :]
        direct_re = direct[:, :CH]
        direct_im = direct[:, CH:]
        rows = pl.ds(frame, inputs_here, stride=frames_here)
        real_part = gain_re * direct_re - gain_im * direct_im
        imag_part = gain_re * direct_im + gain_im * direct_re
        for slab in range(slabs):
            columns = slice(slab * LANES, (slab + 1) * LANES)
            rows_ref[slab, rows, :] = real_part[:, columns]
            rows_ref[slabs + slab, rows, :] = imag_part[:, columns]
    for part in range(2):
        for slab in range(slabs):
            columns = slice(slab * LANES, (slab + 1) * LANES)
            spectra_ref[part, :, columns] = rows_ref[part * slabs + slab].astype(jnp.bfloat16)


def channel_of(time):
    return time % 4


def place_in_plane(near, time, times):
    return (near + NEAR // 2) % NEAR * times + (time + times // 2) % times


def spread_kernel(mine_ref, parcels_ref, turned_ref):
    count, rows, width = parcels_ref.shape
    times = count // NEAR
    stride = mine_ref.shape[1] // rows
    for place in range(0, mine_ref.shape[1], LANES):
        values = mine_ref[:, place : place + LANES].astype(jnp.float32)
        turned_ref[place : place + LANES, :] = values.T
    for near in range(NEAR):
        for channel in range(stride // NEAR):
            start = near * (stride // NEAR) + channel
            values = turned_ref[pl.ds(start, rows, stride=stride), :].astype(jnp.bfloat16)
            for time in range(times):
                if channel_of(time) == channel:
                    parcels_ref[place_in_plane(near, time, times)] = values


def correlate_kernel(frames_all, inputs_here, place_ref, every_ref, packed_ref):
    count, lines, width = every_ref.shape
    blocks, rows, inputs_all = packed_ref.shape
    times = count // NEAR
    main = lines - 2 * EARLY
    carry = None
    lined = []
    for time in range(times):
        pieces = [every_ref[place_in_plane(near, time, times)] for near in range(NEAR)]
        wide = jnp.concatenate([piece.astype(jnp.float32) for piece in pieces], axis=1)
        tiles = [wide[start : start + 8] for start in range(0, lines, 8)]
        if carry is not None:
            early = lax.broadcasted_iota(jnp.int32, carry.shape, 0) < EARLY
            tiles[0] = tiles[0] + jnp.where(early, carry, 0.0)
            tiles[1] = tiles[1] + jnp.where(early, pltpu.roll(carry, 8 - EARLY, 0), 0.0)
        carry = tiles[-1]
        lined += tiles[:-1]
    far = width // inputs_here
    target = lax.broadcasted_iota(jnp.int32, (1, inputs_all), 1)
    near = target // inputs_here % NEAR
    listed = place_in_column(target // (inputs_here * NEAR), far)
    source = near * width + listed * inputs_here + target % inputs_here
    chosen = lax.broadcasted_iota(jnp.int32, (inputs_all, inputs_all), 0) == source
    ordered = jnp.dot(
        jnp.concatenate(lined, axis=0).astype(jnp.bfloat16),
        chosen.astype(jnp.float32).astype(jnp.bfloat16),
        preferred_element_type=jnp.float32,
    )
    right = ordered.astype(jnp.bfloat16)
    twisted = []
    for start in range(0, times * main, 16):
        twisted.append(ordered[start + 8 : start + 16])
        twisted.append(-ordered[start : start + 8])
    twisted = jnp.concatenate(twisted, axis=0).astype(jnp.bfloat16)
    held = blocks * rows
    first = place_ref[0] * held
    col_index = lax.broadcasted_iota(jnp.int32, (held, inputs_all), 1)
    row_index = lax.broadcasted_iota(jnp.int32, (held, inputs_all), 0) + first
    left = [jnp.where(first == 0, side[:, :held], side[:, held:]) for side in (right, twisted)]
    both = lax.dot_general(
        jnp.concatenate(left, axis=1),
        right,
        (((0,), (0,)), ((), ())),
        preferred_element_type=jnp.float32,
    )
    values = jnp.where(row_index <= col_index, both[:held], both[held:]) * (1.0 / frames_all)
    values = values.astype(jnp.bfloat16)
    for block in range(blocks):
        packed_ref[block] = values[block * rows : (block + 1) * rows]


def unpack_kernel(packed_ref, lines_hbm, lines_ref, left):
    channels, count, width = packed_ref.shape
    tiles = width // LANES
    stores = []
    for first in range(0, count, 16):
        start = first * tiles * channels
        for channel in range(channels):
            values = packed_ref[channel, first : first + 16, :].astype(jnp.float32)
            for tile in range(tiles):
                lines = pl.ds(start + tile * channels + channel, 16, stride=tiles * channels)
                lines_ref[lines, :] = values[:, tile * LANES : (tile + 1) * LANES]
        block = pl.ds(start, 16 * tiles * channels)
        stores.append(
            pltpu.make_async_copy(lines_ref.at[block, :], lines_hbm.at[block, :], left.at[len(stores)])
        )
        stores[-1].start()
    for store in stores:
        store.wait()


def body(samples, gains):
    inputs_here = samples.shape[0]
    frames_here = samples.shape[1] // NFFT
    times = lax.axis_size("tm")
    far = lax.axis_size("far")
    groups = far * NEAR
    per_group = CH // groups
    inputs_all = inputs_here * groups
    frames_all = frames_here * times
    block = inputs_here * frames_here

    window = filter_window()
    twiddle = jnp.asarray(build_table(window)[: NFFT // 2])
    window_taps = jnp.asarray(window.astype(np.float32).reshape(TAPS, NFFT))

    sent = frames_here + EARLY
    gains = gains.transpose(0, 2, 1)

    def own_part(*refs):
        own_part_kernel(far, *refs)

    own, passed, parcels = pl.pallas_call(
        own_part,
        out_shape=(
            jax.ShapeDtypeStruct((block, 2 * CH), jnp.float32),
            jax.ShapeDtypeStruct(((TAPS - 1) * inputs_here, 2 * CH), jnp.float32),
            jax.ShapeDtypeStruct((far * inputs_here, sent * 2 * CH // far), jnp.bfloat16),
        ),
        in_specs=[ANY] * 4,
        out_specs=(ANY, ANY, ANY),
        scratch_shapes=[
            pltpu.VMEM(samples.shape, jnp.bfloat16),
            pltpu.VMEM(window_taps.shape, jnp.float32),
            pltpu.VMEM(twiddle.shape, jnp.bfloat16),
            pltpu.VMEM(gains.shape, jnp.float32),
            pltpu.VMEM((sent * inputs_here, 2 * CH), jnp.float32),
            pltpu.VMEM((far * inputs_here, sent * 2 * CH // far), jnp.bfloat16),
            pltpu.SemaphoreType.DMA((3 + NFFT // (2 * STEP),)),
            pltpu.SemaphoreType.DMA((2 + sent // 4,)),
        ],
        compiler_params=pltpu.CompilerParams(vmem_limit_bytes=OWN_PART_VMEM),
        cost_estimate=pl.CostEstimate(
            flops=2 * sent * inputs_here * NFFT * 2 * CH,
            bytes_accessed=3 * 1024 * 1024,
            transcendentals=0,
        ),
        name="own_part",
    )(samples, window_taps, twiddle, gains)

    parcels = parcels.reshape(far, inputs_here, sent * 2 * CH // far)
    column = [sorted(range(far), key=lambda place: place_in_column(place, far))]
    mine = lax.all_to_all(parcels, "far", 0, 0, axis_index_groups=column)
    mine = mine.reshape(far * inputs_here, sent * 2 * CH // far)

    passed = lax.ppermute(passed, "tm", [(source, source + 1) for source in range(times - 1)])
    spectra = pl.pallas_call(
        spectra_kernel,
        out_shape=jax.ShapeDtypeStruct((2, block, CH), jnp.bfloat16),
        in_specs=[VMEM] * 3,
        out_specs=VMEM,
        scratch_shapes=[pltpu.VMEM((2 * CH // LANES, block, LANES), jnp.float32)],
        compiler_params=PARAMS,
        cost_estimate=pl.CostEstimate(
            flops=8 * block * 2 * CH, bytes_accessed=1024 * 1024, transcendentals=0
        ),
        name="spectra",
    )(passed, own, gains)
    mine, spectra = lax.optimization_barrier((mine, spectra))
    spectra = spectra.reshape(2, inputs_here, frames_here, CH).transpose(0, 3, 1, 2)

    lines = 2 * sent
    spread = pl.pallas_call(
        spread_kernel,
        out_shape=jax.ShapeDtypeStruct((NEAR * times, lines, far * inputs_here), jnp.bfloat16),
        in_specs=[VMEM],
        out_specs=VMEM,
        scratch_shapes=[pltpu.VMEM((sent * 2 * CH // far, far * inputs_here), jnp.float32)],
        compiler_params=PARAMS,
        name="spread",
    )(mine)
    place = lax.axis_index("tm").astype(jnp.int32)
    square = (place // 4)[None]
    spread, square = lax.optimization_barrier((spread, square))
    members = [(near, time) for near in range(NEAR) for time in range(times)]
    members.sort(key=lambda member: place_in_plane(*member, times))
    plane = [[near * times + time for near, time in members]]
    every = lax.all_to_all(spread, ("near", "tm"), 0, 0, axis_index_groups=plane)

    def correlate(*refs):
        correlate_kernel(frames_all, inputs_here, *refs)

    rows = inputs_all // times
    packed = pl.pallas_call(
        correlate,
        out_shape=jax.ShapeDtypeStruct((per_group, rows, inputs_all), jnp.bfloat16),
        in_specs=[SMEM, VMEM],
        out_specs=VMEM,
        compiler_params=PARAMS,
        name="correlate",
    )(square, every)
    squares = [[0, 1, 2, 3], [4, 5, 6, 7]]
    packed = lax.all_to_all(packed, "tm", 0, 0, axis_index_groups=squares)
    tiles = inputs_all // LANES
    visibilities = pl.pallas_call(
        unpack_kernel,
        out_shape=jax.ShapeDtypeStruct((rows * tiles * per_group, LANES), jnp.float32),
        in_specs=[VMEM],
        out_specs=ANY,
        scratch_shapes=[
            pltpu.VMEM((rows * tiles * per_group, LANES), jnp.float32),
            pltpu.SemaphoreType.DMA((rows // 16,)),
        ],
        compiler_params=PARAMS,
        name="unpack",
    )(packed)
    visibilities = visibilities.reshape(rows, tiles, per_group, LANES).transpose(0, 2, 1, 3)
    visibilities = visibilities.reshape(rows, per_group, inputs_all)
    return (spectra, visibilities)


def solution(mesh):
    groups, times = mesh.devices.shape
    split = Mesh(mesh.devices.reshape(groups // NEAR, NEAR, times), ("far", "near", "tm"))
    inputs = ("far", "near")
    return jax.shard_map(
        body,
        mesh=split,
        in_specs=(P(inputs, "tm"), P(None, None, inputs)),
        out_specs=(P(None, None, inputs, "tm"), P("tm", inputs, None)),
        check_vma=False,
    )
```

```python
import math

import jax
import jax.numpy as jnp
import numpy as np
from jax import lax
from jax.experimental import pallas as pl
from jax.experimental.pallas import tpu as pltpu
from jax.sharding import Mesh, PartitionSpec as P

NFFT = 2048
CH = 256
FIRST = 384
TAPS = 4
NEAR = 4
EARLY = 4
STEP = 256
LANES = 128
VMEM = pl.BlockSpec(memory_space=pltpu.VMEM)
ANY = pl.BlockSpec(memory_space=pl.ANY)
SMEM = pl.BlockSpec(memory_space=pltpu.SMEM)
OWN_PART_VMEM = 59 * 1024 * 1024 + 768 * 1024
PARAMS = pltpu.CompilerParams(vmem_limit_bytes=32 * 1024 * 1024)


def filter_window():
    length = TAPS * NFFT
    position = np.arange(length, dtype=np.float64)
    centred = (position - 0.5 * length + 0.5) / NFFT
    hann_taper = 0.5 - 0.5 * np.cos(2.0 * math.pi * (position + 0.5) / length)
    return np.sinc(centred) * hann_taper


def build_table(window):
    norm_scale = 1.0 / np.sqrt(np.sum(window * window))
    sample = np.arange(NFFT)[:, None]
    channel = FIRST + np.arange(CH)[None, :]
    phase_angle = 2.0 * math.pi / NFFT * (sample * channel % NFFT)
    cosine = np.cos(phase_angle) * norm_scale
    sine = -np.sin(phase_angle) * norm_scale
    return np.concatenate([cosine, sine], axis=1).astype(jnp.bfloat16)


def tapped_block(samples_ref, window_ref, frames_sent, block):
    inputs_here, count = samples_ref.shape
    frames_here = count // NFFT
    low = block * STEP
    sums = []
    for frame in range(frames_sent):
        total = jnp.zeros((inputs_here, STEP), jnp.float32)
        for tap in range(TAPS):
            source = frame - TAPS + 1 + tap
            if 0 <= source < frames_here:
                start = source * NFFT + low
                values = samples_ref[:, start : start + STEP]
                weights = window_ref[tap : tap + 1, low : low + STEP]
                total = total + weights * values.astype(jnp.float32)
        sums.append(total)
    pairs = [
        jnp.concatenate(sums[frame : frame + 2], axis=0).astype(jnp.bfloat16)
        for frame in range(0, frames_sent, 2)
    ]
    return jnp.concatenate(pairs, axis=0)


def turn_granules(blocks, size):
    count = len(blocks)
    lanes = count * size
    granule = lax.broadcasted_iota(jnp.int32, blocks[0].shape, 1) // size
    blocks = list(blocks)
    distance = count // 2
    while distance:
        upper = (granule & distance) != 0
        shift = distance * size
        for index in range(count):
            if index & distance:
                continue
            low, high = blocks[index], blocks[index + distance]
            blocks[index] = jnp.where(upper, pltpu.roll(high, shift, 1), low)
            blocks[index + distance] = jnp.where(upper, high, pltpu.roll(low, lanes - shift, 1))
        distance //= 2
    return blocks


def place_in_column(place, far):
    return (far * 5 // 8 + far - place) % far


def own_part_kernel(
    far,
    samples_hbm,
    window_hbm,
    twiddle_hbm,
    gains_hbm,
    own_hbm,
    passed_hbm,
    parcels_hbm,
    samples_ref,
    window_ref,
    twiddle_ref,
    gains_ref,
    direct_ref,
    parcels_ref,
    arrived,
    left,
):
    inputs_here = gains_ref.shape[1]
    frames_here = samples_hbm.shape[1] // NFFT
    blocks = range(NFFT // STEP)
    fetches = []

    def fetch(source, target):
        fetches.append(pltpu.make_async_copy(source, target, arrived.at[len(fetches)]))
        fetches[-1].start()
        return fetches[-1]

    samples_in = fetch(samples_hbm, samples_ref)
    window_in = fetch(window_hbm, window_ref)
    table_in = []
    for block in blocks[: len(blocks) // 2]:
        rows = pl.ds(block * STEP, STEP)
        table_in.append(fetch(twiddle_hbm.at[rows, :], twiddle_ref.at[rows, :]))
    gains_in = fetch(gains_hbm, gains_ref)
    samples_in.wait()
    window_in.wait()
    total = None
    sent = frames_here + EARLY
    for block, table in enumerate(table_in):
        tapped = [
            tapped_block(samples_ref, window_ref, sent, half + block)
            for half in (0, len(table_in))
        ]
        table.wait()
        product = jnp.dot(
            jnp.concatenate(tapped, axis=0),
            twiddle_ref[block * STEP : (block + 1) * STEP, :],
            preferred_element_type=jnp.float32,
        )
        total = product if total is None else total + product
    channel = FIRST + lax.broadcasted_iota(jnp.int32, (1, 2 * CH), 1)
    sign = (1 - 2 * (channel % 2)).astype(jnp.float32)
    direct_ref[...] = total[: sent * inputs_here] + sign * total[sent * inputs_here :]
    own_rows = own_hbm.shape[0]
    passed_rows = passed_hbm.shape[0]
    stores = [
        pltpu.make_async_copy(direct_ref.at[pl.ds(0, own_rows), :], own_hbm, left.at[0]),
        pltpu.make_async_copy(
            direct_ref.at[pl.ds(own_rows, passed_rows), :], passed_hbm, left.at[1]
        ),
    ]
    for store in stores:
        store.start()
    gains_in.wait()
    gain_re = gains_ref[0]
    gain_im = gains_ref[1]
    parts = []
    for frame in range(frames_here + EARLY):
        direct = direct_ref[frame * inputs_here : (frame + 1) * inputs_here, :]
        direct_re = direct[:, :CH]
        direct_im = direct[:, CH:]
        parts.append(
            (
                gain_re * direct_re - gain_im * direct_im,
                gain_re * direct_im + gain_im * direct_re,
            )
        )
    slots = [
        [(part, frame) for frame in range(first, first + 8)]
        for first in range(0, frames_here, 8)
        for part in range(2)
    ]
    slots.append([(part, frames_here + frame) for part in range(2) for frame in range(EARLY)])
    per_far = CH // far
    for place, slot in enumerate(slots):
        columns = slice(place * LANES, (place + 1) * LANES)
        blocks = []
        for half in range(CH // LANES):
            lanes = slice(half * LANES, (half + 1) * LANES)
            blocks += turn_granules([parts[frame][part][:, lanes] for part, frame in slot], per_far)
        listed = sorted(range(far), key=lambda target: place_in_column(target, far))
        for index in range(0, far, 2):
            rows = slice(index * inputs_here, (index + 2) * inputs_here)
            parcels_ref[rows, columns] = jnp.concatenate(
                [blocks[target] for target in listed[index : index + 2]], axis=0
            ).astype(jnp.bfloat16)
        lanes = pl.ds(place * LANES, LANES)
        stores.append(
            pltpu.make_async_copy(
                parcels_ref.at[:, lanes], parcels_hbm.at[:, lanes], left.at[len(stores)]
            )
        )
        stores[-1].start()
    for store in stores:
        store.wait()


def spectra_kernel(passed_ref, own_ref, gains_ref, spectra_ref, rows_ref):
    inputs_here = gains_ref.shape[1]
    frames_here = own_ref.shape[0] // inputs_here
    slabs = CH // LANES
    gain_re = gains_ref[0]
    gain_im = gains_ref[1]
    for frame in range(frames_here):
        block = slice(frame * inputs_here, (frame + 1) * inputs_here)
        direct = own_ref[block, :]
        if frame < TAPS - 1:
            direct = direct + passed_ref[block, :]
        direct_re = direct[:, :CH]
        direct_im = direct[:, CH:]
        rows = pl.ds(frame, inputs_here, stride=frames_here)
        real_part = gain_re * direct_re - gain_im * direct_im
        imag_part = gain_re * direct_im + gain_im * direct_re
        for slab in range(slabs):
            columns = slice(slab * LANES, (slab + 1) * LANES)
            rows_ref[slab, rows, :] = real_part[:, columns]
            rows_ref[slabs + slab, rows, :] = imag_part[:, columns]
    for part in range(2):
        for slab in range(slabs):
            columns = slice(slab * LANES, (slab + 1) * LANES)
            spectra_ref[part, :, columns] = rows_ref[part * slabs + slab].astype(jnp.bfloat16)


def channel_of(time):
    return time % 4


def place_in_plane(near, time, times):
    return (near + NEAR // 2) % NEAR * times + (time + times // 2) % times


def spread_kernel(mine_ref, parcels_ref, turned_ref):
    count, rows, width = parcels_ref.shape
    times = count // NEAR
    stride = mine_ref.shape[1] // rows
    for place in range(0, mine_ref.shape[1], LANES):
        values = mine_ref[:, place : place + LANES].astype(jnp.float32)
        turned_ref[place : place + LANES, :] = values.T
    for near in range(NEAR):
        for channel in range(stride // NEAR):
            start = near * (stride // NEAR) + channel
            values = turned_ref[pl.ds(start, rows, stride=stride), :].astype(jnp.bfloat16)
            for time in range(times):
                if channel_of(time) == channel:
                    parcels_ref[place_in_plane(near, time, times)] = values


def correlate_kernel(frames_all, inputs_here, place_ref, every_ref, packed_ref):
    count, lines, width = every_ref.shape
    blocks, rows, inputs_all = packed_ref.shape
    times = count // NEAR
    main = lines - 2 * EARLY
    carry = None
    lined = []
    for time in range(times):
        pieces = [every_ref[place_in_plane(near, time, times)] for near in range(NEAR)]
        wide = jnp.concatenate([piece.astype(jnp.float32) for piece in pieces], axis=1)
        tiles = [wide[start : start + 8] for start in range(0, lines, 8)]
        if carry is not None:
            early = lax.broadcasted_iota(jnp.int32, carry.shape, 0) < EARLY
            tiles[0] = tiles[0] + jnp.where(early, carry, 0.0)
            tiles[1] = tiles[1] + jnp.where(early, pltpu.roll(carry, 8 - EARLY, 0), 0.0)
        carry = tiles[-1]
        lined += tiles[:-1]
    far = width // inputs_here
    target = lax.broadcasted_iota(jnp.int32, (1, inputs_all), 1)
    near = target // inputs_here % NEAR
    listed = place_in_column(target // (inputs_here * NEAR), far)
    source = near * width + listed * inputs_here + target % inputs_here
    chosen = lax.broadcasted_iota(jnp.int32, (inputs_all, inputs_all), 0) == source
    ordered = jnp.dot(
        jnp.concatenate(lined, axis=0).astype(jnp.bfloat16),
        chosen.astype(jnp.float32).astype(jnp.bfloat16),
        preferred_element_type=jnp.float32,
    )
    right = ordered.astype(jnp.bfloat16)
    twisted = []
    for start in range(0, times * main, 16):
        twisted.append(ordered[start + 8 : start + 16])
        twisted.append(-ordered[start : start + 8])
    twisted = jnp.concatenate(twisted, axis=0).astype(jnp.bfloat16)
    held = blocks * rows
    first = place_ref[0] * held
    col_index = lax.broadcasted_iota(jnp.int32, (held, inputs_all), 1)
    row_index = lax.broadcasted_iota(jnp.int32, (held, inputs_all), 0) + first
    left = [jnp.where(first == 0, side[:, :held], side[:, held:]) for side in (right, twisted)]
    both = lax.dot_general(
        jnp.concatenate(left, axis=1),
        right,
        (((0,), (0,)), ((), ())),
        preferred_element_type=jnp.float32,
    )
    values = jnp.where(row_index <= col_index, both[:held], both[held:]) * (1.0 / frames_all)
    values = values.astype(jnp.bfloat16)
    for block in range(blocks):
        packed_ref[block] = values[block * rows : (block + 1) * rows]


def unpack_kernel(packed_ref, lines_hbm, lines_ref, left):
    channels, count, width = packed_ref.shape
    tiles = width // LANES
    stores = []
    for first in range(0, count, 16):
        start = first * tiles * channels
        for channel in range(channels):
            values = packed_ref[channel, first : first + 16, :].astype(jnp.float32)
            for tile in range(tiles):
                lines = pl.ds(start + tile * channels + channel, 16, stride=tiles * channels)
                lines_ref[lines, :] = values[:, tile * LANES : (tile + 1) * LANES]
        block = pl.ds(start, 16 * tiles * channels)
        stores.append(
            pltpu.make_async_copy(lines_ref.at[block, :], lines_hbm.at[block, :], left.at[len(stores)])
        )
        stores[-1].start()
    for store in stores:
        store.wait()


def body(samples, gains):
    inputs_here = samples.shape[0]
    frames_here = samples.shape[1] // NFFT
    times = lax.axis_size("tm")
    far = lax.axis_size("far")
    groups = far * NEAR
    per_group = CH // groups
    inputs_all = inputs_here * groups
    frames_all = frames_here * times
    block = inputs_here * frames_here

    window = filter_window()
    twiddle = jnp.asarray(build_table(window)[: NFFT // 2])
    window_taps = jnp.asarray(window.astype(np.float32).reshape(TAPS, NFFT))

    sent = frames_here + EARLY
    gains = gains.transpose(0, 2, 1)

    def own_part(*refs):
        own_part_kernel(far, *refs)

    own, passed, parcels = pl.pallas_call(
        own_part,
        out_shape=(
            jax.ShapeDtypeStruct((block, 2 * CH), jnp.float32),
            jax.ShapeDtypeStruct(((TAPS - 1) * inputs_here, 2 * CH), jnp.float32),
            jax.ShapeDtypeStruct((far * inputs_here, sent * 2 * CH // far), jnp.bfloat16),
        ),
        in_specs=[ANY] * 4,
        out_specs=(ANY, ANY, ANY),
        scratch_shapes=[
            pltpu.VMEM(samples.shape, jnp.bfloat16),
            pltpu.VMEM(window_taps.shape, jnp.float32),
            pltpu.VMEM(twiddle.shape, jnp.bfloat16),
            pltpu.VMEM(gains.shape, jnp.float32),
            pltpu.VMEM((sent * inputs_here, 2 * CH), jnp.float32),
            pltpu.VMEM((far * inputs_here, sent * 2 * CH // far), jnp.bfloat16),
            pltpu.SemaphoreType.DMA((3 + NFFT // (2 * STEP),)),
            pltpu.SemaphoreType.DMA((2 + sent // 4,)),
        ],
        compiler_params=pltpu.CompilerParams(vmem_limit_bytes=OWN_PART_VMEM),
        cost_estimate=pl.CostEstimate(
            flops=2 * sent * inputs_here * NFFT * 2 * CH,
            bytes_accessed=3 * 1024 * 1024,
            transcendentals=0,
        ),
        name="own_part",
    )(samples, window_taps, twiddle, gains)

    parcels = parcels.reshape(far, inputs_here, sent * 2 * CH // far)
    column = [sorted(range(far), key=lambda place: place_in_column(place, far))]
    mine = lax.all_to_all(parcels, "far", 0, 0, axis_index_groups=column)
    mine = mine.reshape(far * inputs_here, sent * 2 * CH // far)

    passed = lax.ppermute(passed, "tm", [(source, source + 1) for source in range(times - 1)])
    spectra = pl.pallas_call(
        spectra_kernel,
        out_shape=jax.ShapeDtypeStruct((2, block, CH), jnp.bfloat16),
        in_specs=[VMEM] * 3,
        out_specs=VMEM,
        scratch_shapes=[pltpu.VMEM((2 * CH // LANES, block, LANES), jnp.float32)],
        compiler_params=PARAMS,
        cost_estimate=pl.CostEstimate(
            flops=8 * block * 2 * CH, bytes_accessed=1024 * 1024, transcendentals=0
        ),
        name="spectra",
    )(passed, own, gains)
    mine, spectra = lax.optimization_barrier((mine, spectra))
    spectra = spectra.reshape(2, inputs_here, frames_here, CH).transpose(0, 3, 1, 2)

    lines = 2 * sent
    spread = pl.pallas_call(
        spread_kernel,
        out_shape=jax.ShapeDtypeStruct((NEAR * times, lines, far * inputs_here), jnp.bfloat16),
        in_specs=[VMEM],
        out_specs=VMEM,
        scratch_shapes=[pltpu.VMEM((sent * 2 * CH // far, far * inputs_here), jnp.float32)],
        compiler_params=PARAMS,
        name="spread",
    )(mine)
    place = lax.axis_index("tm").astype(jnp.int32)
    square = (place // 4)[None]
    spread, square = lax.optimization_barrier((spread, square))
    members = [(near, time) for near in range(NEAR) for time in range(times)]
    members.sort(key=lambda member: place_in_plane(*member, times))
    plane = [[near * times + time for near, time in members]]
    every = lax.all_to_all(spread, ("near", "tm"), 0, 0, axis_index_groups=plane)

    def correlate(*refs):
        correlate_kernel(frames_all, inputs_here, *refs)

    rows = inputs_all // times
    packed = pl.pallas_call(
        correlate,
        out_shape=jax.ShapeDtypeStruct((per_group, rows, inputs_all), jnp.bfloat16),
        in_specs=[SMEM, VMEM],
        out_specs=VMEM,
        compiler_params=PARAMS,
        name="correlate",
    )(square, every)
    squares = [[0, 1, 2, 3], [4, 5, 6, 7]]
    packed = lax.all_to_all(packed, "tm", 0, 0, axis_index_groups=squares)
    tiles = inputs_all // LANES
    visibilities = pl.pallas_call(
        unpack_kernel,
        out_shape=jax.ShapeDtypeStruct((rows * tiles * per_group, LANES), jnp.float32),
        in_specs=[VMEM],
        out_specs=ANY,
        scratch_shapes=[
            pltpu.VMEM((rows * tiles * per_group, LANES), jnp.float32),
            pltpu.SemaphoreType.DMA((rows // 16,)),
        ],
        compiler_params=PARAMS,
        name="unpack",
    )(packed)
    visibilities = visibilities.reshape(rows, tiles, per_group, LANES).transpose(0, 2, 1, 3)
    visibilities = visibilities.reshape(rows, per_group, inputs_all)
    return (spectra, visibilities)


def solution(mesh):
    groups, times = mesh.devices.shape
    split = Mesh(mesh.devices.reshape(groups // NEAR, NEAR, times), ("far", "near", "tm"))
    inputs = ("far", "near")
    return jax.shard_map(
        body,
        mesh=split,
        in_specs=(P(inputs, "tm"), P(None, None, inputs)),
        out_specs=(P(None, None, inputs, "tm"), P("tm", inputs, None)),
        check_vma=False,
    )
```

```python
import math

import jax
import jax.numpy as jnp
import numpy as np
from jax import lax
from jax.experimental import pallas as pl
from jax.experimental.pallas import tpu as pltpu
from jax.sharding import Mesh, PartitionSpec as P

NFFT = 2048
CH = 256
FIRST = 384
TAPS = 4
NEAR = 4
EARLY = 4
STEP = 256
LANES = 128
VMEM = pl.BlockSpec(memory_space=pltpu.VMEM)
ANY = pl.BlockSpec(memory_space=pl.ANY)
SMEM = pl.BlockSpec(memory_space=pltpu.SMEM)
OWN_PART_VMEM = 59 * 1024 * 1024 + 768 * 1024
PARAMS = pltpu.CompilerParams(vmem_limit_bytes=32 * 1024 * 1024)


def filter_window():
    length = TAPS * NFFT
    position = np.arange(length, dtype=np.float64)
    centred = (position - 0.5 * length + 0.5) / NFFT
    hann_taper = 0.5 - 0.5 * np.cos(2.0 * math.pi * (position + 0.5) / length)
    return np.sinc(centred) * hann_taper


def build_table(window):
    norm_scale = 1.0 / np.sqrt(np.sum(window * window))
    sample = np.arange(NFFT)[:, None]
    channel = FIRST + np.arange(CH)[None, :]
    phase_angle = 2.0 * math.pi / NFFT * (sample * channel % NFFT)
    cosine = np.cos(phase_angle) * norm_scale
    sine = -np.sin(phase_angle) * norm_scale
    return np.concatenate([cosine, sine], axis=1).astype(jnp.bfloat16)


def tapped_block(samples_ref, window_ref, frames_sent, block):
    inputs_here, count = samples_ref.shape
    frames_here = count // NFFT
    low = block * STEP
    sums = []
    for frame in range(frames_sent):
        total = jnp.zeros((inputs_here, STEP), jnp.float32)
        for tap in range(TAPS):
            source = frame - TAPS + 1 + tap
            if 0 <= source < frames_here:
                start = source * NFFT + low
                values = samples_ref[:, start : start + STEP]
                weights = window_ref[tap : tap + 1, low : low + STEP]
                total = total + weights * values.astype(jnp.float32)
        sums.append(total)
    pairs = [
        jnp.concatenate(sums[frame : frame + 2], axis=0).astype(jnp.bfloat16)
        for frame in range(0, frames_sent, 2)
    ]
    return jnp.concatenate(pairs, axis=0)


def turn_granules(blocks, size):
    count = len(blocks)
    lanes = count * size
    granule = lax.broadcasted_iota(jnp.int32, blocks[0].shape, 1) // size
    blocks = list(blocks)
    distance = count // 2
    while distance:
        upper = (granule & distance) != 0
        shift = distance * size
        for index in range(count):
            if index & distance:
                continue
            low, high = blocks[index], blocks[index + distance]
            blocks[index] = jnp.where(upper, pltpu.roll(high, shift, 1), low)
            blocks[index + distance] = jnp.where(upper, high, pltpu.roll(low, lanes - shift, 1))
        distance //= 2
    return blocks


def place_in_column(place, far):
    return (far * 5 // 8 + far - place) % far


def own_part_kernel(
    far,
    samples_hbm,
    window_hbm,
    twiddle_hbm,
    gains_hbm,
    own_hbm,
    passed_hbm,
    parcels_hbm,
    samples_ref,
    window_ref,
    twiddle_ref,
    gains_ref,
    direct_ref,
    parcels_ref,
    arrived,
    left,
):
    inputs_here = gains_ref.shape[1]
    frames_here = samples_hbm.shape[1] // NFFT
    blocks = range(NFFT // STEP)
    fetches = []

    def fetch(source, target):
        fetches.append(pltpu.make_async_copy(source, target, arrived.at[len(fetches)]))
        fetches[-1].start()
        return fetches[-1]

    samples_in = fetch(samples_hbm, samples_ref)
    window_in = fetch(window_hbm, window_ref)
    table_in = []
    for block in blocks[: len(blocks) // 2]:
        rows = pl.ds(block * STEP, STEP)
        table_in.append(fetch(twiddle_hbm.at[rows, :], twiddle_ref.at[rows, :]))
    gains_in = fetch(gains_hbm, gains_ref)
    samples_in.wait()
    window_in.wait()
    total = None
    sent = frames_here + EARLY
    for block, table in enumerate(table_in):
        tapped = [
            tapped_block(samples_ref, window_ref, sent, half + block)
            for half in (0, len(table_in))
        ]
        table.wait()
        product = jnp.dot(
            jnp.concatenate(tapped, axis=0),
            twiddle_ref[block * STEP : (block + 1) * STEP, :],
            preferred_element_type=jnp.float32,
        )
        total = product if total is None else total + product
    channel = FIRST + lax.broadcasted_iota(jnp.int32, (1, 2 * CH), 1)
    sign = (1 - 2 * (channel % 2)).astype(jnp.float32)
    direct_ref[...] = total[: sent * inputs_here] + sign * total[sent * inputs_here :]
    own_rows = own_hbm.shape[0]
    passed_rows = passed_hbm.shape[0]
    stores = [
        pltpu.make_async_copy(direct_ref.at[pl.ds(0, own_rows), :], own_hbm, left.at[0]),
        pltpu.make_async_copy(
            direct_ref.at[pl.ds(own_rows, passed_rows), :], passed_hbm, left.at[1]
        ),
    ]
    for store in stores:
        store.start()
    gains_in.wait()
    gain_re = gains_ref[0]
    gain_im = gains_ref[1]
    parts = []
    for frame in range(frames_here + EARLY):
        direct = direct_ref[frame * inputs_here : (frame + 1) * inputs_here, :]
        direct_re = direct[:, :CH]
        direct_im = direct[:, CH:]
        parts.append(
            (
                gain_re * direct_re - gain_im * direct_im,
                gain_re * direct_im + gain_im * direct_re,
            )
        )
    slots = [
        [(part, frame) for frame in range(first, first + 8)]
        for first in range(0, frames_here, 8)
        for part in range(2)
    ]
    slots.append([(part, frames_here + frame) for part in range(2) for frame in range(EARLY)])
    per_far = CH // far
    for place, slot in enumerate(slots):
        columns = slice(place * LANES, (place + 1) * LANES)
        blocks = []
        for half in range(CH // LANES):
            lanes = slice(half * LANES, (half + 1) * LANES)
            blocks += turn_granules([parts[frame][part][:, lanes] for part, frame in slot], per_far)
        listed = sorted(range(far), key=lambda target: place_in_column(target, far))
        for index in range(0, far, 2):
            rows = slice(index * inputs_here, (index + 2) * inputs_here)
            parcels_ref[rows, columns] = jnp.concatenate(
                [blocks[target] for target in listed[index : index + 2]], axis=0
            ).astype(jnp.bfloat16)
        lanes = pl.ds(place * LANES, LANES)
        stores.append(
            pltpu.make_async_copy(
                parcels_ref.at[:, lanes], parcels_hbm.at[:, lanes], left.at[len(stores)]
            )
        )
        stores[-1].start()
    for store in stores:
        store.wait()


def spectra_kernel(passed_ref, own_ref, gains_ref, spectra_ref, rows_ref):
    inputs_here = gains_ref.shape[1]
    frames_here = own_ref.shape[0] // inputs_here
    slabs = CH // LANES
    gain_re = gains_ref[0]
    gain_im = gains_ref[1]
    for frame in range(frames_here):
        block = slice(frame * inputs_here, (frame + 1) * inputs_here)
        direct = own_ref[block, :]
        if frame < TAPS - 1:
            direct = direct + passed_ref[block, :]
        direct_re = direct[:, :CH]
        direct_im = direct[:, CH:]
        rows = pl.ds(frame, inputs_here, stride=frames_here)
        real_part = gain_re * direct_re - gain_im * direct_im
        imag_part = gain_re * direct_im + gain_im * direct_re
        for slab in range(slabs):
            columns = slice(slab * LANES, (slab + 1) * LANES)
            rows_ref[slab, rows, :] = real_part[:, columns]
            rows_ref[slabs + slab, rows, :] = imag_part[:, columns]
    for part in range(2):
        for slab in range(slabs):
            columns = slice(slab * LANES, (slab + 1) * LANES)
            values = rows_ref[part * slabs + slab, : own_ref.shape[0], :]
            spectra_ref[part, :, columns] = values.astype(jnp.bfloat16)


def channel_of(time):
    return time % 4


def place_in_plane(near, time, times):
    count = NEAR * times
    middle = NEAR // 2 * times + times // 2
    return 3 * (near * times + time + count - middle) % count


def spread_kernel(mine_ref, parcels_ref, turned_ref):
    count, rows, width = parcels_ref.shape
    times = count // NEAR
    stride = mine_ref.shape[1] // rows
    for place in range(0, mine_ref.shape[1], LANES):
        values = mine_ref[:, place : place + LANES].astype(jnp.float32)
        turned_ref[place : place + LANES, :] = values.T
    for near in range(NEAR):
        for channel in range(stride // NEAR):
            start = near * (stride // NEAR) + channel
            values = turned_ref[pl.ds(start, rows, stride=stride), :].astype(jnp.bfloat16)
            for time in range(times):
                if channel_of(time) == channel:
                    parcels_ref[place_in_plane(near, time, times)] = values


def correlate_kernel(frames_all, inputs_here, place_ref, every_ref, packed_ref):
    count, lines, width = every_ref.shape
    blocks, rows, inputs_all = packed_ref.shape
    times = count // NEAR
    main = lines - 2 * EARLY
    carry = None
    lined = []
    for time in range(times):
        pieces = [every_ref[place_in_plane(near, time, times)] for near in range(NEAR)]
        wide = jnp.concatenate([piece.astype(jnp.float32) for piece in pieces], axis=1)
        tiles = [wide[start : start + 8] for start in range(0, lines, 8)]
        if carry is not None:
            early = lax.broadcasted_iota(jnp.int32, carry.shape, 0) < EARLY
            tiles[0] = tiles[0] + jnp.where(early, carry, 0.0)
            tiles[1] = tiles[1] + jnp.where(early, pltpu.roll(carry, 8 - EARLY, 0), 0.0)
        carry = tiles[-1]
        lined += tiles[:-1]
    far = width // inputs_here
    target = lax.broadcasted_iota(jnp.int32, (1, inputs_all), 1)
    near = target // inputs_here % NEAR
    listed = place_in_column(target // (inputs_here * NEAR), far)
    source = near * width + listed * inputs_here + target % inputs_here
    chosen = lax.broadcasted_iota(jnp.int32, (inputs_all, inputs_all), 0) == source
    ordered = jnp.dot(
        jnp.concatenate(lined, axis=0).astype(jnp.bfloat16),
        chosen.astype(jnp.float32).astype(jnp.bfloat16),
        preferred_element_type=jnp.float32,
    )
    right = ordered.astype(jnp.bfloat16)
    twisted = []
    for start in range(0, times * main, 16):
        twisted.append(ordered[start + 8 : start + 16])
        twisted.append(-ordered[start : start + 8])
    twisted = jnp.concatenate(twisted, axis=0).astype(jnp.bfloat16)
    held = blocks * rows
    first = place_ref[0] * held
    col_index = lax.broadcasted_iota(jnp.int32, (held, inputs_all), 1)
    row_index = lax.broadcasted_iota(jnp.int32, (held, inputs_all), 0) + first
    left = [jnp.where(first == 0, side[:, :held], side[:, held:]) for side in (right, twisted)]
    both = lax.dot_general(
        jnp.concatenate(left, axis=1),
        right,
        (((0,), (0,)), ((), ())),
        preferred_element_type=jnp.float32,
    )
    values = jnp.where(row_index <= col_index, both[:held], both[held:]) * (1.0 / frames_all)
    values = values.astype(jnp.bfloat16)
    for block in range(blocks):
        packed_ref[block] = values[block * rows : (block + 1) * rows]


def unpack_kernel(packed_ref, lines_hbm, lines_ref, left):
    channels, count, width = packed_ref.shape
    tiles = width // LANES
    stores = []
    for first in range(0, count, 16):
        start = first * tiles * channels
        for channel in range(channels):
            values = packed_ref[channel, first : first + 16, :].astype(jnp.float32)
            for tile in range(tiles):
                lines = pl.ds(start + tile * channels + channel, 16, stride=tiles * channels)
                lines_ref[lines, :] = values[:, tile * LANES : (tile + 1) * LANES]
        block = pl.ds(start, 16 * tiles * channels)
        stores.append(
            pltpu.make_async_copy(lines_ref.at[block, :], lines_hbm.at[block, :], left.at[len(stores)])
        )
        stores[-1].start()
    for store in stores:
        store.wait()


def body(samples, gains):
    inputs_here = samples.shape[0]
    frames_here = samples.shape[1] // NFFT
    times = lax.axis_size("tm")
    far = lax.axis_size("far")
    groups = far * NEAR
    per_group = CH // groups
    inputs_all = inputs_here * groups
    frames_all = frames_here * times
    block = inputs_here * frames_here

    window = filter_window()
    twiddle = jnp.asarray(build_table(window)[: NFFT // 2])
    window_taps = jnp.asarray(window.astype(np.float32).reshape(TAPS, NFFT))

    sent = frames_here + EARLY
    gains = gains.transpose(0, 2, 1)

    def own_part(*refs):
        own_part_kernel(far, *refs)

    own, passed, parcels = pl.pallas_call(
        own_part,
        out_shape=(
            jax.ShapeDtypeStruct((block, 2 * CH), jnp.float32),
            jax.ShapeDtypeStruct(((TAPS - 1) * inputs_here, 2 * CH), jnp.float32),
            jax.ShapeDtypeStruct((far * inputs_here, sent * 2 * CH // far), jnp.bfloat16),
        ),
        in_specs=[ANY] * 4,
        out_specs=(ANY, ANY, ANY),
        scratch_shapes=[
            pltpu.VMEM(samples.shape, jnp.bfloat16),
            pltpu.VMEM(window_taps.shape, jnp.float32),
            pltpu.VMEM(twiddle.shape, jnp.bfloat16),
            pltpu.VMEM(gains.shape, jnp.float32),
            pltpu.VMEM((sent * inputs_here, 2 * CH), jnp.float32),
            pltpu.VMEM((far * inputs_here, sent * 2 * CH // far), jnp.bfloat16),
            pltpu.SemaphoreType.DMA((3 + NFFT // (2 * STEP),)),
            pltpu.SemaphoreType.DMA((2 + sent // 4,)),
        ],
        compiler_params=pltpu.CompilerParams(vmem_limit_bytes=OWN_PART_VMEM),
        cost_estimate=pl.CostEstimate(
            flops=2 * sent * inputs_here * NFFT * 2 * CH,
            bytes_accessed=3 * 1024 * 1024,
            transcendentals=0,
        ),
        name="own_part",
    )(samples, window_taps, twiddle, gains)

    parcels = parcels.reshape(far, inputs_here, sent * 2 * CH // far)
    column = [sorted(range(far), key=lambda place: place_in_column(place, far))]
    mine = lax.all_to_all(parcels, "far", 0, 0, axis_index_groups=column)
    mine = mine.reshape(far * inputs_here, sent * 2 * CH // far)

    passed = lax.ppermute(passed, "tm", [(source, source + 1) for source in range(times - 1)])
    spectra = pl.pallas_call(
        spectra_kernel,
        out_shape=jax.ShapeDtypeStruct((2, block, CH), jnp.bfloat16),
        in_specs=[VMEM] * 3,
        out_specs=VMEM,
        scratch_shapes=[pltpu.VMEM((2 * CH // LANES, block + frames_here, LANES), jnp.float32)],
        compiler_params=PARAMS,
        cost_estimate=pl.CostEstimate(
            flops=8 * block * 2 * CH, bytes_accessed=1024 * 1024, transcendentals=0
        ),
        name="spectra",
    )(passed, own, gains)
    mine, spectra = lax.optimization_barrier((mine, spectra))
    spectra = spectra.reshape(2, inputs_here, frames_here, CH).transpose(0, 3, 1, 2)

    lines = 2 * sent
    spread = pl.pallas_call(
        spread_kernel,
        out_shape=jax.ShapeDtypeStruct((NEAR * times, lines, far * inputs_here), jnp.bfloat16),
        in_specs=[VMEM],
        out_specs=VMEM,
        scratch_shapes=[pltpu.VMEM(((sent + 1) * 2 * CH // far, far * inputs_here), jnp.float32)],
        compiler_params=PARAMS,
        name="spread",
    )(mine)
    place = lax.axis_index("tm").astype(jnp.int32)
    square = (place // 4)[None]
    spread, square = lax.optimization_barrier((spread, square))
    members = [(near, time) for near in range(NEAR) for time in range(times)]
    members.sort(key=lambda member: place_in_plane(*member, times))
    plane = [[near * times + time for near, time in members]]
    every = lax.all_to_all(spread, ("near", "tm"), 0, 0, axis_index_groups=plane)

    def correlate(*refs):
        correlate_kernel(frames_all, inputs_here, *refs)

    rows = inputs_all // times
    packed = pl.pallas_call(
        correlate,
        out_shape=jax.ShapeDtypeStruct((per_group, rows, inputs_all), jnp.bfloat16),
        in_specs=[SMEM, VMEM],
        out_specs=VMEM,
        compiler_params=PARAMS,
        name="correlate",
    )(square, every)
    squares = [[0, 1, 2, 3], [4, 5, 6, 7]]
    packed = lax.all_to_all(packed, "tm", 0, 0, axis_index_groups=squares)
    tiles = inputs_all // LANES
    visibilities = pl.pallas_call(
        unpack_kernel,
        out_shape=jax.ShapeDtypeStruct((rows * tiles * per_group, LANES), jnp.float32),
        in_specs=[VMEM],
        out_specs=ANY,
        scratch_shapes=[
            pltpu.VMEM(((rows + 1) * tiles * per_group, LANES), jnp.float32),
            pltpu.SemaphoreType.DMA((rows // 16,)),
        ],
        compiler_params=PARAMS,
        name="unpack",
    )(packed)
    visibilities = visibilities.reshape(rows, tiles, per_group, LANES).transpose(0, 2, 1, 3)
    visibilities = visibilities.reshape(rows, per_group, inputs_all)
    return (spectra, visibilities)


def solution(mesh):
    groups, times = mesh.devices.shape
    split = Mesh(mesh.devices.reshape(groups // NEAR, NEAR, times), ("far", "near", "tm"))
    inputs = ("far", "near")
    return jax.shard_map(
        body,
        mesh=split,
        in_specs=(P(inputs, "tm"), P(None, None, inputs)),
        out_specs=(P(None, None, inputs, "tm"), P("tm", inputs, None)),
        check_vma=False,
    )
```

```python
import math

import jax
import jax.numpy as jnp
import numpy as np
from jax import lax
from jax.experimental import pallas as pl
from jax.experimental.pallas import tpu as pltpu
from jax.sharding import Mesh, PartitionSpec as P

NFFT = 2048
CH = 256
FIRST = 384
TAPS = 4
NEAR = 4
EARLY = 4
STEP = 256
LANES = 128
VMEM = pl.BlockSpec(memory_space=pltpu.VMEM)
ANY = pl.BlockSpec(memory_space=pl.ANY)
SMEM = pl.BlockSpec(memory_space=pltpu.SMEM)
OWN_PART_VMEM = 59 * 1024 * 1024 + 768 * 1024
PARAMS = pltpu.CompilerParams(vmem_limit_bytes=32 * 1024 * 1024)


def filter_window():
    length = TAPS * NFFT
    position = np.arange(length, dtype=np.float64)
    centred = (position - 0.5 * length + 0.5) / NFFT
    hann_taper = 0.5 - 0.5 * np.cos(2.0 * math.pi * (position + 0.5) / length)
    return np.sinc(centred) * hann_taper


def build_table(window):
    norm_scale = 1.0 / np.sqrt(np.sum(window * window))
    sample = np.arange(NFFT)[:, None]
    channel = FIRST + np.arange(CH)[None, :]
    phase_angle = 2.0 * math.pi / NFFT * (sample * channel % NFFT)
    cosine = np.cos(phase_angle) * norm_scale
    sine = -np.sin(phase_angle) * norm_scale
    return np.concatenate([cosine, sine], axis=1).astype(jnp.bfloat16)


def tapped_block(samples_ref, wide_ref, window_ref, frames_sent, block):
    inputs_here, count = samples_ref.shape
    frames_here = count // NFFT
    low = block * STEP
    for frame in range(frames_here):
        start = frame * NFFT + low
        wide_ref[block, :, frame * STEP : (frame + 1) * STEP] = samples_ref[
            :, start : start + STEP
        ].astype(jnp.float32)
    sums = []
    for frame in range(frames_sent):
        total = jnp.zeros((inputs_here, STEP), jnp.float32)
        for tap in range(TAPS):
            source = frame - TAPS + 1 + tap
            if 0 <= source < frames_here:
                values = wide_ref[block, :, source * STEP : (source + 1) * STEP]
                total = total + window_ref[tap : tap + 1, low : low + STEP] * values
        sums.append(total)
    pairs = [
        jnp.concatenate(sums[frame : frame + 2], axis=0).astype(jnp.bfloat16)
        for frame in range(0, frames_sent, 2)
    ]
    return jnp.concatenate(pairs, axis=0)


def turn_granules(blocks, size):
    count = len(blocks)
    lanes = count * size
    granule = lax.broadcasted_iota(jnp.int32, blocks[0].shape, 1) // size
    blocks = list(blocks)
    distance = count // 2
    while distance:
        upper = (granule & distance) != 0
        shift = distance * size
        for index in range(count):
            if index & distance:
                continue
            low, high = blocks[index], blocks[index + distance]
            blocks[index] = jnp.where(upper, pltpu.roll(high, shift, 1), low)
            blocks[index + distance] = jnp.where(upper, high, pltpu.roll(low, lanes - shift, 1))
        distance //= 2
    return blocks


def place_in_column(place, far):
    return (far * 5 // 8 + far - place) % far


def own_part_kernel(
    far,
    samples_hbm,
    window_hbm,
    twiddle_hbm,
    gains_hbm,
    own_hbm,
    passed_hbm,
    parcels_hbm,
    samples_ref,
    wide_ref,
    window_ref,
    twiddle_ref,
    gains_ref,
    direct_ref,
    parcels_ref,
    arrived,
    left,
):
    inputs_here = gains_ref.shape[1]
    frames_here = samples_hbm.shape[1] // NFFT
    blocks = range(NFFT // STEP)
    fetches = []

    def fetch(source, target):
        fetches.append(pltpu.make_async_copy(source, target, arrived.at[len(fetches)]))
        fetches[-1].start()
        return fetches[-1]

    samples_in = fetch(samples_hbm, samples_ref)
    window_in = fetch(window_hbm, window_ref)
    table_in = []
    for block in blocks[: len(blocks) // 2]:
        rows = pl.ds(block * STEP, STEP)
        table_in.append(fetch(twiddle_hbm.at[rows, :], twiddle_ref.at[rows, :]))
    gains_in = fetch(gains_hbm, gains_ref)
    samples_in.wait()
    window_in.wait()
    total = None
    sent = frames_here + EARLY
    for block, table in enumerate(table_in):
        tapped = [
            tapped_block(samples_ref, wide_ref, window_ref, sent, half + block)
            for half in (0, len(table_in))
        ]
        table.wait()
        product = jnp.dot(
            jnp.concatenate(tapped, axis=0),
            twiddle_ref[block * STEP : (block + 1) * STEP, :],
            preferred_element_type=jnp.float32,
        )
        total = product if total is None else total + product
    channel = FIRST + lax.broadcasted_iota(jnp.int32, (1, 2 * CH), 1)
    sign = (1 - 2 * (channel % 2)).astype(jnp.float32)
    direct_ref[...] = total[: sent * inputs_here] + sign * total[sent * inputs_here :]
    own_rows = own_hbm.shape[0]
    passed_rows = passed_hbm.shape[0]
    stores = [
        pltpu.make_async_copy(direct_ref.at[pl.ds(0, own_rows), :], own_hbm, left.at[0]),
        pltpu.make_async_copy(
            direct_ref.at[pl.ds(own_rows, passed_rows), :], passed_hbm, left.at[1]
        ),
    ]
    for store in stores:
        store.start()
    gains_in.wait()
    gain_re = gains_ref[0]
    gain_im = gains_ref[1]
    parts = []
    for frame in range(frames_here + EARLY):
        direct = direct_ref[frame * inputs_here : (frame + 1) * inputs_here, :]
        direct_re = direct[:, :CH]
        direct_im = direct[:, CH:]
        parts.append(
            (
                gain_re * direct_re - gain_im * direct_im,
                gain_re * direct_im + gain_im * direct_re,
            )
        )
    slots = [
        [(part, frame) for frame in range(first, first + 8)]
        for first in range(0, frames_here, 8)
        for part in range(2)
    ]
    slots.append([(part, frames_here + frame) for part in range(2) for frame in range(EARLY)])
    per_far = CH // far
    for place, slot in enumerate(slots):
        columns = slice(place * LANES, (place + 1) * LANES)
        blocks = []
        for half in range(CH // LANES):
            lanes = slice(half * LANES, (half + 1) * LANES)
            blocks += turn_granules([parts[frame][part][:, lanes] for part, frame in slot], per_far)
        listed = sorted(range(far), key=lambda target: place_in_column(target, far))
        for index in range(0, far, 2):
            rows = slice(index * inputs_here, (index + 2) * inputs_here)
            parcels_ref[rows, columns] = jnp.concatenate(
                [blocks[target] for target in listed[index : index + 2]], axis=0
            ).astype(jnp.bfloat16)
        lanes = pl.ds(place * LANES, LANES)
        stores.append(
            pltpu.make_async_copy(
                parcels_ref.at[:, lanes], parcels_hbm.at[:, lanes], left.at[len(stores)]
            )
        )
        stores[-1].start()
    for store in stores:
        store.wait()


def spectra_kernel(passed_ref, own_ref, gains_ref, spectra_ref, rows_ref):
    inputs_here = gains_ref.shape[1]
    frames_here = own_ref.shape[0] // inputs_here
    slabs = CH // LANES
    gain_re = gains_ref[0]
    gain_im = gains_ref[1]
    for frame in range(frames_here):
        block = slice(frame * inputs_here, (frame + 1) * inputs_here)
        direct = own_ref[block, :]
        if frame < TAPS - 1:
            direct = direct + passed_ref[block, :]
        direct_re = direct[:, :CH]
        direct_im = direct[:, CH:]
        rows = pl.ds(frame, inputs_here, stride=frames_here)
        real_part = gain_re * direct_re - gain_im * direct_im
        imag_part = gain_re * direct_im + gain_im * direct_re
        for slab in range(slabs):
            columns = slice(slab * LANES, (slab + 1) * LANES)
            rows_ref[slab, rows, :] = real_part[:, columns]
            rows_ref[slabs + slab, rows, :] = imag_part[:, columns]
    for part in range(2):
        for slab in range(slabs):
            columns = slice(slab * LANES, (slab + 1) * LANES)
            values = rows_ref[part * slabs + slab, : own_ref.shape[0], :]
            spectra_ref[part, :, columns] = values.astype(jnp.bfloat16)


def channel_of(time):
    return time % 4


def place_in_plane(near, time, times):
    count = NEAR * times
    middle = NEAR // 2 * times + times // 2
    return 3 * (near * times + time + count - middle) % count


def spread_kernel(mine_ref, parcels_ref, turned_ref):
    count, rows, width = parcels_ref.shape
    times = count // NEAR
    stride = mine_ref.shape[1] // rows
    for place in range(0, mine_ref.shape[1], LANES):
        values = mine_ref[:, place : place + LANES].astype(jnp.float32)
        turned_ref[place : place + LANES, :] = values.T
    for near in range(NEAR):
        for channel in range(stride // NEAR):
            start = near * (stride // NEAR) + channel
            values = turned_ref[pl.ds(start, rows, stride=stride), :].astype(jnp.bfloat16)
            for time in range(times):
                if channel_of(time) == channel:
                    parcels_ref[place_in_plane(near, time, times)] = values


def correlate_kernel(frames_all, inputs_here, place_ref, every_ref, packed_ref):
    count, lines, width = every_ref.shape
    blocks, rows, inputs_all = packed_ref.shape
    times = count // NEAR
    main = lines - 2 * EARLY
    carry = None
    lined = []
    for time in range(times):
        pieces = [every_ref[place_in_plane(near, time, times)] for near in range(NEAR)]
        wide = jnp.concatenate([piece.astype(jnp.float32) for piece in pieces], axis=1)
        tiles = [wide[start : start + 8] for start in range(0, lines, 8)]
        if carry is not None:
            early = lax.broadcasted_iota(jnp.int32, carry.shape, 0) < EARLY
            tiles[0] = tiles[0] + jnp.where(early, carry, 0.0)
            tiles[1] = tiles[1] + jnp.where(early, pltpu.roll(carry, 8 - EARLY, 0), 0.0)
        carry = tiles[-1]
        lined += tiles[:-1]
    far = width // inputs_here
    target = lax.broadcasted_iota(jnp.int32, (1, inputs_all), 1)
    near = target // inputs_here % NEAR
    listed = place_in_column(target // (inputs_here * NEAR), far)
    source = near * width + listed * inputs_here + target % inputs_here
    chosen = lax.broadcasted_iota(jnp.int32, (inputs_all, inputs_all), 0) == source
    ordered = jnp.dot(
        jnp.concatenate(lined, axis=0).astype(jnp.bfloat16),
        chosen.astype(jnp.float32).astype(jnp.bfloat16),
        preferred_element_type=jnp.float32,
    )
    right = ordered.astype(jnp.bfloat16)
    twisted = []
    for start in range(0, times * main, 16):
        twisted.append(ordered[start + 8 : start + 16])
        twisted.append(-ordered[start : start + 8])
    twisted = jnp.concatenate(twisted, axis=0).astype(jnp.bfloat16)
    held = blocks * rows
    first = place_ref[0] * held
    col_index = lax.broadcasted_iota(jnp.int32, (held, inputs_all), 1)
    row_index = lax.broadcasted_iota(jnp.int32, (held, inputs_all), 0) + first
    left = [jnp.where(first == 0, side[:, :held], side[:, held:]) for side in (right, twisted)]
    both = lax.dot_general(
        jnp.concatenate(left, axis=1),
        right,
        (((0,), (0,)), ((), ())),
        preferred_element_type=jnp.float32,
    )
    values = jnp.where(row_index <= col_index, both[:held], both[held:]) * (1.0 / frames_all)
    values = values.astype(jnp.bfloat16)
    for block in range(blocks):
        packed_ref[block] = values[block * rows : (block + 1) * rows]


def unpack_kernel(packed_ref, lines_hbm, lines_ref, left):
    channels, count, width = packed_ref.shape
    tiles = width // LANES
    stores = []
    for first in range(0, count, 16):
        start = first * tiles * channels
        for channel in range(channels):
            values = packed_ref[channel, first : first + 16, :].astype(jnp.float32)
            for tile in range(tiles):
                lines = pl.ds(start + tile * channels + channel, 16, stride=tiles * channels)
                lines_ref[lines, :] = values[:, tile * LANES : (tile + 1) * LANES]
        block = pl.ds(start, 16 * tiles * channels)
        stores.append(
            pltpu.make_async_copy(lines_ref.at[block, :], lines_hbm.at[block, :], left.at[len(stores)])
        )
        stores[-1].start()
    for store in stores:
        store.wait()


def body(samples, gains):
    inputs_here = samples.shape[0]
    frames_here = samples.shape[1] // NFFT
    times = lax.axis_size("tm")
    far = lax.axis_size("far")
    groups = far * NEAR
    per_group = CH // groups
    inputs_all = inputs_here * groups
    frames_all = frames_here * times
    block = inputs_here * frames_here

    window = filter_window()
    twiddle = jnp.asarray(build_table(window)[: NFFT // 2])
    window_taps = jnp.asarray(window.astype(np.float32).reshape(TAPS, NFFT))

    sent = frames_here + EARLY
    gains = gains.transpose(0, 2, 1)

    def own_part(*refs):
        own_part_kernel(far, *refs)

    own, passed, parcels = pl.pallas_call(
        own_part,
        out_shape=(
            jax.ShapeDtypeStruct((block, 2 * CH), jnp.float32),
            jax.ShapeDtypeStruct(((TAPS - 1) * inputs_here, 2 * CH), jnp.float32),
            jax.ShapeDtypeStruct((far * inputs_here, sent * 2 * CH // far), jnp.bfloat16),
        ),
        in_specs=[ANY] * 4,
        out_specs=(ANY, ANY, ANY),
        scratch_shapes=[
            pltpu.VMEM(samples.shape, jnp.bfloat16),
            pltpu.VMEM((NFFT // STEP, inputs_here, frames_here * STEP), jnp.float32),
            pltpu.VMEM(window_taps.shape, jnp.float32),
            pltpu.VMEM(twiddle.shape, jnp.bfloat16),
            pltpu.VMEM(gains.shape, jnp.float32),
            pltpu.VMEM((sent * inputs_here, 2 * CH), jnp.float32),
            pltpu.VMEM((far * inputs_here, sent * 2 * CH // far), jnp.bfloat16),
            pltpu.SemaphoreType.DMA((3 + NFFT // (2 * STEP),)),
            pltpu.SemaphoreType.DMA((2 + sent // 4,)),
        ],
        compiler_params=pltpu.CompilerParams(vmem_limit_bytes=OWN_PART_VMEM),
        cost_estimate=pl.CostEstimate(
            flops=2 * sent * inputs_here * NFFT * 2 * CH,
            bytes_accessed=3 * 1024 * 1024,
            transcendentals=0,
        ),
        name="own_part",
    )(samples, window_taps, twiddle, gains)

    parcels = parcels.reshape(far, inputs_here, sent * 2 * CH // far)
    column = [sorted(range(far), key=lambda place: place_in_column(place, far))]
    mine = lax.all_to_all(parcels, "far", 0, 0, axis_index_groups=column)
    mine = mine.reshape(far * inputs_here, sent * 2 * CH // far)

    passed = lax.ppermute(passed, "tm", [(source, source + 1) for source in range(times - 1)])
    spectra = pl.pallas_call(
        spectra_kernel,
        out_shape=jax.ShapeDtypeStruct((2, block, CH), jnp.bfloat16),
        in_specs=[VMEM] * 3,
        out_specs=VMEM,
        scratch_shapes=[pltpu.VMEM((2 * CH // LANES, block + frames_here, LANES), jnp.float32)],
        compiler_params=PARAMS,
        cost_estimate=pl.CostEstimate(
            flops=8 * block * 2 * CH, bytes_accessed=1024 * 1024, transcendentals=0
        ),
        name="spectra",
    )(passed, own, gains)
    mine, spectra = lax.optimization_barrier((mine, spectra))
    spectra = spectra.reshape(2, inputs_here, frames_here, CH).transpose(0, 3, 1, 2)

    lines = 2 * sent
    spread = pl.pallas_call(
        spread_kernel,
        out_shape=jax.ShapeDtypeStruct((NEAR * times, lines, far * inputs_here), jnp.bfloat16),
        in_specs=[VMEM],
        out_specs=VMEM,
        scratch_shapes=[pltpu.VMEM(((sent + 1) * 2 * CH // far, far * inputs_here), jnp.float32)],
        compiler_params=PARAMS,
        name="spread",
    )(mine)
    place = lax.axis_index("tm").astype(jnp.int32)
    square = (place // 4)[None]
    spread, square = lax.optimization_barrier((spread, square))
    members = [(near, time) for near in range(NEAR) for time in range(times)]
    members.sort(key=lambda member: place_in_plane(*member, times))
    plane = [[near * times + time for near, time in members]]
    every = lax.all_to_all(spread, ("near", "tm"), 0, 0, axis_index_groups=plane)

    def correlate(*refs):
        correlate_kernel(frames_all, inputs_here, *refs)

    rows = inputs_all // times
    packed = pl.pallas_call(
        correlate,
        out_shape=jax.ShapeDtypeStruct((per_group, rows, inputs_all), jnp.bfloat16),
        in_specs=[SMEM, VMEM],
        out_specs=VMEM,
        compiler_params=PARAMS,
        name="correlate",
    )(square, every)
    squares = [[0, 1, 2, 3], [4, 5, 6, 7]]
    packed = lax.all_to_all(packed, "tm", 0, 0, axis_index_groups=squares)
    tiles = inputs_all // LANES
    visibilities = pl.pallas_call(
        unpack_kernel,
        out_shape=jax.ShapeDtypeStruct((rows * tiles * per_group, LANES), jnp.float32),
        in_specs=[VMEM],
        out_specs=ANY,
        scratch_shapes=[
            pltpu.VMEM(((rows + 1) * tiles * per_group, LANES), jnp.float32),
            pltpu.SemaphoreType.DMA((rows // 16,)),
        ],
        compiler_params=PARAMS,
        name="unpack",
    )(packed)
    visibilities = visibilities.reshape(rows, tiles, per_group, LANES).transpose(0, 2, 1, 3)
    visibilities = visibilities.reshape(rows, per_group, inputs_all)
    return (spectra, visibilities)


def solution(mesh):
    groups, times = mesh.devices.shape
    split = Mesh(mesh.devices.reshape(groups // NEAR, NEAR, times), ("far", "near", "tm"))
    inputs = ("far", "near")
    return jax.shard_map(
        body,
        mesh=split,
        in_specs=(P(inputs, "tm"), P(None, None, inputs)),
        out_specs=(P(None, None, inputs, "tm"), P("tm", inputs, None)),
        check_vma=False,
    )
```

```python
import math

import jax
import jax.numpy as jnp
import numpy as np
from jax import lax
from jax.experimental import pallas as pl
from jax.experimental.pallas import tpu as pltpu
from jax.sharding import Mesh, PartitionSpec as P

NFFT = 2048
CH = 256
FIRST = 384
TAPS = 4
NEAR = 4
EARLY = 4
STEP = 256
LANES = 128
VMEM = pl.BlockSpec(memory_space=pltpu.VMEM)
ANY = pl.BlockSpec(memory_space=pl.ANY)
SMEM = pl.BlockSpec(memory_space=pltpu.SMEM)
OWN_PART_VMEM = 59 * 1024 * 1024 + 768 * 1024
PARAMS = pltpu.CompilerParams(vmem_limit_bytes=32 * 1024 * 1024)


def filter_window():
    length = TAPS * NFFT
    position = np.arange(length, dtype=np.float64)
    centred = (position - 0.5 * length + 0.5) / NFFT
    hann_taper = 0.5 - 0.5 * np.cos(2.0 * math.pi * (position + 0.5) / length)
    return np.sinc(centred) * hann_taper


def build_table(window):
    norm_scale = 1.0 / np.sqrt(np.sum(window * window))
    sample = np.arange(NFFT)[:, None]
    channel = FIRST + np.arange(CH)[None, :]
    phase_angle = 2.0 * math.pi / NFFT * (sample * channel % NFFT)
    cosine = np.cos(phase_angle) * norm_scale
    sine = -np.sin(phase_angle) * norm_scale
    return np.concatenate([cosine, sine], axis=1).astype(jnp.bfloat16)


def tapped_block(samples_ref, window_ref, frames_sent, block):
    inputs_here, count = samples_ref.shape
    frames_here = count // NFFT
    low = block * STEP
    sums = []
    for frame in range(frames_sent):
        total = jnp.zeros((inputs_here, STEP), jnp.float32)
        for tap in range(TAPS):
            source = frame - TAPS + 1 + tap
            if 0 <= source < frames_here:
                start = source * NFFT + low
                values = samples_ref[:, start : start + STEP]
                weights = window_ref[tap : tap + 1, low : low + STEP]
                total = total + weights * values.astype(jnp.float32)
        sums.append(total)
    pairs = [
        jnp.concatenate(sums[frame : frame + 2], axis=0).astype(jnp.bfloat16)
        for frame in range(0, frames_sent, 2)
    ]
    return jnp.concatenate(pairs, axis=0)


def turn_granules(blocks, size):
    count = len(blocks)
    lanes = count * size
    granule = lax.broadcasted_iota(jnp.int32, blocks[0].shape, 1) // size
    blocks = list(blocks)
    distance = count // 2
    while distance:
        upper = (granule & distance) != 0
        shift = distance * size
        for index in range(count):
            if index & distance:
                continue
            low, high = blocks[index], blocks[index + distance]
            blocks[index] = jnp.where(upper, pltpu.roll(high, shift, 1), low)
            blocks[index + distance] = jnp.where(upper, high, pltpu.roll(low, lanes - shift, 1))
        distance //= 2
    return blocks


def place_in_column(place, far):
    return (far * 5 // 8 + far - place) % far


def own_part_kernel(
    far,
    samples_hbm,
    window_hbm,
    twiddle_hbm,
    gains_hbm,
    own_hbm,
    passed_hbm,
    parcels_hbm,
    samples_ref,
    window_ref,
    twiddle_ref,
    gains_ref,
    direct_ref,
    parcels_ref,
    arrived,
    left,
):
    inputs_here = gains_ref.shape[1]
    frames_here = samples_hbm.shape[1] // NFFT
    blocks = range(NFFT // STEP)
    fetches = []

    def fetch(source, target):
        fetches.append(pltpu.make_async_copy(source, target, arrived.at[len(fetches)]))
        fetches[-1].start()
        return fetches[-1]

    samples_in = fetch(samples_hbm, samples_ref)
    window_in = fetch(window_hbm, window_ref)
    table_in = []
    for block in blocks[: len(blocks) // 2]:
        rows = pl.ds(block * STEP, STEP)
        table_in.append(fetch(twiddle_hbm.at[rows, :], twiddle_ref.at[rows, :]))
    gains_in = fetch(gains_hbm, gains_ref)
    samples_in.wait()
    window_in.wait()
    total = None
    sent = frames_here + EARLY
    for block, table in enumerate(table_in):
        tapped = [
            tapped_block(samples_ref, window_ref, sent, half + block)
            for half in (0, len(table_in))
        ]
        table.wait()
        product = jnp.dot(
            jnp.concatenate(tapped, axis=0),
            twiddle_ref[block * STEP : (block + 1) * STEP, :],
            preferred_element_type=jnp.float32,
        )
        total = product if total is None else total + product
    channel = FIRST + lax.broadcasted_iota(jnp.int32, (1, 2 * CH), 1)
    sign = (1 - 2 * (channel % 2)).astype(jnp.float32)
    direct_ref[...] = total[: sent * inputs_here] + sign * total[sent * inputs_here :]
    own_rows = own_hbm.shape[0]
    passed_rows = passed_hbm.shape[0]
    stores = [
        pltpu.make_async_copy(direct_ref.at[pl.ds(0, own_rows), :], own_hbm, left.at[0]),
        pltpu.make_async_copy(
            direct_ref.at[pl.ds(own_rows, passed_rows), :], passed_hbm, left.at[1]
        ),
    ]
    for store in stores:
        store.start()
    gains_in.wait()
    gain_re = gains_ref[0]
    gain_im = gains_ref[1]
    parts = []
    for frame in range(frames_here + EARLY):
        direct = direct_ref[frame * inputs_here : (frame + 1) * inputs_here, :]
        direct_re = direct[:, :CH]
        direct_im = direct[:, CH:]
        parts.append(
            (
                gain_re * direct_re - gain_im * direct_im,
                gain_re * direct_im + gain_im * direct_re,
            )
        )
    slots = [
        [(part, frame) for frame in range(first, first + 8)]
        for first in range(0, frames_here, 8)
        for part in range(2)
    ]
    slots.append([(part, frames_here + frame) for part in range(2) for frame in range(EARLY)])
    per_far = CH // far
    for place, slot in enumerate(slots):
        columns = slice(place * LANES, (place + 1) * LANES)
        blocks = []
        for half in range(CH // LANES):
            lanes = slice(half * LANES, (half + 1) * LANES)
            blocks += turn_granules([parts[frame][part][:, lanes] for part, frame in slot], per_far)
        listed = sorted(range(far), key=lambda target: place_in_column(target, far))
        for index in range(0, far, 2):
            rows = slice(index * inputs_here, (index + 2) * inputs_here)
            parcels_ref[rows, columns] = jnp.concatenate(
                [blocks[target] for target in listed[index : index + 2]], axis=0
            ).astype(jnp.bfloat16)
        lanes = pl.ds(place * LANES, LANES)
        stores.append(
            pltpu.make_async_copy(
                parcels_ref.at[:, lanes], parcels_hbm.at[:, lanes], left.at[len(stores)]
            )
        )
        stores[-1].start()
    for store in stores:
        store.wait()


def spectra_kernel(passed_ref, own_ref, gains_ref, spectra_ref, rows_ref):
    inputs_here = gains_ref.shape[1]
    frames_here = own_ref.shape[0] // inputs_here
    slabs = CH // LANES
    gain_re = gains_ref[0]
    gain_im = gains_ref[1]
    for frame in range(frames_here):
        block = slice(frame * inputs_here, (frame + 1) * inputs_here)
        direct = own_ref[block, :]
        if frame < TAPS - 1:
            direct = direct + passed_ref[block, :]
        direct_re = direct[:, :CH]
        direct_im = direct[:, CH:]
        rows = pl.ds(frame, inputs_here, stride=frames_here)
        real_part = gain_re * direct_re - gain_im * direct_im
        imag_part = gain_re * direct_im + gain_im * direct_re
        for slab in range(slabs):
            columns = slice(slab * LANES, (slab + 1) * LANES)
            rows_ref[slab, rows, :] = real_part[:, columns]
            rows_ref[slabs + slab, rows, :] = imag_part[:, columns]
    for part in range(2):
        for slab in range(slabs):
            columns = slice(slab * LANES, (slab + 1) * LANES)
            values = rows_ref[part * slabs + slab, : own_ref.shape[0], :]
            spectra_ref[part, :, columns] = values.astype(jnp.bfloat16)


def channel_of(time):
    return time % 4


def place_in_square(member):
    return member ^ member >> 1


def place_in_plane(near, time, times):
    count = NEAR * times
    middle = NEAR // 2 * times + times // 2
    return 3 * (near * times + time + count - middle) % count


def spread_kernel(mine_ref, parcels_ref, turned_ref):
    count, rows, width = parcels_ref.shape
    times = count // NEAR
    stride = mine_ref.shape[1] // rows
    for place in range(0, mine_ref.shape[1], LANES):
        values = mine_ref[:, place : place + LANES].astype(jnp.float32)
        turned_ref[place : place + LANES, :] = values.T
    for near in range(NEAR):
        for channel in range(stride // NEAR):
            start = near * (stride // NEAR) + channel
            values = turned_ref[pl.ds(start, rows, stride=stride), :].astype(jnp.bfloat16)
            for time in range(times):
                if channel_of(time) == channel:
                    parcels_ref[place_in_plane(near, time, times)] = values


def correlate_kernel(frames_all, inputs_here, place_ref, every_ref, packed_ref):
    count, lines, width = every_ref.shape
    blocks, rows, inputs_all = packed_ref.shape
    times = count // NEAR
    main = lines - 2 * EARLY
    carry = None
    lined = []
    for time in range(times):
        pieces = [every_ref[place_in_plane(near, time, times)] for near in range(NEAR)]
        wide = jnp.concatenate([piece.astype(jnp.float32) for piece in pieces], axis=1)
        tiles = [wide[start : start + 8] for start in range(0, lines, 8)]
        if carry is not None:
            early = lax.broadcasted_iota(jnp.int32, carry.shape, 0) < EARLY
            tiles[0] = tiles[0] + jnp.where(early, carry, 0.0)
            tiles[1] = tiles[1] + jnp.where(early, pltpu.roll(carry, 8 - EARLY, 0), 0.0)
        carry = tiles[-1]
        lined += tiles[:-1]
    far = width // inputs_here
    target = lax.broadcasted_iota(jnp.int32, (1, inputs_all), 1)
    near = target // inputs_here % NEAR
    listed = place_in_column(target // (inputs_here * NEAR), far)
    source = near * width + listed * inputs_here + target % inputs_here
    chosen = lax.broadcasted_iota(jnp.int32, (inputs_all, inputs_all), 0) == source
    ordered = jnp.dot(
        jnp.concatenate(lined, axis=0).astype(jnp.bfloat16),
        chosen.astype(jnp.float32).astype(jnp.bfloat16),
        preferred_element_type=jnp.float32,
    )
    right = ordered.astype(jnp.bfloat16)
    twisted = []
    for start in range(0, times * main, 16):
        twisted.append(ordered[start + 8 : start + 16])
        twisted.append(-ordered[start : start + 8])
    twisted = jnp.concatenate(twisted, axis=0).astype(jnp.bfloat16)
    held = blocks * rows
    first = place_ref[0] * held
    col_index = lax.broadcasted_iota(jnp.int32, (held, inputs_all), 1)
    row_index = lax.broadcasted_iota(jnp.int32, (held, inputs_all), 0) + first
    left = [jnp.where(first == 0, side[:, :held], side[:, held:]) for side in (right, twisted)]
    both = lax.dot_general(
        jnp.concatenate(left, axis=1),
        right,
        (((0,), (0,)), ((), ())),
        preferred_element_type=jnp.float32,
    )
    values = jnp.where(row_index <= col_index, both[:held], both[held:]) * (1.0 / frames_all)
    values = values.astype(jnp.bfloat16)
    for block in range(blocks):
        packed_ref[place_in_square(block)] = values[block * rows : (block + 1) * rows]


def unpack_kernel(packed_ref, lines_hbm, lines_ref, left):
    channels, count, width = packed_ref.shape
    tiles = width // LANES
    stores = []
    for first in range(0, count, 16):
        start = first * tiles * channels
        for channel in range(channels):
            values = packed_ref[place_in_square(channel), first : first + 16, :]
            values = values.astype(jnp.float32)
            for tile in range(tiles):
                lines = pl.ds(start + tile * channels + channel, 16, stride=tiles * channels)
                lines_ref[lines, :] = values[:, tile * LANES : (tile + 1) * LANES]
        block = pl.ds(start, 16 * tiles * channels)
        stores.append(
            pltpu.make_async_copy(lines_ref.at[block, :], lines_hbm.at[block, :], left.at[len(stores)])
        )
        stores[-1].start()
    for store in stores:
        store.wait()


def body(samples, gains):
    inputs_here = samples.shape[0]
    frames_here = samples.shape[1] // NFFT
    times = lax.axis_size("tm")
    far = lax.axis_size("far")
    groups = far * NEAR
    per_group = CH // groups
    inputs_all = inputs_here * groups
    frames_all = frames_here * times
    block = inputs_here * frames_here

    window = filter_window()
    twiddle = jnp.asarray(build_table(window)[: NFFT // 2])
    window_taps = jnp.asarray(window.astype(np.float32).reshape(TAPS, NFFT))

    sent = frames_here + EARLY
    gains = gains.transpose(0, 2, 1)

    def own_part(*refs):
        own_part_kernel(far, *refs)

    own, passed, parcels = pl.pallas_call(
        own_part,
        out_shape=(
            jax.ShapeDtypeStruct((block, 2 * CH), jnp.float32),
            jax.ShapeDtypeStruct(((TAPS - 1) * inputs_here, 2 * CH), jnp.float32),
            jax.ShapeDtypeStruct((far * inputs_here, sent * 2 * CH // far), jnp.bfloat16),
        ),
        in_specs=[ANY] * 4,
        out_specs=(ANY, ANY, ANY),
        scratch_shapes=[
            pltpu.VMEM(samples.shape, jnp.bfloat16),
            pltpu.VMEM(window_taps.shape, jnp.float32),
            pltpu.VMEM(twiddle.shape, jnp.bfloat16),
            pltpu.VMEM(gains.shape, jnp.float32),
            pltpu.VMEM((sent * inputs_here, 2 * CH), jnp.float32),
            pltpu.VMEM((far * inputs_here, sent * 2 * CH // far), jnp.bfloat16),
            pltpu.SemaphoreType.DMA((3 + NFFT // (2 * STEP),)),
            pltpu.SemaphoreType.DMA((2 + sent // 4,)),
        ],
        compiler_params=pltpu.CompilerParams(vmem_limit_bytes=OWN_PART_VMEM),
        cost_estimate=pl.CostEstimate(
            flops=2 * sent * inputs_here * NFFT * 2 * CH,
            bytes_accessed=3 * 1024 * 1024,
            transcendentals=0,
        ),
        name="own_part",
    )(samples, window_taps, twiddle, gains)

    parcels = parcels.reshape(far, inputs_here, sent * 2 * CH // far)
    column = [sorted(range(far), key=lambda place: place_in_column(place, far))]
    mine = lax.all_to_all(parcels, "far", 0, 0, axis_index_groups=column)
    mine = mine.reshape(far * inputs_here, sent * 2 * CH // far)

    passed = lax.ppermute(passed, "tm", [(source, source + 1) for source in range(times - 1)])
    spectra = pl.pallas_call(
        spectra_kernel,
        out_shape=jax.ShapeDtypeStruct((2, block, CH), jnp.bfloat16),
        in_specs=[VMEM] * 3,
        out_specs=VMEM,
        scratch_shapes=[pltpu.VMEM((2 * CH // LANES, block + frames_here, LANES), jnp.float32)],
        compiler_params=PARAMS,
        cost_estimate=pl.CostEstimate(
            flops=8 * block * 2 * CH, bytes_accessed=1024 * 1024, transcendentals=0
        ),
        name="spectra",
    )(passed, own, gains)
    mine, spectra = lax.optimization_barrier((mine, spectra))
    spectra = spectra.reshape(2, inputs_here, frames_here, CH).transpose(0, 3, 1, 2)

    lines = 2 * sent
    spread = pl.pallas_call(
        spread_kernel,
        out_shape=jax.ShapeDtypeStruct((NEAR * times, lines, far * inputs_here), jnp.bfloat16),
        in_specs=[VMEM],
        out_specs=VMEM,
        scratch_shapes=[pltpu.VMEM(((sent + 1) * 2 * CH // far, far * inputs_here), jnp.float32)],
        compiler_params=PARAMS,
        name="spread",
    )(mine)
    place = lax.axis_index("tm").astype(jnp.int32)
    square = (place // 4)[None]
    spread, square = lax.optimization_barrier((spread, square))
    members = [(near, time) for near in range(NEAR) for time in range(times)]
    members.sort(key=lambda member: place_in_plane(*member, times))
    plane = [[near * times + time for near, time in members]]
    every = lax.all_to_all(spread, ("near", "tm"), 0, 0, axis_index_groups=plane)

    def correlate(*refs):
        correlate_kernel(frames_all, inputs_here, *refs)

    rows = inputs_all // times
    packed = pl.pallas_call(
        correlate,
        out_shape=jax.ShapeDtypeStruct((per_group, rows, inputs_all), jnp.bfloat16),
        in_specs=[SMEM, VMEM],
        out_specs=VMEM,
        compiler_params=PARAMS,
        name="correlate",
    )(square, every)
    listed = sorted(range(per_group), key=place_in_square)
    squares = [[start + member for member in listed] for start in (0, per_group)]
    packed = lax.all_to_all(packed, "tm", 0, 0, axis_index_groups=squares)
    tiles = inputs_all // LANES
    visibilities = pl.pallas_call(
        unpack_kernel,
        out_shape=jax.ShapeDtypeStruct((rows * tiles * per_group, LANES), jnp.float32),
        in_specs=[VMEM],
        out_specs=ANY,
        scratch_shapes=[
            pltpu.VMEM(((rows + 1) * tiles * per_group, LANES), jnp.float32),
            pltpu.SemaphoreType.DMA((rows // 16,)),
        ],
        compiler_params=PARAMS,
        name="unpack",
    )(packed)
    visibilities = visibilities.reshape(rows, tiles, per_group, LANES).transpose(0, 2, 1, 3)
    visibilities = visibilities.reshape(rows, per_group, inputs_all)
    return (spectra, visibilities)


def solution(mesh):
    groups, times = mesh.devices.shape
    split = Mesh(mesh.devices.reshape(groups // NEAR, NEAR, times), ("far", "near", "tm"))
    inputs = ("far", "near")
    return jax.shard_map(
        body,
        mesh=split,
        in_specs=(P(inputs, "tm"), P(None, None, inputs)),
        out_specs=(P(None, None, inputs, "tm"), P("tm", inputs, None)),
        check_vma=False,
    )
```

```python
import math

import jax
import jax.numpy as jnp
import numpy as np
from jax import lax
from jax.experimental import pallas as pl
from jax.experimental.pallas import tpu as pltpu
from jax.sharding import Mesh, PartitionSpec as P

NFFT = 2048
CH = 256
FIRST = 384
TAPS = 4
NEAR = 4
EARLY = 4
STEP = 256
LANES = 128
VMEM = pl.BlockSpec(memory_space=pltpu.VMEM)
ANY = pl.BlockSpec(memory_space=pl.ANY)
SMEM = pl.BlockSpec(memory_space=pltpu.SMEM)
OWN_PART_VMEM = 59 * 1024 * 1024 + 768 * 1024
PARAMS = pltpu.CompilerParams(vmem_limit_bytes=32 * 1024 * 1024)


def filter_window():
    length = TAPS * NFFT
    position = np.arange(length, dtype=np.float64)
    centred = (position - 0.5 * length + 0.5) / NFFT
    hann_taper = 0.5 - 0.5 * np.cos(2.0 * math.pi * (position + 0.5) / length)
    return np.sinc(centred) * hann_taper


def build_table(window):
    norm_scale = 1.0 / np.sqrt(np.sum(window * window))
    sample = np.arange(NFFT)[:, None]
    channel = FIRST + np.arange(CH)[None, :]
    phase_angle = 2.0 * math.pi / NFFT * (sample * channel % NFFT)
    cosine = np.cos(phase_angle) * norm_scale
    sine = -np.sin(phase_angle) * norm_scale
    return np.concatenate([cosine, sine], axis=1).astype(jnp.bfloat16)


def tapped_block(samples_ref, window_ref, frames_sent, block):
    inputs_here, count = samples_ref.shape
    frames_here = count // NFFT
    low = block * STEP
    sums = []
    for frame in range(frames_sent):
        total = jnp.zeros((inputs_here, STEP), jnp.float32)
        for tap in range(TAPS):
            source = frame - TAPS + 1 + tap
            if 0 <= source < frames_here:
                start = source * NFFT + low
                values = samples_ref[:, start : start + STEP]
                weights = window_ref[tap : tap + 1, low : low + STEP]
                total = total + weights * values.astype(jnp.float32)
        sums.append(total)
    pairs = [
        jnp.concatenate(sums[frame : frame + 2], axis=0).astype(jnp.bfloat16)
        for frame in range(0, frames_sent, 2)
    ]
    return jnp.concatenate(pairs, axis=0)


def turn_granules(blocks, size):
    count = len(blocks)
    lanes = count * size
    granule = lax.broadcasted_iota(jnp.int32, blocks[0].shape, 1) // size
    blocks = list(blocks)
    distance = count // 2
    while distance:
        upper = (granule & distance) != 0
        shift = distance * size
        for index in range(count):
            if index & distance:
                continue
            low, high = blocks[index], blocks[index + distance]
            blocks[index] = jnp.where(upper, pltpu.roll(high, shift, 1), low)
            blocks[index + distance] = jnp.where(upper, high, pltpu.roll(low, lanes - shift, 1))
        distance //= 2
    return blocks


def place_in_column(place, far):
    return (place + far * 3 // 8) % far


def own_part_kernel(
    far,
    samples_hbm,
    window_hbm,
    twiddle_hbm,
    gains_hbm,
    own_hbm,
    passed_hbm,
    parcels_hbm,
    samples_ref,
    window_ref,
    twiddle_ref,
    gains_ref,
    direct_ref,
    parcels_ref,
    arrived,
    left,
):
    inputs_here = gains_ref.shape[1]
    frames_here = samples_hbm.shape[1] // NFFT
    blocks = range(NFFT // STEP)
    fetches = []

    def fetch(source, target):
        fetches.append(pltpu.make_async_copy(source, target, arrived.at[len(fetches)]))
        fetches[-1].start()
        return fetches[-1]

    samples_in = fetch(samples_hbm, samples_ref)
    window_in = fetch(window_hbm, window_ref)
    table_in = []
    for block in blocks[: len(blocks) // 2]:
        rows = pl.ds(block * STEP, STEP)
        table_in.append(fetch(twiddle_hbm.at[rows, :], twiddle_ref.at[rows, :]))
    gains_in = fetch(gains_hbm, gains_ref)
    samples_in.wait()
    window_in.wait()
    total = None
    sent = frames_here + EARLY
    for block, table in enumerate(table_in):
        tapped = [
            tapped_block(samples_ref, window_ref, sent, half + block)
            for half in (0, len(table_in))
        ]
        table.wait()
        product = jnp.dot(
            jnp.concatenate(tapped, axis=0),
            twiddle_ref[block * STEP : (block + 1) * STEP, :],
            preferred_element_type=jnp.float32,
        )
        total = product if total is None else total + product
    channel = FIRST + lax.broadcasted_iota(jnp.int32, (1, 2 * CH), 1)
    sign = (1 - 2 * (channel % 2)).astype(jnp.float32)
    direct_ref[...] = total[: sent * inputs_here] + sign * total[sent * inputs_here :]
    own_rows = own_hbm.shape[0]
    passed_rows = passed_hbm.shape[0]
    stores = [
        pltpu.make_async_copy(direct_ref.at[pl.ds(0, own_rows), :], own_hbm, left.at[0]),
        pltpu.make_async_copy(
            direct_ref.at[pl.ds(own_rows, passed_rows), :], passed_hbm, left.at[1]
        ),
    ]
    for store in stores:
        store.start()
    gains_in.wait()
    gain_re = gains_ref[0]
    gain_im = gains_ref[1]
    parts = []
    for frame in range(frames_here + EARLY):
        direct = direct_ref[frame * inputs_here : (frame + 1) * inputs_here, :]
        direct_re = direct[:, :CH]
        direct_im = direct[:, CH:]
        parts.append(
            (
                gain_re * direct_re - gain_im * direct_im,
                gain_re * direct_im + gain_im * direct_re,
            )
        )
    slots = [
        [(part, frame) for frame in range(first, first + 8)]
        for first in range(0, frames_here, 8)
        for part in range(2)
    ]
    slots.append([(part, frames_here + frame) for part in range(2) for frame in range(EARLY)])
    per_far = CH // far
    for place, slot in enumerate(slots):
        columns = slice(place * LANES, (place + 1) * LANES)
        blocks = []
        for half in range(CH // LANES):
            lanes = slice(half * LANES, (half + 1) * LANES)
            blocks += turn_granules([parts[frame][part][:, lanes] for part, frame in slot], per_far)
        listed = sorted(range(far), key=lambda target: place_in_column(target, far))
        for index in range(0, far, 2):
            rows = slice(index * inputs_here, (index + 2) * inputs_here)
            parcels_ref[rows, columns] = jnp.concatenate(
                [blocks[target] for target in listed[index : index + 2]], axis=0
            ).astype(jnp.bfloat16)
        lanes = pl.ds(place * LANES, LANES)
        stores.append(
            pltpu.make_async_copy(
                parcels_ref.at[:, lanes], parcels_hbm.at[:, lanes], left.at[len(stores)]
            )
        )
        stores[-1].start()
    for store in stores:
        store.wait()


def spectra_kernel(passed_ref, own_ref, gains_ref, spectra_ref, rows_ref):
    inputs_here = gains_ref.shape[1]
    frames_here = own_ref.shape[0] // inputs_here
    slabs = CH // LANES
    gain_re = gains_ref[0]
    gain_im = gains_ref[1]
    for frame in range(frames_here):
        block = slice(frame * inputs_here, (frame + 1) * inputs_here)
        direct = own_ref[block, :]
        if frame < TAPS - 1:
            direct = direct + passed_ref[block, :]
        direct_re = direct[:, :CH]
        direct_im = direct[:, CH:]
        rows = pl.ds(frame, inputs_here, stride=frames_here)
        real_part = gain_re * direct_re - gain_im * direct_im
        imag_part = gain_re * direct_im + gain_im * direct_re
        for slab in range(slabs):
            columns = slice(slab * LANES, (slab + 1) * LANES)
            rows_ref[slab, rows, :] = real_part[:, columns]
            rows_ref[slabs + slab, rows, :] = imag_part[:, columns]
    for part in range(2):
        for slab in range(slabs):
            columns = slice(slab * LANES, (slab + 1) * LANES)
            values = rows_ref[part * slabs + slab, : own_ref.shape[0], :]
            spectra_ref[part, :, columns] = values.astype(jnp.bfloat16)


def channel_of(time):
    return time % 4


def place_in_plane(near, time, times):
    count = NEAR * times
    middle = NEAR // 2 * times + times // 2
    return 3 * (near * times + time + count - middle) % count


def spread_kernel(mine_ref, parcels_ref, turned_ref):
    count, rows, width = parcels_ref.shape
    times = count // NEAR
    stride = mine_ref.shape[1] // rows
    for place in range(0, mine_ref.shape[1], LANES):
        values = mine_ref[:, place : place + LANES].astype(jnp.float32)
        turned_ref[place : place + LANES, :] = values.T
    for near in range(NEAR):
        for channel in range(stride // NEAR):
            start = near * (stride // NEAR) + channel
            values = turned_ref[pl.ds(start, rows, stride=stride), :].astype(jnp.bfloat16)
            for time in range(times):
                if channel_of(time) == channel:
                    parcels_ref[place_in_plane(near, time, times)] = values


def correlate_kernel(frames_all, inputs_here, place_ref, every_ref, packed_ref):
    count, lines, width = every_ref.shape
    blocks, rows, inputs_all = packed_ref.shape
    times = count // NEAR
    main = lines - 2 * EARLY
    carry = None
    lined = []
    for time in range(times):
        pieces = [every_ref[place_in_plane(near, time, times)] for near in range(NEAR)]
        wide = jnp.concatenate([piece.astype(jnp.float32) for piece in pieces], axis=1)
        tiles = [wide[start : start + 8] for start in range(0, lines, 8)]
        if carry is not None:
            early = lax.broadcasted_iota(jnp.int32, carry.shape, 0) < EARLY
            tiles[0] = tiles[0] + jnp.where(early, carry, 0.0)
            tiles[1] = tiles[1] + jnp.where(early, pltpu.roll(carry, 8 - EARLY, 0), 0.0)
        carry = tiles[-1]
        lined += tiles[:-1]
    far = width // inputs_here
    target = lax.broadcasted_iota(jnp.int32, (1, inputs_all), 1)
    near = target // inputs_here % NEAR
    listed = place_in_column(target // (inputs_here * NEAR), far)
    source = near * width + listed * inputs_here + target % inputs_here
    chosen = lax.broadcasted_iota(jnp.int32, (inputs_all, inputs_all), 0) == source
    ordered = jnp.dot(
        jnp.concatenate(lined, axis=0).astype(jnp.bfloat16),
        chosen.astype(jnp.float32).astype(jnp.bfloat16),
        preferred_element_type=jnp.float32,
    )
    right = ordered.astype(jnp.bfloat16)
    twisted = []
    for start in range(0, times * main, 16):
        twisted.append(ordered[start + 8 : start + 16])
        twisted.append(-ordered[start : start + 8])
    twisted = jnp.concatenate(twisted, axis=0).astype(jnp.bfloat16)
    held = blocks * rows
    first = place_ref[0] * held
    col_index = lax.broadcasted_iota(jnp.int32, (held, inputs_all), 1)
    row_index = lax.broadcasted_iota(jnp.int32, (held, inputs_all), 0) + first
    left = [jnp.where(first == 0, side[:, :held], side[:, held:]) for side in (right, twisted)]
    both = lax.dot_general(
        jnp.concatenate(left, axis=1),
        right,
        (((0,), (0,)), ((), ())),
        preferred_element_type=jnp.float32,
    )
    values = jnp.where(row_index <= col_index, both[:held], both[held:]) * (1.0 / frames_all)
    values = values.astype(jnp.bfloat16)
    for block in range(blocks):
        packed_ref[block] = values[block * rows : (block + 1) * rows]


def unpack_kernel(packed_ref, lines_hbm, lines_ref, left):
    channels, count, width = packed_ref.shape
    tiles = width // LANES
    stores = []
    for first in range(0, count, 16):
        start = first * tiles * channels
        for channel in range(channels):
            values = packed_ref[channel, first : first + 16, :].astype(jnp.float32)
            for tile in range(tiles):
                lines = pl.ds(start + tile * channels + channel, 16, stride=tiles * channels)
                lines_ref[lines, :] = values[:, tile * LANES : (tile + 1) * LANES]
        block = pl.ds(start, 16 * tiles * channels)
        stores.append(
            pltpu.make_async_copy(lines_ref.at[block, :], lines_hbm.at[block, :], left.at[len(stores)])
        )
        stores[-1].start()
    for store in stores:
        store.wait()


def body(samples, gains):
    inputs_here = samples.shape[0]
    frames_here = samples.shape[1] // NFFT
    times = lax.axis_size("tm")
    far = lax.axis_size("far")
    groups = far * NEAR
    per_group = CH // groups
    inputs_all = inputs_here * groups
    frames_all = frames_here * times
    block = inputs_here * frames_here

    window = filter_window()
    twiddle = jnp.asarray(build_table(window)[: NFFT // 2])
    window_taps = jnp.asarray(window.astype(np.float32).reshape(TAPS, NFFT))

    sent = frames_here + EARLY
    gains = gains.transpose(0, 2, 1)

    def own_part(*refs):
        own_part_kernel(far, *refs)

    own, passed, parcels = pl.pallas_call(
        own_part,
        out_shape=(
            jax.ShapeDtypeStruct((block, 2 * CH), jnp.float32),
            jax.ShapeDtypeStruct(((TAPS - 1) * inputs_here, 2 * CH), jnp.float32),
            jax.ShapeDtypeStruct((far * inputs_here, sent * 2 * CH // far), jnp.bfloat16),
        ),
        in_specs=[ANY] * 4,
        out_specs=(ANY, ANY, ANY),
        scratch_shapes=[
            pltpu.VMEM(samples.shape, jnp.bfloat16),
            pltpu.VMEM(window_taps.shape, jnp.float32),
            pltpu.VMEM(twiddle.shape, jnp.bfloat16),
            pltpu.VMEM(gains.shape, jnp.float32),
            pltpu.VMEM((sent * inputs_here, 2 * CH), jnp.float32),
            pltpu.VMEM((far * inputs_here, sent * 2 * CH // far), jnp.bfloat16),
            pltpu.SemaphoreType.DMA((3 + NFFT // (2 * STEP),)),
            pltpu.SemaphoreType.DMA((2 + sent // 4,)),
        ],
        compiler_params=pltpu.CompilerParams(vmem_limit_bytes=OWN_PART_VMEM),
        cost_estimate=pl.CostEstimate(
            flops=2 * sent * inputs_here * NFFT * 2 * CH,
            bytes_accessed=3 * 1024 * 1024,
            transcendentals=0,
        ),
        name="own_part",
    )(samples, window_taps, twiddle, gains)

    parcels = parcels.reshape(far, inputs_here, sent * 2 * CH // far)
    column = [sorted(range(far), key=lambda place: place_in_column(place, far))]
    mine = lax.all_to_all(parcels, "far", 0, 0, axis_index_groups=column)
    mine = mine.reshape(far * inputs_here, sent * 2 * CH // far)

    passed = lax.ppermute(passed, "tm", [(source, source + 1) for source in range(times - 1)])
    spectra = pl.pallas_call(
        spectra_kernel,
        out_shape=jax.ShapeDtypeStruct((2, block, CH), jnp.bfloat16),
        in_specs=[VMEM] * 3,
        out_specs=VMEM,
        scratch_shapes=[pltpu.VMEM((2 * CH // LANES, block + frames_here, LANES), jnp.float32)],
        compiler_params=PARAMS,
        cost_estimate=pl.CostEstimate(
            flops=8 * block * 2 * CH, bytes_accessed=1024 * 1024, transcendentals=0
        ),
        name="spectra",
    )(passed, own, gains)
    mine, spectra = lax.optimization_barrier((mine, spectra))
    spectra = spectra.reshape(2, inputs_here, frames_here, CH).transpose(0, 3, 1, 2)

    lines = 2 * sent
    spread = pl.pallas_call(
        spread_kernel,
        out_shape=jax.ShapeDtypeStruct((NEAR * times, lines, far * inputs_here), jnp.bfloat16),
        in_specs=[VMEM],
        out_specs=VMEM,
        scratch_shapes=[pltpu.VMEM(((sent + 1) * 2 * CH // far, far * inputs_here), jnp.float32)],
        compiler_params=PARAMS,
        name="spread",
    )(mine)
    place = lax.axis_index("tm").astype(jnp.int32)
    square = (place // 4)[None]
    spread, square = lax.optimization_barrier((spread, square))
    members = [(near, time) for near in range(NEAR) for time in range(times)]
    members.sort(key=lambda member: place_in_plane(*member, times))
    plane = [[near * times + time for near, time in members]]
    every = lax.all_to_all(spread, ("near", "tm"), 0, 0, axis_index_groups=plane)

    def correlate(*refs):
        correlate_kernel(frames_all, inputs_here, *refs)

    rows = inputs_all // times
    packed = pl.pallas_call(
        correlate,
        out_shape=jax.ShapeDtypeStruct((per_group, rows, inputs_all), jnp.bfloat16),
        in_specs=[SMEM, VMEM],
        out_specs=VMEM,
        compiler_params=PARAMS,
        name="correlate",
    )(square, every)
    squares = [[0, 1, 2, 3], [4, 5, 6, 7]]
    packed = lax.all_to_all(packed, "tm", 0, 0, axis_index_groups=squares)
    tiles = inputs_all // LANES
    visibilities = pl.pallas_call(
        unpack_kernel,
        out_shape=jax.ShapeDtypeStruct((rows * tiles * per_group, LANES), jnp.float32),
        in_specs=[VMEM],
        out_specs=ANY,
        scratch_shapes=[
            pltpu.VMEM(((rows + 1) * tiles * per_group, LANES), jnp.float32),
            pltpu.SemaphoreType.DMA((rows // 16,)),
        ],
        compiler_params=PARAMS,
        name="unpack",
    )(packed)
    visibilities = visibilities.reshape(rows, tiles, per_group, LANES).transpose(0, 2, 1, 3)
    visibilities = visibilities.reshape(rows, per_group, inputs_all)
    return (spectra, visibilities)


def solution(mesh):
    groups, times = mesh.devices.shape
    split = Mesh(mesh.devices.reshape(groups // NEAR, NEAR, times), ("far", "near", "tm"))
    inputs = ("far", "near")
    return jax.shard_map(
        body,
        mesh=split,
        in_specs=(P(inputs, "tm"), P(None, None, inputs)),
        out_specs=(P(None, None, inputs, "tm"), P("tm", inputs, None)),
        check_vma=False,
    )
```

```python
import math

import jax
import jax.numpy as jnp
import numpy as np
from jax import lax
from jax.experimental import pallas as pl
from jax.experimental.pallas import tpu as pltpu
from jax.sharding import Mesh, PartitionSpec as P

NFFT = 2048
CH = 256
FIRST = 384
TAPS = 4
NEAR = 4
EARLY = 4
STEP = 256
LANES = 128
VMEM = pl.BlockSpec(memory_space=pltpu.VMEM)
ANY = pl.BlockSpec(memory_space=pl.ANY)
SMEM = pl.BlockSpec(memory_space=pltpu.SMEM)
OWN_PART_VMEM = 59 * 1024 * 1024 + 768 * 1024
PARAMS = pltpu.CompilerParams(vmem_limit_bytes=32 * 1024 * 1024)


def filter_window():
    length = TAPS * NFFT
    position = np.arange(length, dtype=np.float64)
    centred = (position - 0.5 * length + 0.5) / NFFT
    hann_taper = 0.5 - 0.5 * np.cos(2.0 * math.pi * (position + 0.5) / length)
    return np.sinc(centred) * hann_taper


def build_table(window):
    norm_scale = 1.0 / np.sqrt(np.sum(window * window))
    sample = np.arange(NFFT)[:, None]
    channel = FIRST + np.arange(CH)[None, :]
    phase_angle = 2.0 * math.pi / NFFT * (sample * channel % NFFT)
    cosine = np.cos(phase_angle) * norm_scale
    sine = -np.sin(phase_angle) * norm_scale
    return np.concatenate([cosine, sine], axis=1).astype(jnp.bfloat16)


def tapped_block(samples_ref, window_ref, frames_sent, block):
    inputs_here, count = samples_ref.shape
    frames_here = count // NFFT
    low = block * STEP
    sums = []
    for frame in range(frames_sent):
        total = jnp.zeros((inputs_here, STEP), jnp.float32)
        for tap in range(TAPS):
            source = frame - TAPS + 1 + tap
            if 0 <= source < frames_here:
                start = source * NFFT + low
                values = samples_ref[:, start : start + STEP]
                weights = window_ref[tap : tap + 1, low : low + STEP]
                total = total + weights * values.astype(jnp.float32)
        sums.append(total)
    pairs = [
        jnp.concatenate(sums[frame : frame + 2], axis=0).astype(jnp.bfloat16)
        for frame in range(0, frames_sent, 2)
    ]
    return jnp.concatenate(pairs, axis=0)


def turn_granules(blocks, size):
    count = len(blocks)
    lanes = count * size
    granule = lax.broadcasted_iota(jnp.int32, blocks[0].shape, 1) // size
    blocks = list(blocks)
    distance = count // 2
    while distance:
        upper = (granule & distance) != 0
        shift = distance * size
        for index in range(count):
            if index & distance:
                continue
            low, high = blocks[index], blocks[index + distance]
            blocks[index] = jnp.where(upper, pltpu.roll(high, shift, 1), low)
            blocks[index + distance] = jnp.where(upper, high, pltpu.roll(low, lanes - shift, 1))
        distance //= 2
    return blocks


def place_in_column(place, far):
    return (far * 5 // 8 + far - place) % far


def own_part_kernel(
    far,
    samples_hbm,
    window_hbm,
    twiddle_hbm,
    gains_hbm,
    own_hbm,
    passed_hbm,
    parcels_hbm,
    samples_ref,
    window_ref,
    twiddle_ref,
    gains_ref,
    direct_ref,
    parcels_ref,
    arrived,
    left,
):
    inputs_here = gains_ref.shape[1]
    frames_here = samples_hbm.shape[1] // NFFT
    blocks = range(NFFT // STEP)
    fetches = []

    def fetch(source, target):
        fetches.append(pltpu.make_async_copy(source, target, arrived.at[len(fetches)]))
        fetches[-1].start()
        return fetches[-1]

    samples_in = fetch(samples_hbm, samples_ref)
    window_in = fetch(window_hbm, window_ref)
    table_in = []
    for block in blocks[: len(blocks) // 2]:
        rows = pl.ds(block * STEP, STEP)
        table_in.append(fetch(twiddle_hbm.at[rows, :], twiddle_ref.at[rows, :]))
    gains_in = fetch(gains_hbm, gains_ref)
    samples_in.wait()
    window_in.wait()
    total = None
    sent = frames_here + EARLY
    for block, table in enumerate(table_in):
        tapped = [
            tapped_block(samples_ref, window_ref, sent, half + block)
            for half in (0, len(table_in))
        ]
        table.wait()
        product = jnp.dot(
            jnp.concatenate(tapped, axis=0),
            twiddle_ref[block * STEP : (block + 1) * STEP, :],
            preferred_element_type=jnp.float32,
        )
        total = product if total is None else total + product
    channel = FIRST + lax.broadcasted_iota(jnp.int32, (1, 2 * CH), 1)
    sign = (1 - 2 * (channel % 2)).astype(jnp.float32)
    direct_ref[...] = total[: sent * inputs_here] + sign * total[sent * inputs_here :]
    own_rows = own_hbm.shape[0]
    passed_rows = passed_hbm.shape[0]
    stores = [
        pltpu.make_async_copy(direct_ref.at[pl.ds(0, own_rows), :], own_hbm, left.at[0]),
        pltpu.make_async_copy(
            direct_ref.at[pl.ds(own_rows, passed_rows), :], passed_hbm, left.at[1]
        ),
    ]
    for store in stores:
        store.start()
    gains_in.wait()
    gain_re = gains_ref[0]
    gain_im = gains_ref[1]
    parts = []
    for frame in range(frames_here + EARLY):
        direct = direct_ref[frame * inputs_here : (frame + 1) * inputs_here, :]
        direct_re = direct[:, :CH]
        direct_im = direct[:, CH:]
        parts.append(
            (
                gain_re * direct_re - gain_im * direct_im,
                gain_re * direct_im + gain_im * direct_re,
            )
        )
    slots = [
        [(part, frame) for frame in range(first, first + 8)]
        for first in range(0, frames_here, 8)
        for part in range(2)
    ]
    slots.append([(part, frames_here + frame) for part in range(2) for frame in range(EARLY)])
    per_far = CH // far
    for place, slot in enumerate(slots):
        columns = slice(place * LANES, (place + 1) * LANES)
        blocks = []
        for half in range(CH // LANES):
            lanes = slice(half * LANES, (half + 1) * LANES)
            blocks += turn_granules([parts[frame][part][:, lanes] for part, frame in slot], per_far)
        listed = sorted(range(far), key=lambda target: place_in_column(target, far))
        for index in range(0, far, 2):
            rows = slice(index * inputs_here, (index + 2) * inputs_here)
            parcels_ref[rows, columns] = jnp.concatenate(
                [blocks[target] for target in listed[index : index + 2]], axis=0
            ).astype(jnp.bfloat16)
        lanes = pl.ds(place * LANES, LANES)
        stores.append(
            pltpu.make_async_copy(
                parcels_ref.at[:, lanes], parcels_hbm.at[:, lanes], left.at[len(stores)]
            )
        )
        stores[-1].start()
    for store in stores:
        store.wait()


def spectra_kernel(passed_ref, own_ref, gains_ref, spectra_ref, rows_ref):
    inputs_here = gains_ref.shape[1]
    frames_here = own_ref.shape[0] // inputs_here
    slabs = CH // LANES
    gain_re = gains_ref[0]
    gain_im = gains_ref[1]
    for frame in range(frames_here):
        block = slice(frame * inputs_here, (frame + 1) * inputs_here)
        direct = own_ref[block, :]
        if frame < TAPS - 1:
            direct = direct + passed_ref[block, :]
        direct_re = direct[:, :CH]
        direct_im = direct[:, CH:]
        rows = pl.ds(frame, inputs_here, stride=frames_here)
        real_part = gain_re * direct_re - gain_im * direct_im
        imag_part = gain_re * direct_im + gain_im * direct_re
        for slab in range(slabs):
            columns = slice(slab * LANES, (slab + 1) * LANES)
            rows_ref[slab, rows, :] = real_part[:, columns]
            rows_ref[slabs + slab, rows, :] = imag_part[:, columns]
    for part in range(2):
        for slab in range(slabs):
            columns = slice(slab * LANES, (slab + 1) * LANES)
            values = rows_ref[part * slabs + slab, : own_ref.shape[0], :]
            spectra_ref[part, :, columns] = values.astype(jnp.bfloat16)


def channel_of(time):
    return time % 4


def place_in_plane(near, time, times):
    count = NEAR * times
    middle = NEAR // 2 * times + times // 2
    return 3 * (near * times + time + count - middle) % count


def spread_kernel(mine_ref, parcels_ref, turned_ref):
    count, rows, width = parcels_ref.shape
    times = count // NEAR
    stride = mine_ref.shape[1] // rows
    for place in range(0, mine_ref.shape[1], LANES):
        values = mine_ref[:, place : place + LANES].astype(jnp.float32)
        turned_ref[place : place + LANES, :] = values.T
    for near in range(NEAR):
        for channel in range(stride // NEAR):
            start = near * (stride // NEAR) + channel
            values = turned_ref[pl.ds(start, rows, stride=stride), :].astype(jnp.bfloat16)
            for time in range(times):
                if channel_of(time) == channel:
                    parcels_ref[place_in_plane(near, time, times)] = values


def correlate_kernel(frames_all, inputs_here, place_ref, every_ref, packed_ref):
    count, lines, width = every_ref.shape
    blocks, rows, inputs_all = packed_ref.shape
    times = count // NEAR
    main = lines - 2 * EARLY
    carry = None
    lined = []
    for time in range(times):
        pieces = [every_ref[place_in_plane(near, time, times)] for near in range(NEAR)]
        wide = jnp.concatenate([piece.astype(jnp.float32) for piece in pieces], axis=1)
        tiles = [wide[start : start + 8] for start in range(0, lines, 8)]
        if carry is not None:
            early = lax.broadcasted_iota(jnp.int32, carry.shape, 0) < EARLY
            tiles[0] = tiles[0] + jnp.where(early, carry, 0.0)
            tiles[1] = tiles[1] + jnp.where(early, pltpu.roll(carry, 8 - EARLY, 0), 0.0)
        carry = tiles[-1]
        lined += tiles[:-1]
    far = width // inputs_here
    target = lax.broadcasted_iota(jnp.int32, (1, inputs_all), 1)
    near = target // inputs_here % NEAR
    listed = place_in_column(target // (inputs_here * NEAR), far)
    source = near * width + listed * inputs_here + target % inputs_here
    chosen = lax.broadcasted_iota(jnp.int32, (inputs_all, inputs_all), 0) == source
    ordered = jnp.dot(
        jnp.concatenate(lined, axis=0).astype(jnp.bfloat16),
        chosen.astype(jnp.float32).astype(jnp.bfloat16),
        preferred_element_type=jnp.float32,
    )
    right = ordered.astype(jnp.bfloat16)
    twisted = []
    for start in range(0, times * main, 16):
        twisted.append(ordered[start + 8 : start + 16])
        twisted.append(-ordered[start : start + 8])
    twisted = jnp.concatenate(twisted, axis=0).astype(jnp.bfloat16)
    held = blocks * rows
    first = place_ref[0] * held
    col_index = lax.broadcasted_iota(jnp.int32, (held, inputs_all), 1)
    row_index = lax.broadcasted_iota(jnp.int32, (held, inputs_all), 0) + first
    left = [jnp.where(first == 0, side[:, :held], side[:, held:]) for side in (right, twisted)]
    both = lax.dot_general(
        jnp.concatenate(left, axis=1),
        right,
        (((0,), (0,)), ((), ())),
        preferred_element_type=jnp.float32,
    )
    values = jnp.where(row_index <= col_index, both[:held], both[held:]) * (1.0 / frames_all)
    values = values.astype(jnp.bfloat16)
    for block in range(blocks):
        packed_ref[blocks - 1 - block] = values[block * rows : (block + 1) * rows]


def unpack_kernel(packed_ref, lines_hbm, lines_ref, left):
    channels, count, width = packed_ref.shape
    tiles = width // LANES
    stores = []
    for first in range(0, count, 16):
        start = first * tiles * channels
        for channel in range(channels):
            values = packed_ref[channels - 1 - channel, first : first + 16, :]
            values = values.astype(jnp.float32)
            for tile in range(tiles):
                lines = pl.ds(start + tile * channels + channel, 16, stride=tiles * channels)
                lines_ref[lines, :] = values[:, tile * LANES : (tile + 1) * LANES]
        block = pl.ds(start, 16 * tiles * channels)
        stores.append(
            pltpu.make_async_copy(lines_ref.at[block, :], lines_hbm.at[block, :], left.at[len(stores)])
        )
        stores[-1].start()
    for store in stores:
        store.wait()


def body(samples, gains):
    inputs_here = samples.shape[0]
    frames_here = samples.shape[1] // NFFT
    times = lax.axis_size("tm")
    far = lax.axis_size("far")
    groups = far * NEAR
    per_group = CH // groups
    inputs_all = inputs_here * groups
    frames_all = frames_here * times
    block = inputs_here * frames_here

    window = filter_window()
    twiddle = jnp.asarray(build_table(window)[: NFFT // 2])
    window_taps = jnp.asarray(window.astype(np.float32).reshape(TAPS, NFFT))

    sent = frames_here + EARLY
    gains = gains.transpose(0, 2, 1)

    def own_part(*refs):
        own_part_kernel(far, *refs)

    own, passed, parcels = pl.pallas_call(
        own_part,
        out_shape=(
            jax.ShapeDtypeStruct((block, 2 * CH), jnp.float32),
            jax.ShapeDtypeStruct(((TAPS - 1) * inputs_here, 2 * CH), jnp.float32),
            jax.ShapeDtypeStruct((far * inputs_here, sent * 2 * CH // far), jnp.bfloat16),
        ),
        in_specs=[ANY] * 4,
        out_specs=(ANY, ANY, ANY),
        scratch_shapes=[
            pltpu.VMEM(samples.shape, jnp.bfloat16),
            pltpu.VMEM(window_taps.shape, jnp.float32),
            pltpu.VMEM(twiddle.shape, jnp.bfloat16),
            pltpu.VMEM(gains.shape, jnp.float32),
            pltpu.VMEM((sent * inputs_here, 2 * CH), jnp.float32),
            pltpu.VMEM((far * inputs_here, sent * 2 * CH // far), jnp.bfloat16),
            pltpu.SemaphoreType.DMA((3 + NFFT // (2 * STEP),)),
            pltpu.SemaphoreType.DMA((2 + sent // 4,)),
        ],
        compiler_params=pltpu.CompilerParams(vmem_limit_bytes=OWN_PART_VMEM),
        cost_estimate=pl.CostEstimate(
            flops=2 * sent * inputs_here * NFFT * 2 * CH,
            bytes_accessed=3 * 1024 * 1024,
            transcendentals=0,
        ),
        name="own_part",
    )(samples, window_taps, twiddle, gains)

    parcels = parcels.reshape(far, inputs_here, sent * 2 * CH // far)
    column = [sorted(range(far), key=lambda place: place_in_column(place, far))]
    mine = lax.all_to_all(parcels, "far", 0, 0, axis_index_groups=column)
    mine = mine.reshape(far * inputs_here, sent * 2 * CH // far)

    passed = lax.ppermute(passed, "tm", [(source, source + 1) for source in range(times - 1)])
    spectra = pl.pallas_call(
        spectra_kernel,
        out_shape=jax.ShapeDtypeStruct((2, block, CH), jnp.bfloat16),
        in_specs=[VMEM] * 3,
        out_specs=VMEM,
        scratch_shapes=[pltpu.VMEM((2 * CH // LANES, block + frames_here, LANES), jnp.float32)],
        compiler_params=PARAMS,
        cost_estimate=pl.CostEstimate(
            flops=8 * block * 2 * CH, bytes_accessed=1024 * 1024, transcendentals=0
        ),
        name="spectra",
    )(passed, own, gains)
    mine, spectra = lax.optimization_barrier((mine, spectra))
    spectra = spectra.reshape(2, inputs_here, frames_here, CH).transpose(0, 3, 1, 2)

    lines = 2 * sent
    spread = pl.pallas_call(
        spread_kernel,
        out_shape=jax.ShapeDtypeStruct((NEAR * times, lines, far * inputs_here), jnp.bfloat16),
        in_specs=[VMEM],
        out_specs=VMEM,
        scratch_shapes=[pltpu.VMEM(((sent + 1) * 2 * CH // far, far * inputs_here), jnp.float32)],
        compiler_params=PARAMS,
        name="spread",
    )(mine)
    place = lax.axis_index("tm").astype(jnp.int32)
    square = (place // 4)[None]
    spread, square = lax.optimization_barrier((spread, square))
    members = [(near, time) for near in range(NEAR) for time in range(times)]
    members.sort(key=lambda member: place_in_plane(*member, times))
    plane = [[near * times + time for near, time in members]]
    every = lax.all_to_all(spread, ("near", "tm"), 0, 0, axis_index_groups=plane)

    def correlate(*refs):
        correlate_kernel(frames_all, inputs_here, *refs)

    rows = inputs_all // times
    packed = pl.pallas_call(
        correlate,
        out_shape=jax.ShapeDtypeStruct((per_group, rows, inputs_all), jnp.bfloat16),
        in_specs=[SMEM, VMEM],
        out_specs=VMEM,
        compiler_params=PARAMS,
        name="correlate",
    )(square, every)
    squares = [[3, 2, 1, 0], [7, 6, 5, 4]]
    packed = lax.all_to_all(packed, "tm", 0, 0, axis_index_groups=squares)
    tiles = inputs_all // LANES
    visibilities = pl.pallas_call(
        unpack_kernel,
        out_shape=jax.ShapeDtypeStruct((rows * tiles * per_group, LANES), jnp.float32),
        in_specs=[VMEM],
        out_specs=ANY,
        scratch_shapes=[
            pltpu.VMEM(((rows + 1) * tiles * per_group, LANES), jnp.float32),
            pltpu.SemaphoreType.DMA((rows // 16,)),
        ],
        compiler_params=PARAMS,
        name="unpack",
    )(packed)
    visibilities = visibilities.reshape(rows, tiles, per_group, LANES).transpose(0, 2, 1, 3)
    visibilities = visibilities.reshape(rows, per_group, inputs_all)
    return (spectra, visibilities)


def solution(mesh):
    groups, times = mesh.devices.shape
    split = Mesh(mesh.devices.reshape(groups // NEAR, NEAR, times), ("far", "near", "tm"))
    inputs = ("far", "near")
    return jax.shard_map(
        body,
        mesh=split,
        in_specs=(P(inputs, "tm"), P(None, None, inputs)),
        out_specs=(P(None, None, inputs, "tm"), P("tm", inputs, None)),
        check_vma=False,
    )
```

```python
import math

import jax
import jax.numpy as jnp
import numpy as np
from jax import lax
from jax.experimental import pallas as pl
from jax.experimental.pallas import tpu as pltpu
from jax.sharding import Mesh, PartitionSpec as P

NFFT = 2048
CH = 256
FIRST = 384
TAPS = 4
NEAR = 4
EARLY = 4
STEP = 256
LANES = 128
VMEM = pl.BlockSpec(memory_space=pltpu.VMEM)
ANY = pl.BlockSpec(memory_space=pl.ANY)
SMEM = pl.BlockSpec(memory_space=pltpu.SMEM)
OWN_PART_VMEM = 59 * 1024 * 1024 + 768 * 1024
PARAMS = pltpu.CompilerParams(vmem_limit_bytes=32 * 1024 * 1024)


def filter_window():
    length = TAPS * NFFT
    position = np.arange(length, dtype=np.float64)
    centred = (position - 0.5 * length + 0.5) / NFFT
    hann_taper = 0.5 - 0.5 * np.cos(2.0 * math.pi * (position + 0.5) / length)
    return np.sinc(centred) * hann_taper


def build_table(window):
    norm_scale = 1.0 / np.sqrt(np.sum(window * window))
    sample = np.arange(NFFT)[:, None]
    channel = FIRST + np.arange(CH)[None, :]
    phase_angle = 2.0 * math.pi / NFFT * (sample * channel % NFFT)
    cosine = np.cos(phase_angle) * norm_scale
    sine = -np.sin(phase_angle) * norm_scale
    return np.concatenate([cosine, sine], axis=1).astype(jnp.bfloat16)


def tapped_block(samples_ref, window_ref, frames_sent, block):
    inputs_here, count = samples_ref.shape
    frames_here = count // NFFT
    low = block * STEP
    sums = []
    for frame in range(frames_sent):
        total = jnp.zeros((inputs_here, STEP), jnp.float32)
        for tap in range(TAPS):
            source = frame - TAPS + 1 + tap
            if 0 <= source < frames_here:
                start = source * NFFT + low
                values = samples_ref[:, start : start + STEP]
                weights = window_ref[tap : tap + 1, low : low + STEP]
                total = total + weights * values.astype(jnp.float32)
        sums.append(total)
    pairs = [
        jnp.concatenate(sums[frame : frame + 2], axis=0).astype(jnp.bfloat16)
        for frame in range(0, frames_sent, 2)
    ]
    return jnp.concatenate(pairs, axis=0)


def turn_granules(blocks, size):
    count = len(blocks)
    lanes = count * size
    granule = lax.broadcasted_iota(jnp.int32, blocks[0].shape, 1) // size
    blocks = list(blocks)
    distance = count // 2
    while distance:
        upper = (granule & distance) != 0
        shift = distance * size
        for index in range(count):
            if index & distance:
                continue
            low, high = blocks[index], blocks[index + distance]
            blocks[index] = jnp.where(upper, pltpu.roll(high, shift, 1), low)
            blocks[index + distance] = jnp.where(upper, high, pltpu.roll(low, lanes - shift, 1))
        distance //= 2
    return blocks


def place_in_column(place, far):
    return (far * 5 // 8 + far - place) % far


def own_part_kernel(
    far,
    samples_hbm,
    window_hbm,
    twiddle_hbm,
    gains_hbm,
    own_hbm,
    passed_hbm,
    parcels_hbm,
    samples_ref,
    window_ref,
    twiddle_ref,
    gains_ref,
    direct_ref,
    parcels_ref,
    arrived,
    left,
):
    inputs_here = gains_ref.shape[1]
    frames_here = samples_hbm.shape[1] // NFFT
    blocks = range(NFFT // STEP)
    fetches = []

    def fetch(source, target):
        fetches.append(pltpu.make_async_copy(source, target, arrived.at[len(fetches)]))
        fetches[-1].start()
        return fetches[-1]

    samples_in = fetch(samples_hbm, samples_ref)
    window_in = fetch(window_hbm, window_ref)
    table_in = []
    for block in blocks[: len(blocks) // 2]:
        rows = pl.ds(block * STEP, STEP)
        table_in.append(fetch(twiddle_hbm.at[rows, :], twiddle_ref.at[rows, :]))
    gains_in = fetch(gains_hbm, gains_ref)
    samples_in.wait()
    window_in.wait()
    total = None
    sent = frames_here + EARLY
    for block, table in enumerate(table_in):
        tapped = [
            tapped_block(samples_ref, window_ref, sent, half + block)
            for half in (0, len(table_in))
        ]
        table.wait()
        product = jnp.dot(
            jnp.concatenate(tapped, axis=0),
            twiddle_ref[block * STEP : (block + 1) * STEP, :],
            preferred_element_type=jnp.float32,
        )
        total = product if total is None else total + product
    channel = FIRST + lax.broadcasted_iota(jnp.int32, (1, 2 * CH), 1)
    sign = (1 - 2 * (channel % 2)).astype(jnp.float32)
    direct_ref[...] = total[: sent * inputs_here] + sign * total[sent * inputs_here :]
    own_rows = own_hbm.shape[0]
    passed_rows = passed_hbm.shape[0]
    stores = [
        pltpu.make_async_copy(direct_ref.at[pl.ds(0, own_rows), :], own_hbm, left.at[0]),
        pltpu.make_async_copy(
            direct_ref.at[pl.ds(own_rows, passed_rows), :], passed_hbm, left.at[1]
        ),
    ]
    for store in stores:
        store.start()
    gains_in.wait()
    gain_re = gains_ref[0]
    gain_im = gains_ref[1]
    parts = []
    for frame in range(frames_here + EARLY):
        direct = direct_ref[frame * inputs_here : (frame + 1) * inputs_here, :]
        direct_re = direct[:, :CH]
        direct_im = direct[:, CH:]
        parts.append(
            (
                gain_re * direct_re - gain_im * direct_im,
                gain_re * direct_im + gain_im * direct_re,
            )
        )
    slots = [
        [(part, frame) for frame in range(first, first + 8)]
        for first in range(0, frames_here, 8)
        for part in range(2)
    ]
    slots.append([(part, frames_here + frame) for part in range(2) for frame in range(EARLY)])
    per_far = CH // far
    for place, slot in enumerate(slots):
        columns = slice(place * LANES, (place + 1) * LANES)
        blocks = []
        for half in range(CH // LANES):
            lanes = slice(half * LANES, (half + 1) * LANES)
            blocks += turn_granules([parts[frame][part][:, lanes] for part, frame in slot], per_far)
        listed = sorted(range(far), key=lambda target: place_in_column(target, far))
        for index in range(0, far, 2):
            rows = slice(index * inputs_here, (index + 2) * inputs_here)
            parcels_ref[rows, columns] = jnp.concatenate(
                [blocks[target] for target in listed[index : index + 2]], axis=0
            ).astype(jnp.bfloat16)
        lanes = pl.ds(place * LANES, LANES)
        stores.append(
            pltpu.make_async_copy(
                parcels_ref.at[:, lanes], parcels_hbm.at[:, lanes], left.at[len(stores)]
            )
        )
        stores[-1].start()
    for store in stores:
        store.wait()


def spectra_kernel(passed_ref, own_ref, gains_ref, spectra_ref, rows_ref):
    inputs_here = gains_ref.shape[1]
    frames_here = own_ref.shape[0] // inputs_here
    slabs = CH // LANES
    gain_re = gains_ref[0]
    gain_im = gains_ref[1]
    for frame in range(frames_here):
        block = slice(frame * inputs_here, (frame + 1) * inputs_here)
        direct = own_ref[block, :]
        if frame < TAPS - 1:
            direct = direct + passed_ref[block, :]
        direct_re = direct[:, :CH]
        direct_im = direct[:, CH:]
        rows = pl.ds(frame, inputs_here, stride=frames_here)
        real_part = gain_re * direct_re - gain_im * direct_im
        imag_part = gain_re * direct_im + gain_im * direct_re
        for slab in range(slabs):
            columns = slice(slab * LANES, (slab + 1) * LANES)
            rows_ref[slab, rows, :] = real_part[:, columns]
            rows_ref[slabs + slab, rows, :] = imag_part[:, columns]
    for part in range(2):
        for slab in range(slabs):
            columns = slice(slab * LANES, (slab + 1) * LANES)
            values = rows_ref[part * slabs + slab, : own_ref.shape[0], :]
            spectra_ref[part, :, columns] = values.astype(jnp.bfloat16)


def channel_of(time):
    return time % 4


def place_in_square(member, square):
    return member ^ (3 - 2 * square)


def place_in_plane(near, time, times):
    count = NEAR * times
    middle = NEAR // 2 * times + times // 2
    return 3 * (near * times + time + count - middle) % count


def spread_kernel(mine_ref, parcels_ref, turned_ref):
    count, rows, width = parcels_ref.shape
    times = count // NEAR
    stride = mine_ref.shape[1] // rows
    for place in range(0, mine_ref.shape[1], LANES):
        values = mine_ref[:, place : place + LANES].astype(jnp.float32)
        turned_ref[place : place + LANES, :] = values.T
    for near in range(NEAR):
        for channel in range(stride // NEAR):
            start = near * (stride // NEAR) + channel
            values = turned_ref[pl.ds(start, rows, stride=stride), :].astype(jnp.bfloat16)
            for time in range(times):
                if channel_of(time) == channel:
                    parcels_ref[place_in_plane(near, time, times)] = values


def correlate_kernel(frames_all, inputs_here, place_ref, every_ref, packed_ref):
    count, lines, width = every_ref.shape
    blocks, rows, inputs_all = packed_ref.shape
    times = count // NEAR
    main = lines - 2 * EARLY
    carry = None
    lined = []
    for time in range(times):
        pieces = [every_ref[place_in_plane(near, time, times)] for near in range(NEAR)]
        wide = jnp.concatenate([piece.astype(jnp.float32) for piece in pieces], axis=1)
        tiles = [wide[start : start + 8] for start in range(0, lines, 8)]
        if carry is not None:
            early = lax.broadcasted_iota(jnp.int32, carry.shape, 0) < EARLY
            tiles[0] = tiles[0] + jnp.where(early, carry, 0.0)
            tiles[1] = tiles[1] + jnp.where(early, pltpu.roll(carry, 8 - EARLY, 0), 0.0)
        carry = tiles[-1]
        lined += tiles[:-1]
    far = width // inputs_here
    target = lax.broadcasted_iota(jnp.int32, (1, inputs_all), 1)
    near = target // inputs_here % NEAR
    listed = place_in_column(target // (inputs_here * NEAR), far)
    source = near * width + listed * inputs_here + target % inputs_here
    chosen = lax.broadcasted_iota(jnp.int32, (inputs_all, inputs_all), 0) == source
    ordered = jnp.dot(
        jnp.concatenate(lined, axis=0).astype(jnp.bfloat16),
        chosen.astype(jnp.float32).astype(jnp.bfloat16),
        preferred_element_type=jnp.float32,
    )
    right = ordered.astype(jnp.bfloat16)
    twisted = []
    for start in range(0, times * main, 16):
        twisted.append(ordered[start + 8 : start + 16])
        twisted.append(-ordered[start : start + 8])
    twisted = jnp.concatenate(twisted, axis=0).astype(jnp.bfloat16)
    held = blocks * rows
    first = place_ref[0] * held
    col_index = lax.broadcasted_iota(jnp.int32, (held, inputs_all), 1)
    row_index = lax.broadcasted_iota(jnp.int32, (held, inputs_all), 0) + first
    left = [jnp.where(first == 0, side[:, :held], side[:, held:]) for side in (right, twisted)]
    both = lax.dot_general(
        jnp.concatenate(left, axis=1),
        right,
        (((0,), (0,)), ((), ())),
        preferred_element_type=jnp.float32,
    )
    values = jnp.where(row_index <= col_index, both[:held], both[held:]) * (1.0 / frames_all)
    values = values.astype(jnp.bfloat16)
    for block in range(blocks):
        target = place_in_square(block, place_ref[0])
        packed_ref[target] = values[block * rows : (block + 1) * rows]


def unpack_kernel(place_ref, packed_ref, lines_hbm, lines_ref, left):
    channels, count, width = packed_ref.shape
    tiles = width // LANES
    stores = []
    for first in range(0, count, 16):
        start = first * tiles * channels
        for channel in range(channels):
            values = packed_ref[place_in_square(channel, place_ref[0]), first : first + 16, :]
            values = values.astype(jnp.float32)
            for tile in range(tiles):
                lines = pl.ds(start + tile * channels + channel, 16, stride=tiles * channels)
                lines_ref[lines, :] = values[:, tile * LANES : (tile + 1) * LANES]
        block = pl.ds(start, 16 * tiles * channels)
        stores.append(
            pltpu.make_async_copy(lines_ref.at[block, :], lines_hbm.at[block, :], left.at[len(stores)])
        )
        stores[-1].start()
    for store in stores:
        store.wait()


def body(samples, gains):
    inputs_here = samples.shape[0]
    frames_here = samples.shape[1] // NFFT
    times = lax.axis_size("tm")
    far = lax.axis_size("far")
    groups = far * NEAR
    per_group = CH // groups
    inputs_all = inputs_here * groups
    frames_all = frames_here * times
    block = inputs_here * frames_here

    window = filter_window()
    twiddle = jnp.asarray(build_table(window)[: NFFT // 2])
    window_taps = jnp.asarray(window.astype(np.float32).reshape(TAPS, NFFT))

    sent = frames_here + EARLY
    gains = gains.transpose(0, 2, 1)

    def own_part(*refs):
        own_part_kernel(far, *refs)

    own, passed, parcels = pl.pallas_call(
        own_part,
        out_shape=(
            jax.ShapeDtypeStruct((block, 2 * CH), jnp.float32),
            jax.ShapeDtypeStruct(((TAPS - 1) * inputs_here, 2 * CH), jnp.float32),
            jax.ShapeDtypeStruct((far * inputs_here, sent * 2 * CH // far), jnp.bfloat16),
        ),
        in_specs=[ANY] * 4,
        out_specs=(ANY, ANY, ANY),
        scratch_shapes=[
            pltpu.VMEM(samples.shape, jnp.bfloat16),
            pltpu.VMEM(window_taps.shape, jnp.float32),
            pltpu.VMEM(twiddle.shape, jnp.bfloat16),
            pltpu.VMEM(gains.shape, jnp.float32),
            pltpu.VMEM((sent * inputs_here, 2 * CH), jnp.float32),
            pltpu.VMEM((far * inputs_here, sent * 2 * CH // far), jnp.bfloat16),
            pltpu.SemaphoreType.DMA((3 + NFFT // (2 * STEP),)),
            pltpu.SemaphoreType.DMA((2 + sent // 4,)),
        ],
        compiler_params=pltpu.CompilerParams(vmem_limit_bytes=OWN_PART_VMEM),
        cost_estimate=pl.CostEstimate(
            flops=2 * sent * inputs_here * NFFT * 2 * CH,
            bytes_accessed=3 * 1024 * 1024,
            transcendentals=0,
        ),
        name="own_part",
    )(samples, window_taps, twiddle, gains)

    parcels = parcels.reshape(far, inputs_here, sent * 2 * CH // far)
    column = [sorted(range(far), key=lambda place: place_in_column(place, far))]
    mine = lax.all_to_all(parcels, "far", 0, 0, axis_index_groups=column)
    mine = mine.reshape(far * inputs_here, sent * 2 * CH // far)

    passed = lax.ppermute(passed, "tm", [(source, source + 1) for source in range(times - 1)])
    spectra = pl.pallas_call(
        spectra_kernel,
        out_shape=jax.ShapeDtypeStruct((2, block, CH), jnp.bfloat16),
        in_specs=[VMEM] * 3,
        out_specs=VMEM,
        scratch_shapes=[pltpu.VMEM((2 * CH // LANES, block + frames_here, LANES), jnp.float32)],
        compiler_params=PARAMS,
        cost_estimate=pl.CostEstimate(
            flops=8 * block * 2 * CH, bytes_accessed=1024 * 1024, transcendentals=0
        ),
        name="spectra",
    )(passed, own, gains)
    mine, spectra = lax.optimization_barrier((mine, spectra))
    spectra = spectra.reshape(2, inputs_here, frames_here, CH).transpose(0, 3, 1, 2)

    lines = 2 * sent
    spread = pl.pallas_call(
        spread_kernel,
        out_shape=jax.ShapeDtypeStruct((NEAR * times, lines, far * inputs_here), jnp.bfloat16),
        in_specs=[VMEM],
        out_specs=VMEM,
        scratch_shapes=[pltpu.VMEM(((sent + 1) * 2 * CH // far, far * inputs_here), jnp.float32)],
        compiler_params=PARAMS,
        name="spread",
    )(mine)
    place = lax.axis_index("tm").astype(jnp.int32)
    square = (place // 4)[None]
    spread, square = lax.optimization_barrier((spread, square))
    members = [(near, time) for near in range(NEAR) for time in range(times)]
    members.sort(key=lambda member: place_in_plane(*member, times))
    plane = [[near * times + time for near, time in members]]
    every = lax.all_to_all(spread, ("near", "tm"), 0, 0, axis_index_groups=plane)

    def correlate(*refs):
        correlate_kernel(frames_all, inputs_here, *refs)

    rows = inputs_all // times
    packed = pl.pallas_call(
        correlate,
        out_shape=jax.ShapeDtypeStruct((per_group, rows, inputs_all), jnp.bfloat16),
        in_specs=[SMEM, VMEM],
        out_specs=VMEM,
        compiler_params=PARAMS,
        name="correlate",
    )(square, every)
    squares = [
        [4 * side + place_in_square(member, side) for member in range(per_group)]
        for side in range(2)
    ]
    packed = lax.all_to_all(packed, "tm", 0, 0, axis_index_groups=squares)
    tiles = inputs_all // LANES
    visibilities = pl.pallas_call(
        unpack_kernel,
        out_shape=jax.ShapeDtypeStruct((rows * tiles * per_group, LANES), jnp.float32),
        in_specs=[SMEM, VMEM],
        out_specs=ANY,
        scratch_shapes=[
            pltpu.VMEM(((rows + 1) * tiles * per_group, LANES), jnp.float32),
            pltpu.SemaphoreType.DMA((rows // 16,)),
        ],
        compiler_params=PARAMS,
        name="unpack",
    )(square, packed)
    visibilities = visibilities.reshape(rows, tiles, per_group, LANES).transpose(0, 2, 1, 3)
    visibilities = visibilities.reshape(rows, per_group, inputs_all)
    return (spectra, visibilities)


def solution(mesh):
    groups, times = mesh.devices.shape
    split = Mesh(mesh.devices.reshape(groups // NEAR, NEAR, times), ("far", "near", "tm"))
    inputs = ("far", "near")
    return jax.shard_map(
        body,
        mesh=split,
        in_specs=(P(inputs, "tm"), P(None, None, inputs)),
        out_specs=(P(None, None, inputs, "tm"), P("tm", inputs, None)),
        check_vma=False,
    )
```

```python
import math

import jax
import jax.numpy as jnp
import numpy as np
from jax import lax
from jax.experimental import pallas as pl
from jax.experimental.pallas import tpu as pltpu
from jax.sharding import Mesh, PartitionSpec as P

NFFT = 2048
CH = 256
FIRST = 384
TAPS = 4
NEAR = 4
EARLY = 4
STEP = 256
LANES = 128
VMEM = pl.BlockSpec(memory_space=pltpu.VMEM)
ANY = pl.BlockSpec(memory_space=pl.ANY)
SMEM = pl.BlockSpec(memory_space=pltpu.SMEM)
OWN_PART_VMEM = 59 * 1024 * 1024 + 768 * 1024
PARAMS = pltpu.CompilerParams(vmem_limit_bytes=32 * 1024 * 1024)


def filter_window():
    length = TAPS * NFFT
    position = np.arange(length, dtype=np.float64)
    centred = (position - 0.5 * length + 0.5) / NFFT
    hann_taper = 0.5 - 0.5 * np.cos(2.0 * math.pi * (position + 0.5) / length)
    return np.sinc(centred) * hann_taper


def build_table(window):
    norm_scale = 1.0 / np.sqrt(np.sum(window * window))
    sample = np.arange(NFFT)[:, None]
    channel = FIRST + np.arange(CH)[None, :]
    phase_angle = 2.0 * math.pi / NFFT * (sample * channel % NFFT)
    cosine = np.cos(phase_angle) * norm_scale
    sine = -np.sin(phase_angle) * norm_scale
    return np.concatenate([cosine, sine], axis=1).astype(jnp.bfloat16)


def tapped_block(samples_ref, window_ref, frames_sent, block):
    inputs_here, count = samples_ref.shape
    frames_here = count // NFFT
    low = block * STEP
    sums = []
    for frame in range(frames_sent):
        total = jnp.zeros((inputs_here, STEP), jnp.float32)
        for tap in range(TAPS):
            source = frame - TAPS + 1 + tap
            if 0 <= source < frames_here:
                start = source * NFFT + low
                values = samples_ref[:, start : start + STEP]
                weights = window_ref[tap : tap + 1, low : low + STEP]
                total = total + weights * values.astype(jnp.float32)
        sums.append(total)
    pairs = [
        jnp.concatenate(sums[frame : frame + 2], axis=0).astype(jnp.bfloat16)
        for frame in range(0, frames_sent, 2)
    ]
    return jnp.concatenate(pairs, axis=0)


def turn_granules(blocks, size):
    count = len(blocks)
    lanes = count * size
    granule = lax.broadcasted_iota(jnp.int32, blocks[0].shape, 1) // size
    blocks = list(blocks)
    distance = count // 2
    while distance:
        upper = (granule & distance) != 0
        shift = distance * size
        for index in range(count):
            if index & distance:
                continue
            low, high = blocks[index], blocks[index + distance]
            blocks[index] = jnp.where(upper, pltpu.roll(high, shift, 1), low)
            blocks[index + distance] = jnp.where(upper, high, pltpu.roll(low, lanes - shift, 1))
        distance //= 2
    return blocks


def place_in_column(place, far):
    return (far * 5 // 8 + far - place) % far


def own_part_kernel(
    far,
    samples_hbm,
    window_hbm,
    twiddle_hbm,
    gains_hbm,
    own_hbm,
    passed_hbm,
    parcels_hbm,
    samples_ref,
    window_ref,
    twiddle_ref,
    gains_ref,
    direct_ref,
    parcels_ref,
    arrived,
    left,
):
    inputs_here = gains_ref.shape[1]
    frames_here = samples_hbm.shape[1] // NFFT
    blocks = range(NFFT // STEP)
    fetches = []

    def fetch(source, target):
        fetches.append(pltpu.make_async_copy(source, target, arrived.at[len(fetches)]))
        fetches[-1].start()
        return fetches[-1]

    samples_in = fetch(samples_hbm, samples_ref)
    window_in = fetch(window_hbm, window_ref)
    table_in = []
    for block in blocks[: len(blocks) // 2]:
        rows = pl.ds(block * STEP, STEP)
        table_in.append(fetch(twiddle_hbm.at[rows, :], twiddle_ref.at[rows, :]))
    gains_in = fetch(gains_hbm, gains_ref)
    samples_in.wait()
    window_in.wait()
    total = None
    sent = frames_here + EARLY
    for block, table in enumerate(table_in):
        tapped = [
            tapped_block(samples_ref, window_ref, sent, half + block)
            for half in (0, len(table_in))
        ]
        table.wait()
        product = jnp.dot(
            jnp.concatenate(tapped, axis=0),
            twiddle_ref[block * STEP : (block + 1) * STEP, :],
            preferred_element_type=jnp.float32,
        )
        total = product if total is None else total + product
    channel = FIRST + lax.broadcasted_iota(jnp.int32, (1, 2 * CH), 1)
    sign = (1 - 2 * (channel % 2)).astype(jnp.float32)
    direct_ref[...] = total[: sent * inputs_here] + sign * total[sent * inputs_here :]
    own_rows = own_hbm.shape[0]
    passed_rows = passed_hbm.shape[0]
    stores = [
        pltpu.make_async_copy(direct_ref.at[pl.ds(0, own_rows), :], own_hbm, left.at[0]),
        pltpu.make_async_copy(
            direct_ref.at[pl.ds(own_rows, passed_rows), :], passed_hbm, left.at[1]
        ),
    ]
    for store in stores:
        store.start()
    gains_in.wait()
    gain_re = gains_ref[0]
    gain_im = gains_ref[1]
    parts = []
    for frame in range(frames_here + EARLY):
        direct = direct_ref[frame * inputs_here : (frame + 1) * inputs_here, :]
        direct_re = direct[:, :CH]
        direct_im = direct[:, CH:]
        parts.append(
            (
                gain_re * direct_re - gain_im * direct_im,
                gain_re * direct_im + gain_im * direct_re,
            )
        )
    slots = [
        [(part, frame) for frame in range(first, first + 8)]
        for first in range(0, frames_here, 8)
        for part in range(2)
    ]
    slots.append([(part, frames_here + frame) for part in range(2) for frame in range(EARLY)])
    per_far = CH // far
    for place, slot in enumerate(slots):
        columns = slice(place * LANES, (place + 1) * LANES)
        blocks = []
        for half in range(CH // LANES):
            lanes = slice(half * LANES, (half + 1) * LANES)
            blocks += turn_granules([parts[frame][part][:, lanes] for part, frame in slot], per_far)
        listed = sorted(range(far), key=lambda target: place_in_column(target, far))
        for index in range(0, far, 2):
            rows = slice(index * inputs_here, (index + 2) * inputs_here)
            parcels_ref[rows, columns] = jnp.concatenate(
                [blocks[target] for target in listed[index : index + 2]], axis=0
            ).astype(jnp.bfloat16)
        lanes = pl.ds(place * LANES, LANES)
        stores.append(
            pltpu.make_async_copy(
                parcels_ref.at[:, lanes], parcels_hbm.at[:, lanes], left.at[len(stores)]
            )
        )
        stores[-1].start()
    for store in stores:
        store.wait()


def spectra_kernel(passed_ref, own_ref, gains_ref, spectra_ref, rows_ref):
    inputs_here = gains_ref.shape[1]
    frames_here = own_ref.shape[0] // inputs_here
    slabs = CH // LANES
    gain_re = gains_ref[0]
    gain_im = gains_ref[1]
    for frame in range(frames_here):
        block = slice(frame * inputs_here, (frame + 1) * inputs_here)
        direct = own_ref[block, :]
        if frame < TAPS - 1:
            direct = direct + passed_ref[block, :]
        direct_re = direct[:, :CH]
        direct_im = direct[:, CH:]
        rows = pl.ds(frame, inputs_here, stride=frames_here)
        real_part = gain_re * direct_re - gain_im * direct_im
        imag_part = gain_re * direct_im + gain_im * direct_re
        for slab in range(slabs):
            columns = slice(slab * LANES, (slab + 1) * LANES)
            rows_ref[slab, rows, :] = real_part[:, columns]
            rows_ref[slabs + slab, rows, :] = imag_part[:, columns]
    for part in range(2):
        for slab in range(slabs):
            columns = slice(slab * LANES, (slab + 1) * LANES)
            values = rows_ref[part * slabs + slab, : own_ref.shape[0], :]
            spectra_ref[part, :, columns] = values.astype(jnp.bfloat16)


def channel_of(time):
    return time % 4


def place_in_plane(near, time, times):
    count = NEAR * times
    middle = NEAR // 2 * times + times // 2
    return 29 * (near * times + time + count - middle) % count


def spread_kernel(mine_ref, parcels_ref, turned_ref):
    count, rows, width = parcels_ref.shape
    times = count // NEAR
    stride = mine_ref.shape[1] // rows
    for place in range(0, mine_ref.shape[1], LANES):
        values = mine_ref[:, place : place + LANES].astype(jnp.float32)
        turned_ref[place : place + LANES, :] = values.T
    for near in range(NEAR):
        for channel in range(stride // NEAR):
            start = near * (stride // NEAR) + channel
            values = turned_ref[pl.ds(start, rows, stride=stride), :].astype(jnp.bfloat16)
            for time in range(times):
                if channel_of(time) == channel:
                    parcels_ref[place_in_plane(near, time, times)] = values


def correlate_kernel(frames_all, inputs_here, place_ref, every_ref, packed_ref):
    count, lines, width = every_ref.shape
    blocks, rows, inputs_all = packed_ref.shape
    times = count // NEAR
    main = lines - 2 * EARLY
    carry = None
    lined = []
    for time in range(times):
        pieces = [every_ref[place_in_plane(near, time, times)] for near in range(NEAR)]
        wide = jnp.concatenate([piece.astype(jnp.float32) for piece in pieces], axis=1)
        tiles = [wide[start : start + 8] for start in range(0, lines, 8)]
        if carry is not None:
            early = lax.broadcasted_iota(jnp.int32, carry.shape, 0) < EARLY
            tiles[0] = tiles[0] + jnp.where(early, carry, 0.0)
            tiles[1] = tiles[1] + jnp.where(early, pltpu.roll(carry, 8 - EARLY, 0), 0.0)
        carry = tiles[-1]
        lined += tiles[:-1]
    far = width // inputs_here
    target = lax.broadcasted_iota(jnp.int32, (1, inputs_all), 1)
    near = target // inputs_here % NEAR
    listed = place_in_column(target // (inputs_here * NEAR), far)
    source = near * width + listed * inputs_here + target % inputs_here
    chosen = lax.broadcasted_iota(jnp.int32, (inputs_all, inputs_all), 0) == source
    ordered = jnp.dot(
        jnp.concatenate(lined, axis=0).astype(jnp.bfloat16),
        chosen.astype(jnp.float32).astype(jnp.bfloat16),
        preferred_element_type=jnp.float32,
    )
    right = ordered.astype(jnp.bfloat16)
    twisted = []
    for start in range(0, times * main, 16):
        twisted.append(ordered[start + 8 : start + 16])
        twisted.append(-ordered[start : start + 8])
    twisted = jnp.concatenate(twisted, axis=0).astype(jnp.bfloat16)
    held = blocks * rows
    first = place_ref[0] * held
    col_index = lax.broadcasted_iota(jnp.int32, (held, inputs_all), 1)
    row_index = lax.broadcasted_iota(jnp.int32, (held, inputs_all), 0) + first
    left = [jnp.where(first == 0, side[:, :held], side[:, held:]) for side in (right, twisted)]
    both = lax.dot_general(
        jnp.concatenate(left, axis=1),
        right,
        (((0,), (0,)), ((), ())),
        preferred_element_type=jnp.float32,
    )
    values = jnp.where(row_index <= col_index, both[:held], both[held:]) * (1.0 / frames_all)
    values = values.astype(jnp.bfloat16)
    for block in range(blocks):
        packed_ref[blocks - 1 - block] = values[block * rows : (block + 1) * rows]


def unpack_kernel(packed_ref, lines_hbm, lines_ref, left):
    channels, count, width = packed_ref.shape
    tiles = width // LANES
    stores = []
    for first in range(0, count, 16):
        start = first * tiles * channels
        for channel in range(channels):
            values = packed_ref[channels - 1 - channel, first : first + 16, :]
            values = values.astype(jnp.float32)
            for tile in range(tiles):
                lines = pl.ds(start + tile * channels + channel, 16, stride=tiles * channels)
                lines_ref[lines, :] = values[:, tile * LANES : (tile + 1) * LANES]
        block = pl.ds(start, 16 * tiles * channels)
        stores.append(
            pltpu.make_async_copy(lines_ref.at[block, :], lines_hbm.at[block, :], left.at[len(stores)])
        )
        stores[-1].start()
    for store in stores:
        store.wait()


def body(samples, gains):
    inputs_here = samples.shape[0]
    frames_here = samples.shape[1] // NFFT
    times = lax.axis_size("tm")
    far = lax.axis_size("far")
    groups = far * NEAR
    per_group = CH // groups
    inputs_all = inputs_here * groups
    frames_all = frames_here * times
    block = inputs_here * frames_here

    window = filter_window()
    twiddle = jnp.asarray(build_table(window)[: NFFT // 2])
    window_taps = jnp.asarray(window.astype(np.float32).reshape(TAPS, NFFT))

    sent = frames_here + EARLY
    gains = gains.transpose(0, 2, 1)

    def own_part(*refs):
        own_part_kernel(far, *refs)

    own, passed, parcels = pl.pallas_call(
        own_part,
        out_shape=(
            jax.ShapeDtypeStruct((block, 2 * CH), jnp.float32),
            jax.ShapeDtypeStruct(((TAPS - 1) * inputs_here, 2 * CH), jnp.float32),
            jax.ShapeDtypeStruct((far * inputs_here, sent * 2 * CH // far), jnp.bfloat16),
        ),
        in_specs=[ANY] * 4,
        out_specs=(ANY, ANY, ANY),
        scratch_shapes=[
            pltpu.VMEM(samples.shape, jnp.bfloat16),
            pltpu.VMEM(window_taps.shape, jnp.float32),
            pltpu.VMEM(twiddle.shape, jnp.bfloat16),
            pltpu.VMEM(gains.shape, jnp.float32),
            pltpu.VMEM((sent * inputs_here, 2 * CH), jnp.float32),
            pltpu.VMEM((far * inputs_here, sent * 2 * CH // far), jnp.bfloat16),
            pltpu.SemaphoreType.DMA((3 + NFFT // (2 * STEP),)),
            pltpu.SemaphoreType.DMA((2 + sent // 4,)),
        ],
        compiler_params=pltpu.CompilerParams(vmem_limit_bytes=OWN_PART_VMEM),
        cost_estimate=pl.CostEstimate(
            flops=2 * sent * inputs_here * NFFT * 2 * CH,
            bytes_accessed=3 * 1024 * 1024,
            transcendentals=0,
        ),
        name="own_part",
    )(samples, window_taps, twiddle, gains)

    parcels = parcels.reshape(far, inputs_here, sent * 2 * CH // far)
    column = [sorted(range(far), key=lambda place: place_in_column(place, far))]
    mine = lax.all_to_all(parcels, "far", 0, 0, axis_index_groups=column)
    mine = mine.reshape(far * inputs_here, sent * 2 * CH // far)

    passed = lax.ppermute(passed, "tm", [(source, source + 1) for source in range(times - 1)])
    spectra = pl.pallas_call(
        spectra_kernel,
        out_shape=jax.ShapeDtypeStruct((2, block, CH), jnp.bfloat16),
        in_specs=[VMEM] * 3,
        out_specs=VMEM,
        scratch_shapes=[pltpu.VMEM((2 * CH // LANES, block + frames_here, LANES), jnp.float32)],
        compiler_params=PARAMS,
        cost_estimate=pl.CostEstimate(
            flops=8 * block * 2 * CH, bytes_accessed=1024 * 1024, transcendentals=0
        ),
        name="spectra",
    )(passed, own, gains)
    mine, spectra = lax.optimization_barrier((mine, spectra))
    spectra = spectra.reshape(2, inputs_here, frames_here, CH).transpose(0, 3, 1, 2)

    lines = 2 * sent
    spread = pl.pallas_call(
        spread_kernel,
        out_shape=jax.ShapeDtypeStruct((NEAR * times, lines, far * inputs_here), jnp.bfloat16),
        in_specs=[VMEM],
        out_specs=VMEM,
        scratch_shapes=[pltpu.VMEM(((sent + 1) * 2 * CH // far, far * inputs_here), jnp.float32)],
        compiler_params=PARAMS,
        name="spread",
    )(mine)
    place = lax.axis_index("tm").astype(jnp.int32)
    square = (place // 4)[None]
    spread, square = lax.optimization_barrier((spread, square))
    members = [(near, time) for near in range(NEAR) for time in range(times)]
    members.sort(key=lambda member: place_in_plane(*member, times))
    plane = [[near * times + time for near, time in members]]
    every = lax.all_to_all(spread, ("near", "tm"), 0, 0, axis_index_groups=plane)

    def correlate(*refs):
        correlate_kernel(frames_all, inputs_here, *refs)

    rows = inputs_all // times
    packed = pl.pallas_call(
        correlate,
        out_shape=jax.ShapeDtypeStruct((per_group, rows, inputs_all), jnp.bfloat16),
        in_specs=[SMEM, VMEM],
        out_specs=VMEM,
        compiler_params=PARAMS,
        name="correlate",
    )(square, every)
    squares = [[3, 2, 1, 0], [7, 6, 5, 4]]
    packed = lax.all_to_all(packed, "tm", 0, 0, axis_index_groups=squares)
    tiles = inputs_all // LANES
    visibilities = pl.pallas_call(
        unpack_kernel,
        out_shape=jax.ShapeDtypeStruct((rows * tiles * per_group, LANES), jnp.float32),
        in_specs=[VMEM],
        out_specs=ANY,
        scratch_shapes=[
            pltpu.VMEM(((rows + 1) * tiles * per_group, LANES), jnp.float32),
            pltpu.SemaphoreType.DMA((rows // 16,)),
        ],
        compiler_params=PARAMS,
        name="unpack",
    )(packed)
    visibilities = visibilities.reshape(rows, tiles, per_group, LANES).transpose(0, 2, 1, 3)
    visibilities = visibilities.reshape(rows, per_group, inputs_all)
    return (spectra, visibilities)


def solution(mesh):
    groups, times = mesh.devices.shape
    split = Mesh(mesh.devices.reshape(groups // NEAR, NEAR, times), ("far", "near", "tm"))
    inputs = ("far", "near")
    return jax.shard_map(
        body,
        mesh=split,
        in_specs=(P(inputs, "tm"), P(None, None, inputs)),
        out_specs=(P(None, None, inputs, "tm"), P("tm", inputs, None)),
        check_vma=False,
    )
```

```python
import math

import jax
import jax.numpy as jnp
import numpy as np
from jax import lax
from jax.experimental import pallas as pl
from jax.experimental.pallas import tpu as pltpu
from jax.sharding import Mesh, PartitionSpec as P

NFFT = 2048
CH = 256
FIRST = 384
TAPS = 4
NEAR = 4
EARLY = 4
STEP = 256
LANES = 128
VMEM = pl.BlockSpec(memory_space=pltpu.VMEM)
ANY = pl.BlockSpec(memory_space=pl.ANY)
SMEM = pl.BlockSpec(memory_space=pltpu.SMEM)
OWN_PART_VMEM = 59 * 1024 * 1024 + 768 * 1024
PARAMS = pltpu.CompilerParams(vmem_limit_bytes=32 * 1024 * 1024)


def filter_window():
    length = TAPS * NFFT
    position = np.arange(length, dtype=np.float64)
    centred = (position - 0.5 * length + 0.5) / NFFT
    hann_taper = 0.5 - 0.5 * np.cos(2.0 * math.pi * (position + 0.5) / length)
    return np.sinc(centred) * hann_taper


def build_table(window):
    norm_scale = 1.0 / np.sqrt(np.sum(window * window))
    sample = np.arange(NFFT)[:, None]
    channel = FIRST + np.arange(CH)[None, :]
    phase_angle = 2.0 * math.pi / NFFT * (sample * channel % NFFT)
    cosine = np.cos(phase_angle) * norm_scale
    sine = -np.sin(phase_angle) * norm_scale
    return np.concatenate([cosine, sine], axis=1).astype(jnp.bfloat16)


def tapped_block(samples_ref, window_ref, frames_sent, block):
    inputs_here, count = samples_ref.shape
    frames_here = count // NFFT
    low = block * STEP
    sums = []
    for frame in range(frames_sent):
        total = jnp.zeros((inputs_here, STEP), jnp.float32)
        for tap in range(TAPS):
            source = frame - TAPS + 1 + tap
            if 0 <= source < frames_here:
                start = source * NFFT + low
                values = samples_ref[:, start : start + STEP]
                weights = window_ref[tap : tap + 1, low : low + STEP]
                total = total + weights * values.astype(jnp.float32)
        sums.append(total)
    pairs = [
        jnp.concatenate(sums[frame : frame + 2], axis=0).astype(jnp.bfloat16)
        for frame in range(0, frames_sent, 2)
    ]
    return jnp.concatenate(pairs, axis=0)


def turn_granules(blocks, size):
    count = len(blocks)
    lanes = count * size
    granule = lax.broadcasted_iota(jnp.int32, blocks[0].shape, 1) // size
    blocks = list(blocks)
    distance = count // 2
    while distance:
        upper = (granule & distance) != 0
        shift = distance * size
        for index in range(count):
            if index & distance:
                continue
            low, high = blocks[index], blocks[index + distance]
            blocks[index] = jnp.where(upper, pltpu.roll(high, shift, 1), low)
            blocks[index + distance] = jnp.where(upper, high, pltpu.roll(low, lanes - shift, 1))
        distance //= 2
    return blocks


def place_in_column(place, far):
    return (far * 5 // 8 + far - place) % far


def own_part_kernel(
    far,
    samples_hbm,
    window_hbm,
    twiddle_hbm,
    gains_hbm,
    own_hbm,
    passed_hbm,
    parcels_hbm,
    samples_ref,
    window_ref,
    twiddle_ref,
    gains_ref,
    direct_ref,
    parcels_ref,
    arrived,
    left,
):
    inputs_here = gains_ref.shape[1]
    frames_here = samples_hbm.shape[1] // NFFT
    blocks = range(NFFT // STEP)
    fetches = []

    def fetch(source, target):
        fetches.append(pltpu.make_async_copy(source, target, arrived.at[len(fetches)]))
        fetches[-1].start()
        return fetches[-1]

    samples_in = []
    for frame in range(0, frames_here, 2):
        columns = pl.ds(frame * NFFT, 2 * NFFT)
        samples_in.append(fetch(samples_hbm.at[:, columns], samples_ref.at[:, columns]))
    window_in = fetch(window_hbm, window_ref)
    table_in = []
    for block in blocks[: len(blocks) // 2]:
        pieces = []
        for start in (block * STEP, block * STEP + STEP // 2):
            rows = pl.ds(start, STEP // 2)
            pieces.append(fetch(twiddle_hbm.at[rows, :], twiddle_ref.at[rows, :]))
        table_in.append(pieces)
    gains_in = fetch(gains_hbm, gains_ref)
    for piece in samples_in:
        piece.wait()
    window_in.wait()
    total = None
    sent = frames_here + EARLY
    for block, table in enumerate(table_in):
        tapped = [
            tapped_block(samples_ref, window_ref, sent, half + block)
            for half in (0, len(table_in))
        ]
        for piece in table:
            piece.wait()
        product = jnp.dot(
            jnp.concatenate(tapped, axis=0),
            twiddle_ref[block * STEP : (block + 1) * STEP, :],
            preferred_element_type=jnp.float32,
        )
        total = product if total is None else total + product
    channel = FIRST + lax.broadcasted_iota(jnp.int32, (1, 2 * CH), 1)
    sign = (1 - 2 * (channel % 2)).astype(jnp.float32)
    direct_ref[...] = total[: sent * inputs_here] + sign * total[sent * inputs_here :]
    own_rows = own_hbm.shape[0]
    passed_rows = passed_hbm.shape[0]
    stores = [
        pltpu.make_async_copy(direct_ref.at[pl.ds(0, own_rows), :], own_hbm, left.at[0]),
        pltpu.make_async_copy(
            direct_ref.at[pl.ds(own_rows, passed_rows), :], passed_hbm, left.at[1]
        ),
    ]
    for store in stores:
        store.start()
    gains_in.wait()
    gain_re = gains_ref[0]
    gain_im = gains_ref[1]
    parts = []
    for frame in range(frames_here + EARLY):
        direct = direct_ref[frame * inputs_here : (frame + 1) * inputs_here, :]
        direct_re = direct[:, :CH]
        direct_im = direct[:, CH:]
        parts.append(
            (
                gain_re * direct_re - gain_im * direct_im,
                gain_re * direct_im + gain_im * direct_re,
            )
        )
    slots = [
        [(part, frame) for frame in range(first, first + 8)]
        for first in range(0, frames_here, 8)
        for part in range(2)
    ]
    slots.append([(part, frames_here + frame) for part in range(2) for frame in range(EARLY)])
    per_far = CH // far
    for place, slot in enumerate(slots):
        columns = slice(place * LANES, (place + 1) * LANES)
        blocks = []
        for half in range(CH // LANES):
            lanes = slice(half * LANES, (half + 1) * LANES)
            blocks += turn_granules([parts[frame][part][:, lanes] for part, frame in slot], per_far)
        listed = sorted(range(far), key=lambda target: place_in_column(target, far))
        for index in range(0, far, 2):
            rows = slice(index * inputs_here, (index + 2) * inputs_here)
            parcels_ref[rows, columns] = jnp.concatenate(
                [blocks[target] for target in listed[index : index + 2]], axis=0
            ).astype(jnp.bfloat16)
        lanes = pl.ds(place * LANES, LANES)
        stores.append(
            pltpu.make_async_copy(
                parcels_ref.at[:, lanes], parcels_hbm.at[:, lanes], left.at[len(stores)]
            )
        )
        stores[-1].start()
    for store in stores:
        store.wait()


def spectra_kernel(passed_ref, own_ref, gains_ref, spectra_ref, rows_ref):
    inputs_here = gains_ref.shape[1]
    frames_here = own_ref.shape[0] // inputs_here
    slabs = CH // LANES
    gain_re = gains_ref[0]
    gain_im = gains_ref[1]
    for frame in range(frames_here):
        block = slice(frame * inputs_here, (frame + 1) * inputs_here)
        direct = own_ref[block, :]
        if frame < TAPS - 1:
            direct = direct + passed_ref[block, :]
        direct_re = direct[:, :CH]
        direct_im = direct[:, CH:]
        rows = pl.ds(frame, inputs_here, stride=frames_here)
        real_part = gain_re * direct_re - gain_im * direct_im
        imag_part = gain_re * direct_im + gain_im * direct_re
        for slab in range(slabs):
            columns = slice(slab * LANES, (slab + 1) * LANES)
            rows_ref[slab, rows, :] = real_part[:, columns]
            rows_ref[slabs + slab, rows, :] = imag_part[:, columns]
    for part in range(2):
        for slab in range(slabs):
            columns = slice(slab * LANES, (slab + 1) * LANES)
            values = rows_ref[part * slabs + slab, : own_ref.shape[0], :]
            spectra_ref[part, :, columns] = values.astype(jnp.bfloat16)


def channel_of(time):
    return time % 4


def place_in_plane(near, time, times):
    count = NEAR * times
    middle = NEAR // 2 * times + times // 2
    return 3 * (near * times + time + count - middle) % count


def spread_kernel(mine_ref, parcels_ref, turned_ref):
    count, rows, width = parcels_ref.shape
    times = count // NEAR
    stride = mine_ref.shape[1] // rows
    for place in range(0, mine_ref.shape[1], LANES):
        values = mine_ref[:, place : place + LANES].astype(jnp.float32)
        turned_ref[place : place + LANES, :] = values.T
    for near in range(NEAR):
        for channel in range(stride // NEAR):
            start = near * (stride // NEAR) + channel
            values = turned_ref[pl.ds(start, rows, stride=stride), :].astype(jnp.bfloat16)
            for time in range(times):
                if channel_of(time) == channel:
                    parcels_ref[place_in_plane(near, time, times)] = values


def correlate_kernel(frames_all, inputs_here, place_ref, every_ref, packed_ref):
    count, lines, width = every_ref.shape
    blocks, rows, inputs_all = packed_ref.shape
    times = count // NEAR
    main = lines - 2 * EARLY
    carry = None
    lined = []
    for time in range(times):
        pieces = [every_ref[place_in_plane(near, time, times)] for near in range(NEAR)]
        wide = jnp.concatenate([piece.astype(jnp.float32) for piece in pieces], axis=1)
        tiles = [wide[start : start + 8] for start in range(0, lines, 8)]
        if carry is not None:
            early = lax.broadcasted_iota(jnp.int32, carry.shape, 0) < EARLY
            tiles[0] = tiles[0] + jnp.where(early, carry, 0.0)
            tiles[1] = tiles[1] + jnp.where(early, pltpu.roll(carry, 8 - EARLY, 0), 0.0)
        carry = tiles[-1]
        lined += tiles[:-1]
    far = width // inputs_here
    target = lax.broadcasted_iota(jnp.int32, (1, inputs_all), 1)
    near = target // inputs_here % NEAR
    listed = place_in_column(target // (inputs_here * NEAR), far)
    source = near * width + listed * inputs_here + target % inputs_here
    chosen = lax.broadcasted_iota(jnp.int32, (inputs_all, inputs_all), 0) == source
    ordered = jnp.dot(
        jnp.concatenate(lined, axis=0).astype(jnp.bfloat16),
        chosen.astype(jnp.float32).astype(jnp.bfloat16),
        preferred_element_type=jnp.float32,
    )
    right = ordered.astype(jnp.bfloat16)
    twisted = []
    for start in range(0, times * main, 16):
        twisted.append(ordered[start + 8 : start + 16])
        twisted.append(-ordered[start : start + 8])
    twisted = jnp.concatenate(twisted, axis=0).astype(jnp.bfloat16)
    held = blocks * rows
    first = place_ref[0] * held
    col_index = lax.broadcasted_iota(jnp.int32, (held, inputs_all), 1)
    row_index = lax.broadcasted_iota(jnp.int32, (held, inputs_all), 0) + first
    left = [jnp.where(first == 0, side[:, :held], side[:, held:]) for side in (right, twisted)]
    both = lax.dot_general(
        jnp.concatenate(left, axis=1),
        right,
        (((0,), (0,)), ((), ())),
        preferred_element_type=jnp.float32,
    )
    values = jnp.where(row_index <= col_index, both[:held], both[held:]) * (1.0 / frames_all)
    values = values.astype(jnp.bfloat16)
    for block in range(blocks):
        packed_ref[blocks - 1 - block] = values[block * rows : (block + 1) * rows]


def unpack_kernel(packed_ref, lines_hbm, lines_ref, left):
    channels, count, width = packed_ref.shape
    tiles = width // LANES
    stores = []
    for first in range(0, count, 16):
        start = first * tiles * channels
        for channel in range(channels):
            values = packed_ref[channels - 1 - channel, first : first + 16, :]
            values = values.astype(jnp.float32)
            for tile in range(tiles):
                lines = pl.ds(start + tile * channels + channel, 16, stride=tiles * channels)
                lines_ref[lines, :] = values[:, tile * LANES : (tile + 1) * LANES]
        block = pl.ds(start, 16 * tiles * channels)
        stores.append(
            pltpu.make_async_copy(lines_ref.at[block, :], lines_hbm.at[block, :], left.at[len(stores)])
        )
        stores[-1].start()
    for store in stores:
        store.wait()


def body(samples, gains):
    inputs_here = samples.shape[0]
    frames_here = samples.shape[1] // NFFT
    times = lax.axis_size("tm")
    far = lax.axis_size("far")
    groups = far * NEAR
    per_group = CH // groups
    inputs_all = inputs_here * groups
    frames_all = frames_here * times
    block = inputs_here * frames_here

    window = filter_window()
    twiddle = jnp.asarray(build_table(window)[: NFFT // 2])
    window_taps = jnp.asarray(window.astype(np.float32).reshape(TAPS, NFFT))

    sent = frames_here + EARLY
    gains = gains.transpose(0, 2, 1)

    def own_part(*refs):
        own_part_kernel(far, *refs)

    own, passed, parcels = pl.pallas_call(
        own_part,
        out_shape=(
            jax.ShapeDtypeStruct((block, 2 * CH), jnp.float32),
            jax.ShapeDtypeStruct(((TAPS - 1) * inputs_here, 2 * CH), jnp.float32),
            jax.ShapeDtypeStruct((far * inputs_here, sent * 2 * CH // far), jnp.bfloat16),
        ),
        in_specs=[ANY] * 4,
        out_specs=(ANY, ANY, ANY),
        scratch_shapes=[
            pltpu.VMEM(samples.shape, jnp.bfloat16),
            pltpu.VMEM(window_taps.shape, jnp.float32),
            pltpu.VMEM(twiddle.shape, jnp.bfloat16),
            pltpu.VMEM(gains.shape, jnp.float32),
            pltpu.VMEM((sent * inputs_here, 2 * CH), jnp.float32),
            pltpu.VMEM((far * inputs_here, sent * 2 * CH // far), jnp.bfloat16),
            pltpu.SemaphoreType.DMA((2 + frames_here // 2 + NFFT // STEP,)),
            pltpu.SemaphoreType.DMA((2 + sent // 4,)),
        ],
        compiler_params=pltpu.CompilerParams(vmem_limit_bytes=OWN_PART_VMEM),
        cost_estimate=pl.CostEstimate(
            flops=2 * sent * inputs_here * NFFT * 2 * CH,
            bytes_accessed=3 * 1024 * 1024,
            transcendentals=0,
        ),
        name="own_part",
    )(samples, window_taps, twiddle, gains)

    parcels = parcels.reshape(far, inputs_here, sent * 2 * CH // far)
    column = [sorted(range(far), key=lambda place: place_in_column(place, far))]
    mine = lax.all_to_all(parcels, "far", 0, 0, axis_index_groups=column)
    mine = mine.reshape(far * inputs_here, sent * 2 * CH // far)

    passed = lax.ppermute(passed, "tm", [(source, source + 1) for source in range(times - 1)])
    spectra = pl.pallas_call(
        spectra_kernel,
        out_shape=jax.ShapeDtypeStruct((2, block, CH), jnp.bfloat16),
        in_specs=[VMEM] * 3,
        out_specs=VMEM,
        scratch_shapes=[pltpu.VMEM((2 * CH // LANES, block + frames_here, LANES), jnp.float32)],
        compiler_params=PARAMS,
        cost_estimate=pl.CostEstimate(
            flops=8 * block * 2 * CH, bytes_accessed=1024 * 1024, transcendentals=0
        ),
        name="spectra",
    )(passed, own, gains)
    mine, spectra = lax.optimization_barrier((mine, spectra))
    spectra = spectra.reshape(2, inputs_here, frames_here, CH).transpose(0, 3, 1, 2)

    lines = 2 * sent
    spread = pl.pallas_call(
        spread_kernel,
        out_shape=jax.ShapeDtypeStruct((NEAR * times, lines, far * inputs_here), jnp.bfloat16),
        in_specs=[VMEM],
        out_specs=VMEM,
        scratch_shapes=[pltpu.VMEM(((sent + 1) * 2 * CH // far, far * inputs_here), jnp.float32)],
        compiler_params=PARAMS,
        name="spread",
    )(mine)
    place = lax.axis_index("tm").astype(jnp.int32)
    square = (place // 4)[None]
    spread, square = lax.optimization_barrier((spread, square))
    members = [(near, time) for near in range(NEAR) for time in range(times)]
    members.sort(key=lambda member: place_in_plane(*member, times))
    plane = [[near * times + time for near, time in members]]
    every = lax.all_to_all(spread, ("near", "tm"), 0, 0, axis_index_groups=plane)

    def correlate(*refs):
        correlate_kernel(frames_all, inputs_here, *refs)

    rows = inputs_all // times
    packed = pl.pallas_call(
        correlate,
        out_shape=jax.ShapeDtypeStruct((per_group, rows, inputs_all), jnp.bfloat16),
        in_specs=[SMEM, VMEM],
        out_specs=VMEM,
        compiler_params=PARAMS,
        name="correlate",
    )(square, every)
    squares = [[3, 2, 1, 0], [7, 6, 5, 4]]
    packed = lax.all_to_all(packed, "tm", 0, 0, axis_index_groups=squares)
    tiles = inputs_all // LANES
    visibilities = pl.pallas_call(
        unpack_kernel,
        out_shape=jax.ShapeDtypeStruct((rows * tiles * per_group, LANES), jnp.float32),
        in_specs=[VMEM],
        out_specs=ANY,
        scratch_shapes=[
            pltpu.VMEM(((rows + 1) * tiles * per_group, LANES), jnp.float32),
            pltpu.SemaphoreType.DMA((rows // 16,)),
        ],
        compiler_params=PARAMS,
        name="unpack",
    )(packed)
    visibilities = visibilities.reshape(rows, tiles, per_group, LANES).transpose(0, 2, 1, 3)
    visibilities = visibilities.reshape(rows, per_group, inputs_all)
    return (spectra, visibilities)


def solution(mesh):
    groups, times = mesh.devices.shape
    split = Mesh(mesh.devices.reshape(groups // NEAR, NEAR, times), ("far", "near", "tm"))
    inputs = ("far", "near")
    return jax.shard_map(
        body,
        mesh=split,
        in_specs=(P(inputs, "tm"), P(None, None, inputs)),
        out_specs=(P(None, None, inputs, "tm"), P("tm", inputs, None)),
        check_vma=False,
    )
```

```python
import math

import jax
import jax.numpy as jnp
import numpy as np
from jax import lax
from jax.experimental import pallas as pl
from jax.experimental.pallas import tpu as pltpu
from jax.sharding import Mesh, PartitionSpec as P

NFFT = 2048
CH = 256
FIRST = 384
TAPS = 4
NEAR = 4
EARLY = 4
STEP = 256
LANES = 128
VMEM = pl.BlockSpec(memory_space=pltpu.VMEM)
ANY = pl.BlockSpec(memory_space=pl.ANY)
SMEM = pl.BlockSpec(memory_space=pltpu.SMEM)
OWN_PART_VMEM = 59 * 1024 * 1024 + 768 * 1024
PARAMS = pltpu.CompilerParams(vmem_limit_bytes=32 * 1024 * 1024)


def filter_window():
    length = TAPS * NFFT
    position = np.arange(length, dtype=np.float64)
    centred = (position - 0.5 * length + 0.5) / NFFT
    hann_taper = 0.5 - 0.5 * np.cos(2.0 * math.pi * (position + 0.5) / length)
    return np.sinc(centred) * hann_taper


def build_table(window):
    norm_scale = 1.0 / np.sqrt(np.sum(window * window))
    sample = np.arange(NFFT)[:, None]
    channel = FIRST + np.arange(CH)[None, :]
    phase_angle = 2.0 * math.pi / NFFT * (sample * channel % NFFT)
    cosine = np.cos(phase_angle) * norm_scale
    sine = -np.sin(phase_angle) * norm_scale
    return np.concatenate([cosine, sine], axis=1).astype(jnp.bfloat16)


def tapped_block(samples_ref, window_ref, frames_sent, block):
    inputs_here, count = samples_ref.shape
    frames_here = count // NFFT
    low = block * STEP
    sums = []
    for frame in range(frames_sent):
        total = jnp.zeros((inputs_here, STEP), jnp.float32)
        for tap in range(TAPS):
            source = frame - TAPS + 1 + tap
            if 0 <= source < frames_here:
                start = source * NFFT + low
                values = samples_ref[:, start : start + STEP]
                weights = window_ref[tap : tap + 1, low : low + STEP]
                total = total + weights * values.astype(jnp.float32)
        sums.append(total)
    pairs = [
        jnp.concatenate(sums[frame : frame + 2], axis=0).astype(jnp.bfloat16)
        for frame in range(0, frames_sent, 2)
    ]
    return jnp.concatenate(pairs, axis=0)


def turn_granules(blocks, size):
    count = len(blocks)
    lanes = count * size
    granule = lax.broadcasted_iota(jnp.int32, blocks[0].shape, 1) // size
    blocks = list(blocks)
    distance = count // 2
    while distance:
        upper = (granule & distance) != 0
        shift = distance * size
        for index in range(count):
            if index & distance:
                continue
            low, high = blocks[index], blocks[index + distance]
            blocks[index] = jnp.where(upper, pltpu.roll(high, shift, 1), low)
            blocks[index + distance] = jnp.where(upper, high, pltpu.roll(low, lanes - shift, 1))
        distance //= 2
    return blocks


def place_in_column(place, far):
    return (far * 5 // 8 + far - place) % far


def own_part_kernel(
    far,
    samples_hbm,
    window_hbm,
    twiddle_hbm,
    gains_hbm,
    own_hbm,
    passed_hbm,
    parcels_hbm,
    samples_ref,
    window_ref,
    twiddle_ref,
    gains_ref,
    direct_ref,
    parcels_ref,
    arrived,
    left,
):
    inputs_here = gains_ref.shape[1]
    frames_here = samples_hbm.shape[1] // NFFT
    blocks = range(NFFT // STEP)
    fetches = []

    def fetch(source, target):
        fetches.append(pltpu.make_async_copy(source, target, arrived.at[len(fetches)]))
        fetches[-1].start()
        return fetches[-1]

    samples_in = fetch(samples_hbm, samples_ref)
    window_in = fetch(window_hbm, window_ref)
    table_in = []
    for block in range(0, len(blocks) // 2, 2):
        rows = pl.ds(block * STEP, 2 * STEP)
        table_in += [fetch(twiddle_hbm.at[rows, :], twiddle_ref.at[rows, :]), None]
    gains_in = fetch(gains_hbm, gains_ref)
    samples_in.wait()
    window_in.wait()
    total = None
    sent = frames_here + EARLY
    for block, table in enumerate(table_in):
        tapped = [
            tapped_block(samples_ref, window_ref, sent, half + block)
            for half in (0, len(table_in))
        ]
        if table is not None:
            table.wait()
        product = jnp.dot(
            jnp.concatenate(tapped, axis=0),
            twiddle_ref[block * STEP : (block + 1) * STEP, :],
            preferred_element_type=jnp.float32,
        )
        total = product if total is None else total + product
    channel = FIRST + lax.broadcasted_iota(jnp.int32, (1, 2 * CH), 1)
    sign = (1 - 2 * (channel % 2)).astype(jnp.float32)
    direct_ref[...] = total[: sent * inputs_here] + sign * total[sent * inputs_here :]
    own_rows = own_hbm.shape[0]
    passed_rows = passed_hbm.shape[0]
    stores = [
        pltpu.make_async_copy(direct_ref.at[pl.ds(0, own_rows), :], own_hbm, left.at[0]),
        pltpu.make_async_copy(
            direct_ref.at[pl.ds(own_rows, passed_rows), :], passed_hbm, left.at[1]
        ),
    ]
    for store in stores:
        store.start()
    gains_in.wait()
    gain_re = gains_ref[0]
    gain_im = gains_ref[1]
    parts = []
    for frame in range(frames_here + EARLY):
        direct = direct_ref[frame * inputs_here : (frame + 1) * inputs_here, :]
        direct_re = direct[:, :CH]
        direct_im = direct[:, CH:]
        parts.append(
            (
                gain_re * direct_re - gain_im * direct_im,
                gain_re * direct_im + gain_im * direct_re,
            )
        )
    slots = [
        [(part, frame) for frame in range(first, first + 8)]
        for first in range(0, frames_here, 8)
        for part in range(2)
    ]
    slots.append([(part, frames_here + frame) for part in range(2) for frame in range(EARLY)])
    per_far = CH // far
    for place, slot in enumerate(slots):
        columns = slice(place * LANES, (place + 1) * LANES)
        blocks = []
        for half in range(CH // LANES):
            lanes = slice(half * LANES, (half + 1) * LANES)
            blocks += turn_granules([parts[frame][part][:, lanes] for part, frame in slot], per_far)
        listed = sorted(range(far), key=lambda target: place_in_column(target, far))
        for index in range(0, far, 2):
            rows = slice(index * inputs_here, (index + 2) * inputs_here)
            parcels_ref[rows, columns] = jnp.concatenate(
                [blocks[target] for target in listed[index : index + 2]], axis=0
            ).astype(jnp.bfloat16)
        if place in (2, len(slots) - 1):
            first = 0 if place == 2 else 3
            lanes = pl.ds(first * LANES, (place + 1 - first) * LANES)
            stores.append(
                pltpu.make_async_copy(
                    parcels_ref.at[:, lanes], parcels_hbm.at[:, lanes], left.at[len(stores)]
                )
            )
            stores[-1].start()
    for store in stores:
        store.wait()


def spectra_kernel(passed_ref, own_ref, gains_ref, spectra_ref, rows_ref):
    inputs_here = gains_ref.shape[1]
    frames_here = own_ref.shape[0] // inputs_here
    slabs = CH // LANES
    gain_re = gains_ref[0]
    gain_im = gains_ref[1]
    for frame in range(frames_here):
        block = slice(frame * inputs_here, (frame + 1) * inputs_here)
        direct = own_ref[block, :]
        if frame < TAPS - 1:
            direct = direct + passed_ref[block, :]
        direct_re = direct[:, :CH]
        direct_im = direct[:, CH:]
        rows = pl.ds(frame, inputs_here, stride=frames_here)
        real_part = gain_re * direct_re - gain_im * direct_im
        imag_part = gain_re * direct_im + gain_im * direct_re
        for slab in range(slabs):
            columns = slice(slab * LANES, (slab + 1) * LANES)
            rows_ref[slab, rows, :] = real_part[:, columns]
            rows_ref[slabs + slab, rows, :] = imag_part[:, columns]
    for part in range(2):
        for slab in range(slabs):
            columns = slice(slab * LANES, (slab + 1) * LANES)
            values = rows_ref[part * slabs + slab, : own_ref.shape[0], :]
            spectra_ref[part, :, columns] = values.astype(jnp.bfloat16)


def channel_of(time):
    return time % 4


def place_in_plane(near, time, times):
    count = NEAR * times
    middle = NEAR // 2 * times + times // 2
    return 3 * (near * times + time + count - middle) % count


def spread_kernel(mine_ref, parcels_ref, turned_ref):
    count, rows, width = parcels_ref.shape
    times = count // NEAR
    stride = mine_ref.shape[1] // rows
    for place in range(0, mine_ref.shape[1], LANES):
        values = mine_ref[:, place : place + LANES].astype(jnp.float32)
        turned_ref[place : place + LANES, :] = values.T
    for near in range(NEAR):
        for channel in range(stride // NEAR):
            start = near * (stride // NEAR) + channel
            values = turned_ref[pl.ds(start, rows, stride=stride), :].astype(jnp.bfloat16)
            for time in range(times):
                if channel_of(time) == channel:
                    parcels_ref[place_in_plane(near, time, times)] = values


def correlate_kernel(frames_all, inputs_here, place_ref, every_ref, packed_ref):
    count, lines, width = every_ref.shape
    blocks, rows, inputs_all = packed_ref.shape
    times = count // NEAR
    main = lines - 2 * EARLY
    carry = None
    lined = []
    for time in range(times):
        pieces = [every_ref[place_in_plane(near, time, times)] for near in range(NEAR)]
        wide = jnp.concatenate([piece.astype(jnp.float32) for piece in pieces], axis=1)
        tiles = [wide[start : start + 8] for start in range(0, lines, 8)]
        if carry is not None:
            early = lax.broadcasted_iota(jnp.int32, carry.shape, 0) < EARLY
            tiles[0] = tiles[0] + jnp.where(early, carry, 0.0)
            tiles[1] = tiles[1] + jnp.where(early, pltpu.roll(carry, 8 - EARLY, 0), 0.0)
        carry = tiles[-1]
        lined += tiles[:-1]
    far = width // inputs_here
    target = lax.broadcasted_iota(jnp.int32, (1, inputs_all), 1)
    near = target // inputs_here % NEAR
    listed = place_in_column(target // (inputs_here * NEAR), far)
    source = near * width + listed * inputs_here + target % inputs_here
    chosen = lax.broadcasted_iota(jnp.int32, (inputs_all, inputs_all), 0) == source
    ordered = jnp.dot(
        jnp.concatenate(lined, axis=0).astype(jnp.bfloat16),
        chosen.astype(jnp.float32).astype(jnp.bfloat16),
        preferred_element_type=jnp.float32,
    )
    right = ordered.astype(jnp.bfloat16)
    twisted = []
    for start in range(0, times * main, 16):
        twisted.append(ordered[start + 8 : start + 16])
        twisted.append(-ordered[start : start + 8])
    twisted = jnp.concatenate(twisted, axis=0).astype(jnp.bfloat16)
    held = blocks * rows
    first = place_ref[0] * held
    col_index = lax.broadcasted_iota(jnp.int32, (held, inputs_all), 1)
    row_index = lax.broadcasted_iota(jnp.int32, (held, inputs_all), 0) + first
    left = [jnp.where(first == 0, side[:, :held], side[:, held:]) for side in (right, twisted)]
    both = lax.dot_general(
        jnp.concatenate(left, axis=1),
        right,
        (((0,), (0,)), ((), ())),
        preferred_element_type=jnp.float32,
    )
    values = jnp.where(row_index <= col_index, both[:held], both[held:]) * (1.0 / frames_all)
    values = values.astype(jnp.bfloat16)
    for block in range(blocks):
        packed_ref[blocks - 1 - block] = values[block * rows : (block + 1) * rows]


def unpack_kernel(packed_ref, lines_hbm, lines_ref, left):
    channels, count, width = packed_ref.shape
    tiles = width // LANES
    stores = []
    for first in range(0, count, 32):
        start = first * tiles * channels
        for channel in range(channels):
            values = packed_ref[channels - 1 - channel, first : first + 32, :]
            values = values.astype(jnp.float32)
            for tile in range(tiles):
                lines = pl.ds(start + tile * channels + channel, 32, stride=tiles * channels)
                lines_ref[lines, :] = values[:, tile * LANES : (tile + 1) * LANES]
        block = pl.ds(start, 32 * tiles * channels)
        stores.append(
            pltpu.make_async_copy(lines_ref.at[block, :], lines_hbm.at[block, :], left.at[len(stores)])
        )
        stores[-1].start()
    for store in stores:
        store.wait()


def body(samples, gains):
    inputs_here = samples.shape[0]
    frames_here = samples.shape[1] // NFFT
    times = lax.axis_size("tm")
    far = lax.axis_size("far")
    groups = far * NEAR
    per_group = CH // groups
    inputs_all = inputs_here * groups
    frames_all = frames_here * times
    block = inputs_here * frames_here

    window = filter_window()
    twiddle = jnp.asarray(build_table(window)[: NFFT // 2])
    window_taps = jnp.asarray(window.astype(np.float32).reshape(TAPS, NFFT))

    sent = frames_here + EARLY
    gains = gains.transpose(0, 2, 1)

    def own_part(*refs):
        own_part_kernel(far, *refs)

    own, passed, parcels = pl.pallas_call(
        own_part,
        out_shape=(
            jax.ShapeDtypeStruct((block, 2 * CH), jnp.float32),
            jax.ShapeDtypeStruct(((TAPS - 1) * inputs_here, 2 * CH), jnp.float32),
            jax.ShapeDtypeStruct((far * inputs_here, sent * 2 * CH // far), jnp.bfloat16),
        ),
        in_specs=[ANY] * 4,
        out_specs=(ANY, ANY, ANY),
        scratch_shapes=[
            pltpu.VMEM(samples.shape, jnp.bfloat16),
            pltpu.VMEM(window_taps.shape, jnp.float32),
            pltpu.VMEM(twiddle.shape, jnp.bfloat16),
            pltpu.VMEM(gains.shape, jnp.float32),
            pltpu.VMEM((sent * inputs_here, 2 * CH), jnp.float32),
            pltpu.VMEM((far * inputs_here, sent * 2 * CH // far), jnp.bfloat16),
            pltpu.SemaphoreType.DMA((3 + NFFT // (4 * STEP),)),
            pltpu.SemaphoreType.DMA((4,)),
        ],
        compiler_params=pltpu.CompilerParams(vmem_limit_bytes=OWN_PART_VMEM),
        cost_estimate=pl.CostEstimate(
            flops=2 * sent * inputs_here * NFFT * 2 * CH,
            bytes_accessed=3 * 1024 * 1024,
            transcendentals=0,
        ),
        name="own_part",
    )(samples, window_taps, twiddle, gains)

    parcels = parcels.reshape(far, inputs_here, sent * 2 * CH // far)
    column = [sorted(range(far), key=lambda place: place_in_column(place, far))]
    mine = lax.all_to_all(parcels, "far", 0, 0, axis_index_groups=column)
    mine = mine.reshape(far * inputs_here, sent * 2 * CH // far)

    passed = lax.ppermute(passed, "tm", [(source, source + 1) for source in range(times - 1)])
    spectra = pl.pallas_call(
        spectra_kernel,
        out_shape=jax.ShapeDtypeStruct((2, block, CH), jnp.bfloat16),
        in_specs=[VMEM] * 3,
        out_specs=VMEM,
        scratch_shapes=[pltpu.VMEM((2 * CH // LANES, block + frames_here, LANES), jnp.float32)],
        compiler_params=PARAMS,
        cost_estimate=pl.CostEstimate(
            flops=8 * block * 2 * CH, bytes_accessed=1024 * 1024, transcendentals=0
        ),
        name="spectra",
    )(passed, own, gains)
    mine, spectra = lax.optimization_barrier((mine, spectra))
    spectra = spectra.reshape(2, inputs_here, frames_here, CH).transpose(0, 3, 1, 2)

    lines = 2 * sent
    spread = pl.pallas_call(
        spread_kernel,
        out_shape=jax.ShapeDtypeStruct((NEAR * times, lines, far * inputs_here), jnp.bfloat16),
        in_specs=[VMEM],
        out_specs=VMEM,
        scratch_shapes=[pltpu.VMEM(((sent + 1) * 2 * CH // far, far * inputs_here), jnp.float32)],
        compiler_params=PARAMS,
        name="spread",
    )(mine)
    place = lax.axis_index("tm").astype(jnp.int32)
    square = (place // 4)[None]
    spread, square = lax.optimization_barrier((spread, square))
    members = [(near, time) for near in range(NEAR) for time in range(times)]
    members.sort(key=lambda member: place_in_plane(*member, times))
    plane = [[near * times + time for near, time in members]]
    every = lax.all_to_all(spread, ("near", "tm"), 0, 0, axis_index_groups=plane)

    def correlate(*refs):
        correlate_kernel(frames_all, inputs_here, *refs)

    rows = inputs_all // times
    packed = pl.pallas_call(
        correlate,
        out_shape=jax.ShapeDtypeStruct((per_group, rows, inputs_all), jnp.bfloat16),
        in_specs=[SMEM, VMEM],
        out_specs=VMEM,
        compiler_params=PARAMS,
        name="correlate",
    )(square, every)
    squares = [[3, 2, 1, 0], [7, 6, 5, 4]]
    packed = lax.all_to_all(packed, "tm", 0, 0, axis_index_groups=squares)
    tiles = inputs_all // LANES
    visibilities = pl.pallas_call(
        unpack_kernel,
        out_shape=jax.ShapeDtypeStruct((rows * tiles * per_group, LANES), jnp.float32),
        in_specs=[VMEM],
        out_specs=ANY,
        scratch_shapes=[
            pltpu.VMEM(((rows + 1) * tiles * per_group, LANES), jnp.float32),
            pltpu.SemaphoreType.DMA((rows // 32,)),
        ],
        compiler_params=PARAMS,
        name="unpack",
    )(packed)
    visibilities = visibilities.reshape(rows, tiles, per_group, LANES).transpose(0, 2, 1, 3)
    visibilities = visibilities.reshape(rows, per_group, inputs_all)
    return (spectra, visibilities)


def solution(mesh):
    groups, times = mesh.devices.shape
    split = Mesh(mesh.devices.reshape(groups // NEAR, NEAR, times), ("far", "near", "tm"))
    inputs = ("far", "near")
    return jax.shard_map(
        body,
        mesh=split,
        in_specs=(P(inputs, "tm"), P(None, None, inputs)),
        out_specs=(P(None, None, inputs, "tm"), P("tm", inputs, None)),
        check_vma=False,
    )
```

```python
import math

import jax
import jax.numpy as jnp
import numpy as np
from jax import lax
from jax.experimental import pallas as pl
from jax.experimental.pallas import tpu as pltpu
from jax.sharding import Mesh, PartitionSpec as P

NFFT = 2048
CH = 256
FIRST = 384
TAPS = 4
NEAR = 4
EARLY = 4
STEP = 256
LANES = 128
VMEM = pl.BlockSpec(memory_space=pltpu.VMEM)
ANY = pl.BlockSpec(memory_space=pl.ANY)
SMEM = pl.BlockSpec(memory_space=pltpu.SMEM)
OWN_PART_VMEM = 59 * 1024 * 1024 + 768 * 1024
PARAMS = pltpu.CompilerParams(vmem_limit_bytes=32 * 1024 * 1024)


def filter_window():
    length = TAPS * NFFT
    position = np.arange(length, dtype=np.float64)
    centred = (position - 0.5 * length + 0.5) / NFFT
    hann_taper = 0.5 - 0.5 * np.cos(2.0 * math.pi * (position + 0.5) / length)
    return np.sinc(centred) * hann_taper


def build_table(window):
    norm_scale = 1.0 / np.sqrt(np.sum(window * window))
    sample = np.arange(NFFT)[:, None]
    channel = FIRST + np.arange(CH)[None, :]
    phase_angle = 2.0 * math.pi / NFFT * (sample * channel % NFFT)
    cosine = np.cos(phase_angle) * norm_scale
    sine = -np.sin(phase_angle) * norm_scale
    return np.concatenate([cosine, sine], axis=1).astype(jnp.bfloat16)


def tapped_block(samples_ref, window_ref, frames_sent, block):
    inputs_here, count = samples_ref.shape
    frames_here = count // NFFT
    low = block * STEP
    sums = []
    for frame in range(frames_sent):
        total = jnp.zeros((inputs_here, STEP), jnp.float32)
        for tap in range(TAPS):
            source = frame - TAPS + 1 + tap
            if 0 <= source < frames_here:
                start = source * NFFT + low
                values = samples_ref[:, start : start + STEP]
                weights = window_ref[tap : tap + 1, low : low + STEP]
                total = total + weights * values.astype(jnp.float32)
        sums.append(total)
    pairs = [
        jnp.concatenate(sums[frame : frame + 2], axis=0).astype(jnp.bfloat16)
        for frame in range(0, frames_sent, 2)
    ]
    return jnp.concatenate(pairs, axis=0)


def turn_granules(blocks, size):
    count = len(blocks)
    lanes = count * size
    granule = lax.broadcasted_iota(jnp.int32, blocks[0].shape, 1) // size
    blocks = list(blocks)
    distance = count // 2
    while distance:
        upper = (granule & distance) != 0
        shift = distance * size
        for index in range(count):
            if index & distance:
                continue
            low, high = blocks[index], blocks[index + distance]
            blocks[index] = jnp.where(upper, pltpu.roll(high, shift, 1), low)
            blocks[index + distance] = jnp.where(upper, high, pltpu.roll(low, lanes - shift, 1))
        distance //= 2
    return blocks


def place_in_column(place, far):
    return (far * 5 // 8 + far - place) % far


def own_part_kernel(
    far,
    samples_hbm,
    window_hbm,
    twiddle_hbm,
    gains_hbm,
    own_hbm,
    passed_hbm,
    parcels_hbm,
    samples_ref,
    window_ref,
    twiddle_ref,
    gains_ref,
    direct_ref,
    parcels_ref,
    arrived,
    left,
):
    inputs_here = gains_ref.shape[1]
    frames_here = samples_hbm.shape[1] // NFFT
    blocks = range(NFFT // STEP)
    fetches = []

    def fetch(source, target):
        fetches.append(pltpu.make_async_copy(source, target, arrived.at[len(fetches)]))
        fetches[-1].start()
        return fetches[-1]

    samples_in = fetch(samples_hbm, samples_ref)
    window_in = fetch(window_hbm, window_ref)
    table_in = []
    for block in range(0, len(blocks) // 2, 2):
        rows = pl.ds(block * STEP, 2 * STEP)
        table_in += [fetch(twiddle_hbm.at[rows, :], twiddle_ref.at[rows, :]), None]
    gains_in = fetch(gains_hbm, gains_ref)
    samples_in.wait()
    window_in.wait()
    total = None
    sent = frames_here + EARLY
    for block, table in enumerate(table_in):
        tapped = [
            tapped_block(samples_ref, window_ref, sent, half + block)
            for half in (0, len(table_in))
        ]
        if table is not None:
            table.wait()
        product = jnp.dot(
            jnp.concatenate(tapped, axis=0),
            twiddle_ref[block * STEP : (block + 1) * STEP, :],
            preferred_element_type=jnp.float32,
        )
        total = product if total is None else total + product
    channel = FIRST + lax.broadcasted_iota(jnp.int32, (1, 2 * CH), 1)
    sign = (1 - 2 * (channel % 2)).astype(jnp.float32)
    direct_ref[...] = total[: sent * inputs_here] + sign * total[sent * inputs_here :]
    own_rows = own_hbm.shape[0]
    passed_rows = passed_hbm.shape[0]
    stores = [
        pltpu.make_async_copy(direct_ref.at[pl.ds(0, own_rows), :], own_hbm, left.at[0]),
        pltpu.make_async_copy(
            direct_ref.at[pl.ds(own_rows, passed_rows), :], passed_hbm, left.at[1]
        ),
    ]
    for store in stores:
        store.start()
    gains_in.wait()
    gain_re = gains_ref[0]
    gain_im = gains_ref[1]
    parts = []
    for frame in range(frames_here + EARLY):
        direct = direct_ref[frame * inputs_here : (frame + 1) * inputs_here, :]
        direct_re = direct[:, :CH]
        direct_im = direct[:, CH:]
        parts.append(
            (
                gain_re * direct_re - gain_im * direct_im,
                gain_re * direct_im + gain_im * direct_re,
            )
        )
    slots = [
        [(part, frame) for frame in range(first, first + 8)]
        for first in range(0, frames_here, 8)
        for part in range(2)
    ]
    slots.append([(part, frames_here + frame) for part in range(2) for frame in range(EARLY)])
    per_far = CH // far
    for place, slot in enumerate(slots):
        columns = slice(place * LANES, (place + 1) * LANES)
        blocks = []
        for half in range(CH // LANES):
            lanes = slice(half * LANES, (half + 1) * LANES)
            blocks += turn_granules([parts[frame][part][:, lanes] for part, frame in slot], per_far)
        listed = sorted(range(far), key=lambda target: place_in_column(target, far))
        for index in range(0, far, 2):
            rows = slice(index * inputs_here, (index + 2) * inputs_here)
            parcels_ref[rows, columns] = jnp.concatenate(
                [blocks[target] for target in listed[index : index + 2]], axis=0
            ).astype(jnp.bfloat16)
        if place in (2, len(slots) - 1):
            first = 0 if place == 2 else 3
            lanes = pl.ds(first * LANES, (place + 1 - first) * LANES)
            stores.append(
                pltpu.make_async_copy(
                    parcels_ref.at[:, lanes], parcels_hbm.at[:, lanes], left.at[len(stores)]
                )
            )
            stores[-1].start()
    for store in stores:
        store.wait()


def spectra_kernel(passed_ref, own_ref, gains_ref, spectra_ref, rows_ref):
    inputs_here = gains_ref.shape[1]
    frames_here = own_ref.shape[0] // inputs_here
    slabs = CH // LANES
    gain_re = gains_ref[0]
    gain_im = gains_ref[1]
    for frame in range(frames_here):
        block = slice(frame * inputs_here, (frame + 1) * inputs_here)
        direct = own_ref[block, :]
        if frame < TAPS - 1:
            direct = direct + passed_ref[block, :]
        direct_re = direct[:, :CH]
        direct_im = direct[:, CH:]
        rows = pl.ds(frame, inputs_here, stride=frames_here)
        real_part = gain_re * direct_re - gain_im * direct_im
        imag_part = gain_re * direct_im + gain_im * direct_re
        for slab in range(slabs):
            columns = slice(slab * LANES, (slab + 1) * LANES)
            rows_ref[slab, rows, :] = real_part[:, columns]
            rows_ref[slabs + slab, rows, :] = imag_part[:, columns]
    for part in range(2):
        for slab in range(slabs):
            columns = slice(slab * LANES, (slab + 1) * LANES)
            values = rows_ref[part * slabs + slab, : own_ref.shape[0], :]
            spectra_ref[part, :, columns] = values.astype(jnp.bfloat16)


def channel_of(time):
    return time % 4


def place_in_square(member, square):
    return member ^ (3 - 2 * square)


def place_in_plane(near, time, times):
    count = NEAR * times
    middle = NEAR // 2 * times + times // 2
    return 3 * (near * times + time + count - middle) % count


def spread_kernel(mine_ref, parcels_ref, turned_ref):
    count, rows, width = parcels_ref.shape
    times = count // NEAR
    stride = mine_ref.shape[1] // rows
    for place in range(0, mine_ref.shape[1], LANES):
        values = mine_ref[:, place : place + LANES].astype(jnp.float32)
        turned_ref[place : place + LANES, :] = values.T
    for near in range(NEAR):
        for channel in range(stride // NEAR):
            start = near * (stride // NEAR) + channel
            values = turned_ref[pl.ds(start, rows, stride=stride), :].astype(jnp.bfloat16)
            for time in range(times):
                if channel_of(time) == channel:
                    parcels_ref[place_in_plane(near, time, times)] = values


def correlate_kernel(frames_all, inputs_here, place_ref, every_ref, packed_ref):
    count, lines, width = every_ref.shape
    blocks, rows, inputs_all = packed_ref.shape
    times = count // NEAR
    main = lines - 2 * EARLY
    carry = None
    lined = []
    for time in range(times):
        pieces = [every_ref[place_in_plane(near, time, times)] for near in range(NEAR)]
        wide = jnp.concatenate([piece.astype(jnp.float32) for piece in pieces], axis=1)
        tiles = [wide[start : start + 8] for start in range(0, lines, 8)]
        if carry is not None:
            early = lax.broadcasted_iota(jnp.int32, carry.shape, 0) < EARLY
            tiles[0] = tiles[0] + jnp.where(early, carry, 0.0)
            tiles[1] = tiles[1] + jnp.where(early, pltpu.roll(carry, 8 - EARLY, 0), 0.0)
        carry = tiles[-1]
        lined += tiles[:-1]
    far = width // inputs_here
    target = lax.broadcasted_iota(jnp.int32, (1, inputs_all), 1)
    near = target // inputs_here % NEAR
    listed = place_in_column(target // (inputs_here * NEAR), far)
    source = near * width + listed * inputs_here + target % inputs_here
    chosen = lax.broadcasted_iota(jnp.int32, (inputs_all, inputs_all), 0) == source
    ordered = jnp.dot(
        jnp.concatenate(lined, axis=0).astype(jnp.bfloat16),
        chosen.astype(jnp.float32).astype(jnp.bfloat16),
        preferred_element_type=jnp.float32,
    )
    right = ordered.astype(jnp.bfloat16)
    twisted = []
    for start in range(0, times * main, 16):
        twisted.append(ordered[start + 8 : start + 16])
        twisted.append(-ordered[start : start + 8])
    twisted = jnp.concatenate(twisted, axis=0).astype(jnp.bfloat16)
    held = blocks * rows
    first = place_ref[0] * held
    col_index = lax.broadcasted_iota(jnp.int32, (held, inputs_all), 1)
    row_index = lax.broadcasted_iota(jnp.int32, (held, inputs_all), 0) + first
    left = [jnp.where(first == 0, side[:, :held], side[:, held:]) for side in (right, twisted)]
    both = lax.dot_general(
        jnp.concatenate(left, axis=1),
        right,
        (((0,), (0,)), ((), ())),
        preferred_element_type=jnp.float32,
    )
    values = jnp.where(row_index <= col_index, both[:held], both[held:]) * (1.0 / frames_all)
    values = values.astype(jnp.bfloat16)
    for block in range(blocks):
        target = place_in_square(block, place_ref[0])
        packed_ref[target] = values[block * rows : (block + 1) * rows]


def unpack_kernel(place_ref, packed_ref, lines_hbm, lines_ref, left):
    channels, count, width = packed_ref.shape
    tiles = width // LANES
    stores = []
    for first in range(0, count, 16):
        start = first * tiles * channels
        for channel in range(channels):
            values = packed_ref[place_in_square(channel, place_ref[0]), first : first + 16, :]
            values = values.astype(jnp.float32)
            for tile in range(tiles):
                lines = pl.ds(start + tile * channels + channel, 16, stride=tiles * channels)
                lines_ref[lines, :] = values[:, tile * LANES : (tile + 1) * LANES]
        block = pl.ds(start, 16 * tiles * channels)
        stores.append(
            pltpu.make_async_copy(lines_ref.at[block, :], lines_hbm.at[block, :], left.at[len(stores)])
        )
        stores[-1].start()
    for store in stores:
        store.wait()


def body(samples, gains):
    inputs_here = samples.shape[0]
    frames_here = samples.shape[1] // NFFT
    times = lax.axis_size("tm")
    far = lax.axis_size("far")
    groups = far * NEAR
    per_group = CH // groups
    inputs_all = inputs_here * groups
    frames_all = frames_here * times
    block = inputs_here * frames_here

    window = filter_window()
    twiddle = jnp.asarray(build_table(window)[: NFFT // 2])
    window_taps = jnp.asarray(window.astype(np.float32).reshape(TAPS, NFFT))

    sent = frames_here + EARLY
    gains = gains.transpose(0, 2, 1)

    def own_part(*refs):
        own_part_kernel(far, *refs)

    own, passed, parcels = pl.pallas_call(
        own_part,
        out_shape=(
            jax.ShapeDtypeStruct((block, 2 * CH), jnp.float32),
            jax.ShapeDtypeStruct(((TAPS - 1) * inputs_here, 2 * CH), jnp.float32),
            jax.ShapeDtypeStruct((far * inputs_here, sent * 2 * CH // far), jnp.bfloat16),
        ),
        in_specs=[ANY] * 4,
        out_specs=(ANY, ANY, ANY),
        scratch_shapes=[
            pltpu.VMEM(samples.shape, jnp.bfloat16),
            pltpu.VMEM(window_taps.shape, jnp.float32),
            pltpu.VMEM(twiddle.shape, jnp.bfloat16),
            pltpu.VMEM(gains.shape, jnp.float32),
            pltpu.VMEM((sent * inputs_here, 2 * CH), jnp.float32),
            pltpu.VMEM((far * inputs_here, sent * 2 * CH // far), jnp.bfloat16),
            pltpu.SemaphoreType.DMA((3 + NFFT // (4 * STEP),)),
            pltpu.SemaphoreType.DMA((4,)),
        ],
        compiler_params=pltpu.CompilerParams(vmem_limit_bytes=OWN_PART_VMEM),
        cost_estimate=pl.CostEstimate(
            flops=2 * sent * inputs_here * NFFT * 2 * CH,
            bytes_accessed=3 * 1024 * 1024,
            transcendentals=0,
        ),
        name="own_part",
    )(samples, window_taps, twiddle, gains)

    parcels = parcels.reshape(far, inputs_here, sent * 2 * CH // far)
    column = [sorted(range(far), key=lambda place: place_in_column(place, far))]
    mine = lax.all_to_all(parcels, "far", 0, 0, axis_index_groups=column)
    mine = mine.reshape(far * inputs_here, sent * 2 * CH // far)

    passed = lax.ppermute(passed, "tm", [(source, source + 1) for source in range(times - 1)])
    spectra = pl.pallas_call(
        spectra_kernel,
        out_shape=jax.ShapeDtypeStruct((2, block, CH), jnp.bfloat16),
        in_specs=[VMEM] * 3,
        out_specs=VMEM,
        scratch_shapes=[pltpu.VMEM((2 * CH // LANES, block + frames_here, LANES), jnp.float32)],
        compiler_params=PARAMS,
        cost_estimate=pl.CostEstimate(
            flops=8 * block * 2 * CH, bytes_accessed=1024 * 1024, transcendentals=0
        ),
        name="spectra",
    )(passed, own, gains)
    mine, spectra = lax.optimization_barrier((mine, spectra))
    spectra = spectra.reshape(2, inputs_here, frames_here, CH).transpose(0, 3, 1, 2)

    lines = 2 * sent
    spread = pl.pallas_call(
        spread_kernel,
        out_shape=jax.ShapeDtypeStruct((NEAR * times, lines, far * inputs_here), jnp.bfloat16),
        in_specs=[VMEM],
        out_specs=VMEM,
        scratch_shapes=[pltpu.VMEM(((sent + 1) * 2 * CH // far, far * inputs_here), jnp.float32)],
        compiler_params=PARAMS,
        name="spread",
    )(mine)
    place = lax.axis_index("tm").astype(jnp.int32)
    square = (place // 4)[None]
    spread, square = lax.optimization_barrier((spread, square))
    members = [(near, time) for near in range(NEAR) for time in range(times)]
    members.sort(key=lambda member: place_in_plane(*member, times))
    plane = [[near * times + time for near, time in members]]
    every = lax.all_to_all(spread, ("near", "tm"), 0, 0, axis_index_groups=plane)

    def correlate(*refs):
        correlate_kernel(frames_all, inputs_here, *refs)

    rows = inputs_all // times
    packed = pl.pallas_call(
        correlate,
        out_shape=jax.ShapeDtypeStruct((per_group, rows, inputs_all), jnp.bfloat16),
        in_specs=[SMEM, VMEM],
        out_specs=VMEM,
        compiler_params=PARAMS,
        name="correlate",
    )(square, every)
    squares = [
        [4 * side + place_in_square(member, side) for member in range(per_group)]
        for side in range(2)
    ]
    packed = lax.all_to_all(packed, "tm", 0, 0, axis_index_groups=squares)
    tiles = inputs_all // LANES
    visibilities = pl.pallas_call(
        unpack_kernel,
        out_shape=jax.ShapeDtypeStruct((rows * tiles * per_group, LANES), jnp.float32),
        in_specs=[SMEM, VMEM],
        out_specs=ANY,
        scratch_shapes=[
            pltpu.VMEM(((rows + 1) * tiles * per_group, LANES), jnp.float32),
            pltpu.SemaphoreType.DMA((rows // 16,)),
        ],
        compiler_params=PARAMS,
        name="unpack",
    )(square, packed)
    visibilities = visibilities.reshape(rows, tiles, per_group, LANES).transpose(0, 2, 1, 3)
    visibilities = visibilities.reshape(rows, per_group, inputs_all)
    return (spectra, visibilities)


def solution(mesh):
    groups, times = mesh.devices.shape
    split = Mesh(mesh.devices.reshape(groups // NEAR, NEAR, times), ("far", "near", "tm"))
    inputs = ("far", "near")
    return jax.shard_map(
        body,
        mesh=split,
        in_specs=(P(inputs, "tm"), P(None, None, inputs)),
        out_specs=(P(None, None, inputs, "tm"), P("tm", inputs, None)),
        check_vma=False,
    )
```

```python
import math

import jax
import jax.numpy as jnp
import numpy as np
from jax import lax
from jax.experimental import pallas as pl
from jax.experimental.pallas import tpu as pltpu
from jax.sharding import Mesh, PartitionSpec as P

NFFT = 2048
CH = 256
FIRST = 384
TAPS = 4
NEAR = 4
EARLY = 4
STEP = 256
LANES = 128
VMEM = pl.BlockSpec(memory_space=pltpu.VMEM)
ANY = pl.BlockSpec(memory_space=pl.ANY)
SMEM = pl.BlockSpec(memory_space=pltpu.SMEM)
OWN_PART_VMEM = 59 * 1024 * 1024 + 768 * 1024
PARAMS = pltpu.CompilerParams(vmem_limit_bytes=32 * 1024 * 1024)


def filter_window():
    length = TAPS * NFFT
    position = np.arange(length, dtype=np.float64)
    centred = (position - 0.5 * length + 0.5) / NFFT
    hann_taper = 0.5 - 0.5 * np.cos(2.0 * math.pi * (position + 0.5) / length)
    return np.sinc(centred) * hann_taper


def build_table(window):
    norm_scale = 1.0 / np.sqrt(np.sum(window * window))
    sample = np.arange(NFFT)[:, None]
    channel = FIRST + np.arange(CH)[None, :]
    phase_angle = 2.0 * math.pi / NFFT * (sample * channel % NFFT)
    cosine = np.cos(phase_angle) * norm_scale
    sine = -np.sin(phase_angle) * norm_scale
    return np.concatenate([cosine, sine], axis=1).astype(jnp.bfloat16)


def tapped_block(samples_ref, window_ref, frames_sent, block):
    inputs_here, count = samples_ref.shape
    frames_here = count // NFFT
    low = block * STEP
    sums = []
    for frame in range(frames_sent):
        total = jnp.zeros((inputs_here, STEP), jnp.float32)
        for tap in range(TAPS):
            source = frame - TAPS + 1 + tap
            if 0 <= source < frames_here:
                start = source * NFFT + low
                values = samples_ref[:, start : start + STEP]
                weights = window_ref[tap : tap + 1, low : low + STEP]
                total = total + weights * values.astype(jnp.float32)
        sums.append(total)
    pairs = [
        jnp.concatenate(sums[frame : frame + 2], axis=0).astype(jnp.bfloat16)
        for frame in range(0, frames_sent, 2)
    ]
    return jnp.concatenate(pairs, axis=0)


def turn_granules(blocks, size):
    count = len(blocks)
    lanes = count * size
    granule = lax.broadcasted_iota(jnp.int32, blocks[0].shape, 1) // size
    blocks = list(blocks)
    distance = count // 2
    while distance:
        upper = (granule & distance) != 0
        shift = distance * size
        for index in range(count):
            if index & distance:
                continue
            low, high = blocks[index], blocks[index + distance]
            blocks[index] = jnp.where(upper, pltpu.roll(high, shift, 1), low)
            blocks[index + distance] = jnp.where(upper, high, pltpu.roll(low, lanes - shift, 1))
        distance //= 2
    return blocks


def place_in_column(place, far):
    return (far * 5 // 8 + far - place) % far


def own_part_kernel(
    far,
    samples_hbm,
    window_hbm,
    twiddle_hbm,
    gains_hbm,
    own_hbm,
    passed_hbm,
    parcels_hbm,
    samples_ref,
    window_ref,
    twiddle_ref,
    gains_ref,
    direct_ref,
    parcels_ref,
    arrived,
    left,
):
    inputs_here = gains_ref.shape[1]
    frames_here = samples_hbm.shape[1] // NFFT
    blocks = range(NFFT // STEP)
    fetches = []

    def fetch(source, target):
        fetches.append(pltpu.make_async_copy(source, target, arrived.at[len(fetches)]))
        fetches[-1].start()
        return fetches[-1]

    samples_in = fetch(samples_hbm, samples_ref)
    window_in = fetch(window_hbm, window_ref)
    table_in = []
    for block in blocks[: len(blocks) // 2]:
        rows = pl.ds(block * STEP, STEP)
        table_in.append(fetch(twiddle_hbm.at[rows, :], twiddle_ref.at[rows, :]))
    gains_in = fetch(gains_hbm, gains_ref)
    samples_in.wait()
    window_in.wait()
    total = None
    sent = frames_here + EARLY
    for block, table in enumerate(table_in):
        tapped = [
            tapped_block(samples_ref, window_ref, sent, half + block)
            for half in (0, len(table_in))
        ]
        table.wait()
        product = jnp.dot(
            jnp.concatenate(tapped, axis=0),
            twiddle_ref[block * STEP : (block + 1) * STEP, :],
            preferred_element_type=jnp.float32,
        )
        total = product if total is None else total + product
    channel = FIRST + lax.broadcasted_iota(jnp.int32, (1, 2 * CH), 1)
    sign = (1 - 2 * (channel % 2)).astype(jnp.float32)
    direct_ref[...] = total[: sent * inputs_here] + sign * total[sent * inputs_here :]
    own_rows = own_hbm.shape[0]
    passed_rows = passed_hbm.shape[0]
    stores = [
        pltpu.make_async_copy(direct_ref.at[pl.ds(0, own_rows), :], own_hbm, left.at[0]),
        pltpu.make_async_copy(
            direct_ref.at[pl.ds(own_rows, passed_rows), :], passed_hbm, left.at[1]
        ),
    ]
    for store in stores:
        store.start()
    gains_in.wait()
    gain_re = gains_ref[0]
    gain_im = gains_ref[1]
    parts = []
    for frame in range(frames_here + EARLY):
        direct = direct_ref[frame * inputs_here : (frame + 1) * inputs_here, :]
        direct_re = direct[:, :CH]
        direct_im = direct[:, CH:]
        parts.append(
            (
                gain_re * direct_re - gain_im * direct_im,
                gain_re * direct_im + gain_im * direct_re,
            )
        )
    slots = [
        [(part, frame) for frame in range(first, first + 8)]
        for first in range(0, frames_here, 8)
        for part in range(2)
    ]
    slots.append([(part, frames_here + frame) for part in range(2) for frame in range(EARLY)])
    per_far = CH // far
    for place, slot in enumerate(slots):
        columns = slice(place * LANES, (place + 1) * LANES)
        blocks = []
        for half in range(CH // LANES):
            lanes = slice(half * LANES, (half + 1) * LANES)
            blocks += turn_granules([parts[frame][part][:, lanes] for part, frame in slot], per_far)
        listed = sorted(range(far), key=lambda target: place_in_column(target, far))
        for index in range(0, far, 2):
            rows = slice(index * inputs_here, (index + 2) * inputs_here)
            parcels_ref[rows, columns] = jnp.concatenate(
                [blocks[target] for target in listed[index : index + 2]], axis=0
            ).astype(jnp.bfloat16)
        lanes = pl.ds(place * LANES, LANES)
        stores.append(
            pltpu.make_async_copy(
                parcels_ref.at[:, lanes], parcels_hbm.at[:, lanes], left.at[len(stores)]
            )
        )
        stores[-1].start()
    for store in stores:
        store.wait()


def spectra_kernel(passed_ref, own_ref, gains_ref, spectra_ref, rows_ref):
    inputs_here = gains_ref.shape[1]
    frames_here = own_ref.shape[0] // inputs_here
    slabs = CH // LANES
    gain_re = gains_ref[0]
    gain_im = gains_ref[1]
    for frame in range(frames_here):
        block = slice(frame * inputs_here, (frame + 1) * inputs_here)
        direct = own_ref[block, :]
        if frame < TAPS - 1:
            direct = direct + passed_ref[block, :]
        direct_re = direct[:, :CH]
        direct_im = direct[:, CH:]
        rows = pl.ds(frame, inputs_here, stride=frames_here)
        real_part = gain_re * direct_re - gain_im * direct_im
        imag_part = gain_re * direct_im + gain_im * direct_re
        for slab in range(slabs):
            columns = slice(slab * LANES, (slab + 1) * LANES)
            rows_ref[slab, rows, :] = real_part[:, columns]
            rows_ref[slabs + slab, rows, :] = imag_part[:, columns]
    for part in range(2):
        for slab in range(slabs):
            columns = slice(slab * LANES, (slab + 1) * LANES)
            values = rows_ref[part * slabs + slab, : own_ref.shape[0], :]
            spectra_ref[part, :, columns] = values.astype(jnp.bfloat16)


def channel_of(time):
    return time % 4


def place_in_square(member, square):
    return member ^ (3 - 3 * square)


def place_in_plane(near, time, times):
    count = NEAR * times
    middle = NEAR // 2 * times + times // 2
    return 3 * (near * times + time + count - middle) % count


def spread_kernel(mine_ref, parcels_ref, turned_ref):
    count, rows, width = parcels_ref.shape
    times = count // NEAR
    stride = mine_ref.shape[1] // rows
    for place in range(0, mine_ref.shape[1], LANES):
        values = mine_ref[:, place : place + LANES].astype(jnp.float32)
        turned_ref[place : place + LANES, :] = values.T
    for near in range(NEAR):
        for channel in range(stride // NEAR):
            start = near * (stride // NEAR) + channel
            values = turned_ref[pl.ds(start, rows, stride=stride), :].astype(jnp.bfloat16)
            for time in range(times):
                if channel_of(time) == channel:
                    parcels_ref[place_in_plane(near, time, times)] = values


def correlate_kernel(frames_all, inputs_here, place_ref, every_ref, packed_ref):
    count, lines, width = every_ref.shape
    blocks, rows, inputs_all = packed_ref.shape
    times = count // NEAR
    main = lines - 2 * EARLY
    carry = None
    lined = []
    for time in range(times):
        pieces = [every_ref[place_in_plane(near, time, times)] for near in range(NEAR)]
        wide = jnp.concatenate([piece.astype(jnp.float32) for piece in pieces], axis=1)
        tiles = [wide[start : start + 8] for start in range(0, lines, 8)]
        if carry is not None:
            early = lax.broadcasted_iota(jnp.int32, carry.shape, 0) < EARLY
            tiles[0] = tiles[0] + jnp.where(early, carry, 0.0)
            tiles[1] = tiles[1] + jnp.where(early, pltpu.roll(carry, 8 - EARLY, 0), 0.0)
        carry = tiles[-1]
        lined += tiles[:-1]
    far = width // inputs_here
    target = lax.broadcasted_iota(jnp.int32, (1, inputs_all), 1)
    near = target // inputs_here % NEAR
    listed = place_in_column(target // (inputs_here * NEAR), far)
    source = near * width + listed * inputs_here + target % inputs_here
    chosen = lax.broadcasted_iota(jnp.int32, (inputs_all, inputs_all), 0) == source
    ordered = jnp.dot(
        jnp.concatenate(lined, axis=0).astype(jnp.bfloat16),
        chosen.astype(jnp.float32).astype(jnp.bfloat16),
        preferred_element_type=jnp.float32,
    )
    right = ordered.astype(jnp.bfloat16)
    twisted = []
    for start in range(0, times * main, 16):
        twisted.append(ordered[start + 8 : start + 16])
        twisted.append(-ordered[start : start + 8])
    twisted = jnp.concatenate(twisted, axis=0).astype(jnp.bfloat16)
    held = blocks * rows
    first = place_ref[0] * held
    col_index = lax.broadcasted_iota(jnp.int32, (held, inputs_all), 1)
    row_index = lax.broadcasted_iota(jnp.int32, (held, inputs_all), 0) + first
    left = [jnp.where(first == 0, side[:, :held], side[:, held:]) for side in (right, twisted)]
    both = lax.dot_general(
        jnp.concatenate(left, axis=1),
        right,
        (((0,), (0,)), ((), ())),
        preferred_element_type=jnp.float32,
    )
    values = jnp.where(row_index <= col_index, both[:held], both[held:]) * (1.0 / frames_all)
    values = values.astype(jnp.bfloat16)
    for block in range(blocks):
        target = place_in_square(block, place_ref[0])
        packed_ref[target] = values[block * rows : (block + 1) * rows]


def unpack_kernel(place_ref, packed_ref, lines_hbm, lines_ref, left):
    channels, count, width = packed_ref.shape
    tiles = width // LANES
    stores = []
    for first in range(0, count, 16):
        start = first * tiles * channels
        for channel in range(channels):
            values = packed_ref[place_in_square(channel, place_ref[0]), first : first + 16, :]
            values = values.astype(jnp.float32)
            for tile in range(tiles):
                lines = pl.ds(start + tile * channels + channel, 16, stride=tiles * channels)
                lines_ref[lines, :] = values[:, tile * LANES : (tile + 1) * LANES]
        block = pl.ds(start, 16 * tiles * channels)
        stores.append(
            pltpu.make_async_copy(lines_ref.at[block, :], lines_hbm.at[block, :], left.at[len(stores)])
        )
        stores[-1].start()
    for store in stores:
        store.wait()


def body(samples, gains):
    inputs_here = samples.shape[0]
    frames_here = samples.shape[1] // NFFT
    times = lax.axis_size("tm")
    far = lax.axis_size("far")
    groups = far * NEAR
    per_group = CH // groups
    inputs_all = inputs_here * groups
    frames_all = frames_here * times
    block = inputs_here * frames_here

    window = filter_window()
    twiddle = jnp.asarray(build_table(window)[: NFFT // 2])
    window_taps = jnp.asarray(window.astype(np.float32).reshape(TAPS, NFFT))

    sent = frames_here + EARLY
    gains = gains.transpose(0, 2, 1)

    def own_part(*refs):
        own_part_kernel(far, *refs)

    own, passed, parcels = pl.pallas_call(
        own_part,
        out_shape=(
            jax.ShapeDtypeStruct((block, 2 * CH), jnp.float32),
            jax.ShapeDtypeStruct(((TAPS - 1) * inputs_here, 2 * CH), jnp.float32),
            jax.ShapeDtypeStruct((far * inputs_here, sent * 2 * CH // far), jnp.bfloat16),
        ),
        in_specs=[ANY] * 4,
        out_specs=(ANY, ANY, ANY),
        scratch_shapes=[
            pltpu.VMEM(samples.shape, jnp.bfloat16),
            pltpu.VMEM(window_taps.shape, jnp.float32),
            pltpu.VMEM(twiddle.shape, jnp.bfloat16),
            pltpu.VMEM(gains.shape, jnp.float32),
            pltpu.VMEM((sent * inputs_here, 2 * CH), jnp.float32),
            pltpu.VMEM((far * inputs_here, sent * 2 * CH // far), jnp.bfloat16),
            pltpu.SemaphoreType.DMA((3 + NFFT // (2 * STEP),)),
            pltpu.SemaphoreType.DMA((2 + sent // 4,)),
        ],
        compiler_params=pltpu.CompilerParams(vmem_limit_bytes=OWN_PART_VMEM),
        cost_estimate=pl.CostEstimate(
            flops=2 * sent * inputs_here * NFFT * 2 * CH,
            bytes_accessed=3 * 1024 * 1024,
            transcendentals=0,
        ),
        name="own_part",
    )(samples, window_taps, twiddle, gains)

    parcels = parcels.reshape(far, inputs_here, sent * 2 * CH // far)
    column = [sorted(range(far), key=lambda place: place_in_column(place, far))]
    mine = lax.all_to_all(parcels, "far", 0, 0, axis_index_groups=column)
    mine = mine.reshape(far * inputs_here, sent * 2 * CH // far)

    passed = lax.ppermute(passed, "tm", [(source, source + 1) for source in range(times - 1)])
    spectra = pl.pallas_call(
        spectra_kernel,
        out_shape=jax.ShapeDtypeStruct((2, block, CH), jnp.bfloat16),
        in_specs=[VMEM] * 3,
        out_specs=VMEM,
        scratch_shapes=[pltpu.VMEM((2 * CH // LANES, block + frames_here, LANES), jnp.float32)],
        compiler_params=PARAMS,
        cost_estimate=pl.CostEstimate(
            flops=8 * block * 2 * CH, bytes_accessed=1024 * 1024, transcendentals=0
        ),
        name="spectra",
    )(passed, own, gains)
    mine, spectra = lax.optimization_barrier((mine, spectra))
    spectra = spectra.reshape(2, inputs_here, frames_here, CH).transpose(0, 3, 1, 2)

    lines = 2 * sent
    spread = pl.pallas_call(
        spread_kernel,
        out_shape=jax.ShapeDtypeStruct((NEAR * times, lines, far * inputs_here), jnp.bfloat16),
        in_specs=[VMEM],
        out_specs=VMEM,
        scratch_shapes=[pltpu.VMEM(((sent + 1) * 2 * CH // far, far * inputs_here), jnp.float32)],
        compiler_params=PARAMS,
        name="spread",
    )(mine)
    place = lax.axis_index("tm").astype(jnp.int32)
    square = (place // 4)[None]
    spread, square = lax.optimization_barrier((spread, square))
    members = [(near, time) for near in range(NEAR) for time in range(times)]
    members.sort(key=lambda member: place_in_plane(*member, times))
    plane = [[near * times + time for near, time in members]]
    every = lax.all_to_all(spread, ("near", "tm"), 0, 0, axis_index_groups=plane)

    def correlate(*refs):
        correlate_kernel(frames_all, inputs_here, *refs)

    rows = inputs_all // times
    packed = pl.pallas_call(
        correlate,
        out_shape=jax.ShapeDtypeStruct((per_group, rows, inputs_all), jnp.bfloat16),
        in_specs=[SMEM, VMEM],
        out_specs=VMEM,
        compiler_params=PARAMS,
        name="correlate",
    )(square, every)
    squares = [
        [4 * side + place_in_square(member, side) for member in range(per_group)]
        for side in range(2)
    ]
    packed = lax.all_to_all(packed, "tm", 0, 0, axis_index_groups=squares)
    tiles = inputs_all // LANES
    visibilities = pl.pallas_call(
        unpack_kernel,
        out_shape=jax.ShapeDtypeStruct((rows * tiles * per_group, LANES), jnp.float32),
        in_specs=[SMEM, VMEM],
        out_specs=ANY,
        scratch_shapes=[
            pltpu.VMEM(((rows + 1) * tiles * per_group, LANES), jnp.float32),
            pltpu.SemaphoreType.DMA((rows // 16,)),
        ],
        compiler_params=PARAMS,
        name="unpack",
    )(square, packed)
    visibilities = visibilities.reshape(rows, tiles, per_group, LANES).transpose(0, 2, 1, 3)
    visibilities = visibilities.reshape(rows, per_group, inputs_all)
    return (spectra, visibilities)


def solution(mesh):
    groups, times = mesh.devices.shape
    split = Mesh(mesh.devices.reshape(groups // NEAR, NEAR, times), ("far", "near", "tm"))
    inputs = ("far", "near")
    return jax.shard_map(
        body,
        mesh=split,
        in_specs=(P(inputs, "tm"), P(None, None, inputs)),
        out_specs=(P(None, None, inputs, "tm"), P("tm", inputs, None)),
        check_vma=False,
    )
```
